128 devices in a mesh: section: 2 (over x_hi), ctx: 16 (over x_lo, z, core), fsdp: 4 (over y).
Axes of the slice: x: 4 (x_hi: 2, x_lo: 2; x = x_hi * 2 + x_lo), y: 4, z: 4, core: 2. Of those that a mesh axis runs over, the one named last changes fastest.
Arguments:
- inputs: bfloat16 [2, 4, 2048, 768], P(None, 'fsdp', 'ctx'), may hold values from -6 to 6
- out_grad: bfloat16 [2, 4, 2048, 768], P(None, 'fsdp', 'ctx'), may hold values from -6 to 6
- doc_lengths: int32 [2, 4, 4], P(None, 'fsdp'), may hold values from 0 to 2048, as said below
- attn_gain: bfloat16 [2, 768], P('section', 'fsdp'), may hold values from 0.099609375 to 1.8984375
- qkv_weight: bfloat16 [2, 768, 2304], P('section', 'fsdp'), may hold values from -0.21875 to 0.21875
- proj_weight: bfloat16 [2, 768, 768], P('section', 'fsdp'), may hold values from -1.25 to 1.25
- mlp_gain: bfloat16 [2, 768], P('section', 'fsdp'), may hold values from 0.099609375 to 1.8984375
- lift_weight: bfloat16 [2, 768, 2304], P('section', 'fsdp'), may hold values from -0.21875 to 0.21875
- down_weight: bfloat16 [2, 1152, 768], P('section', 'fsdp'), may hold values from -0.1875 to 0.1875
Outputs:
- acts: bfloat16 [2, 2, 4, 2048, 768], P('section', None, 'fsdp', 'ctx')
- in_grads: bfloat16 [2, 2, 4, 2048, 768], P('section', None, 'fsdp', 'ctx')
- attn_gain_grad: float32 [2, 768], P('section', 'fsdp')
- qkv_grad: float32 [2, 768, 2304], P('section', 'fsdp')
- proj_grad: float32 [2, 768, 768], P('section', 'fsdp')
- mlp_gain_grad: float32 [2, 768], P('section', 'fsdp')
- lift_grad: float32 [2, 768, 2304], P('section', 'fsdp')
- down_grad: float32 [2, 1152, 768], P('section', 'fsdp')
The draws below stay inside these ranges and needn't reach their ends.
Inputs may be any that keep to these rules, and one draw needn't show every extreme that they name: `doc_lengths`: each sequence's 4 document lengths sum to 2048; some may be zero; one sequence, chosen at random, is a single document.
All inputs are finite; a program needn't handle non-finite values.
Results may differ from the reference program's by a relative error of at most 0.035.
Values may be sent and summed in bfloat16 or wider, within the bound.
No kernel may reach another device: no remote copies, remote signals or barrier semaphores. Data moves between devices by JAX's collectives and lax.ppermute only.
A program may use at most 128 MiB of HBM per device.

```python
import math
import jax
import jax.numpy as jnp
from jax import lax

D = 768
HEADS = 12
HD = 64
FF = 1152
HALF = 64
DOCS = 4
MB = 2
SEQ_LEN = 2048
SECTIONS = 2
BATCH = 4


def draw_doc_lengths(key, part):
    key = jax.random.fold_in(key, 11)
    cut_key, pick_key = jax.random.split(key)
    seq_count = MB * BATCH
    cut_points = jax.random.randint(cut_key, (seq_count, DOCS - 1), 0, SEQ_LEN + 1)
    cut_points = jnp.sort(cut_points, axis=-1)
    zero_col = jnp.zeros((seq_count, 1), jnp.int32)
    full_col = jnp.full((seq_count, 1), SEQ_LEN, jnp.int32)
    bounds = jnp.concatenate([zero_col, cut_points.astype(jnp.int32), full_col], axis=-1)
    lengths = bounds[:, 1:] - bounds[:, :-1]
    chosen = jax.random.randint(pick_key, (), 0, seq_count)
    whole_row = jnp.where(jnp.arange(DOCS) == 0, SEQ_LEN, 0).astype(jnp.int32)
    marked = (jnp.arange(seq_count) == chosen)[:, None]
    lengths = jnp.where(marked, whole_row[None, :], lengths)
    return lengths.reshape(MB, BATCH, DOCS).astype(jnp.int32)


def levels(own_key, dims, cuts, least, top_value):
    def one(dim, blocks):
        heights = jax.random.uniform(jax.random.fold_in(jax.random.fold_in(own_key, 6), dim), (blocks,), jnp.float32, least / len(cuts), top_value / len(cuts))
        return jnp.repeat(jnp.exp(heights), dims[dim] // blocks).reshape((-1,) + (1,) * (len(dims) - dim - 1))

    factor_of = one(*cuts[0])
    for cut in cuts[1:]:
        factor_of = factor_of * one(*cut)
    return factor_of


def normal_values(own_key, shape, deviation, limit, cuts=(), kind=jnp.bfloat16):
    factor_of = levels(own_key, shape, cuts, -0.22, 0.18) if cuts else 1.0
    array = jax.random.normal(own_key, shape, jnp.float32) * deviation * factor_of
    return jnp.minimum(jnp.maximum(array, -limit), limit).astype(kind)


def setup_inputs(seed: int = 0) -> dict:
    keys = jax.random.split(jax.random.key(seed), 10)
    return {
        "inputs": normal_values(keys[0], (MB, BATCH, SEQ_LEN, D), 1.0, 6.0, ((1, 4), (2, 16))),
        "out_grad": normal_values(keys[1], (MB, BATCH, SEQ_LEN, D), 1.0, 6.0, ((1, 4), (2, 16))),
        "doc_lengths": draw_doc_lengths(jax.random.fold_in(keys[9], 71), 0),
        "attn_gain": jnp.clip(1.0 + 0.18 * jax.random.normal(keys[3], (SECTIONS, D), jnp.float32), 0.099609375, 1.8984375).astype(jnp.bfloat16),
        "qkv_weight": normal_values(keys[4], (SECTIONS, D, 3 * D), D ** -0.5, 0.21875, ((0, 2), (1, 4))),
        "proj_weight": normal_values(keys[5], (SECTIONS, D, D), (D // 32) ** -0.5, 1.25, ((0, 2), (1, 4))),
        "mlp_gain": jnp.clip(1.0 + 0.18 * jax.random.normal(keys[6], (SECTIONS, D), jnp.float32), 0.099609375, 1.8984375).astype(jnp.bfloat16),
        "lift_weight": normal_values(keys[7], (SECTIONS, D, 2 * FF), D ** -0.5, 0.21875, ((0, 2), (1, 4))),
        "down_weight": normal_values(keys[8], (SECTIONS, FF, D), FF ** -0.5, 0.1875, ((0, 2), (1, 4))),
    }


@jax.custom_vjp
def low(v):
    return lax.optimization_barrier(v.astype(jnp.bfloat16)).astype(jnp.float32)

@jax.custom_vjp
def low_back(v):
    return v

def low_keep(v):
    return (low(v), None)

def low_pass(kept, grad):
    return (grad,)

def back_keep(v):
    return (v, None)

def back_low(kept, grad):
    return (low(grad),)
low.defvjp(low_keep, low_pass)
low_back.defvjp(back_keep, back_low)
norm_eps = 1e-05
rope_base = 10000.0
masked_score = -1e+30

def layer_norm(hidden, gain):
    centre = hidden - lax.optimization_barrier(jnp.mean(hidden, axis=-1, keepdims=True))
    scale_inv = lax.rsqrt(lax.optimization_barrier(jnp.mean(centre * centre, axis=-1, keepdims=True)) + norm_eps)
    return centre * scale_inv * gain

def rope_tables(positions):
    half_dim = HD // 2
    frequencies = rope_base ** (-(jnp.arange(half_dim, dtype=jnp.float32) * 2.0) / HD)
    angles = positions.astype(jnp.float32)[:, None] * frequencies[None, :]
    angles = jnp.concatenate([angles, angles], axis=1)
    return (jnp.cos(angles)[:, None, :], jnp.sin(angles)[:, None, :])

def rotate(values_in, cosine_table, sine_table, turn_sign):
    half_dim = values_in.shape[-1] // 2
    turned = jnp.concatenate([-values_in[..., half_dim:], values_in[..., :half_dim]], axis=-1)
    return values_in * cosine_table + turn_sign * (turned * sine_table)

def doc_numbers(positions, lengths):
    doc_ends = jnp.cumsum(lengths)
    return lax.optimization_barrier(jnp.sum((positions[:, None] >= doc_ends[None, :]).astype(jnp.int32), axis=1))

def key_mask(query_pos, key_pos, lengths):
    within = jnp.abs(query_pos[:, None] - key_pos[None, :]) <= HALF
    inside = (key_pos >= 0) & (key_pos < SEQ_LEN)
    same_doc = doc_numbers(query_pos, lengths)[:, None] == doc_numbers(key_pos, lengths)[None, :]
    return within & inside[None, :] & same_doc

def attend(queries, key_rot, values, lengths):
    block_rows = min(512, SEQ_LEN)
    key_span = block_rows + 2 * HALF
    key_pad = jnp.pad(key_rot, ((HALF, HALF), (0, 0), (0, 0)))
    value_pad = jnp.pad(values, ((HALF, HALF), (0, 0), (0, 0)))
    score_scale = 1.0 / math.sqrt(HD)
    highest = lax.Precision.HIGHEST

    def one_block(block_index):
        row_start = block_index * block_rows
        query_blk = lax.dynamic_slice_in_dim(queries, row_start, block_rows, 0)
        key_blk = lax.dynamic_slice_in_dim(key_pad, row_start, key_span, 0)
        value_blk = lax.dynamic_slice_in_dim(value_pad, row_start, key_span, 0)
        query_pos = row_start + jnp.arange(block_rows, dtype=jnp.int32)
        key_pos = row_start - HALF + jnp.arange(key_span, dtype=jnp.int32)
        allowed = key_mask(query_pos, key_pos, lengths)
        scores = low_back(jnp.einsum('ihd,jhd->hij', query_blk, key_blk, precision=highest) * score_scale)
        scores = jnp.where(allowed[None], scores, masked_score)
        row_peak = lax.optimization_barrier(jnp.max(scores, axis=-1, keepdims=True))
        expo_terms = jnp.exp(scores - row_peak)
        attn_probs = expo_terms / lax.optimization_barrier(jnp.sum(expo_terms, axis=-1, keepdims=True))
        return jnp.einsum('hij,jhd->ihd', low(attn_probs), value_blk, precision=highest)
    blocks = lax.map(jax.checkpoint(one_block), jnp.arange(SEQ_LEN // block_rows, dtype=jnp.int32))
    return blocks.reshape(SEQ_LEN, HEADS, HD)

def encoder_layer(params, hidden, lengths):
    attn_gain, qkv_weight, proj_weight, mlp_gain, lift_weight, down_weight = params
    highest = lax.Precision.HIGHEST
    normed = low(layer_norm(hidden, attn_gain))
    packed = low_back(jnp.dot(normed, qkv_weight, precision=highest, preferred_element_type=jnp.float32))
    cosine_table, sine_table = rope_tables(jnp.arange(SEQ_LEN, dtype=jnp.int32))
    queries = low(rotate(packed[:, :D].reshape(SEQ_LEN, HEADS, HD), cosine_table, sine_table, 1.0))
    key_rot = low(rotate(packed[:, D:2 * D].reshape(SEQ_LEN, HEADS, HD), cosine_table, sine_table, 1.0))
    values = low(packed[:, 2 * D:].reshape(SEQ_LEN, HEADS, HD))
    attended = low(low_back(attend(queries, key_rot, values, lengths).reshape(SEQ_LEN, D)))
    mixed_sum = hidden + low_back(jnp.dot(attended, proj_weight, precision=highest, preferred_element_type=jnp.float32))
    mlp_input = low(layer_norm(mixed_sum, mlp_gain))
    lifted = low_back(jnp.dot(mlp_input, lift_weight, precision=highest, preferred_element_type=jnp.float32))
    active = low(jax.nn.gelu(lifted[:, :FF], approximate=False) * lifted[:, FF:])
    return mixed_sum + low_back(jnp.dot(active, down_weight, precision=highest, preferred_element_type=jnp.float32))

def reference(inputs, out_grad, doc_lengths, attn_gain, qkv_weight, proj_weight, mlp_gain, lift_weight, down_weight):
    stacked = tuple((a.astype(jnp.float32) for a in (attn_gain, qkv_weight, proj_weight, mlp_gain, lift_weight, down_weight)))
    first_params = tuple((a[0] for a in stacked))
    second_params = tuple((a[1] for a in stacked))
    seq_count = MB * BATCH
    seq_inputs = inputs.astype(jnp.float32).reshape(seq_count, SEQ_LEN, D)
    seq_cots = out_grad.astype(jnp.float32).reshape(seq_count, SEQ_LEN, D)
    seq_lengths = doc_lengths.reshape(seq_count, DOCS)

    def one_sequence(totals, scan_item):
        hidden, cotangent, lengths = scan_item

        def both_layers(hidden_in, probe_zero, first_set, second_set):
            low_four = low(encoder_layer(first_set, hidden_in, lengths))
            low_five = low(encoder_layer(second_set, low_back(low_four + probe_zero), lengths))
            return (low_four, low_five)
        probe_zero = jnp.zeros_like(hidden)
        (act_four, act_five), pullback = jax.vjp(both_layers, hidden, probe_zero, first_params, second_params)
        grad_in, grad_probe, grad_first, grad_second = pullback((jnp.zeros_like(act_four), cotangent))
        totals = jax.tree.map(lambda total, first_term, second_term: total + jnp.stack([first_term, second_term]), totals, grad_first, grad_second)
        return (totals, (act_four, act_five, grad_in, grad_probe))
    zero_grads = tuple((jnp.zeros_like(a) for a in stacked))
    totals, (act_four, act_five, grad_in, grad_probe) = lax.scan(one_sequence, zero_grads, (seq_inputs, seq_cots, seq_lengths))
    out_shape = (MB, BATCH, SEQ_LEN, D)
    acts = jnp.stack([act_four.reshape(out_shape), act_five.reshape(out_shape)]).astype(jnp.bfloat16)
    in_grads = jnp.stack([grad_in.reshape(out_shape), grad_probe.reshape(out_shape)]).astype(jnp.bfloat16)
    return (acts, in_grads, totals[0], totals[1], totals[2], totals[3], totals[4], totals[5])
```

```python
import functools

import jax
import jax.numpy as jnp
from jax import lax
from jax.experimental import pallas as pl
from jax.experimental.pallas import tpu as pltpu
from jax.sharding import PartitionSpec as P

D = 768
HD = 64
HALF = 64
SEQ_LEN = 2048
FF = 1152
WIDE = 2304
ROWS = 128
EXT = ROWS + 2 * HALF
MICRO = 2
OWN = MICRO * ROWS
SHARDS = 4
TILES = D // 128
norm_eps = 1e-05
rope_base = 10000.0
masked_score = -1e30
root_half = 0.7071067811865476
inv_root_tau = 0.3989422804014327
F32 = jnp.float32
BF16 = jnp.bfloat16


def mm(left, right):
    return lax.dot_general(left, right, (((1,), (0,)), ((), ())), preferred_element_type=F32)


def mm_nt(left, right):
    return lax.dot_general(left, right, (((1,), (1,)), ((), ())), preferred_element_type=F32)


def mm_tn(left, right):
    return lax.dot_general(left, right, (((0,), (0,)), ((), ())), preferred_element_type=F32)


def norm_parts(hidden):
    centre = hidden - jnp.mean(hidden, axis=-1, keepdims=True)
    inv_scale = lax.rsqrt(jnp.mean(centre * centre, axis=-1, keepdims=True) + norm_eps)
    return centre * inv_scale, inv_scale


def norm_back(grad_out, gain, normed, inv_scale):
    grad_normed = grad_out * gain
    inner = (
        grad_normed
        - jnp.mean(grad_normed, axis=-1, keepdims=True)
        - normed * jnp.mean(grad_normed * normed, axis=-1, keepdims=True)
    )
    return inner * inv_scale


def lane_is_low(shape, period):
    return lax.broadcasted_iota(jnp.int32, shape, 1) % period < period // 2


def turn(x):
    return jnp.where(lane_is_low(x.shape, HD), pltpu.roll(x, 96, 1), pltpu.roll(x, 32, 1))


def rotate(x, cosine, sine):
    return x * cosine + turn(x) * sine


def rotate_back(x, cosine, sine):
    return x * cosine - turn(x) * sine


def stack_heads(x):
    low = lane_is_low(x.shape, 128)
    zero = jnp.zeros_like(x)
    return jnp.concatenate([jnp.where(low, x, zero), jnp.where(low, zero, x)], axis=0)


def join_heads(x):
    half = x.shape[0] // 2
    low = lane_is_low((half, 128), 128)
    return jnp.where(low, x[:half], x[half:])


def start_weights(packed, buffers, sems, wanted):
    qkv, proj, lift, down = buffers
    waits = {}

    def go(name, index, src, dst):
        copy = pltpu.make_async_copy(src, dst, sems.at[index])
        copy.start()
        waits.setdefault(name, []).append(copy)

    shard_rows = packed.shape[0] // SHARDS
    for name in wanted:
        for f in range(SHARDS):
            at = f * shard_rows
            if name == "qkv":
                go(name, f, packed.at[pl.ds(at, 192)], qkv.at[pl.ds(f * 192, 192)])
            if name == "lift":
                go(name, 4 + f, packed.at[pl.ds(at + 192, 192)], lift.at[pl.ds(f * 192, 192)])
            for block in range(3):
                cols = pl.ds(block * D, D)
                if name == "proj":
                    go(
                        name,
                        8 + 3 * f + block,
                        packed.at[pl.ds(at + 384, 64), cols],
                        proj.at[pl.ds(f * 192 + block * 64, 64)],
                    )
                if name == "down":
                    go(
                        name,
                        20 + 3 * f + block,
                        packed.at[pl.ds(at + 448, 96), cols],
                        down.at[pl.ds(f * 288 + block * 96, 96)],
                    )
    return waits


def finish(waits, name):
    for copy in waits[name]:
        copy.wait()


def load_stream(flag, own, low, high, other, ext):
    for m in range(MICRO):
        for ref, alt, start, size in (
            (low, other[1], 0, HALF),
            (own, other[0], HALF, ROWS),
            (high, other[2], HALF + ROWS, HALF),
        ):
            value = ref[m]
            if alt is not None:
                value = jnp.where(flag, value, alt[m])
            ext[pl.ds(m * EXT + start, size), :] = value


def own_rows(x):
    return jnp.concatenate([x[HALF : HALF + ROWS], x[EXT + HALF : EXT + HALF + ROWS]], axis=0)


def forward_attention(ext, gain, wqkv, cos_ref, sin_ref, bias_ref, a_ext, q_ref, k_ref, v_ref, p_ref, o_ref):
    normed, _ = norm_parts(ext[...].astype(F32))
    a_ext[...] = (normed * gain).astype(BF16)
    a_own = own_rows(a_ext[...])
    cosine, sine = cos_ref[...], sin_ref[...]
    cos_own, sin_own = cosine[HALF : HALF + ROWS], sine[HALF : HALF + ROWS]
    for t in range(3):
        queries = mm(a_own, wqkv[:, 256 * t : 256 * t + 256])
        for s in range(2):
            cols = pl.ds(256 * t + 128 * s, 128)
            for m in range(MICRO):
                part = queries[m * ROWS : (m + 1) * ROWS, 128 * s : 128 * s + 128]
                q_ref[pl.ds(m * ROWS, ROWS), cols] = rotate(part, cos_own, sin_own).astype(
                    BF16
                ) * jnp.asarray(0.125, BF16)
        keys = mm(a_ext[...], wqkv[:, D + 256 * t : D + 256 * t + 256])
        for s in range(2):
            cols = pl.ds(256 * t + 128 * s, 128)
            for m in range(MICRO):
                part = keys[m * EXT : (m + 1) * EXT, 128 * s : 128 * s + 128]
                k_ref[pl.ds(m * EXT, EXT), cols] = rotate(part, cosine, sine).astype(BF16)
        values = mm(a_ext[...], wqkv[:, 2 * D + 256 * t : 2 * D + 256 * t + 256])
        v_ref[:, pl.ds(256 * t, 256)] = values.astype(BF16)

    def unit(t, carry):
        cols = pl.ds(pl.multiple_of(t * 128, 128), 128)
        for m in range(MICRO):
            q2 = stack_heads(q_ref[pl.ds(m * ROWS, ROWS), cols])
            keys = k_ref[pl.ds(m * EXT, EXT), cols]
            values = v_ref[pl.ds(m * EXT, EXT), cols]
            bias = bias_ref[m]
            scores = mm_nt(q2, keys) + jnp.concatenate([bias, bias], axis=0)
            peak = jnp.max(scores, axis=-1, keepdims=True)
            terms = jnp.exp(scores - peak)
            probs = (terms * (1.0 / jnp.sum(terms, axis=-1, keepdims=True))).astype(BF16)
            p_ref[m, t] = probs
            o_ref[pl.ds(m * ROWS, ROWS), cols] = join_heads(mm(probs, values)).astype(BF16)
        return carry

    lax.fori_loop(0, TILES, unit, 0)


def forward_mlp(ext, o_ref, wproj, mlp_gain, wlift, wdown, h2_ref, m_ref, left_ref, right_ref, waits):
    hidden = own_rows(ext[...]).astype(F32)
    finish(waits, "proj")
    mixed = hidden + mm(o_ref[...], wproj[...])
    h2_ref[...] = mixed
    normed, _ = norm_parts(mixed)
    b = (normed * mlp_gain).astype(BF16)
    finish(waits, "lift")
    for t in range(FF // 128):
        cols = pl.ds(128 * t, 128)
        gate = mm(b, wlift[:, 128 * t : 128 * t + 128])
        up = mm(b, wlift[:, FF + 128 * t : FF + 128 * t + 128])
        cdf = 0.5 * (1.0 + lax.erf(gate * root_half))
        gelu = gate * cdf
        m_ref[:, cols] = (gelu * up).astype(BF16)
        if left_ref is not None:
            pdf = jnp.exp(-0.5 * gate * gate) * inv_root_tau
            left_ref[:, cols] = up * (cdf + gate * pdf)
            right_ref[:, cols] = gelu
    finish(waits, "down")
    return mixed + mm(m_ref[...], wdown[...])


def backward_mlp(grad_low, h2_ref, mlp_gain, wproj, wlift, wdown, left_ref, right_ref, du_ref, do_ref):
    for t in range(3):
        cols = pl.ds(384 * t, 384)
        dm = mm_nt(grad_low, wdown[384 * t : 384 * t + 384, :])
        du_ref[:, cols] = (dm * left_ref[:, cols]).astype(BF16)
        du_ref[:, pl.ds(FF + 384 * t, 384)] = (dm * right_ref[:, cols]).astype(BF16)
    db = mm_nt(du_ref[...], wlift[...])
    normed, inv_scale = norm_parts(h2_ref[...])
    gain_grad = jnp.sum(db * normed, axis=0, keepdims=True)
    dh2 = grad_low.astype(F32) + norm_back(db, mlp_gain, normed, inv_scale)
    gb = dh2.astype(BF16)
    do_ref[...] = mm_nt(gb, wproj[...]).astype(BF16)
    return dh2, gb, gain_grad, normed


def backward_attention(q_ref, k_ref, v_ref, p_ref, do_ref, cos_ref, sin_ref, dq_ref, dkv_ref, low_ref, high_ref):
    cosine, sine = cos_ref[...], sin_ref[...]
    cos_own, sin_own = cosine[HALF : HALF + ROWS], sine[HALF : HALF + ROWS]

    def unit(t, carry):
        cols = pl.ds(pl.multiple_of(t * 128, 128), 128)
        value_cols = pl.ds(pl.multiple_of(D + t * 128, 128), 128)
        for m in range(MICRO):
            rows = pl.ds(m * ROWS, ROWS)
            q2 = stack_heads(q_ref[rows, cols])
            keys = k_ref[pl.ds(m * EXT, EXT), cols]
            values = v_ref[pl.ds(m * EXT, EXT), cols]
            do2 = stack_heads(do_ref[rows, cols])
            probs = p_ref[m, t]
            dprobs = mm_nt(do2, values)
            wide = probs.astype(F32)
            inner = jnp.sum(wide * dprobs, axis=-1, keepdims=True)
            ds = (wide * (dprobs - inner)).astype(BF16)
            dq = join_heads(mm(ds, keys)) * 0.125
            dq_ref[rows, cols] = rotate_back(dq, cos_own, sin_own).astype(BF16)
            dk = rotate_back(mm_tn(ds, q2), cosine, sine)
            dv = mm_tn(probs, do2)
            for grad, where in ((dk, cols), (dv, value_cols)):
                low_ref[m, :, where] = grad[:HALF].astype(BF16)
                dkv_ref[rows, where] = grad[HALF : HALF + ROWS]
                high_ref[m, :, where] = grad[HALF + ROWS :].astype(BF16)
        return carry

    lax.fori_loop(0, TILES, unit, 0)


def forward_kernel(own, low, high, gains, cos_ref, sin_ref, bias_ref, packed, h3_ref,
                   wqkv, wproj, wlift, wdown, ext, a_ext, q, k, v, p, o, h2, m_out, sems):
    waits = start_weights(packed, (wqkv, wproj, wlift, wdown), sems, ("qkv", "proj", "lift", "down"))
    load_stream(None, own, low, high, (None, None, None), ext)
    finish(waits, "qkv")
    forward_attention(ext, gains[0:1], wqkv, cos_ref, sin_ref, bias_ref, a_ext, q, k, v, p, o)
    h3 = forward_mlp(ext, o, wproj, gains[1:2], wlift, wdown, h2, m_out, None, None, waits)
    for m in range(MICRO):
        h3_ref[m] = h3[m * ROWS : (m + 1) * ROWS].astype(BF16)


def turning_kernel(flag_ref, own, low, high, other_own, other_low, other_high, cotangent, gains,
                   cos_ref, sin_ref, bias_ref, packed,
                   h3_ref, q, k, v, p, o, h2, m_out, left, right, src, dh2_ref, dq, dkv, to_low, to_high,
                   wqkv, wproj, wlift, wdown, ext, a_ext, du, do, sems):
    waits = start_weights(packed, (wqkv, wproj, wlift, wdown), sems, ("qkv", "proj", "lift", "down"))
    flag = flag_ref[0] == 1
    load_stream(flag, own, low, high, (other_own, other_low, other_high), ext)
    src[...] = own_rows(ext[...])
    finish(waits, "qkv")
    forward_attention(ext, gains[0:1], wqkv, cos_ref, sin_ref, bias_ref, a_ext, q, k, v, p, o)
    h3 = forward_mlp(ext, o, wproj, gains[1:2], wlift, wdown, h2, m_out, left, right, waits)
    for m in range(MICRO):
        h3_ref[m] = h3[m * ROWS : (m + 1) * ROWS].astype(BF16)
    grad_low = jnp.concatenate([cotangent[0], cotangent[1]], axis=0)
    dh2, _, _, _ = backward_mlp(grad_low, h2, gains[1:2], wproj, wlift, wdown, left, right, du, do)
    dh2_ref[...] = dh2
    backward_attention(q, k, v, p, do, cos_ref, sin_ref, dq, dkv, to_low, to_high)


def back_kernel(flag_ref, incoming, cotangent, gains, cos_ref, sin_ref, packed, q, k, v, p, h2, left, right,
                grad_ref, du, gb_ref, b_ref, mlp_ref, dh2_ref, dq, dkv, to_low, to_high,
                wproj, wlift, wdown, do, sems):
    waits = start_weights(packed, (None, wproj, wlift, wdown), sems, ("down", "lift", "proj"))
    flag = flag_ref[0] == 1
    grad_low = jnp.concatenate(
        [jnp.where(flag, incoming[m], cotangent[m]) for m in range(MICRO)], axis=0
    )
    grad_ref[...] = grad_low
    for name in ("down", "lift", "proj"):
        finish(waits, name)
    dh2, gb, gain_grad, normed = backward_mlp(
        grad_low, h2, gains[1:2], wproj, wlift, wdown, left, right, du, do
    )
    gb_ref[...] = gb
    b_ref[...] = (normed * gains[1:2]).astype(BF16)
    mlp_ref[...] = gain_grad
    dh2_ref[...] = dh2
    backward_attention(q, k, v, p, do, cos_ref, sin_ref, dq, dkv, to_low, to_high)


def joined_grads(dq, dkv, from_low, from_high, dqkv):
    dqkv[:, :D] = dq[...]
    for m in range(MICRO):
        first, last = pl.ds(m * ROWS, HALF), pl.ds(m * ROWS + HALF, HALF)
        dqkv[first, D:] = (dkv[first, :] + from_low[m].astype(F32)).astype(BF16)
        dqkv[last, D:] = (dkv[last, :] + from_high[m].astype(F32)).astype(BF16)


def source_kernel(src, gains, dh2, dq, dkv, from_low, from_high, packed, out_ref, wqkv, dqkv, sems):
    waits = start_weights(packed, (wqkv, None, None, None), sems, ("qkv",))
    joined_grads(dq, dkv, from_low, from_high, dqkv)
    normed, inv_scale = norm_parts(src[...].astype(F32))
    finish(waits, "qkv")
    da = mm_nt(dqkv[...], wqkv[...])
    dh = dh2[...] + norm_back(da, gains[0:1], normed, inv_scale)
    for m in range(MICRO):
        out_ref[m] = dh[m * ROWS : (m + 1) * ROWS].astype(BF16)


def source_grad_kernel(src, gains, dh2, dq, dkv, from_low, from_high, packed, out_ref, attn_ref, qkv_ref,
                       wqkv, dqkv, sems):
    waits = start_weights(packed, (wqkv, None, None, None), sems, ("qkv",))
    joined_grads(dq, dkv, from_low, from_high, dqkv)
    normed, inv_scale = norm_parts(src[...].astype(F32))
    a = (normed * gains[0:1]).astype(BF16)
    for t in range(9):
        cols = pl.ds(256 * t, 256)
        qkv_ref[:, cols] = mm_tn(a, dqkv[:, cols]).astype(BF16)
    finish(waits, "qkv")
    da = mm_nt(dqkv[...], wqkv[...])
    attn_ref[...] = jnp.sum(da * normed, axis=0, keepdims=True)
    dh = dh2[...] + norm_back(da, gains[0:1], normed, inv_scale)
    for m in range(MICRO):
        out_ref[m] = dh[m * ROWS : (m + 1) * ROWS].astype(BF16)


def weight_grad_kernel(m_ref, grad_ref, b_ref, du, o_ref, gb_ref, down_ref, lift_ref, proj_ref):
    for t in range(3):
        cols = pl.ds(256 * t, 256)
        down_ref[:, cols] = mm_tn(m_ref[...], grad_ref[:, cols]).astype(BF16)
        proj_ref[:, cols] = mm_tn(o_ref[...], gb_ref[:, cols]).astype(BF16)
    for t in range(9):
        cols = pl.ds(256 * t, 256)
        lift_ref[:, cols] = mm_tn(b_ref[...], du[:, cols]).astype(BF16)


def vmem(count):
    return [pl.BlockSpec(memory_space=pltpu.VMEM)] * count


def call(kernel, name, ins, outs, scratch, flops):
    places = {"v": pltpu.VMEM, "a": pl.ANY, "s": pltpu.SMEM}
    return pl.pallas_call(
        kernel,
        name=name,
        out_shape=[jax.ShapeDtypeStruct(shape, kind) for shape, kind in outs],
        in_specs=[pl.BlockSpec(memory_space=places[place]) for _, place in ins],
        out_specs=vmem(len(outs)),
        scratch_shapes=scratch,
        compiler_params=pltpu.CompilerParams(vmem_limit_bytes=56 * 2**20),
        cost_estimate=pl.CostEstimate(flops=flops, bytes_accessed=10 * 2**20, transcendentals=0),
    )(*[array for array, _ in ins])


def halo_rows(block, axis):
    count = lax.axis_size(axis)
    up = [(i, i + 1) for i in range(count - 1)]
    down = [(i + 1, i) for i in range(count - 1)]
    return (
        lax.ppermute(block[:, ROWS - HALF :], axis, up),
        lax.ppermute(block[:, :HALF], axis, down),
    )


def tables(first_row, lengths):
    half = HD // 2
    frequencies = rope_base ** (-(jnp.arange(half, dtype=F32) * 2.0) / HD)
    positions = first_row - HALF + jnp.arange(EXT, dtype=jnp.int32)
    angles = positions.astype(F32)[:, None] * frequencies[None, :]
    cosine, sine = jnp.cos(angles), jnp.sin(angles)
    cosine = jnp.concatenate([cosine] * 4, axis=1)
    sine = jnp.concatenate([-sine, sine, -sine, sine], axis=1)
    ends = jnp.cumsum(lengths, axis=1)
    doc = jnp.sum((positions[None, :, None] >= ends[:, None, :]).astype(jnp.int32), axis=2)
    query = positions[HALF : HALF + ROWS]
    allowed = (
        (jnp.abs(query[:, None] - positions[None, :]) <= HALF)
        & (positions >= 0)[None, :]
        & (positions < SEQ_LEN)[None, :]
    )[None] & (doc[:, HALF : HALF + ROWS, None] == doc[:, None, :])
    return cosine, sine, jnp.where(allowed, 0.0, masked_score).astype(F32)


def pack_weights(qkv, lift, proj, down):
    thirds = lambda w: jnp.concatenate(jnp.split(w, 3, axis=0), axis=1)
    return jnp.concatenate([qkv, lift, thirds(proj), thirds(down)], axis=0)


def unpack_grads(block):
    wide = lambda w: jnp.concatenate(jnp.split(w, 3, axis=1), axis=0)
    return block[:192], block[192:384], wide(block[384:448]), wide(block[448:544])


WEIGHTS = [
    pltpu.VMEM((D, WIDE), BF16),
    pltpu.VMEM((D, D), BF16),
    pltpu.VMEM((D, WIDE), BF16),
    pltpu.VMEM((FF, D), BF16),
]
SEMS = pltpu.SemaphoreType.DMA((32,))
SAVED = [
    ((OWN, D), BF16),
    ((MICRO * EXT, D), BF16),
    ((MICRO * EXT, D), BF16),
    ((MICRO, TILES, 2 * ROWS, EXT), BF16),
    ((OWN, D), BF16),
    ((OWN, D), F32),
    ((OWN, FF), BF16),
    ((OWN, FF), F32),
    ((OWN, FF), F32),
]
STREAM = [pltpu.VMEM((MICRO * EXT, D), BF16)] * 2
GRADS_OUT = [
    ((OWN, D), F32),
    ((OWN, D), BF16),
    ((OWN, 2 * D), F32),
    ((MICRO, HALF, 2 * D), BF16),
    ((MICRO, HALF, 2 * D), BF16),
]


def body(
    inputs, out_grad, doc_lengths, attn_gain, qkv_weight, proj_weight, mlp_gain, lift_weight, down_weight
):
    on_first = lax.axis_index("section") == 0
    flag = on_first.astype(jnp.int32).reshape(1)
    packed = lax.all_gather(
        pack_weights(qkv_weight[0], lift_weight[0], proj_weight[0], down_weight[0]),
        "fsdp", axis=0, tiled=True,
    )
    gains = lax.all_gather(
        jnp.stack([attn_gain[0], mlp_gain[0]]), "fsdp", axis=1, tiled=True
    ).astype(F32)
    first_row = lax.axis_index("ctx") * ROWS
    cosine, sine, bias = tables(first_row, doc_lengths[:, 0])
    own, cotangent = inputs[:, 0], out_grad[:, 0]
    low, high = halo_rows(own, "ctx")
    stream = ((MICRO, ROWS, D), BF16)

    (relay,) = call(
        forward_kernel, "layer_forward",
        [(own, "v"), (low, "v"), (high, "v"), (gains, "v"), (cosine, "v"), (sine, "v"), (bias, "v"), (packed, "a")],
        [stream],
        WEIGHTS + STREAM + [pltpu.VMEM(s, k) for s, k in SAVED[:7]] + [SEMS],
        3_200_000_000,
    )
    relayed = lax.ppermute(relay, "section", [(0, 1)])
    other_low, other_high = halo_rows(relayed, "ctx")
    (h3, q, k, v, p, o, h2, m_act, left, right, src, dh2, dq, dkv, to_low, to_high) = call(
        turning_kernel, "layer_turn",
        [(flag, "s"), (own, "v"), (low, "v"), (high, "v"), (relayed, "v"), (other_low, "v"), (other_high, "v"),
         (cotangent, "v"), (gains, "v"), (cosine, "v"), (sine, "v"), (bias, "v"), (packed, "a")],
        [stream] + SAVED + [((OWN, D), BF16)] + GRADS_OUT,
        WEIGHTS + STREAM + [pltpu.VMEM((OWN, WIDE), BF16), pltpu.VMEM((OWN, D), BF16), SEMS],
        6_000_000_000,
    )

    def swap_halos(to_low, to_high):
        count = lax.axis_size("ctx")
        up = [(i, i + 1) for i in range(count - 1)]
        down = [(i + 1, i) for i in range(count - 1)]
        return lax.ppermute(to_high, "ctx", up), lax.ppermute(to_low, "ctx", down)

    from_low, from_high = swap_halos(to_low, to_high)
    (grad_relay,) = call(
        source_kernel, "layer_source",
        [(src, "v"), (gains, "v"), (dh2, "v"), (dq, "v"), (dkv, "v"), (from_low, "v"), (from_high, "v"), (packed, "a")],
        [stream],
        [WEIGHTS[0], pltpu.VMEM((OWN, WIDE), BF16), SEMS],
        900_000_000,
    )
    incoming = lax.ppermute(grad_relay, "section", [(1, 0)])
    (grad_low, du, gb, b, mlp_gain_grad, dh2, dq, dkv, to_low, to_high) = call(
        back_kernel, "layer_back",
        [(flag, "s"), (incoming, "v"), (cotangent, "v"), (gains, "v"), (cosine, "v"), (sine, "v"), (packed, "a"),
         (q, "v"), (k, "v"), (v, "v"), (p, "v"), (h2, "v"), (left, "v"), (right, "v")],
        [((OWN, D), BF16), ((OWN, WIDE), BF16), ((OWN, D), BF16), ((OWN, D), BF16), ((1, D), F32)] + GRADS_OUT,
        [*WEIGHTS[1:], pltpu.VMEM((OWN, D), BF16), SEMS],
        3_000_000_000,
    )
    from_low, from_high = swap_halos(to_low, to_high)
    down_grad, lift_grad, proj_grad = call(
        weight_grad_kernel, "weight_grads",
        [(m_act, "v"), (grad_low, "v"), (b, "v"), (du, "v"), (o, "v"), (gb, "v")],
        [((FF, D), BF16), ((D, WIDE), BF16), ((D, D), BF16)],
        [],
        1_600_000_000,
    )
    in_grad, attn_gain_grad, qkv_grad = call(
        source_grad_kernel, "layer_source_grads",
        [(src, "v"), (gains, "v"), (dh2, "v"), (dq, "v"), (dkv, "v"), (from_low, "v"), (from_high, "v"), (packed, "a")],
        [stream, ((1, D), F32), ((D, WIDE), BF16)],
        [WEIGHTS[0], pltpu.VMEM((OWN, WIDE), BF16), SEMS],
        1_800_000_000,
    )
    scatter = lambda g: lax.psum_scatter(g, "fsdp", scatter_dimension=0, tiled=True)
    finals = lax.psum(
        [scatter(g) for g in (qkv_grad, lift_grad, proj_grad, down_grad)], "ctx"
    )
    qkv_sum, lift_sum, proj_sum, down_sum = [g.astype(F32) for g in finals]
    gain_sums = lax.psum(
        lax.psum_scatter(
            jnp.concatenate([attn_gain_grad, mlp_gain_grad], axis=0), "fsdp", scatter_dimension=1, tiled=True
        ),
        "ctx",
    )
    return (
        h3_pair(h3, relay, on_first)[None, :, None],
        in_grad[None, :, None],
        gain_sums[0][None],
        qkv_sum[None],
        proj_sum[None],
        gain_sums[1][None],
        lift_sum[None],
        down_sum[None],
    )


def h3_pair(h3, relay, on_first):
    return h3


def solution(mesh):
    placed = (
        P(None, "fsdp", "ctx", None),
        P(None, "fsdp", "ctx", None),
        P(None, "fsdp", None),
        P("section", "fsdp"),
        P("section", "fsdp", None),
        P("section", "fsdp", None),
        P("section", "fsdp"),
        P("section", "fsdp", None),
        P("section", "fsdp", None),
    )
    return jax.shard_map(
        body,
        mesh=mesh,
        in_specs=placed,
        out_specs=(
            P("section", None, "fsdp", "ctx", None),
            P("section", None, "fsdp", "ctx", None),
            P("section", "fsdp"),
            P("section", "fsdp", None),
            P("section", "fsdp", None),
            P("section", "fsdp"),
            P("section", "fsdp", None),
            P("section", "fsdp", None),
        ),
        check_vma=False,
    )
```

```python
import functools

import jax
import jax.numpy as jnp
from jax import lax
from jax.experimental import pallas as pl
from jax.experimental.pallas import tpu as pltpu
from jax.sharding import PartitionSpec as P

D = 768
HD = 64
HALF = 64
SEQ_LEN = 2048
FF = 1152
WIDE = 2304
ROWS = 128
EXT = ROWS + 2 * HALF
MICRO = 2
OWN = MICRO * ROWS
SHARDS = 4
TILES = D // 128
norm_eps = 1e-05
rope_base = 10000.0
masked_score = -1e30
root_half = 0.7071067811865476
inv_root_tau = 0.3989422804014327
F32 = jnp.float32
BF16 = jnp.bfloat16


def mm(left, right):
    return lax.dot_general(left, right, (((1,), (0,)), ((), ())), preferred_element_type=F32)


def mm_nt(left, right):
    return lax.dot_general(left, right, (((1,), (1,)), ((), ())), preferred_element_type=F32)


def mm_tn(left, right):
    return lax.dot_general(left, right, (((0,), (0,)), ((), ())), preferred_element_type=F32)


def norm_parts(hidden):
    centre = hidden - jnp.mean(hidden, axis=-1, keepdims=True)
    inv_scale = lax.rsqrt(jnp.mean(centre * centre, axis=-1, keepdims=True) + norm_eps)
    return centre * inv_scale, inv_scale


def norm_back(grad_out, gain, normed, inv_scale):
    grad_normed = grad_out * gain
    inner = (
        grad_normed
        - jnp.mean(grad_normed, axis=-1, keepdims=True)
        - normed * jnp.mean(grad_normed * normed, axis=-1, keepdims=True)
    )
    return inner * inv_scale


def lane_is_low(shape, period):
    return lax.broadcasted_iota(jnp.int32, shape, 1) % period < period // 2


def turn(x):
    return jnp.where(lane_is_low(x.shape, HD), pltpu.roll(x, 96, 1), pltpu.roll(x, 32, 1))


def rotate(x, cosine, sine):
    return x * cosine + turn(x) * sine


def rotate_back(x, cosine, sine):
    return x * cosine - turn(x) * sine


def stack_heads(x):
    low = lane_is_low(x.shape, 128)
    zero = jnp.zeros_like(x)
    return jnp.concatenate([jnp.where(low, x, zero), jnp.where(low, zero, x)], axis=0)


def join_heads(x):
    half = x.shape[0] // 2
    low = lane_is_low((half, 128), 128)
    return jnp.where(low, x[:half], x[half:])


def start_weights(sources, buffers, sems):
    waits = {}
    for index, (name, source) in enumerate(sources.items()):
        copy = pltpu.make_async_copy(source, buffers[name], sems.at[index])
        copy.start()
        waits[name] = [copy]
    return waits


def finish(waits, name):
    for copy in waits[name]:
        copy.wait()


def load_stream(flag, own, low, high, other, ext):
    for m in range(MICRO):
        for ref, alt, start, size in (
            (low, other[1], 0, HALF),
            (own, other[0], HALF, ROWS),
            (high, other[2], HALF + ROWS, HALF),
        ):
            value = ref[m]
            if alt is not None:
                value = jnp.where(flag, value, alt[m])
            ext[pl.ds(m * EXT + start, size), :] = value


def own_rows(x):
    return jnp.concatenate([x[HALF : HALF + ROWS], x[EXT + HALF : EXT + HALF + ROWS]], axis=0)


def forward_attention(ext, gain, wqkv, cos_ref, sin_ref, bias_ref, a_ext, q_ref, k_ref, v_ref, p_ref, o_ref):
    normed, _ = norm_parts(ext[...].astype(F32))
    a_ext[...] = (normed * gain).astype(BF16)
    a_own = own_rows(a_ext[...])
    cosine, sine = cos_ref[...], sin_ref[...]
    cos_own, sin_own = cosine[HALF : HALF + ROWS], sine[HALF : HALF + ROWS]
    for t in range(3):
        queries = mm(a_own, wqkv[:, 256 * t : 256 * t + 256])
        for s in range(2):
            cols = pl.ds(256 * t + 128 * s, 128)
            for m in range(MICRO):
                part = queries[m * ROWS : (m + 1) * ROWS, 128 * s : 128 * s + 128]
                q_ref[pl.ds(m * ROWS, ROWS), cols] = rotate(part, cos_own, sin_own).astype(
                    BF16
                ) * jnp.asarray(0.125, BF16)
        keys = mm(a_ext[...], wqkv[:, D + 256 * t : D + 256 * t + 256])
        for s in range(2):
            cols = pl.ds(256 * t + 128 * s, 128)
            for m in range(MICRO):
                part = keys[m * EXT : (m + 1) * EXT, 128 * s : 128 * s + 128]
                k_ref[pl.ds(m * EXT, EXT), cols] = rotate(part, cosine, sine).astype(BF16)
        values = mm(a_ext[...], wqkv[:, 2 * D + 256 * t : 2 * D + 256 * t + 256])
        v_ref[:, pl.ds(256 * t, 256)] = values.astype(BF16)

    def unit(t, carry):
        cols = pl.ds(pl.multiple_of(t * 128, 128), 128)
        for m in range(MICRO):
            q2 = stack_heads(q_ref[pl.ds(m * ROWS, ROWS), cols])
            keys = k_ref[pl.ds(m * EXT, EXT), cols]
            values = v_ref[pl.ds(m * EXT, EXT), cols]
            bias = bias_ref[m]
            scores = mm_nt(q2, keys) + jnp.concatenate([bias, bias], axis=0)
            peak = jnp.max(scores, axis=-1, keepdims=True)
            terms = jnp.exp(scores - peak)
            probs = (terms * (1.0 / jnp.sum(terms, axis=-1, keepdims=True))).astype(BF16)
            p_ref[m, t] = probs
            o_ref[pl.ds(m * ROWS, ROWS), cols] = join_heads(mm(probs, values)).astype(BF16)
        return carry

    lax.fori_loop(0, TILES, unit, 0)


def forward_mlp(hidden, o_ref, wproj, mlp_gain, wlift, wdown, h2_ref, m_ref, left_ref, right_ref, waits):
    finish(waits, "proj")
    mixed = hidden + mm(o_ref[...], wproj[...])
    h2_ref[...] = mixed
    normed, _ = norm_parts(mixed)
    b = (normed * mlp_gain).astype(BF16)
    finish(waits, "lift")
    for t in range(FF // 128):
        cols = pl.ds(128 * t, 128)
        gate = mm(b, wlift[:, 128 * t : 128 * t + 128])
        up = mm(b, wlift[:, FF + 128 * t : FF + 128 * t + 128])
        cdf = 0.5 * (1.0 + lax.erf(gate * root_half))
        gelu = gate * cdf
        m_ref[:, cols] = (gelu * up).astype(BF16)
        if left_ref is not None:
            pdf = jnp.exp(-0.5 * gate * gate) * inv_root_tau
            left_ref[:, cols] = up * (cdf + gate * pdf)
            right_ref[:, cols] = gelu
    finish(waits, "down")
    return mixed + mm(m_ref[...], wdown[...])


def backward_mlp(grad_low, h2_ref, mlp_gain, wproj, wlift, wdown, left_ref, right_ref, du_ref, do_ref):
    for t in range(3):
        cols = pl.ds(384 * t, 384)
        dm = mm_nt(grad_low, wdown[384 * t : 384 * t + 384, :])
        du_ref[:, cols] = (dm * left_ref[:, cols]).astype(BF16)
        du_ref[:, pl.ds(FF + 384 * t, 384)] = (dm * right_ref[:, cols]).astype(BF16)
    db = mm_nt(du_ref[...], wlift[...])
    normed, inv_scale = norm_parts(h2_ref[...])
    gain_grad = jnp.sum(db * normed, axis=0, keepdims=True)
    dh2 = grad_low.astype(F32) + norm_back(db, mlp_gain, normed, inv_scale)
    gb = dh2.astype(BF16)
    do_ref[...] = mm_nt(gb, wproj[...]).astype(BF16)
    return dh2, gb, gain_grad, normed


def backward_attention(q_ref, k_ref, v_ref, p_ref, do_ref, cos_ref, sin_ref, dq_ref, dkv_ref, low_ref, high_ref):
    cosine, sine = cos_ref[...], sin_ref[...]
    cos_own, sin_own = cosine[HALF : HALF + ROWS], sine[HALF : HALF + ROWS]

    def unit(t, carry):
        cols = pl.ds(pl.multiple_of(t * 128, 128), 128)
        value_cols = pl.ds(pl.multiple_of(D + t * 128, 128), 128)
        for m in range(MICRO):
            rows = pl.ds(m * ROWS, ROWS)
            q2 = stack_heads(q_ref[rows, cols])
            keys = k_ref[pl.ds(m * EXT, EXT), cols]
            values = v_ref[pl.ds(m * EXT, EXT), cols]
            do2 = stack_heads(do_ref[rows, cols])
            probs = p_ref[m, t]
            dprobs = mm_nt(do2, values)
            wide = probs.astype(F32)
            inner = jnp.sum(wide * dprobs, axis=-1, keepdims=True)
            ds = (wide * (dprobs - inner)).astype(BF16)
            dq = join_heads(mm(ds, keys)) * 0.125
            dq_ref[rows, cols] = rotate_back(dq, cos_own, sin_own).astype(BF16)
            dk = rotate_back(mm_tn(ds, q2), cosine, sine)
            dv = mm_tn(probs, do2)
            for grad, where in ((dk, cols), (dv, value_cols)):
                low_ref[m, :, where] = grad[:HALF].astype(BF16)
                dkv_ref[rows, where] = grad[HALF : HALF + ROWS]
                high_ref[m, :, where] = grad[HALF + ROWS :].astype(BF16)
        return carry

    lax.fori_loop(0, TILES, unit, 0)


def place_shards(index, own, first, first_other, second, second_other, put):
    f, core = index[1], index[2]
    put(own, f, None)
    put(first, lax.rem(f + 3 + 2 * core, 4), None)
    put(first_other, lax.rem(f + 1 + 2 * core, 4), None)
    put(second, lax.rem(f + 2, 4), core)
    put(second_other, lax.rem(f + 2, 4), 1 - core)


def pack_kernel(index, qkv, lift, proj, down, qkv_half, rest, rest_half, sems):
    core = index[2]
    copies = []

    def go(src, dst):
        copy = pltpu.make_async_copy(src, dst, sems.at[len(copies)])
        copy.start()
        copies.append(copy)

    half = lambda size: pl.ds(pl.multiple_of(core * size, 16), size)
    go(qkv.at[half(96)], qkv_half)
    go(lift, rest.at[pl.ds(0, 192)])
    go(lift.at[half(96)], rest_half.at[pl.ds(0, 96)])
    for block in range(3):
        cols = pl.ds(block * D, D)
        go(proj.at[pl.ds(64 * block, 64)], rest.at[pl.ds(192, 64), cols])
        go(down.at[pl.ds(96 * block, 96)], rest.at[pl.ds(256, 96), cols])
        go(
            proj.at[pl.ds(pl.multiple_of(64 * block + core * 32, 16), 32)],
            rest_half.at[pl.ds(96, 32), cols],
        )
        go(
            down.at[pl.ds(pl.multiple_of(96 * block + core * 48, 16), 48)],
            rest_half.at[pl.ds(128, 48), cols],
        )
    for copy in copies:
        copy.wait()


def forward_attention_kernel(index, own, low, high, gains, cos_ref, sin_ref, bias_ref,
                             shard, first, first_other, second, second_other,
                             o, whole, wqkv, ext, a_ext, q, k, v, p, sems, out_sem):
    copies = []

    def put(piece, f, half):
        at, size = (f * 192, 192) if half is None else (f * 192 + half * 96, 96)
        copy = pltpu.make_async_copy(
            piece, wqkv.at[pl.ds(pl.multiple_of(at, 16), size)], sems.at[len(copies)]
        )
        copy.start()
        copies.append(copy)

    place_shards(index, shard, first, first_other, second, second_other, put)
    load_stream(None, own, low, high, (None, None, None), ext)
    for copy in copies:
        copy.wait()
    out = pltpu.make_async_copy(wqkv, whole, out_sem)
    out.start()
    forward_attention(ext, gains[0:1], wqkv, cos_ref, sin_ref, bias_ref, a_ext, q, k, v, p, o)
    out.wait()


def forward_mlp_kernel(index, own, o, gains, lift, proj, down, first, first_other, second, second_other,
                       h3_ref, whole_proj, whole_lift, whole_down, wproj, wlift, wdown, h2, m_out, sems):
    waits = {"proj": [], "lift": [], "down": []}
    count = [0]

    def go(name, src, dst):
        copy = pltpu.make_async_copy(src, dst, sems.at[count[0]])
        copy.start()
        count[0] += 1
        waits[name].append(copy)

    f = index[1]

    def put(piece, s, half):
        rows = lambda at, size: pl.ds(pl.multiple_of(at, 16), size)
        if piece is None:
            go("proj", proj, wproj.at[rows(f * 192, 192)])
            go("lift", lift, wlift.at[rows(f * 192, 192)])
            go("down", down, wdown.at[rows(f * 288, 288)])
            return
        n = 2 if half is None else 1
        h = 0 if half is None else half
        go("lift", piece.at[pl.ds(0, 96 * n)], wlift.at[rows(s * 192 + h * 96, 96 * n)])
        for b in range(3):
            cols = pl.ds(b * D, D)
            go("proj", piece.at[pl.ds(96 * n, 32 * n), cols], wproj.at[rows(s * 192 + b * 64 + h * 32, 32 * n)])
            go("down", piece.at[pl.ds(128 * n, 48 * n), cols], wdown.at[rows(s * 288 + b * 96 + h * 48, 48 * n)])

    place_shards(index, None, first, first_other, second, second_other, put)
    outs = []
    for name, buffer, whole in (("proj", wproj, whole_proj), ("lift", wlift, whole_lift), ("down", wdown, whole_down)):
        finish(waits, name)
        copy = pltpu.make_async_copy(buffer, whole, sems.at[count[0]])
        copy.start()
        count[0] += 1
        outs.append(copy)
        waits[name] = []
    hidden = jnp.concatenate([own[0], own[1]], axis=0).astype(F32)
    h3 = forward_mlp(hidden, o, wproj, gains[1:2], wlift, wdown, h2, m_out, None, None, waits)
    for m in range(MICRO):
        h3_ref[m] = h3[m * ROWS : (m + 1) * ROWS].astype(BF16)
    for copy in outs:
        copy.wait()


def turning_kernel(flag_ref, own, low, high, other_own, other_low, other_high, cotangent, gains,
                   cos_ref, sin_ref, bias_ref, qkv_hbm, proj_hbm, lift_hbm, down_hbm,
                   h3_ref, q, k, v, p, o, h2, m_out, left, right, src, dh2_ref, dq, dkv, to_low, to_high,
                   wqkv, wproj, wlift, wdown, ext, a_ext, du, do, sems):
    waits = start_weights(
        {"qkv": qkv_hbm, "proj": proj_hbm, "lift": lift_hbm, "down": down_hbm},
        {"qkv": wqkv, "proj": wproj, "lift": wlift, "down": wdown}, sems,
    )
    flag = flag_ref[0] == 1
    load_stream(flag, own, low, high, (other_own, other_low, other_high), ext)
    src[...] = own_rows(ext[...])
    finish(waits, "qkv")
    forward_attention(ext, gains[0:1], wqkv, cos_ref, sin_ref, bias_ref, a_ext, q, k, v, p, o)
    h3 = forward_mlp(src[...].astype(F32), o, wproj, gains[1:2], wlift, wdown, h2, m_out, left, right, waits)
    for m in range(MICRO):
        h3_ref[m] = h3[m * ROWS : (m + 1) * ROWS].astype(BF16)
    grad_low = jnp.concatenate([cotangent[0], cotangent[1]], axis=0)
    dh2, _, _, _ = backward_mlp(grad_low, h2, gains[1:2], wproj, wlift, wdown, left, right, du, do)
    dh2_ref[...] = dh2
    backward_attention(q, k, v, p, do, cos_ref, sin_ref, dq, dkv, to_low, to_high)


def back_kernel(flag_ref, incoming, cotangent, gains, cos_ref, sin_ref, proj_hbm, lift_hbm, down_hbm,
                q, k, v, p, h2, left, right,
                grad_ref, du, gb_ref, b_ref, mlp_ref, dh2_ref, dq, dkv, to_low, to_high,
                wproj, wlift, wdown, do, sems):
    waits = start_weights(
        {"down": down_hbm, "lift": lift_hbm, "proj": proj_hbm},
        {"down": wdown, "lift": wlift, "proj": wproj}, sems,
    )
    flag = flag_ref[0] == 1
    grad_low = jnp.concatenate(
        [jnp.where(flag, incoming[m], cotangent[m]) for m in range(MICRO)], axis=0
    )
    grad_ref[...] = grad_low
    for name in ("down", "lift", "proj"):
        finish(waits, name)
    dh2, gb, gain_grad, normed = backward_mlp(
        grad_low, h2, gains[1:2], wproj, wlift, wdown, left, right, du, do
    )
    gb_ref[...] = gb
    b_ref[...] = (normed * gains[1:2]).astype(BF16)
    mlp_ref[...] = gain_grad
    dh2_ref[...] = dh2
    backward_attention(q, k, v, p, do, cos_ref, sin_ref, dq, dkv, to_low, to_high)


def joined_grads(dq, dkv, from_low, from_high, dqkv):
    dqkv[:, :D] = dq[...]
    for m in range(MICRO):
        first, last = pl.ds(m * ROWS, HALF), pl.ds(m * ROWS + HALF, HALF)
        dqkv[first, D:] = (dkv[first, :] + from_low[m].astype(F32)).astype(BF16)
        dqkv[last, D:] = (dkv[last, :] + from_high[m].astype(F32)).astype(BF16)


def source_kernel(src, gains, dh2, dq, dkv, from_low, from_high, qkv_hbm, out_ref, wqkv, dqkv, sems):
    waits = start_weights({"qkv": qkv_hbm}, {"qkv": wqkv}, sems)
    joined_grads(dq, dkv, from_low, from_high, dqkv)
    normed, inv_scale = norm_parts(src[...].astype(F32))
    finish(waits, "qkv")
    da = mm_nt(dqkv[...], wqkv[...])
    dh = dh2[...] + norm_back(da, gains[0:1], normed, inv_scale)
    for m in range(MICRO):
        out_ref[m] = dh[m * ROWS : (m + 1) * ROWS].astype(BF16)


def gain_block(attn, mlp, f):
    rows = []
    for gain in (attn, mlp):
        rows.append(gain[:, 192 * f : 192 * f + 128])
        rows.append(jnp.concatenate([gain[:, 192 * f + 128 : 192 * f + 192], jnp.zeros((1, 64), F32)], axis=1))
    return jnp.concatenate(rows + [jnp.zeros((92, 128), F32)], axis=0).astype(BF16)


def source_grad_kernel(index, src, gains, dh2, dq, dkv, from_low, from_high, mlp_grad, qkv_hbm,
                       out_ref, keep, send, wqkv, dqkv, qkv_ref, gain_ref, sems):
    waits = start_weights({"qkv": qkv_hbm}, {"qkv": wqkv}, sems)
    joined_grads(dq, dkv, from_low, from_high, dqkv)
    normed, inv_scale = norm_parts(src[...].astype(F32))
    finish(waits, "qkv")
    da = mm_nt(dqkv[...], wqkv[...])
    attn_grad = jnp.sum(da * normed, axis=0, keepdims=True)
    mlp = mlp_grad[...]
    for f in range(SHARDS):
        gain_ref[f] = gain_block(attn_grad, mlp, f)
    a = (normed * gains[0:1]).astype(BF16)
    for t in range(9):
        cols = pl.ds(256 * t, 256)
        qkv_ref[:, cols] = mm_tn(a, dqkv[:, cols]).astype(BF16)
    copies = []
    for target, half in ((send, 1 - index[2]), (keep, index[2])):
        for f in range(SHARDS):
            rows = pl.ds(pl.multiple_of(f * 192 + half * 96, 16), 96)
            for src_ref, dst_ref in (
                (qkv_ref.at[rows], target.at[f, :, pl.ds(0, WIDE)]),
                (gain_ref.at[f], target.at[f, :, pl.ds(WIDE, 128)]),
            ):
                copy = pltpu.make_async_copy(src_ref, dst_ref, sems.at[1 + len(copies)])
                copy.start()
                copies.append(copy)
    dh = dh2[...] + norm_back(da, gains[0:1], normed, inv_scale)
    for m in range(MICRO):
        out_ref[m] = dh[m * ROWS : (m + 1) * ROWS].astype(BF16)
    for copy in copies:
        copy.wait()


def weight_grad_kernel(index, m_ref, grad_ref, b_ref, du, o_ref, gb_ref, keep, send,
                       down_ref, lift_ref, proj_ref, pad_ref, sems):
    core = index[2]
    copies = []

    def go(src, dst):
        copy = pltpu.make_async_copy(src, dst, sems.at[len(copies)])
        copy.start()
        copies.append(copy)

    sides = ((send, 1 - core), (keep, core))
    rows = lambda at, size: pl.ds(pl.multiple_of(at, 16), size)
    pad_ref[...] = jnp.zeros_like(pad_ref)
    for target, _ in sides:
        for f in range(SHARDS):
            go(pad_ref, target.at[f, pl.ds(176, 16)])
    for t in range(9):
        cols = pl.ds(256 * t, 256)
        lift_ref[:, cols] = mm_tn(b_ref[...], du[:, cols]).astype(BF16)
    for target, half in sides:
        for f in range(SHARDS):
            go(lift_ref.at[rows(f * 192 + half * 96, 96)], target.at[f, pl.ds(0, 96)])
    for t in range(3):
        cols = pl.ds(256 * t, 256)
        down_ref[:, cols] = mm_tn(m_ref[...], grad_ref[:, cols]).astype(BF16)
        proj_ref[:, cols] = mm_tn(o_ref[...], gb_ref[:, cols]).astype(BF16)
    for target, half in sides:
        for f in range(SHARDS):
            for b in range(3):
                cols = pl.ds(b * D, D)
                go(proj_ref.at[rows(f * 192 + b * 64 + half * 32, 32)], target.at[f, pl.ds(96, 32), cols])
                go(down_ref.at[rows(f * 288 + b * 96 + half * 48, 48)], target.at[f, pl.ds(128, 48), cols])
    for copy in copies:
        copy.wait()


def add_up(parts):
    total = parts[0].astype(F32)
    for part in parts[1:]:
        total = total + part.astype(F32)
    return total.astype(BF16)


def rest_core_kernel(index, keep, other, *outs):
    for d, out in enumerate(outs):
        rows = pl.ds(pl.multiple_of(lax.rem(index[0] + d, 4) * 48, 16), 48)
        for f in range(SHARDS):
            out[f] = add_up([keep[f, rows, :], other[f, rows, :]])


def rest_z_kernel(index, own, a, b, c, *outs):
    for d, out in enumerate(outs):
        f = lax.rem(index[1] + d, 4)
        out[...] = add_up([own[f], a[f], b[f], c[f]])


def qkv_core_kernel(index, keep, other, *outs):
    for d, out in enumerate(outs):
        f = lax.rem(index[1] + d, 4)
        out[...] = add_up([keep[f], other[f]])


def qkv_y_kernel(index, own, a, b, c, out_0, out_1, out_2, out_3, total):
    total[...] = add_up([own[...], a[...], b[...], c[...]])
    for d, out in enumerate((out_0, out_1, out_2, out_3)):
        z = lax.rem(index[0] + d, 4)
        rows = pl.ds(pl.multiple_of(lax.div(z, 2) * 48, 16), 48)
        cols = pl.ds(pl.multiple_of(lax.rem(z, 2) * 1152, 128), 1152)
        out[:, pl.ds(0, 1152)] = total[rows, cols]
        out[:, pl.ds(1152, 128)] = total[pl.ds(0, 48), pl.ds(WIDE, 128)]


def joint_kernel(r0, r1, r2, r3, q0, q1, q2, q3, out):
    out[:, pl.ds(0, WIDE)] = add_up([r0[...], r1[...], r2[...], r3[...]])
    out[:, pl.ds(WIDE, 1280)] = add_up([q0[...], q1[...], q2[...], q3[...]])


def pair_kernel(a, b, out):
    out[...] = add_up([a[...], b[...]])


def final_kernel(index, *refs):
    pieces, (qkv_out, proj_out, lift_out, down_out, gain_out, rest) = refs[:8], refs[8:]
    core = index[2]
    for side in range(2):
        half = core if side == 0 else 1 - core
        for d in range(4):
            piece = pieces[4 * side + d]
            z = lax.rem(index[0] - d + 4, 4)
            rest[side, pl.ds(pl.multiple_of(z * 48, 16), 48), :] = piece[:, pl.ds(0, WIDE)]
            qkv_out[
                pl.ds(pl.multiple_of(half * 96 + lax.div(z, 2) * 48, 16), 48),
                pl.ds(pl.multiple_of(lax.rem(z, 2) * 1152, 128), 1152),
            ] = piece[:, pl.ds(WIDE, 1152)].astype(F32)
        rows = lambda at, size: pl.ds(pl.multiple_of(at, 16), size)
        lift_out[rows(half * 96, 96), :] = rest[side, pl.ds(0, 96), :].astype(F32)
        for b in range(3):
            cols = pl.ds(b * D, D)
            proj_out[rows(b * 64 + half * 32, 32), :] = rest[side, pl.ds(96, 32), cols].astype(F32)
            down_out[rows(b * 96 + half * 48, 48), :] = rest[side, pl.ds(128, 48), cols].astype(F32)
    gain_out[...] = pieces[0][pl.ds(0, 16), pl.ds(WIDE + 1152, 128)].astype(F32)


def call(kernel, name, ins, outs, scratch, flops, limit=56):
    places = {"v": pltpu.VMEM, "a": pl.ANY, "s": pltpu.SMEM}
    return pl.pallas_call(
        kernel,
        name=name,
        out_shape=[jax.ShapeDtypeStruct(out[0], out[1]) for out in outs],
        in_specs=[pl.BlockSpec(memory_space=places[place]) for _, place in ins],
        out_specs=[pl.BlockSpec(memory_space=places[out[2] if len(out) > 2 else "v"]) for out in outs],
        scratch_shapes=scratch,
        compiler_params=pltpu.CompilerParams(vmem_limit_bytes=limit * 2**20),
        cost_estimate=pl.CostEstimate(flops=flops, bytes_accessed=10 * 2**20, transcendentals=0),
    )(*[array for array, _ in ins])


def travel(block, target):
    pairs = []
    for ctx in range(16):
        for f in range(SHARDS):
            xlo, z, core, g = target(ctx // 8, ctx // 2 % 4, ctx % 2, f)
            pairs.append((ctx * SHARDS + f, (xlo * 8 + z % 4 * 2 + core) * SHARDS + g % 4))
    return lax.ppermute(block, ("ctx", "fsdp"), pairs)


def along_y(block, d):
    return travel(block, lambda x, z, c, f: (x, z, c, f + d))


def along_z(block, d):
    return travel(block, lambda x, z, c, f: (x, z + d, c, f))


def swap_core(block):
    return travel(block, lambda x, z, c, f: (x, z, 1 - c, f))


def swap_x(block):
    return travel(block, lambda x, z, c, f: (1 - x, z, c, f))


def gather_pieces(whole, half):
    first = travel(whole, lambda x, z, c, f: (x, z, c, f + 1 - 2 * c))
    second = along_y(half, 2)
    return first, swap_core(first), second, swap_core(second)


def gather_gains(gains, f):
    parts = [along_y(gains, 3), along_y(gains, 2), along_y(gains, 1), gains]
    twice = jnp.stack(parts + parts[:3])
    ordered = lax.dynamic_slice_in_dim(twice, 3 - f, 4, 0)
    return ordered.transpose(1, 0, 2).reshape(2, D)


def halo_rows(block, axis):
    count = lax.axis_size(axis)
    up = [(i, i + 1) for i in range(count - 1)]
    down = [(i + 1, i) for i in range(count - 1)]
    return (
        lax.ppermute(block[:, ROWS - HALF :], axis, up),
        lax.ppermute(block[:, :HALF], axis, down),
    )


def swap_halos(to_low, to_high):
    count = lax.axis_size("ctx")
    up = [(i, i + 1) for i in range(count - 1)]
    down = [(i + 1, i) for i in range(count - 1)]
    return lax.ppermute(to_high, "ctx", up), lax.ppermute(to_low, "ctx", down)


def tables(first_row, lengths):
    half = HD // 2
    frequencies = rope_base ** (-(jnp.arange(half, dtype=F32) * 2.0) / HD)
    positions = first_row - HALF + jnp.arange(EXT, dtype=jnp.int32)
    angles = positions.astype(F32)[:, None] * frequencies[None, :]
    cosine, sine = jnp.cos(angles), jnp.sin(angles)
    cosine = jnp.concatenate([cosine] * 4, axis=1)
    sine = jnp.concatenate([-sine, sine, -sine, sine], axis=1)
    ends = jnp.cumsum(lengths, axis=1)
    doc = jnp.sum((positions[None, :, None] >= ends[:, None, :]).astype(jnp.int32), axis=2)
    query = positions[HALF : HALF + ROWS]
    allowed = (
        (jnp.abs(query[:, None] - positions[None, :]) <= HALF)
        & (positions >= 0)[None, :]
        & (positions < SEQ_LEN)[None, :]
    )[None] & (doc[:, HALF : HALF + ROWS, None] == doc[:, None, :])
    return cosine, sine, jnp.where(allowed, 0.0, masked_score).astype(F32)


WQKV, WPROJ, WLIFT, WDOWN = [
    pltpu.VMEM((D, WIDE), BF16),
    pltpu.VMEM((D, D), BF16),
    pltpu.VMEM((D, WIDE), BF16),
    pltpu.VMEM((FF, D), BF16),
]
SAVED = [
    ((OWN, D), BF16),
    ((MICRO * EXT, D), BF16),
    ((MICRO * EXT, D), BF16),
    ((MICRO, TILES, 2 * ROWS, EXT), BF16),
    ((OWN, D), BF16),
    ((OWN, D), F32),
    ((OWN, FF), BF16),
    ((OWN, FF), F32),
    ((OWN, FF), F32),
]
STREAM = [pltpu.VMEM((MICRO * EXT, D), BF16)] * 2
GRADS_OUT = [
    ((OWN, D), F32),
    ((OWN, D), BF16),
    ((OWN, 2 * D), F32),
    ((MICRO, HALF, 2 * D), BF16),
    ((MICRO, HALF, 2 * D), BF16),
]


def sems(count):
    return pltpu.SemaphoreType.DMA((count,))


def body(
    inputs, out_grad, doc_lengths, attn_gain, qkv_weight, proj_weight, mlp_gain, lift_weight, down_weight
):
    on_first = lax.axis_index("section") == 0
    flag = on_first.astype(jnp.int32).reshape(1)
    ctx, f = lax.axis_index("ctx"), lax.axis_index("fsdp")
    index = jnp.stack([ctx // 2 % 4, f, ctx % 2]).astype(jnp.int32)
    qkv_shard, lift_shard, proj_shard, down_shard = qkv_weight[0], lift_weight[0], proj_weight[0], down_weight[0]
    qkv_half, rest, rest_half = call(
        pack_kernel, "pack_weights",
        [(index, "s"), (qkv_shard, "a"), (lift_shard, "a"), (proj_shard, "a"), (down_shard, "a")],
        [((96, WIDE), BF16, "a"), ((352, WIDE), BF16, "a"), ((176, WIDE), BF16, "a")],
        [sems(15)], 0, 8,
    )
    qkv_pieces = gather_pieces(qkv_shard, qkv_half)
    rest_pieces = gather_pieces(rest, rest_half)
    gains = gather_gains(jnp.stack([attn_gain[0], mlp_gain[0]]).astype(F32), f)
    cosine, sine, bias = tables(ctx * ROWS, doc_lengths[:, 0])
    own, cotangent = inputs[:, 0], out_grad[:, 0]
    low, high = halo_rows(own, "ctx")
    stream = ((MICRO, ROWS, D), BF16)
    scratch = lambda items: [pltpu.VMEM(s, k) for s, k in items]

    o, wqkv = call(
        forward_attention_kernel, "forward_attention",
        [(index, "s"), (own, "v"), (low, "v"), (high, "v"), (gains, "v"), (cosine, "v"), (sine, "v"), (bias, "v"),
         (qkv_shard, "a"), *[(piece, "a") for piece in qkv_pieces]],
        [((OWN, D), BF16), ((D, WIDE), BF16, "a")],
        [WQKV] + STREAM + scratch(SAVED[:4]) + [sems(5), pltpu.SemaphoreType.DMA(())],
        1_400_000_000,
    )
    relay, wproj, wlift, wdown = call(
        forward_mlp_kernel, "forward_mlp",
        [(index, "s"), (own, "v"), (o, "v"), (gains, "v"), (lift_shard, "a"), (proj_shard, "a"), (down_shard, "a"),
         *[(piece, "a") for piece in rest_pieces]],
        [stream, ((D, D), BF16, "a"), ((D, WIDE), BF16, "a"), ((FF, D), BF16, "a")],
        [WPROJ, WLIFT, WDOWN] + scratch(SAVED[5:7]) + [sems(34)],
        1_800_000_000,
    )
    relayed = lax.ppermute(relay, "section", [(0, 1)])
    other_low, other_high = halo_rows(relayed, "ctx")
    (h3, q, k, v, p, o, h2, m_act, left, right, src, dh2, dq, dkv, to_low, to_high) = call(
        turning_kernel, "layer_turn",
        [(flag, "s"), (own, "v"), (low, "v"), (high, "v"), (relayed, "v"), (other_low, "v"), (other_high, "v"),
         (cotangent, "v"), (gains, "v"), (cosine, "v"), (sine, "v"), (bias, "v"),
         (wqkv, "a"), (wproj, "a"), (wlift, "a"), (wdown, "a")],
        [stream] + SAVED + [((OWN, D), BF16)] + GRADS_OUT,
        [WQKV, WPROJ, WLIFT, WDOWN] + STREAM
        + [pltpu.VMEM((OWN, WIDE), BF16), pltpu.VMEM((OWN, D), BF16), sems(4)],
        6_000_000_000,
    )
    from_low, from_high = swap_halos(to_low, to_high)
    (grad_relay,) = call(
        source_kernel, "layer_source",
        [(src, "v"), (gains, "v"), (dh2, "v"), (dq, "v"), (dkv, "v"), (from_low, "v"), (from_high, "v"), (wqkv, "a")],
        [stream],
        [WQKV, pltpu.VMEM((OWN, WIDE), BF16), sems(1)],
        900_000_000,
    )
    incoming = lax.ppermute(grad_relay, "section", [(1, 0)])
    (grad_low, du, gb, b, mlp_gain_grad, dh2, dq, dkv, to_low, to_high) = call(
        back_kernel, "layer_back",
        [(flag, "s"), (incoming, "v"), (cotangent, "v"), (gains, "v"), (cosine, "v"), (sine, "v"),
         (wproj, "a"), (wlift, "a"), (wdown, "a"),
         (q, "v"), (k, "v"), (v, "v"), (p, "v"), (h2, "v"), (left, "v"), (right, "v")],
        [((OWN, D), BF16), ((OWN, WIDE), BF16), ((OWN, D), BF16), ((OWN, D), BF16), ((1, D), F32)] + GRADS_OUT,
        [WPROJ, WLIFT, WDOWN, pltpu.VMEM((OWN, D), BF16), sems(3)],
        3_000_000_000,
    )
    from_low, from_high = swap_halos(to_low, to_high)
    rest_keep, rest_send = call(
        weight_grad_kernel, "weight_grads",
        [(index, "s"), (m_act, "v"), (grad_low, "v"), (b, "v"), (du, "v"), (o, "v"), (gb, "v")],
        [((SHARDS, 192, WIDE), BF16, "a")] * 2,
        [WDOWN, WLIFT, WPROJ, pltpu.VMEM((16, WIDE), BF16), sems(64)],
        1_600_000_000,
    )
    rest_other = swap_core(rest_send)
    in_grad, qkv_keep, qkv_send = call(
        source_grad_kernel, "layer_source_grads",
        [(index, "s"), (src, "v"), (gains, "v"), (dh2, "v"), (dq, "v"), (dkv, "v"), (from_low, "v"),
         (from_high, "v"), (mlp_gain_grad, "v"), (wqkv, "a")],
        [stream, ((SHARDS, 96, 2432), BF16, "a"), ((SHARDS, 96, 2432), BF16, "a")],
        [WQKV, pltpu.VMEM((OWN, WIDE), BF16), WQKV, pltpu.VMEM((SHARDS, 96, 128), BF16), sems(17)],
        1_800_000_000,
    )
    qkv_other = swap_core(qkv_send)

    rest_z = call(
        rest_core_kernel, "rest_core_sum", [(index, "s"), (rest_keep, "v"), (rest_other, "v")],
        [((SHARDS, 48, WIDE), BF16)] * 4, [], 10_000_000, 24,
    )
    rest_y = call(
        rest_z_kernel, "rest_z_sum",
        [(index, "s"), (rest_z[0], "v"), *[(along_z(rest_z[d], d), "v") for d in (1, 2, 3)]],
        [((48, WIDE), BF16)] * 4, [], 10_000_000, 24,
    )
    qkv_y = call(
        qkv_core_kernel, "qkv_core_sum", [(index, "s"), (qkv_keep, "v"), (qkv_other, "v")],
        [((96, 2432), BF16)] * 4, [], 10_000_000, 24,
    )
    qkv_z = call(
        qkv_y_kernel, "qkv_y_sum",
        [(index, "s"), (qkv_y[0], "v"), *[(along_y(qkv_y[d], d), "v") for d in (1, 2, 3)]],
        [((48, 1280), BF16)] * 4, [pltpu.VMEM((96, 2432), BF16)], 10_000_000, 24,
    )
    (joint,) = call(
        joint_kernel, "joint_sum",
        [(rest_y[0], "v"), *[(along_y(rest_y[d], d), "v") for d in (1, 2, 3)],
         (qkv_z[0], "v"), *[(along_z(qkv_z[d], d), "v") for d in (1, 2, 3)]],
        [((48, 3584), BF16)], [], 10_000_000, 24,
    )
    (joint,) = call(
        pair_kernel, "pair_sum", [(joint, "v"), (swap_x(joint), "v")], [((48, 3584), BF16)], [], 10_000_000, 24
    )
    mine = [joint] + [along_z(joint, d) for d in (1, 2, 3)]
    theirs = [swap_core(piece) for piece in mine]
    qkv_sum, proj_sum, lift_sum, down_sum, gain_sums = call(
        final_kernel, "final_shard", [(index, "s"), *[(piece, "v") for piece in mine + theirs]],
        [((192, WIDE), F32), ((192, D), F32), ((192, WIDE), F32), ((288, D), F32), ((16, 128), F32)],
        [pltpu.VMEM((2, 192, WIDE), BF16)], 10_000_000, 24,
    )
    return (
        h3[None, :, None],
        in_grad[None, :, None],
        gain_sums[0:2].reshape(1, 256)[:, :192],
        qkv_sum[None],
        proj_sum[None],
        gain_sums[2:4].reshape(1, 256)[:, :192],
        lift_sum[None],
        down_sum[None],
    )


def solution(mesh):
    placed = (
        P(None, "fsdp", "ctx", None),
        P(None, "fsdp", "ctx", None),
        P(None, "fsdp", None),
        P("section", "fsdp"),
        P("section", "fsdp", None),
        P("section", "fsdp", None),
        P("section", "fsdp"),
        P("section", "fsdp", None),
        P("section", "fsdp", None),
    )
    return jax.shard_map(
        body,
        mesh=mesh,
        in_specs=placed,
        out_specs=(
            P("section", None, "fsdp", "ctx", None),
            P("section", None, "fsdp", "ctx", None),
            P("section", "fsdp"),
            P("section", "fsdp", None),
            P("section", "fsdp", None),
            P("section", "fsdp"),
            P("section", "fsdp", None),
            P("section", "fsdp", None),
        ),
        check_vma=False,
    )
```

```python
import functools

import jax
import jax.numpy as jnp
from jax import lax
from jax.experimental import pallas as pl
from jax.experimental.pallas import tpu as pltpu
from jax.sharding import PartitionSpec as P

D = 768
HD = 64
HALF = 64
SEQ_LEN = 2048
FF = 1152
WIDE = 2304
ROWS = 128
EXT = ROWS + 2 * HALF
MICRO = 2
OWN = MICRO * ROWS
SHARDS = 4
TILES = D // 128
norm_eps = 1e-05
rope_base = 10000.0
masked_score = -1e30
root_half = 0.7071067811865476
inv_root_tau = 0.3989422804014327
F32 = jnp.float32
BF16 = jnp.bfloat16


def mm(left, right):
    return lax.dot_general(left, right, (((1,), (0,)), ((), ())), preferred_element_type=F32)


def mm_nt(left, right):
    return lax.dot_general(left, right, (((1,), (1,)), ((), ())), preferred_element_type=F32)


def mm_tn(left, right):
    return lax.dot_general(left, right, (((0,), (0,)), ((), ())), preferred_element_type=F32)


def norm_parts(hidden):
    centre = hidden - jnp.mean(hidden, axis=-1, keepdims=True)
    inv_scale = lax.rsqrt(jnp.mean(centre * centre, axis=-1, keepdims=True) + norm_eps)
    return centre * inv_scale, inv_scale


def norm_back(grad_out, gain, normed, inv_scale):
    grad_normed = grad_out * gain
    inner = (
        grad_normed
        - jnp.mean(grad_normed, axis=-1, keepdims=True)
        - normed * jnp.mean(grad_normed * normed, axis=-1, keepdims=True)
    )
    return inner * inv_scale


def lane_is_low(shape, period):
    return lax.broadcasted_iota(jnp.int32, shape, 1) % period < period // 2


def turn(x):
    return jnp.where(lane_is_low(x.shape, HD), pltpu.roll(x, 96, 1), pltpu.roll(x, 32, 1))


def rotate(x, cosine, sine):
    return x * cosine + turn(x) * sine


def rotate_back(x, cosine, sine):
    return x * cosine - turn(x) * sine


def stack_heads(x):
    low = lane_is_low(x.shape, 128)
    zero = jnp.zeros_like(x)
    return jnp.concatenate([jnp.where(low, x, zero), jnp.where(low, zero, x)], axis=0)


def join_heads(x):
    half = x.shape[0] // 2
    low = lane_is_low((half, 128), 128)
    return jnp.where(low, x[:half], x[half:])


def start_weights(sources, buffers, sems):
    waits = {}
    for index, (name, source) in enumerate(sources.items()):
        copy = pltpu.make_async_copy(source, buffers[name], sems.at[index])
        copy.start()
        waits[name] = [copy]
    return waits


def finish(waits, name):
    for copy in waits[name]:
        copy.wait()


def load_stream(flag, own, low, high, other, ext):
    for m in range(MICRO):
        for ref, alt, start, size in (
            (low, other[1], 0, HALF),
            (own, other[0], HALF, ROWS),
            (high, other[2], HALF + ROWS, HALF),
        ):
            value = ref[m]
            if alt is not None:
                value = jnp.where(flag, value, alt[m])
            ext[pl.ds(m * EXT + start, size), :] = value


def own_rows(x):
    return jnp.concatenate([x[HALF : HALF + ROWS], x[EXT + HALF : EXT + HALF + ROWS]], axis=0)


def forward_attention(ext, gain, wqkv, cos_ref, sin_ref, bias_ref, a_ext, q_ref, k_ref, v_ref, p_ref, o_ref):
    normed, _ = norm_parts(ext[...].astype(F32))
    a_ext[...] = (normed * gain).astype(BF16)
    a_own = own_rows(a_ext[...])
    cosine, sine = cos_ref[...], sin_ref[...]
    cos_own, sin_own = cosine[HALF : HALF + ROWS], sine[HALF : HALF + ROWS]
    for t in range(3):
        queries = mm(a_own, wqkv[:, 256 * t : 256 * t + 256])
        for s in range(2):
            cols = pl.ds(256 * t + 128 * s, 128)
            for m in range(MICRO):
                part = queries[m * ROWS : (m + 1) * ROWS, 128 * s : 128 * s + 128]
                q_ref[pl.ds(m * ROWS, ROWS), cols] = rotate(part, cos_own, sin_own).astype(
                    BF16
                ) * jnp.asarray(0.125, BF16)
        keys = mm(a_ext[...], wqkv[:, D + 256 * t : D + 256 * t + 256])
        for s in range(2):
            cols = pl.ds(256 * t + 128 * s, 128)
            for m in range(MICRO):
                part = keys[m * EXT : (m + 1) * EXT, 128 * s : 128 * s + 128]
                k_ref[pl.ds(m * EXT, EXT), cols] = rotate(part, cosine, sine).astype(BF16)
        values = mm(a_ext[...], wqkv[:, 2 * D + 256 * t : 2 * D + 256 * t + 256])
        v_ref[:, pl.ds(256 * t, 256)] = values.astype(BF16)

    def unit(t, carry):
        cols = pl.ds(pl.multiple_of(t * 128, 128), 128)
        for m in range(MICRO):
            q2 = stack_heads(q_ref[pl.ds(m * ROWS, ROWS), cols])
            keys = k_ref[pl.ds(m * EXT, EXT), cols]
            values = v_ref[pl.ds(m * EXT, EXT), cols]
            bias = bias_ref[m]
            scores = mm_nt(q2, keys) + jnp.concatenate([bias, bias], axis=0)
            peak = jnp.max(scores, axis=-1, keepdims=True)
            terms = jnp.exp(scores - peak)
            probs = (terms * (1.0 / jnp.sum(terms, axis=-1, keepdims=True))).astype(BF16)
            p_ref[m, t] = probs
            o_ref[pl.ds(m * ROWS, ROWS), cols] = join_heads(mm(probs, values)).astype(BF16)
        return carry

    lax.fori_loop(0, TILES, unit, 0)


def forward_mlp(hidden, o_ref, wproj, mlp_gain, wlift, wdown, h2_ref, m_ref, left_ref, right_ref, waits):
    finish(waits, "proj")
    mixed = hidden + mm(o_ref[...], wproj[...])
    h2_ref[...] = mixed
    normed, _ = norm_parts(mixed)
    b = (normed * mlp_gain).astype(BF16)
    finish(waits, "lift")
    for t in range(FF // 128):
        cols = pl.ds(128 * t, 128)
        gate = mm(b, wlift[:, 128 * t : 128 * t + 128])
        up = mm(b, wlift[:, FF + 128 * t : FF + 128 * t + 128])
        cdf = 0.5 * (1.0 + lax.erf(gate * root_half))
        gelu = gate * cdf
        m_ref[:, cols] = (gelu * up).astype(BF16)
        if left_ref is not None:
            pdf = jnp.exp(-0.5 * gate * gate) * inv_root_tau
            left_ref[:, cols] = up * (cdf + gate * pdf)
            right_ref[:, cols] = gelu
    finish(waits, "down")
    return mixed + mm(m_ref[...], wdown[...])


def backward_mlp(grad_low, h2_ref, mlp_gain, wproj, wlift, wdown, left_ref, right_ref, du_ref, do_ref):
    for t in range(3):
        cols = pl.ds(384 * t, 384)
        dm = mm_nt(grad_low, wdown[384 * t : 384 * t + 384, :])
        du_ref[:, cols] = (dm * left_ref[:, cols]).astype(BF16)
        du_ref[:, pl.ds(FF + 384 * t, 384)] = (dm * right_ref[:, cols]).astype(BF16)
    db = mm_nt(du_ref[...], wlift[...])
    normed, inv_scale = norm_parts(h2_ref[...])
    gain_grad = jnp.sum(db * normed, axis=0, keepdims=True)
    dh2 = grad_low.astype(F32) + norm_back(db, mlp_gain, normed, inv_scale)
    gb = dh2.astype(BF16)
    do_ref[...] = mm_nt(gb, wproj[...]).astype(BF16)
    return dh2, gb, gain_grad, normed


def backward_attention(q_ref, k_ref, v_ref, p_ref, do_ref, cos_ref, sin_ref, dq_ref, dkv_ref, low_ref, high_ref):
    cosine, sine = cos_ref[...], sin_ref[...]
    cos_own, sin_own = cosine[HALF : HALF + ROWS], sine[HALF : HALF + ROWS]

    def unit(t, carry):
        cols = pl.ds(pl.multiple_of(t * 128, 128), 128)
        value_cols = pl.ds(pl.multiple_of(D + t * 128, 128), 128)
        for m in range(MICRO):
            rows = pl.ds(m * ROWS, ROWS)
            q2 = stack_heads(q_ref[rows, cols])
            keys = k_ref[pl.ds(m * EXT, EXT), cols]
            values = v_ref[pl.ds(m * EXT, EXT), cols]
            do2 = stack_heads(do_ref[rows, cols])
            probs = p_ref[m, t]
            dprobs = mm_nt(do2, values)
            wide = probs.astype(F32)
            inner = jnp.sum(wide * dprobs, axis=-1, keepdims=True)
            ds = (wide * (dprobs - inner)).astype(BF16)
            dq = join_heads(mm(ds, keys)) * 0.125
            dq_ref[rows, cols] = rotate_back(dq, cos_own, sin_own).astype(BF16)
            dk = rotate_back(mm_tn(ds, q2), cosine, sine)
            dv = mm_tn(probs, do2)
            for grad, where in ((dk, cols), (dv, value_cols)):
                low_ref[m, :, where] = grad[:HALF].astype(BF16)
                dkv_ref[rows, where] = grad[HALF : HALF + ROWS]
                high_ref[m, :, where] = grad[HALF + ROWS :].astype(BF16)
        return carry

    lax.fori_loop(0, TILES, unit, 0)


def place_shards(index, own, first, first_other, second, second_other, put):
    f, core = index[1], index[2]
    put(own, f, None)
    put(first, lax.rem(f + 3 + 2 * core, 4), None)
    put(first_other, lax.rem(f + 1 + 2 * core, 4), None)
    put(second, lax.rem(f + 2, 4), core)
    put(second_other, lax.rem(f + 2, 4), 1 - core)


def pack_qkv_kernel(index, qkv, gains, whole, half, sems):
    rows = pl.ds(pl.multiple_of(index[2] * 96, 16), 96)
    copies = [
        pltpu.make_async_copy(src, dst, sems.at[n])
        for n, (src, dst) in enumerate((
            (qkv, whole.at[:, pl.ds(0, WIDE)]),
            (gains, whole.at[pl.ds(0, 16), pl.ds(WIDE, 128)]),
            (qkv.at[rows], half.at[:, pl.ds(0, WIDE)]),
            (gains, half.at[pl.ds(0, 16), pl.ds(WIDE, 128)]),
        ))
    ]
    for copy in copies:
        copy.start()
    for copy in copies:
        copy.wait()


def pack_kernel(index, lift, proj, down, rest, rest_half, sems):
    core = index[2]
    copies = []

    def go(src, dst):
        copy = pltpu.make_async_copy(src, dst, sems.at[len(copies)])
        copy.start()
        copies.append(copy)

    half = lambda size: pl.ds(pl.multiple_of(core * size, 16), size)
    go(lift, rest.at[pl.ds(0, 192)])
    go(lift.at[half(96)], rest_half.at[pl.ds(0, 96)])
    for block in range(3):
        cols = pl.ds(block * D, D)
        go(proj.at[pl.ds(64 * block, 64)], rest.at[pl.ds(192, 64), cols])
        go(down.at[pl.ds(96 * block, 96)], rest.at[pl.ds(256, 96), cols])
        go(
            proj.at[pl.ds(pl.multiple_of(64 * block + core * 32, 16), 32)],
            rest_half.at[pl.ds(96, 32), cols],
        )
        go(
            down.at[pl.ds(pl.multiple_of(96 * block + core * 48, 16), 48)],
            rest_half.at[pl.ds(128, 48), cols],
        )
    for copy in copies:
        copy.wait()


def gather_gain(tiles, row):
    parts = []
    for tile in tiles:
        parts += [tile[row : row + 1, :], tile[row + 1 : row + 2, :64]]
    return jnp.concatenate(parts, axis=1)


def forward_attention_kernel(index, own, low, high, gain_tile, cos_ref, sin_ref, bias_ref,
                             shard, first, first_other, second, second_other,
                             o, gains, whole, wqkv, tiles, ext, a_ext, q, k, v, p, sems, out_sem):
    copies = []

    def go(src, dst):
        copy = pltpu.make_async_copy(src, dst, sems.at[len(copies)])
        copy.start()
        copies.append(copy)

    def put(piece, f, half):
        at, size = (f * 192, 192) if half is None else (f * 192 + half * 96, 96)
        rows = pl.ds(pl.multiple_of(at, 16), size)
        go(piece if piece is shard else piece.at[:, pl.ds(0, WIDE)], wqkv.at[rows])
        if piece is not shard and piece is not second_other:
            go(piece.at[pl.ds(0, 16), pl.ds(WIDE, 128)], tiles.at[f])

    place_shards(index, shard, first, first_other, second, second_other, put)
    go(gain_tile, tiles.at[index[1]])
    load_stream(None, own, low, high, (None, None, None), ext)
    for copy in copies:
        copy.wait()
    out = pltpu.make_async_copy(wqkv, whole, out_sem)
    out.start()
    shards = [tiles[f].astype(F32) for f in range(SHARDS)]
    gains[0:1, :] = gather_gain(shards, 0)
    gains[1:2, :] = gather_gain(shards, 2)
    forward_attention(ext, gains[0:1], wqkv, cos_ref, sin_ref, bias_ref, a_ext, q, k, v, p, o)
    out.wait()


def forward_mlp_kernel(index, own, o, gains, lift, proj, down, first, first_other, second, second_other,
                       h3_ref, whole_proj, whole_lift, whole_down, wproj, wlift, wdown, h2, m_out, sems):
    waits = {"proj": [], "lift": [], "down": []}
    count = [0]

    def go(name, src, dst):
        copy = pltpu.make_async_copy(src, dst, sems.at[count[0]])
        copy.start()
        count[0] += 1
        waits[name].append(copy)

    f = index[1]

    def put(piece, s, half):
        rows = lambda at, size: pl.ds(pl.multiple_of(at, 16), size)
        if piece is None:
            go("proj", proj, wproj.at[rows(f * 192, 192)])
            go("lift", lift, wlift.at[rows(f * 192, 192)])
            go("down", down, wdown.at[rows(f * 288, 288)])
            return
        n = 2 if half is None else 1
        h = 0 if half is None else half
        go("lift", piece.at[pl.ds(0, 96 * n)], wlift.at[rows(s * 192 + h * 96, 96 * n)])
        for b in range(3):
            cols = pl.ds(b * D, D)
            go("proj", piece.at[pl.ds(96 * n, 32 * n), cols], wproj.at[rows(s * 192 + b * 64 + h * 32, 32 * n)])
            go("down", piece.at[pl.ds(128 * n, 48 * n), cols], wdown.at[rows(s * 288 + b * 96 + h * 48, 48 * n)])

    place_shards(index, None, first, first_other, second, second_other, put)
    outs = []
    for name, buffer, whole in (("proj", wproj, whole_proj), ("lift", wlift, whole_lift), ("down", wdown, whole_down)):
        finish(waits, name)
        copy = pltpu.make_async_copy(buffer, whole, sems.at[count[0]])
        copy.start()
        count[0] += 1
        outs.append(copy)
        waits[name] = []
    hidden = jnp.concatenate([own[0], own[1]], axis=0).astype(F32)
    h3 = forward_mlp(hidden, o, wproj, gains[1:2], wlift, wdown, h2, m_out, None, None, waits)
    for m in range(MICRO):
        h3_ref[m] = h3[m * ROWS : (m + 1) * ROWS].astype(BF16)
    for copy in outs:
        copy.wait()


def turning_kernel(flag_ref, own, low, high, other_own, other_low, other_high, cotangent, gains,
                   cos_ref, sin_ref, bias_ref, qkv_hbm, proj_hbm, lift_hbm, down_hbm,
                   h3_ref, q, k, v, p, o, h2, m_out, left, right, src, dh2_ref, dq, dkv, to_low, to_high,
                   wqkv, wproj, wlift, wdown, ext, a_ext, du, do, sems):
    waits = start_weights(
        {"qkv": qkv_hbm, "proj": proj_hbm, "lift": lift_hbm, "down": down_hbm},
        {"qkv": wqkv, "proj": wproj, "lift": wlift, "down": wdown}, sems,
    )
    flag = flag_ref[0] == 1
    load_stream(flag, own, low, high, (other_own, other_low, other_high), ext)
    src[...] = own_rows(ext[...])
    finish(waits, "qkv")
    forward_attention(ext, gains[0:1], wqkv, cos_ref, sin_ref, bias_ref, a_ext, q, k, v, p, o)
    h3 = forward_mlp(src[...].astype(F32), o, wproj, gains[1:2], wlift, wdown, h2, m_out, left, right, waits)
    for m in range(MICRO):
        h3_ref[m] = h3[m * ROWS : (m + 1) * ROWS].astype(BF16)
    grad_low = jnp.concatenate([cotangent[0], cotangent[1]], axis=0)
    dh2, _, _, _ = backward_mlp(grad_low, h2, gains[1:2], wproj, wlift, wdown, left, right, du, do)
    dh2_ref[...] = dh2
    backward_attention(q, k, v, p, do, cos_ref, sin_ref, dq, dkv, to_low, to_high)


def back_kernel(flag_ref, incoming, cotangent, gains, cos_ref, sin_ref, proj_hbm, lift_hbm, down_hbm,
                q, k, v, p, h2, left, right,
                grad_ref, du, gb_ref, b_ref, mlp_ref, dh2_ref, dq, dkv, to_low, to_high,
                wproj, wlift, wdown, do, sems):
    waits = start_weights(
        {"down": down_hbm, "lift": lift_hbm, "proj": proj_hbm},
        {"down": wdown, "lift": wlift, "proj": wproj}, sems,
    )
    flag = flag_ref[0] == 1
    grad_low = jnp.concatenate(
        [jnp.where(flag, incoming[m], cotangent[m]) for m in range(MICRO)], axis=0
    )
    grad_ref[...] = grad_low
    for name in ("down", "lift", "proj"):
        finish(waits, name)
    dh2, gb, gain_grad, normed = backward_mlp(
        grad_low, h2, gains[1:2], wproj, wlift, wdown, left, right, du, do
    )
    gb_ref[...] = gb
    b_ref[...] = (normed * gains[1:2]).astype(BF16)
    mlp_ref[...] = gain_grad
    dh2_ref[...] = dh2
    backward_attention(q, k, v, p, do, cos_ref, sin_ref, dq, dkv, to_low, to_high)


def joined_grads(dq, dkv, from_low, from_high, dqkv):
    dqkv[:, :D] = dq[...]
    for m in range(MICRO):
        first, last = pl.ds(m * ROWS, HALF), pl.ds(m * ROWS + HALF, HALF)
        dqkv[first, D:] = (dkv[first, :] + from_low[m].astype(F32)).astype(BF16)
        dqkv[last, D:] = (dkv[last, :] + from_high[m].astype(F32)).astype(BF16)


def source_kernel(src, gains, dh2, dq, dkv, from_low, from_high, qkv_hbm, out_ref, wqkv, dqkv, sems):
    waits = start_weights({"qkv": qkv_hbm}, {"qkv": wqkv}, sems)
    joined_grads(dq, dkv, from_low, from_high, dqkv)
    normed, inv_scale = norm_parts(src[...].astype(F32))
    finish(waits, "qkv")
    da = mm_nt(dqkv[...], wqkv[...])
    dh = dh2[...] + norm_back(da, gains[0:1], normed, inv_scale)
    for m in range(MICRO):
        out_ref[m] = dh[m * ROWS : (m + 1) * ROWS].astype(BF16)


def gain_block(attn, mlp, f):
    rows = []
    for gain in (attn, mlp):
        rows.append(gain[:, 192 * f : 192 * f + 128])
        rows.append(jnp.concatenate([gain[:, 192 * f + 128 : 192 * f + 192], jnp.zeros((1, 64), F32)], axis=1))
    return jnp.concatenate(rows + [jnp.zeros((92, 128), F32)], axis=0).astype(BF16)


def source_grad_kernel(index, src, gains, dh2, dq, dkv, from_low, from_high, mlp_grad, qkv_hbm,
                       out_ref, keep, send, wqkv, dqkv, qkv_ref, gain_ref, sems):
    waits = start_weights({"qkv": qkv_hbm}, {"qkv": wqkv}, sems)
    joined_grads(dq, dkv, from_low, from_high, dqkv)
    normed, inv_scale = norm_parts(src[...].astype(F32))
    finish(waits, "qkv")
    da = mm_nt(dqkv[...], wqkv[...])
    attn_grad = jnp.sum(da * normed, axis=0, keepdims=True)
    mlp = mlp_grad[...]
    for f in range(SHARDS):
        gain_ref[f] = gain_block(attn_grad, mlp, f)
    a = (normed * gains[0:1]).astype(BF16)
    for t in range(9):
        cols = pl.ds(256 * t, 256)
        qkv_ref[:, cols] = mm_tn(a, dqkv[:, cols]).astype(BF16)
    copies = []
    for target, half in ((send, 1 - index[2]), (keep, index[2])):
        for f in range(SHARDS):
            rows = pl.ds(pl.multiple_of(f * 192 + half * 96, 16), 96)
            for src_ref, dst_ref in (
                (qkv_ref.at[rows], target.at[f, :, pl.ds(0, WIDE)]),
                (gain_ref.at[f], target.at[f, :, pl.ds(WIDE, 128)]),
            ):
                copy = pltpu.make_async_copy(src_ref, dst_ref, sems.at[1 + len(copies)])
                copy.start()
                copies.append(copy)
    dh = dh2[...] + norm_back(da, gains[0:1], normed, inv_scale)
    for m in range(MICRO):
        out_ref[m] = dh[m * ROWS : (m + 1) * ROWS].astype(BF16)
    for copy in copies:
        copy.wait()


def weight_grad_kernel(index, m_ref, grad_ref, b_ref, du, o_ref, gb_ref, keep, send,
                       down_ref, lift_ref, proj_ref, pad_ref, sems):
    core = index[2]
    copies = []

    def go(src, dst):
        copy = pltpu.make_async_copy(src, dst, sems.at[len(copies)])
        copy.start()
        copies.append(copy)

    sides = ((send, 1 - core), (keep, core))
    rows = lambda at, size: pl.ds(pl.multiple_of(at, 16), size)
    pad_ref[...] = jnp.zeros_like(pad_ref)
    for target, _ in sides:
        for f in range(SHARDS):
            go(pad_ref, target.at[f, pl.ds(176, 16)])
    for t in range(9):
        cols = pl.ds(256 * t, 256)
        lift_ref[:, cols] = mm_tn(b_ref[...], du[:, cols]).astype(BF16)
    for target, half in sides:
        for f in range(SHARDS):
            go(lift_ref.at[rows(f * 192 + half * 96, 96)], target.at[f, pl.ds(0, 96)])
    for t in range(3):
        cols = pl.ds(256 * t, 256)
        down_ref[:, cols] = mm_tn(m_ref[...], grad_ref[:, cols]).astype(BF16)
        proj_ref[:, cols] = mm_tn(o_ref[...], gb_ref[:, cols]).astype(BF16)
    for target, half in sides:
        for f in range(SHARDS):
            for b in range(3):
                cols = pl.ds(b * D, D)
                go(proj_ref.at[rows(f * 192 + b * 64 + half * 32, 32)], target.at[f, pl.ds(96, 32), cols])
                go(down_ref.at[rows(f * 288 + b * 96 + half * 48, 48)], target.at[f, pl.ds(128, 48), cols])
    for copy in copies:
        copy.wait()


def add_up(parts):
    total = parts[0].astype(F32)
    for part in parts[1:]:
        total = total + part.astype(F32)
    return total.astype(BF16)


def rest_core_kernel(index, keep, other, *outs):
    for d, out in enumerate(outs):
        rows = pl.ds(pl.multiple_of(lax.rem(index[0] + d, 4) * 48, 16), 48)
        for f in range(SHARDS):
            out[f] = add_up([keep[f, rows, :], other[f, rows, :]])


def rest_z_kernel(index, own, a, b, c, *outs):
    for d, out in enumerate(outs):
        f = lax.rem(index[1] + d, 4)
        out[...] = add_up([own[f], a[f], b[f], c[f]])


def qkv_core_kernel(index, keep, other, *outs):
    for d, out in enumerate(outs):
        f = lax.rem(index[1] + d, 4)
        out[...] = add_up([keep[f], other[f]])


def qkv_y_kernel(index, own, a, b, c, out_0, out_1, out_2, out_3, total):
    total[...] = add_up([own[...], a[...], b[...], c[...]])
    for d, out in enumerate((out_0, out_1, out_2, out_3)):
        z = lax.rem(index[0] + d, 4)
        rows = pl.ds(pl.multiple_of(lax.div(z, 2) * 48, 16), 48)
        cols = pl.ds(pl.multiple_of(lax.rem(z, 2) * 1152, 128), 1152)
        out[:, pl.ds(0, 1152)] = total[rows, cols]
        out[:, pl.ds(1152, 128)] = total[pl.ds(0, 48), pl.ds(WIDE, 128)]


def joint_kernel(r0, r1, r2, r3, q0, q1, q2, q3, out):
    out[:, pl.ds(0, WIDE)] = add_up([r0[...], r1[...], r2[...], r3[...]])
    out[:, pl.ds(WIDE, 1280)] = add_up([q0[...], q1[...], q2[...], q3[...]])


def pair_kernel(a, b, out):
    out[...] = add_up([a[...], b[...]])


def final_kernel(index, *refs):
    pieces, (qkv_out, proj_out, lift_out, down_out, gain_out, rest) = refs[:8], refs[8:]
    core = index[2]
    for side in range(2):
        half = core if side == 0 else 1 - core
        for d in range(4):
            piece = pieces[4 * side + d]
            z = lax.rem(index[0] - d + 4, 4)
            rest[side, pl.ds(pl.multiple_of(z * 48, 16), 48), :] = piece[:, pl.ds(0, WIDE)]
            qkv_out[
                pl.ds(pl.multiple_of(half * 96 + lax.div(z, 2) * 48, 16), 48),
                pl.ds(pl.multiple_of(lax.rem(z, 2) * 1152, 128), 1152),
            ] = piece[:, pl.ds(WIDE, 1152)].astype(F32)
        rows = lambda at, size: pl.ds(pl.multiple_of(at, 16), size)
        lift_out[rows(half * 96, 96), :] = rest[side, pl.ds(0, 96), :].astype(F32)
        for b in range(3):
            cols = pl.ds(b * D, D)
            proj_out[rows(b * 64 + half * 32, 32), :] = rest[side, pl.ds(96, 32), cols].astype(F32)
            down_out[rows(b * 96 + half * 48, 48), :] = rest[side, pl.ds(128, 48), cols].astype(F32)
    gain_out[...] = pieces[0][pl.ds(0, 16), pl.ds(WIDE + 1152, 128)].astype(F32)


def call(kernel, name, ins, outs, scratch, flops, limit=56):
    places = {"v": pltpu.VMEM, "a": pl.ANY, "s": pltpu.SMEM}
    return pl.pallas_call(
        kernel,
        name=name,
        out_shape=[jax.ShapeDtypeStruct(out[0], out[1]) for out in outs],
        in_specs=[pl.BlockSpec(memory_space=places[place]) for _, place in ins],
        out_specs=[pl.BlockSpec(memory_space=places[out[2] if len(out) > 2 else "v"]) for out in outs],
        scratch_shapes=scratch,
        compiler_params=pltpu.CompilerParams(vmem_limit_bytes=limit * 2**20),
        cost_estimate=pl.CostEstimate(flops=flops, bytes_accessed=flops // 300, transcendentals=0),
    )(*[array for array, _ in ins])


def travel(block, target):
    pairs = []
    for ctx in range(16):
        for f in range(SHARDS):
            xlo, z, core, g = target(ctx // 8, ctx // 2 % 4, ctx % 2, f)
            pairs.append((ctx * SHARDS + f, (xlo * 8 + z % 4 * 2 + core) * SHARDS + g % 4))
    return lax.ppermute(block, ("ctx", "fsdp"), pairs)


def along_y(block, d):
    return travel(block, lambda x, z, c, f: (x, z, c, f + d))


def along_z(block, d):
    return travel(block, lambda x, z, c, f: (x, z + d, c, f))


def swap_core(block):
    return travel(block, lambda x, z, c, f: (x, z, 1 - c, f))


def swap_x(block):
    return travel(block, lambda x, z, c, f: (1 - x, z, c, f))


def gather_pieces(whole, half):
    first = travel(whole, lambda x, z, c, f: (x, z, c, f + 1 - 2 * c))
    second = along_y(half, 2)
    return first, swap_core(first), second, swap_core(second)


def halo_rows(block, axis):
    count = lax.axis_size(axis)
    up = [(i, i + 1) for i in range(count - 1)]
    down = [(i + 1, i) for i in range(count - 1)]
    return (
        lax.ppermute(block[:, ROWS - HALF :], axis, up),
        lax.ppermute(block[:, :HALF], axis, down),
    )


def swap_halos(to_low, to_high):
    count = lax.axis_size("ctx")
    up = [(i, i + 1) for i in range(count - 1)]
    down = [(i + 1, i) for i in range(count - 1)]
    return lax.ppermute(to_high, "ctx", up), lax.ppermute(to_low, "ctx", down)


def tables(first_row, lengths):
    half = HD // 2
    frequencies = rope_base ** (-(jnp.arange(half, dtype=F32) * 2.0) / HD)
    positions = first_row - HALF + jnp.arange(EXT, dtype=jnp.int32)
    angles = positions.astype(F32)[:, None] * frequencies[None, :]
    cosine, sine = jnp.cos(angles), jnp.sin(angles)
    cosine = jnp.concatenate([cosine] * 4, axis=1)
    sine = jnp.concatenate([-sine, sine, -sine, sine], axis=1)
    ends = jnp.cumsum(lengths, axis=1)
    doc = jnp.sum((positions[None, :, None] >= ends[:, None, :]).astype(jnp.int32), axis=2)
    query = positions[HALF : HALF + ROWS]
    allowed = (
        (jnp.abs(query[:, None] - positions[None, :]) <= HALF)
        & (positions >= 0)[None, :]
        & (positions < SEQ_LEN)[None, :]
    )[None] & (doc[:, HALF : HALF + ROWS, None] == doc[:, None, :])
    return cosine, sine, jnp.where(allowed, 0.0, masked_score).astype(F32)


WQKV, WPROJ, WLIFT, WDOWN = [
    pltpu.VMEM((D, WIDE), BF16),
    pltpu.VMEM((D, D), BF16),
    pltpu.VMEM((D, WIDE), BF16),
    pltpu.VMEM((FF, D), BF16),
]
SAVED = [
    ((OWN, D), BF16),
    ((MICRO * EXT, D), BF16),
    ((MICRO * EXT, D), BF16),
    ((MICRO, TILES, 2 * ROWS, EXT), BF16),
    ((OWN, D), BF16),
    ((OWN, D), F32),
    ((OWN, FF), BF16),
    ((OWN, FF), F32),
    ((OWN, FF), F32),
]
STREAM = [pltpu.VMEM((MICRO * EXT, D), BF16)] * 2
GRADS_OUT = [
    ((OWN, D), F32),
    ((OWN, D), BF16),
    ((OWN, 2 * D), F32),
    ((MICRO, HALF, 2 * D), BF16),
    ((MICRO, HALF, 2 * D), BF16),
]


def sems(count):
    return pltpu.SemaphoreType.DMA((count,))


def body(
    inputs, out_grad, doc_lengths, attn_gain, qkv_weight, proj_weight, mlp_gain, lift_weight, down_weight
):
    on_first = lax.axis_index("section") == 0
    flag = on_first.astype(jnp.int32).reshape(1)
    ctx, f = lax.axis_index("ctx"), lax.axis_index("fsdp")
    index = jnp.stack([ctx // 2 % 4, f, ctx % 2]).astype(jnp.int32)
    qkv_shard, lift_shard, proj_shard, down_shard = qkv_weight[0], lift_weight[0], proj_weight[0], down_weight[0]
    own, cotangent = inputs[:, 0], out_grad[:, 0]
    low, high = halo_rows(own, "ctx")
    gain_tile = jnp.pad(
        jnp.pad(jnp.stack([attn_gain[0], mlp_gain[0]]), ((0, 0), (0, 64))).reshape(4, 128), ((0, 12), (0, 0))
    )
    qkv_pack, qkv_half = call(
        pack_qkv_kernel, "pack_qkv",
        [(index, "s"), (qkv_shard, "a"), (gain_tile, "a")],
        [((192, 2432), BF16, "a"), ((96, 2432), BF16, "a")],
        [sems(4)], 0, 8,
    )
    rest, rest_half = call(
        pack_kernel, "pack_rest",
        [(index, "s"), (lift_shard, "a"), (proj_shard, "a"), (down_shard, "a")],
        [((352, WIDE), BF16, "a"), ((176, WIDE), BF16, "a")],
        [sems(14)], 0, 8,
    )
    first = travel(qkv_pack, lambda x, z, c, f: (x, z, c, f + 1 - 2 * c))
    second = along_y(qkv_half, 2)
    first, rest = lax.optimization_barrier((first, rest))
    second, rest_half = lax.optimization_barrier((second, rest_half))
    qkv_pieces = first, swap_core(first), second, swap_core(second)
    rest_pieces = gather_pieces(rest, rest_half)
    cosine, sine, bias = tables(ctx * ROWS, doc_lengths[:, 0])
    stream = ((MICRO, ROWS, D), BF16)
    scratch = lambda items: [pltpu.VMEM(s, k) for s, k in items]

    o, gains, wqkv = call(
        forward_attention_kernel, "forward_attention",
        [(index, "s"), (own, "v"), (low, "v"), (high, "v"), (gain_tile, "a"), (cosine, "v"), (sine, "v"), (bias, "v"),
         (qkv_shard, "a"), *[(piece, "a") for piece in qkv_pieces]],
        [((OWN, D), BF16), ((2, D), F32), ((D, WIDE), BF16, "a")],
        [WQKV, pltpu.VMEM((SHARDS, 16, 128), BF16)] + STREAM + scratch(SAVED[:4]) + [sems(9), pltpu.SemaphoreType.DMA(())],
        1_400_000_000,
    )
    relay, wproj, wlift, wdown = call(
        forward_mlp_kernel, "forward_mlp",
        [(index, "s"), (own, "v"), (o, "v"), (gains, "v"), (lift_shard, "a"), (proj_shard, "a"), (down_shard, "a"),
         *[(piece, "a") for piece in rest_pieces]],
        [stream, ((D, D), BF16, "a"), ((D, WIDE), BF16, "a"), ((FF, D), BF16, "a")],
        [WPROJ, WLIFT, WDOWN] + scratch(SAVED[5:7]) + [sems(34)],
        1_800_000_000,
    )
    relayed = lax.ppermute(relay, "section", [(0, 1)])
    other_low, other_high = halo_rows(relayed, "ctx")
    (h3, q, k, v, p, o, h2, m_act, left, right, src, dh2, dq, dkv, to_low, to_high) = call(
        turning_kernel, "layer_turn",
        [(flag, "s"), (own, "v"), (low, "v"), (high, "v"), (relayed, "v"), (other_low, "v"), (other_high, "v"),
         (cotangent, "v"), (gains, "v"), (cosine, "v"), (sine, "v"), (bias, "v"),
         (wqkv, "a"), (wproj, "a"), (wlift, "a"), (wdown, "a")],
        [stream] + SAVED + [((OWN, D), BF16)] + GRADS_OUT,
        [WQKV, WPROJ, WLIFT, WDOWN] + STREAM
        + [pltpu.VMEM((OWN, WIDE), BF16), pltpu.VMEM((OWN, D), BF16), sems(4)],
        6_000_000_000,
    )
    from_low, from_high = swap_halos(to_low, to_high)
    (grad_relay,) = call(
        source_kernel, "layer_source",
        [(src, "v"), (gains, "v"), (dh2, "v"), (dq, "v"), (dkv, "v"), (from_low, "v"), (from_high, "v"), (wqkv, "a")],
        [stream],
        [WQKV, pltpu.VMEM((OWN, WIDE), BF16), sems(1)],
        900_000_000,
    )
    incoming = lax.ppermute(grad_relay, "section", [(1, 0)])
    (grad_low, du, gb, b, mlp_gain_grad, dh2, dq, dkv, to_low, to_high) = call(
        back_kernel, "layer_back",
        [(flag, "s"), (incoming, "v"), (cotangent, "v"), (gains, "v"), (cosine, "v"), (sine, "v"),
         (wproj, "a"), (wlift, "a"), (wdown, "a"),
         (q, "v"), (k, "v"), (v, "v"), (p, "v"), (h2, "v"), (left, "v"), (right, "v")],
        [((OWN, D), BF16), ((OWN, WIDE), BF16), ((OWN, D), BF16), ((OWN, D), BF16), ((1, D), F32)] + GRADS_OUT,
        [WPROJ, WLIFT, WDOWN, pltpu.VMEM((OWN, D), BF16), sems(3)],
        3_000_000_000,
    )
    from_low, from_high = swap_halos(to_low, to_high)
    rest_keep, rest_send = call(
        weight_grad_kernel, "weight_grads",
        [(index, "s"), (m_act, "v"), (grad_low, "v"), (b, "v"), (du, "v"), (o, "v"), (gb, "v")],
        [((SHARDS, 192, WIDE), BF16, "a")] * 2,
        [WDOWN, WLIFT, WPROJ, pltpu.VMEM((16, WIDE), BF16), sems(64)],
        1_600_000_000,
    )
    rest_other = swap_core(rest_send)
    rest_z = call(
        rest_core_kernel, "rest_core_sum", [(index, "s"), (rest_keep, "v"), (rest_other, "v")],
        [((SHARDS, 48, WIDE), BF16)] * 4, [], 0, 24,
    )
    rest_z, from_low, from_high = lax.optimization_barrier((rest_z, from_low, from_high))
    in_grad, qkv_keep, qkv_send = call(
        source_grad_kernel, "layer_source_grads",
        [(index, "s"), (src, "v"), (gains, "v"), (dh2, "v"), (dq, "v"), (dkv, "v"), (from_low, "v"),
         (from_high, "v"), (mlp_gain_grad, "v"), (wqkv, "a")],
        [stream, ((SHARDS, 96, 2432), BF16, "a"), ((SHARDS, 96, 2432), BF16, "a")],
        [WQKV, pltpu.VMEM((OWN, WIDE), BF16), WQKV, pltpu.VMEM((SHARDS, 96, 128), BF16), sems(17)],
        1_800_000_000,
    )
    qkv_other = swap_core(qkv_send)

    rest_y = call(
        rest_z_kernel, "rest_z_sum",
        [(index, "s"), (rest_z[0], "v"), *[(along_z(rest_z[d], d), "v") for d in (1, 2, 3)]],
        [((48, WIDE), BF16)] * 4, [], 0, 24,
    )
    qkv_y = call(
        qkv_core_kernel, "qkv_core_sum", [(index, "s"), (qkv_keep, "v"), (qkv_other, "v")],
        [((96, 2432), BF16)] * 4, [], 0, 24,
    )
    qkv_z = call(
        qkv_y_kernel, "qkv_y_sum",
        [(index, "s"), (qkv_y[0], "v"), *[(along_y(qkv_y[d], d), "v") for d in (1, 2, 3)]],
        [((48, 1280), BF16)] * 4, [pltpu.VMEM((96, 2432), BF16)], 0, 24,
    )
    (joint,) = call(
        joint_kernel, "joint_sum",
        [(rest_y[0], "v"), *[(along_y(rest_y[d], d), "v") for d in (1, 2, 3)],
         (qkv_z[0], "v"), *[(along_z(qkv_z[d], d), "v") for d in (1, 2, 3)]],
        [((48, 3584), BF16)], [], 0, 24,
    )
    (joint,) = call(
        pair_kernel, "pair_sum", [(joint, "v"), (swap_x(joint), "v")], [((48, 3584), BF16)], [], 0, 24
    )
    mine = [joint] + [along_z(joint, d) for d in (1, 2, 3)]
    theirs = [swap_core(piece) for piece in mine]
    qkv_sum, proj_sum, lift_sum, down_sum, gain_sums = call(
        final_kernel, "final_shard", [(index, "s"), *[(piece, "v") for piece in mine + theirs]],
        [((192, WIDE), F32), ((192, D), F32), ((192, WIDE), F32), ((288, D), F32), ((16, 128), F32)],
        [pltpu.VMEM((2, 192, WIDE), BF16)], 0, 24,
    )
    return (
        h3[None, :, None],
        in_grad[None, :, None],
        gain_sums[0:2].reshape(1, 256)[:, :192],
        qkv_sum[None],
        proj_sum[None],
        gain_sums[2:4].reshape(1, 256)[:, :192],
        lift_sum[None],
        down_sum[None],
    )


def solution(mesh):
    placed = (
        P(None, "fsdp", "ctx", None),
        P(None, "fsdp", "ctx", None),
        P(None, "fsdp", None),
        P("section", "fsdp"),
        P("section", "fsdp", None),
        P("section", "fsdp", None),
        P("section", "fsdp"),
        P("section", "fsdp", None),
        P("section", "fsdp", None),
    )
    return jax.shard_map(
        body,
        mesh=mesh,
        in_specs=placed,
        out_specs=(
            P("section", None, "fsdp", "ctx", None),
            P("section", None, "fsdp", "ctx", None),
            P("section", "fsdp"),
            P("section", "fsdp", None),
            P("section", "fsdp", None),
            P("section", "fsdp"),
            P("section", "fsdp", None),
            P("section", "fsdp", None),
        ),
        check_vma=False,
    )
```

```python
import functools

import jax
import jax.numpy as jnp
from jax import lax
from jax.experimental import pallas as pl
from jax.experimental.pallas import tpu as pltpu
from jax.sharding import PartitionSpec as P

D = 768
HD = 64
HALF = 64
SEQ_LEN = 2048
FF = 1152
WIDE = 2304
ROWS = 128
EXT = ROWS + 2 * HALF
MICRO = 2
OWN = MICRO * ROWS
SHARDS = 4
TILES = D // 128
norm_eps = 1e-05
rope_base = 10000.0
masked_score = -1e30
root_half = 0.7071067811865476
inv_root_tau = 0.3989422804014327
F32 = jnp.float32
BF16 = jnp.bfloat16


def mm(left, right):
    return lax.dot_general(left, right, (((1,), (0,)), ((), ())), preferred_element_type=F32)


def mm_nt(left, right):
    return lax.dot_general(left, right, (((1,), (1,)), ((), ())), preferred_element_type=F32)


def mm_tn(left, right):
    return lax.dot_general(left, right, (((0,), (0,)), ((), ())), preferred_element_type=F32)


def norm_parts(hidden):
    centre = hidden - jnp.mean(hidden, axis=-1, keepdims=True)
    inv_scale = lax.rsqrt(jnp.mean(centre * centre, axis=-1, keepdims=True) + norm_eps)
    return centre * inv_scale, inv_scale


def norm_back(grad_out, gain, normed, inv_scale):
    grad_normed = grad_out * gain
    inner = (
        grad_normed
        - jnp.mean(grad_normed, axis=-1, keepdims=True)
        - normed * jnp.mean(grad_normed * normed, axis=-1, keepdims=True)
    )
    return inner * inv_scale


def lane_is_low(shape, period):
    return lax.broadcasted_iota(jnp.int32, shape, 1) % period < period // 2


def turn(x):
    return jnp.where(lane_is_low(x.shape, HD), pltpu.roll(x, 96, 1), pltpu.roll(x, 32, 1))


def rotate(x, cosine, sine):
    return x * cosine + turn(x) * sine


def rotate_back(x, cosine, sine):
    return x * cosine - turn(x) * sine


def stack_heads(x):
    low = lane_is_low(x.shape, 128)
    zero = jnp.zeros_like(x)
    return jnp.concatenate([jnp.where(low, x, zero), jnp.where(low, zero, x)], axis=0)


def join_heads(x):
    half = x.shape[0] // 2
    low = lane_is_low((half, 128), 128)
    return jnp.where(low, x[:half], x[half:])


def start_weights(sources, buffers, sems):
    waits = {}
    for index, (name, source) in enumerate(sources.items()):
        copy = pltpu.make_async_copy(source, buffers[name], sems.at[index])
        copy.start()
        waits[name] = [copy]
    return waits


def finish(waits, name):
    for copy in waits[name]:
        copy.wait()


def load_stream(flag, own, low, high, other, ext):
    for m in range(MICRO):
        for ref, alt, start, size in (
            (low, other[1], 0, HALF),
            (own, other[0], HALF, ROWS),
            (high, other[2], HALF + ROWS, HALF),
        ):
            value = ref[m]
            if alt is not None:
                value = jnp.where(flag, value, alt[m])
            ext[pl.ds(m * EXT + start, size), :] = value


def own_rows(x):
    return jnp.concatenate([x[HALF : HALF + ROWS], x[EXT + HALF : EXT + HALF + ROWS]], axis=0)


def forward_attention(ext, gain, wqkv, cos_ref, sin_ref, bias_ref, a_ext, q_ref, k_ref, v_ref, p_ref, o_ref):
    normed, _ = norm_parts(ext[...].astype(F32))
    a_ext[...] = (normed * gain).astype(BF16)
    a_own = own_rows(a_ext[...])
    cosine, sine = cos_ref[...], sin_ref[...]
    cos_own, sin_own = cosine[HALF : HALF + ROWS], sine[HALF : HALF + ROWS]
    for t in range(3):
        queries = mm(a_own, wqkv[:, 256 * t : 256 * t + 256])
        for s in range(2):
            cols = pl.ds(256 * t + 128 * s, 128)
            for m in range(MICRO):
                part = queries[m * ROWS : (m + 1) * ROWS, 128 * s : 128 * s + 128]
                q_ref[pl.ds(m * ROWS, ROWS), cols] = rotate(part, cos_own, sin_own).astype(
                    BF16
                ) * jnp.asarray(0.125, BF16)
        keys = mm(a_ext[...], wqkv[:, D + 256 * t : D + 256 * t + 256])
        for s in range(2):
            cols = pl.ds(256 * t + 128 * s, 128)
            for m in range(MICRO):
                part = keys[m * EXT : (m + 1) * EXT, 128 * s : 128 * s + 128]
                k_ref[pl.ds(m * EXT, EXT), cols] = rotate(part, cosine, sine).astype(BF16)
        values = mm(a_ext[...], wqkv[:, 2 * D + 256 * t : 2 * D + 256 * t + 256])
        v_ref[:, pl.ds(256 * t, 256)] = values.astype(BF16)

    for t in range(TILES):
        cols = pl.ds(t * 128, 128)
        for m in range(MICRO):
            q2 = stack_heads(q_ref[pl.ds(m * ROWS, ROWS), cols])
            scores = mm_nt(k_ref[pl.ds(m * EXT, EXT), cols], q2) + bias_ref[m]
            terms = jnp.exp(scores - jnp.max(scores, axis=0, keepdims=True))
            probs = (terms * (1.0 / jnp.sum(terms, axis=0, keepdims=True))).astype(BF16)
            p_ref[m, t] = probs
            attended = mm_tn(probs, v_ref[pl.ds(m * EXT, EXT), cols])
            o_ref[pl.ds(m * ROWS, ROWS), cols] = join_heads(attended).astype(BF16)


def forward_mlp(hidden, o_ref, wproj, mlp_gain, wlift, wdown, h2_ref, m_ref, left_ref, right_ref, waits):
    finish(waits, "proj")
    mixed = hidden + mm(o_ref[...], wproj[...])
    h2_ref[...] = mixed
    normed, _ = norm_parts(mixed)
    b = (normed * mlp_gain).astype(BF16)
    finish(waits, "lift")
    for t in range(FF // 128):
        cols = pl.ds(128 * t, 128)
        gate = mm(b, wlift[:, 128 * t : 128 * t + 128])
        up = mm(b, wlift[:, FF + 128 * t : FF + 128 * t + 128])
        cdf = 0.5 * (1.0 + lax.erf(gate * root_half))
        gelu = gate * cdf
        m_ref[:, cols] = (gelu * up).astype(BF16)
        if left_ref is not None:
            pdf = jnp.exp(-0.5 * gate * gate) * inv_root_tau
            left_ref[:, cols] = up * (cdf + gate * pdf)
            right_ref[:, cols] = gelu
    finish(waits, "down")
    return mixed + mm(m_ref[...], wdown[...])


def backward_mlp(grad_low, h2_ref, mlp_gain, wproj, wlift, wdown, left_ref, right_ref, du_ref, do_ref):
    for t in range(3):
        cols = pl.ds(384 * t, 384)
        dm = mm_nt(grad_low, wdown[384 * t : 384 * t + 384, :])
        du_ref[:, cols] = (dm * left_ref[:, cols]).astype(BF16)
        du_ref[:, pl.ds(FF + 384 * t, 384)] = (dm * right_ref[:, cols]).astype(BF16)
    db = mm_nt(du_ref[...], wlift[...])
    normed, inv_scale = norm_parts(h2_ref[...])
    gain_grad = jnp.sum(db * normed, axis=0, keepdims=True)
    dh2 = grad_low.astype(F32) + norm_back(db, mlp_gain, normed, inv_scale)
    gb = dh2.astype(BF16)
    do_ref[...] = mm_nt(gb, wproj[...]).astype(BF16)
    return dh2, gb, gain_grad, normed


def backward_attention(q_ref, k_ref, v_ref, p_ref, do_ref, cos_ref, sin_ref, dq_ref, dkv_ref, low_ref, high_ref):
    cosine, sine = cos_ref[...], sin_ref[...]
    cos_own, sin_own = cosine[HALF : HALF + ROWS], sine[HALF : HALF + ROWS]

    for t in range(TILES):
        cols, value_cols = pl.ds(t * 128, 128), pl.ds(D + t * 128, 128)
        for m in range(MICRO):
            rows = pl.ds(m * ROWS, ROWS)
            q2 = stack_heads(q_ref[rows, cols])
            do2 = stack_heads(do_ref[rows, cols])
            probs = p_ref[m, t]
            dprobs = mm_nt(v_ref[pl.ds(m * EXT, EXT), cols], do2)
            wide = probs.astype(F32)
            inner = jnp.sum(wide * dprobs, axis=0, keepdims=True)
            ds = (wide * (dprobs - inner)).astype(BF16)
            dq = join_heads(mm_tn(ds, k_ref[pl.ds(m * EXT, EXT), cols])) * 0.125
            dq_ref[rows, cols] = rotate_back(dq, cos_own, sin_own).astype(BF16)
            dk = rotate_back(mm(ds, q2), cosine, sine)
            dv = mm(probs, do2)
            for grad, where in ((dk, cols), (dv, value_cols)):
                low_ref[m, :, where] = grad[:HALF].astype(BF16)
                dkv_ref[rows, where] = grad[HALF : HALF + ROWS]
                high_ref[m, :, where] = grad[HALF + ROWS :].astype(BF16)


def place_shards(index, own, first, first_other, second, second_other, put):
    f, core = index[1], index[2]
    put(own, f, None)
    put(first, lax.rem(f + 3 + 2 * core, 4), None)
    put(first_other, lax.rem(f + 1 + 2 * core, 4), None)
    put(second, lax.rem(f + 2, 4), core)
    put(second_other, lax.rem(f + 2, 4), 1 - core)


def pack_qkv_kernel(index, qkv, gains, whole, half, sems):
    rows = pl.ds(pl.multiple_of(index[2] * 96, 16), 96)
    copies = [
        pltpu.make_async_copy(src, dst, sems.at[n])
        for n, (src, dst) in enumerate((
            (qkv, whole.at[:, pl.ds(0, WIDE)]),
            (gains, whole.at[pl.ds(0, 16), pl.ds(WIDE, 128)]),
            (qkv.at[rows], half.at[:, pl.ds(0, WIDE)]),
            (gains, half.at[pl.ds(0, 16), pl.ds(WIDE, 128)]),
        ))
    ]
    for copy in copies:
        copy.start()
    for copy in copies:
        copy.wait()


def pack_kernel(index, lift, proj, down, rest, rest_half, sems):
    core = index[2]
    copies = []

    def go(src, dst):
        copy = pltpu.make_async_copy(src, dst, sems.at[len(copies)])
        copy.start()
        copies.append(copy)

    half = lambda size: pl.ds(pl.multiple_of(core * size, 16), size)
    go(lift, rest.at[pl.ds(0, 192)])
    go(lift.at[half(96)], rest_half.at[pl.ds(0, 96)])
    for block in range(3):
        cols = pl.ds(block * D, D)
        go(proj.at[pl.ds(64 * block, 64)], rest.at[pl.ds(192, 64), cols])
        go(down.at[pl.ds(96 * block, 96)], rest.at[pl.ds(256, 96), cols])
        go(
            proj.at[pl.ds(pl.multiple_of(64 * block + core * 32, 16), 32)],
            rest_half.at[pl.ds(96, 32), cols],
        )
        go(
            down.at[pl.ds(pl.multiple_of(96 * block + core * 48, 16), 48)],
            rest_half.at[pl.ds(128, 48), cols],
        )
    for copy in copies:
        copy.wait()


def gather_gain(tiles, row):
    parts = []
    for tile in tiles:
        parts += [tile[row : row + 1, :], tile[row + 1 : row + 2, :64]]
    return jnp.concatenate(parts, axis=1)


def forward_attention_kernel(index, own, low, high, gain_tile, cos_ref, sin_ref, bias_ref,
                             shard, first, first_other, second, second_other,
                             o, gains, whole, wqkv, tiles, ext, a_ext, q, k, v, p, sems, out_sem):
    copies = []

    def go(src, dst):
        copy = pltpu.make_async_copy(src, dst, sems.at[len(copies)])
        copy.start()
        copies.append(copy)

    def put(piece, f, half):
        at, size = (f * 192, 192) if half is None else (f * 192 + half * 96, 96)
        rows = pl.ds(pl.multiple_of(at, 16), size)
        go(piece if piece is shard else piece.at[:, pl.ds(0, WIDE)], wqkv.at[rows])
        if piece is not shard and piece is not second_other:
            go(piece.at[pl.ds(0, 16), pl.ds(WIDE, 128)], tiles.at[f])

    place_shards(index, shard, first, first_other, second, second_other, put)
    go(gain_tile, tiles.at[index[1]])
    load_stream(None, own, low, high, (None, None, None), ext)
    for copy in copies:
        copy.wait()
    out = pltpu.make_async_copy(wqkv, whole, out_sem)
    out.start()
    shards = [tiles[f].astype(F32) for f in range(SHARDS)]
    gains[0:1, :] = gather_gain(shards, 0)
    gains[1:2, :] = gather_gain(shards, 2)
    forward_attention(ext, gains[0:1], wqkv, cos_ref, sin_ref, bias_ref, a_ext, q, k, v, p, o)
    out.wait()


def forward_mlp_kernel(index, own, o, gains, lift, proj, down, first, first_other, second, second_other,
                       h3_ref, whole_proj, whole_lift, whole_down, wproj, wlift, wdown, h2, m_out, sems):
    waits = {"proj": [], "lift": [], "down": []}
    count = [0]

    def go(name, src, dst):
        copy = pltpu.make_async_copy(src, dst, sems.at[count[0]])
        copy.start()
        count[0] += 1
        waits[name].append(copy)

    f = index[1]

    def put(piece, s, half):
        rows = lambda at, size: pl.ds(pl.multiple_of(at, 16), size)
        if piece is None:
            go("proj", proj, wproj.at[rows(f * 192, 192)])
            go("lift", lift, wlift.at[rows(f * 192, 192)])
            go("down", down, wdown.at[rows(f * 288, 288)])
            return
        n = 2 if half is None else 1
        h = 0 if half is None else half
        go("lift", piece.at[pl.ds(0, 96 * n)], wlift.at[rows(s * 192 + h * 96, 96 * n)])
        for b in range(3):
            cols = pl.ds(b * D, D)
            go("proj", piece.at[pl.ds(96 * n, 32 * n), cols], wproj.at[rows(s * 192 + b * 64 + h * 32, 32 * n)])
            go("down", piece.at[pl.ds(128 * n, 48 * n), cols], wdown.at[rows(s * 288 + b * 96 + h * 48, 48 * n)])

    place_shards(index, None, first, first_other, second, second_other, put)
    outs = []
    for name, buffer, whole in (("proj", wproj, whole_proj), ("lift", wlift, whole_lift), ("down", wdown, whole_down)):
        finish(waits, name)
        copy = pltpu.make_async_copy(buffer, whole, sems.at[count[0]])
        copy.start()
        count[0] += 1
        outs.append(copy)
        waits[name] = []
    hidden = jnp.concatenate([own[0], own[1]], axis=0).astype(F32)
    h3 = forward_mlp(hidden, o, wproj, gains[1:2], wlift, wdown, h2, m_out, None, None, waits)
    for m in range(MICRO):
        h3_ref[m] = h3[m * ROWS : (m + 1) * ROWS].astype(BF16)
    for copy in outs:
        copy.wait()


def start_all(pairs, sems, first):
    copies = [pltpu.make_async_copy(src, dst, sems.at[first + n]) for n, (src, dst) in enumerate(pairs)]
    for copy in copies:
        copy.start()
    return copies


def turning_kernel(flag_ref, own, low, high, other_own, other_low, other_high, cotangent, gains,
                   cos_ref, sin_ref, bias_ref, qkv_hbm, proj_hbm, lift_hbm, down_hbm, *refs):
    kept, (dh2_ref, dq, dkv, to_low, to_high) = refs[:11], refs[11:16]
    wqkv, wproj, wlift, wdown, ext, a_ext, du, do, h3_ref, q, k, v, p, o, h2, m_out, left, right, src, sems = refs[16:]
    waits = start_weights(
        {"qkv": qkv_hbm, "proj": proj_hbm, "lift": lift_hbm, "down": down_hbm},
        {"qkv": wqkv, "proj": wproj, "lift": wlift, "down": wdown}, sems,
    )
    flag = flag_ref[0] == 1
    load_stream(flag, own, low, high, (other_own, other_low, other_high), ext)
    src[...] = own_rows(ext[...])
    finish(waits, "qkv")
    forward_attention(ext, gains[0:1], wqkv, cos_ref, sin_ref, bias_ref, a_ext, q, k, v, p, o)
    outs = start_all(zip((q, k, v, p, o, src), kept[1:6] + kept[10:]), sems, 4)
    h3 = forward_mlp(src[...].astype(F32), o, wproj, gains[1:2], wlift, wdown, h2, m_out, left, right, waits)
    for m in range(MICRO):
        h3_ref[m] = h3[m * ROWS : (m + 1) * ROWS].astype(BF16)
    outs += start_all(zip((h3_ref, h2, m_out, left, right), kept[:1] + kept[6:10]), sems, 10)
    grad_low = jnp.concatenate([cotangent[0], cotangent[1]], axis=0)
    dh2, _, _, _ = backward_mlp(grad_low, h2, gains[1:2], wproj, wlift, wdown, left, right, du, do)
    dh2_ref[...] = dh2
    backward_attention(q, k, v, p, do, cos_ref, sin_ref, dq, dkv, to_low, to_high)
    for copy in outs:
        copy.wait()


def back_kernel(flag_ref, incoming, cotangent, gains, cos_ref, sin_ref, proj_hbm, lift_hbm, down_hbm,
                q_hbm, k_hbm, v_hbm, p_hbm, h2_hbm, left_hbm, right_hbm, *refs):
    kept, (mlp_ref, dh2_ref, dq, dkv, to_low, to_high) = refs[:4], refs[4:10]
    wproj, wlift, wdown, do, q, k, v, p, h2, left, right, grad_ref, du, gb_ref, b_ref, sems = refs[10:]
    early = start_all(
        ((down_hbm, wdown), (left_hbm, left), (right_hbm, right), (lift_hbm, wlift), (h2_hbm, h2), (proj_hbm, wproj)),
        sems, 0,
    )
    late = start_all(((q_hbm, q), (v_hbm, v), (p_hbm, p), (k_hbm, k)), sems, 6)
    flag = flag_ref[0] == 1
    grad_low = jnp.concatenate(
        [jnp.where(flag, incoming[m], cotangent[m]) for m in range(MICRO)], axis=0
    )
    grad_ref[...] = grad_low
    for copy in early:
        copy.wait()
    dh2, gb, gain_grad, normed = backward_mlp(
        grad_low, h2, gains[1:2], wproj, wlift, wdown, left, right, du, do
    )
    gb_ref[...] = gb
    b_ref[...] = (normed * gains[1:2]).astype(BF16)
    outs = start_all(zip((grad_ref, du, gb_ref, b_ref), kept), sems, 10)
    mlp_ref[...] = gain_grad
    dh2_ref[...] = dh2
    for copy in late:
        copy.wait()
    backward_attention(q, k, v, p, do, cos_ref, sin_ref, dq, dkv, to_low, to_high)
    for copy in outs:
        copy.wait()


def joined_grads(dq, dkv, from_low, from_high, dqkv):
    dqkv[:, :D] = dq[...]
    for m in range(MICRO):
        first, last = pl.ds(m * ROWS, HALF), pl.ds(m * ROWS + HALF, HALF)
        dqkv[first, D:] = (dkv[first, :] + from_low[m].astype(F32)).astype(BF16)
        dqkv[last, D:] = (dkv[last, :] + from_high[m].astype(F32)).astype(BF16)


def source_kernel(src, gains, dh2, dq, dkv, from_low, from_high, qkv_hbm, out_ref, wqkv, dqkv, sems):
    waits = start_weights({"qkv": qkv_hbm}, {"qkv": wqkv}, sems)
    joined_grads(dq, dkv, from_low, from_high, dqkv)
    normed, inv_scale = norm_parts(src[...].astype(F32))
    finish(waits, "qkv")
    da = mm_nt(dqkv[...], wqkv[...])
    dh = dh2[...] + norm_back(da, gains[0:1], normed, inv_scale)
    for m in range(MICRO):
        out_ref[m] = dh[m * ROWS : (m + 1) * ROWS].astype(BF16)


def gain_block(attn, mlp, f):
    rows = []
    for gain in (attn, mlp):
        rows.append(gain[:, 192 * f : 192 * f + 128])
        rows.append(jnp.concatenate([gain[:, 192 * f + 128 : 192 * f + 192], jnp.zeros((1, 64), F32)], axis=1))
    return jnp.concatenate(rows + [jnp.zeros((92, 128), F32)], axis=0).astype(BF16)


def source_grad_kernel(index, src, gains, dh2, dq, dkv, from_low, from_high, mlp_grad, qkv_hbm,
                       out_ref, keep, send, wqkv, dqkv, qkv_ref, gain_ref, sems):
    waits = start_weights({"qkv": qkv_hbm}, {"qkv": wqkv}, sems)
    joined_grads(dq, dkv, from_low, from_high, dqkv)
    normed, inv_scale = norm_parts(src[...].astype(F32))
    finish(waits, "qkv")
    da = mm_nt(dqkv[...], wqkv[...])
    attn_grad = jnp.sum(da * normed, axis=0, keepdims=True)
    mlp = mlp_grad[...]
    for f in range(SHARDS):
        gain_ref[f] = gain_block(attn_grad, mlp, f)
    a = (normed * gains[0:1]).astype(BF16)
    for t in range(9):
        cols = pl.ds(256 * t, 256)
        qkv_ref[:, cols] = mm_tn(a, dqkv[:, cols]).astype(BF16)
    copies = []
    for target, half in ((send, 1 - index[2]), (keep, index[2])):
        for f in range(SHARDS):
            rows = pl.ds(pl.multiple_of(f * 192 + half * 96, 16), 96)
            for src_ref, dst_ref in (
                (qkv_ref.at[rows], target.at[f, :, pl.ds(0, WIDE)]),
                (gain_ref.at[f], target.at[f, :, pl.ds(WIDE, 128)]),
            ):
                copy = pltpu.make_async_copy(src_ref, dst_ref, sems.at[1 + len(copies)])
                copy.start()
                copies.append(copy)
    dh = dh2[...] + norm_back(da, gains[0:1], normed, inv_scale)
    for m in range(MICRO):
        out_ref[m] = dh[m * ROWS : (m + 1) * ROWS].astype(BF16)
    for copy in copies:
        copy.wait()


def weight_grad_kernel(index, m_ref, grad_ref, b_ref, du, o_ref, gb_ref, keep, send,
                       down_ref, lift_ref, proj_ref, pad_ref, sems):
    core = index[2]
    copies = []

    def go(src, dst):
        copy = pltpu.make_async_copy(src, dst, sems.at[len(copies)])
        copy.start()
        copies.append(copy)

    sides = ((send, 1 - core), (keep, core))
    rows = lambda at, size: pl.ds(pl.multiple_of(at, 16), size)
    pad_ref[...] = jnp.zeros_like(pad_ref)
    for target, _ in sides:
        for f in range(SHARDS):
            go(pad_ref, target.at[f, pl.ds(176, 16)])
    for t in range(9):
        cols = pl.ds(256 * t, 256)
        lift_ref[:, cols] = mm_tn(b_ref[...], du[:, cols]).astype(BF16)
    for target, half in sides:
        for f in range(SHARDS):
            go(lift_ref.at[rows(f * 192 + half * 96, 96)], target.at[f, pl.ds(0, 96)])
    for t in range(3):
        cols = pl.ds(256 * t, 256)
        down_ref[:, cols] = mm_tn(m_ref[...], grad_ref[:, cols]).astype(BF16)
        proj_ref[:, cols] = mm_tn(o_ref[...], gb_ref[:, cols]).astype(BF16)
    for target, half in sides:
        for f in range(SHARDS):
            for b in range(3):
                cols = pl.ds(b * D, D)
                go(proj_ref.at[rows(f * 192 + b * 64 + half * 32, 32)], target.at[f, pl.ds(96, 32), cols])
                go(down_ref.at[rows(f * 288 + b * 96 + half * 48, 48)], target.at[f, pl.ds(128, 48), cols])
    for copy in copies:
        copy.wait()


def add_up(parts):
    total = parts[0].astype(F32)
    for part in parts[1:]:
        total = total + part.astype(F32)
    return total.astype(BF16)


def rest_core_kernel(index, keep, other, *outs):
    for d, out in enumerate(outs):
        rows = pl.ds(pl.multiple_of(lax.rem(index[0] + d, 4) * 48, 16), 48)
        for f in range(SHARDS):
            out[f] = add_up([keep[f, rows, :], other[f, rows, :]])


def rest_z_kernel(index, own, a, b, c, *outs):
    for d, out in enumerate(outs):
        f = lax.rem(index[1] + d, 4)
        out[...] = add_up([own[f], a[f], b[f], c[f]])


def qkv_core_kernel(index, keep, other, *outs):
    for d, out in enumerate(outs):
        f = lax.rem(index[1] + d, 4)
        out[...] = add_up([keep[f], other[f]])


def qkv_y_kernel(index, own, a, b, c, out_0, out_1, out_2, out_3, total):
    total[...] = add_up([own[...], a[...], b[...], c[...]])
    for d, out in enumerate((out_0, out_1, out_2, out_3)):
        z = lax.rem(index[0] + d, 4)
        rows = pl.ds(pl.multiple_of(lax.div(z, 2) * 48, 16), 48)
        cols = pl.ds(pl.multiple_of(lax.rem(z, 2) * 1152, 128), 1152)
        out[:, pl.ds(0, 1152)] = total[rows, cols]
        out[:, pl.ds(1152, 128)] = total[pl.ds(0, 48), pl.ds(WIDE, 128)]


def joint_kernel(r0, r1, r2, r3, q0, q1, q2, q3, out):
    out[:, pl.ds(0, WIDE)] = add_up([r0[...], r1[...], r2[...], r3[...]])
    out[:, pl.ds(WIDE, 1280)] = add_up([q0[...], q1[...], q2[...], q3[...]])


def pair_kernel(a, b, out):
    out[...] = add_up([a[...], b[...]])


def final_kernel(index, *refs):
    pieces, (qkv_out, proj_out, lift_out, down_out, gain_out, rest) = refs[:8], refs[8:]
    core = index[2]
    for side in range(2):
        half = core if side == 0 else 1 - core
        for d in range(4):
            piece = pieces[4 * side + d]
            z = lax.rem(index[0] - d + 4, 4)
            rest[side, pl.ds(pl.multiple_of(z * 48, 16), 48), :] = piece[:, pl.ds(0, WIDE)]
            qkv_out[
                pl.ds(pl.multiple_of(half * 96 + lax.div(z, 2) * 48, 16), 48),
                pl.ds(pl.multiple_of(lax.rem(z, 2) * 1152, 128), 1152),
            ] = piece[:, pl.ds(WIDE, 1152)].astype(F32)
        rows = lambda at, size: pl.ds(pl.multiple_of(at, 16), size)
        lift_out[rows(half * 96, 96), :] = rest[side, pl.ds(0, 96), :].astype(F32)
        for b in range(3):
            cols = pl.ds(b * D, D)
            proj_out[rows(b * 64 + half * 32, 32), :] = rest[side, pl.ds(96, 32), cols].astype(F32)
            down_out[rows(b * 96 + half * 48, 48), :] = rest[side, pl.ds(128, 48), cols].astype(F32)
    gain_out[...] = pieces[0][pl.ds(0, 16), pl.ds(WIDE + 1152, 128)].astype(F32)


def call(kernel, name, ins, outs, scratch, flops, limit=24):
    places = {"v": pltpu.VMEM, "a": pl.ANY, "s": pltpu.SMEM}
    return pl.pallas_call(
        kernel,
        name=name,
        out_shape=[jax.ShapeDtypeStruct(out[0], out[1]) for out in outs],
        in_specs=[pl.BlockSpec(memory_space=places[place]) for _, place in ins],
        out_specs=[pl.BlockSpec(memory_space=places[out[2] if len(out) > 2 else "v"]) for out in outs],
        scratch_shapes=scratch,
        compiler_params=pltpu.CompilerParams(vmem_limit_bytes=limit * 2**20),
        cost_estimate=pl.CostEstimate(flops=flops, bytes_accessed=flops // 300, transcendentals=0),
    )(*[array for array, _ in ins])


def travel(block, target):
    pairs = []
    for ctx in range(16):
        for f in range(SHARDS):
            xlo, z, core, g = target(ctx // 8, ctx // 2 % 4, ctx % 2, f)
            pairs.append((ctx * SHARDS + f, (xlo * 8 + z % 4 * 2 + core) * SHARDS + g % 4))
    return lax.ppermute(block, ("ctx", "fsdp"), pairs)


def along_y(block, d):
    return travel(block, lambda x, z, c, f: (x, z, c, f + d))


def along_z(block, d):
    return travel(block, lambda x, z, c, f: (x, z + d, c, f))


def next_shard(block):
    return travel(block, lambda x, z, c, f: (x, z, c, f + 1 - 2 * c))


def swap_core(block):
    return travel(block, lambda x, z, c, f: (x, z, 1 - c, f))


def swap_x(block):
    return travel(block, lambda x, z, c, f: (1 - x, z, c, f))


def halo_rows(block, axis):
    count = lax.axis_size(axis)
    up = [(i, i + 1) for i in range(count - 1)]
    down = [(i + 1, i) for i in range(count - 1)]
    return (
        lax.ppermute(block[:, ROWS - HALF :], axis, up),
        lax.ppermute(block[:, :HALF], axis, down),
    )


def swap_halos(to_low, to_high):
    count = lax.axis_size("ctx")
    up = [(i, i + 1) for i in range(count - 1)]
    down = [(i + 1, i) for i in range(count - 1)]
    return lax.ppermute(to_high, "ctx", up), lax.ppermute(to_low, "ctx", down)


def tables(first_row, lengths):
    half = HD // 2
    frequencies = rope_base ** (-(jnp.arange(half, dtype=F32) * 2.0) / HD)
    positions = first_row - HALF + jnp.arange(EXT, dtype=jnp.int32)
    angles = positions.astype(F32)[:, None] * frequencies[None, :]
    cosine, sine = jnp.cos(angles), jnp.sin(angles)
    cosine = jnp.concatenate([cosine] * 4, axis=1)
    sine = jnp.concatenate([-sine, sine, -sine, sine], axis=1)
    ends = jnp.cumsum(lengths, axis=1)
    doc = jnp.sum((positions[None, :, None] >= ends[:, None, :]).astype(jnp.int32), axis=2)
    query = positions[HALF : HALF + ROWS]
    allowed = (
        (jnp.abs(query[None, :] - positions[:, None]) <= HALF)
        & (positions >= 0)[:, None]
        & (positions < SEQ_LEN)[:, None]
    )[None] & (doc[:, :, None] == doc[:, None, HALF : HALF + ROWS])
    bias = jnp.where(allowed, 0.0, masked_score).astype(F32)
    return cosine, sine, jnp.concatenate([bias, bias], axis=2)


WQKV, WPROJ, WLIFT, WDOWN = [
    pltpu.VMEM((D, WIDE), BF16),
    pltpu.VMEM((D, D), BF16),
    pltpu.VMEM((D, WIDE), BF16),
    pltpu.VMEM((FF, D), BF16),
]
SAVED = [
    ((OWN, D), BF16),
    ((MICRO * EXT, D), BF16),
    ((MICRO * EXT, D), BF16),
    ((MICRO, TILES, EXT, 2 * ROWS), BF16),
    ((OWN, D), BF16),
    ((OWN, D), F32),
    ((OWN, FF), BF16),
    ((OWN, FF), F32),
    ((OWN, FF), F32),
]
STREAM = [pltpu.VMEM((MICRO * EXT, D), BF16)] * 2
GRADS_OUT = [
    ((OWN, D), F32),
    ((OWN, D), BF16),
    ((OWN, 2 * D), F32),
    ((MICRO, HALF, 2 * D), BF16),
    ((MICRO, HALF, 2 * D), BF16),
]


TURN_OUT = [((MICRO, ROWS, D), BF16)] + SAVED + [((OWN, D), BF16)]
BACK_OUT = [((OWN, D), BF16), ((OWN, WIDE), BF16), ((OWN, D), BF16), ((OWN, D), BF16)]


def sems(count):
    return pltpu.SemaphoreType.DMA((count,))


def body(
    inputs, out_grad, doc_lengths, attn_gain, qkv_weight, proj_weight, mlp_gain, lift_weight, down_weight
):
    on_first = lax.axis_index("section") == 0
    flag = on_first.astype(jnp.int32).reshape(1)
    ctx, f = lax.axis_index("ctx"), lax.axis_index("fsdp")
    index = jnp.stack([ctx // 2 % 4, f, ctx % 2]).astype(jnp.int32)
    qkv_shard, lift_shard, proj_shard, down_shard = qkv_weight[0], lift_weight[0], proj_weight[0], down_weight[0]
    own, cotangent = inputs[:, 0], out_grad[:, 0]
    low, high = halo_rows(own, "ctx")
    gain_tile = jnp.pad(
        jnp.pad(jnp.stack([attn_gain[0], mlp_gain[0]]), ((0, 0), (0, 64))).reshape(4, 128), ((0, 12), (0, 0))
    )
    qkv_pack, qkv_half = call(
        pack_qkv_kernel, "pack_qkv",
        [(index, "s"), (qkv_shard, "a"), (gain_tile, "a")],
        [((192, 2432), BF16, "a"), ((96, 2432), BF16, "a")],
        [sems(4)], 0, 8,
    )
    rest, rest_half = call(
        pack_kernel, "pack_rest",
        [(index, "s"), (lift_shard, "a"), (proj_shard, "a"), (down_shard, "a")],
        [((352, WIDE), BF16, "a"), ((176, WIDE), BF16, "a")],
        [sems(14)], 0, 8,
    )
    first = next_shard(qkv_pack)
    second = along_y(qkv_half, 2)
    cosine, sine, bias = tables(ctx * ROWS, doc_lengths[:, 0])
    first, second, rest, rest_half, cosine, sine, bias, low, high = lax.optimization_barrier(
        (first, second, rest, rest_half, cosine, sine, bias, low, high)
    )
    qkv_pieces = first, swap_core(first), second, swap_core(second)
    stream = ((MICRO, ROWS, D), BF16)
    scratch = lambda items: [pltpu.VMEM(s, k) for s, k in items]

    o, gains, wqkv = call(
        forward_attention_kernel, "forward_attention",
        [(index, "s"), (own, "v"), (low, "v"), (high, "v"), (gain_tile, "a"), (cosine, "v"), (sine, "v"), (bias, "v"),
         (qkv_shard, "a"), *[(piece, "a") for piece in qkv_pieces]],
        [((OWN, D), BF16), ((2, D), F32), ((D, WIDE), BF16, "a")],
        [WQKV, pltpu.VMEM((SHARDS, 16, 128), BF16)] + STREAM + scratch(SAVED[:4]) + [sems(9), pltpu.SemaphoreType.DMA(())],
        1_400_000_000,
    )
    rest_first, rest_second, o = lax.optimization_barrier((next_shard(rest), along_y(rest_half, 2), o))
    rest_pieces = rest_first, swap_core(rest_first), rest_second, swap_core(rest_second)
    relay, wproj, wlift, wdown = call(
        forward_mlp_kernel, "forward_mlp",
        [(index, "s"), (own, "v"), (o, "v"), (gains, "v"), (lift_shard, "a"), (proj_shard, "a"), (down_shard, "a"),
         *[(piece, "a") for piece in rest_pieces]],
        [stream, ((D, D), BF16, "a"), ((D, WIDE), BF16, "a"), ((FF, D), BF16, "a")],
        [WPROJ, WLIFT, WDOWN] + scratch(SAVED[5:7]) + [sems(34)],
        1_800_000_000,
    )
    relayed = lax.ppermute(relay, "section", [(0, 1)])
    other_low, other_high = halo_rows(relayed, "ctx")
    (h3, q, k, v, p, o, h2, m_act, left, right, src, dh2, dq, dkv, to_low, to_high) = call(
        turning_kernel, "layer_turn",
        [(flag, "s"), (own, "v"), (low, "v"), (high, "v"), (relayed, "v"), (other_low, "v"), (other_high, "v"),
         (cotangent, "v"), (gains, "v"), (cosine, "v"), (sine, "v"), (bias, "v"),
         (wqkv, "a"), (wproj, "a"), (wlift, "a"), (wdown, "a")],
        [(*item, "a") for item in TURN_OUT] + GRADS_OUT,
        [WQKV, WPROJ, WLIFT, WDOWN] + STREAM
        + [pltpu.VMEM((OWN, WIDE), BF16), pltpu.VMEM((OWN, D), BF16)] + scratch(TURN_OUT) + [sems(15)],
        6_000_000_000, 44,
    )
    from_low, from_high = swap_halos(to_low, to_high)
    (grad_relay,) = call(
        source_kernel, "layer_source",
        [(src, "v"), (gains, "v"), (dh2, "v"), (dq, "v"), (dkv, "v"), (from_low, "v"), (from_high, "v"), (wqkv, "a")],
        [stream],
        [WQKV, pltpu.VMEM((OWN, WIDE), BF16), sems(1)],
        900_000_000,
    )
    incoming = lax.ppermute(grad_relay, "section", [(1, 0)])
    (grad_low, du, gb, b, mlp_gain_grad, dh2, dq, dkv, to_low, to_high) = call(
        back_kernel, "layer_back",
        [(flag, "s"), (incoming, "v"), (cotangent, "v"), (gains, "v"), (cosine, "v"), (sine, "v"),
         (wproj, "a"), (wlift, "a"), (wdown, "a"),
         *[(array, "a") for array in (q, k, v, p, h2, left, right)]],
        [(*item, "a") for item in BACK_OUT] + [((1, D), F32)] + GRADS_OUT,
        [WPROJ, WLIFT, WDOWN, pltpu.VMEM((OWN, D), BF16)]
        + scratch(SAVED[:4] + SAVED[5:6] + SAVED[7:] + BACK_OUT) + [sems(14)],
        3_000_000_000, 40,
    )
    from_low, from_high = swap_halos(to_low, to_high)
    rest_keep, rest_send = call(
        weight_grad_kernel, "weight_grads",
        [(index, "s"), (m_act, "v"), (grad_low, "v"), (b, "v"), (du, "v"), (o, "v"), (gb, "v")],
        [((SHARDS, 192, WIDE), BF16, "a")] * 2,
        [WDOWN, WLIFT, WPROJ, pltpu.VMEM((16, WIDE), BF16), sems(64)],
        1_600_000_000,
    )
    from_low, from_high, rest_send = lax.optimization_barrier((from_low, from_high, rest_send))
    rest_other = swap_core(rest_send)
    in_grad, qkv_keep, qkv_send = call(
        source_grad_kernel, "layer_source_grads",
        [(index, "s"), (src, "v"), (gains, "v"), (dh2, "v"), (dq, "v"), (dkv, "v"), (from_low, "v"),
         (from_high, "v"), (mlp_gain_grad, "v"), (wqkv, "a")],
        [stream, ((SHARDS, 96, 2432), BF16, "a"), ((SHARDS, 96, 2432), BF16, "a")],
        [WQKV, pltpu.VMEM((OWN, WIDE), BF16), WQKV, pltpu.VMEM((SHARDS, 96, 128), BF16), sems(17)],
        1_800_000_000,
    )
    qkv_other = swap_core(qkv_send)

    rest_z = call(
        rest_core_kernel, "rest_core_sum", [(index, "s"), (rest_keep, "v"), (rest_other, "v")],
        [((SHARDS, 48, WIDE), BF16)] * 4, [], 0, 24,
    )
    qkv_keep, _ = lax.optimization_barrier((qkv_keep, rest_z[0]))
    rest_y = call(
        rest_z_kernel, "rest_z_sum",
        [(index, "s"), (rest_z[0], "v"), *[(along_z(rest_z[d], d), "v") for d in (1, 2, 3)]],
        [((48, WIDE), BF16)] * 4, [], 0, 24,
    )
    qkv_y = call(
        qkv_core_kernel, "qkv_core_sum", [(index, "s"), (qkv_keep, "v"), (qkv_other, "v")],
        [((96, 2432), BF16)] * 4, [], 0, 24,
    )
    qkv_z = call(
        qkv_y_kernel, "qkv_y_sum",
        [(index, "s"), (qkv_y[0], "v"), *[(along_y(qkv_y[d], d), "v") for d in (1, 2, 3)]],
        [((48, 1280), BF16)] * 4, [pltpu.VMEM((96, 2432), BF16)], 0, 24,
    )
    (joint,) = call(
        joint_kernel, "joint_sum",
        [(rest_y[0], "v"), *[(along_y(rest_y[d], d), "v") for d in (1, 2, 3)],
         (qkv_z[0], "v"), *[(along_z(qkv_z[d], d), "v") for d in (1, 2, 3)]],
        [((48, 3584), BF16)], [], 0, 24,
    )
    (joint,) = call(
        pair_kernel, "pair_sum", [(joint, "v"), (swap_x(joint), "v")], [((48, 3584), BF16)], [], 0, 24
    )
    mine = [joint] + [along_z(joint, d) for d in (1, 2, 3)]
    theirs = [swap_core(piece) for piece in mine]
    qkv_sum, proj_sum, lift_sum, down_sum, gain_sums = call(
        final_kernel, "final_shard", [(index, "s"), *[(piece, "v") for piece in mine + theirs]],
        [((192, WIDE), F32), ((192, D), F32), ((192, WIDE), F32), ((288, D), F32), ((16, 128), F32)],
        [pltpu.VMEM((2, 192, WIDE), BF16)], 0, 24,
    )
    return (
        h3[None, :, None],
        in_grad[None, :, None],
        gain_sums[0:2].reshape(1, 256)[:, :192],
        qkv_sum[None],
        proj_sum[None],
        gain_sums[2:4].reshape(1, 256)[:, :192],
        lift_sum[None],
        down_sum[None],
    )


def solution(mesh):
    placed = (
        P(None, "fsdp", "ctx", None),
        P(None, "fsdp", "ctx", None),
        P(None, "fsdp", None),
        P("section", "fsdp"),
        P("section", "fsdp", None),
        P("section", "fsdp", None),
        P("section", "fsdp"),
        P("section", "fsdp", None),
        P("section", "fsdp", None),
    )
    return jax.shard_map(
        body,
        mesh=mesh,
        in_specs=placed,
        out_specs=(
            P("section", None, "fsdp", "ctx", None),
            P("section", None, "fsdp", "ctx", None),
            P("section", "fsdp"),
            P("section", "fsdp", None),
            P("section", "fsdp", None),
            P("section", "fsdp"),
            P("section", "fsdp", None),
            P("section", "fsdp", None),
        ),
        check_vma=False,
    )
```

```python
import functools

import jax
import jax.numpy as jnp
from jax import lax
from jax.experimental import pallas as pl
from jax.experimental.pallas import tpu as pltpu
from jax.sharding import PartitionSpec as P

D = 768
HD = 64
HALF = 64
SEQ_LEN = 2048
FF = 1152
WIDE = 2304
ROWS = 128
EXT = ROWS + 2 * HALF
MICRO = 2
OWN = MICRO * ROWS
SHARDS = 4
TILES = D // 128
GROUP = 2
norm_eps = 1e-05
rope_base = 10000.0
masked_score = -1e30
root_half = 0.7071067811865476
inv_root_tau = 0.3989422804014327
F32 = jnp.float32
BF16 = jnp.bfloat16


def mm(left, right):
    return lax.dot_general(left, right, (((1,), (0,)), ((), ())), preferred_element_type=F32)


def mm_nt(left, right):
    return lax.dot_general(left, right, (((1,), (1,)), ((), ())), preferred_element_type=F32)


def mm_tn(left, right):
    return lax.dot_general(left, right, (((0,), (0,)), ((), ())), preferred_element_type=F32)


def norm_parts(hidden):
    centre = hidden - jnp.mean(hidden, axis=-1, keepdims=True)
    inv_scale = lax.rsqrt(jnp.mean(centre * centre, axis=-1, keepdims=True) + norm_eps)
    return centre * inv_scale, inv_scale


def norm_back(grad_out, gain, normed, inv_scale):
    grad_normed = grad_out * gain
    inner = (
        grad_normed
        - jnp.mean(grad_normed, axis=-1, keepdims=True)
        - normed * jnp.mean(grad_normed * normed, axis=-1, keepdims=True)
    )
    return inner * inv_scale


def lane_is_low(shape, period):
    return lax.broadcasted_iota(jnp.int32, shape, 1) % period < period // 2


def turn(x):
    return jnp.where(lane_is_low(x.shape, HD), pltpu.roll(x, 96, 1), pltpu.roll(x, 32, 1))


def rotate(x, cosine, sine):
    return x * cosine + turn(x) * sine


def rotate_back(x, cosine, sine):
    return x * cosine - turn(x) * sine


def stack_heads(x):
    low = lane_is_low(x.shape, 128)
    zero = jnp.zeros_like(x)
    return jnp.concatenate([jnp.where(low, x, zero), jnp.where(low, zero, x)], axis=0)


def join_heads(x):
    half = x.shape[0] // 2
    low = lane_is_low((half, 128), 128)
    return jnp.where(low, x[:half], x[half:])


def start_weights(sources, buffers, sems):
    waits = {}
    for index, (name, source) in enumerate(sources.items()):
        copy = pltpu.make_async_copy(source, buffers[name], sems.at[index])
        copy.start()
        waits[name] = [copy]
    return waits


def finish(waits, name):
    for copy in waits[name]:
        copy.wait()


def load_stream(flag, own, low, high, other, ext):
    for m in range(MICRO):
        for ref, alt, start, size in (
            (low, other[1], 0, HALF),
            (own, other[0], HALF, ROWS),
            (high, other[2], HALF + ROWS, HALF),
        ):
            value = ref[m]
            if alt is not None:
                value = jnp.where(flag, value, alt[m])
            ext[pl.ds(m * EXT + start, size), :] = value


def own_rows(x):
    return jnp.concatenate([x[HALF : HALF + ROWS], x[EXT + HALF : EXT + HALF + ROWS]], axis=0)


def repeat(count, step):
    lax.fori_loop(0, count, lambda i, carry: (step(i), carry)[1], 0)


def span(start, size, unit=128):
    return pl.ds(pl.multiple_of(start, unit), size)


def by_tiles(unit):
    def step(i):
        for j in range(GROUP):
            unit(i * GROUP + j)

    repeat(TILES // GROUP, step)


def norm_rows(source, gain, target):
    def step(i):
        rows = span(i * 128, 128)
        normed, _ = norm_parts(source[rows, :].astype(F32))
        target[rows, :] = (normed * gain).astype(BF16)

    repeat(source.shape[0] // 128, step)


def forward_attention(ext, gain, wqkv, cos_ref, sin_ref, bias_ref, a_ext, q_ref, k_ref, v_ref, p_ref, o_ref):
    norm_rows(ext, gain, a_ext)
    a_own = o_ref
    a_own[...] = own_rows(a_ext[...])
    own_span = pl.ds(HALF, ROWS)

    def project(t):
        cols = span(256 * t, 256)
        queries = mm(a_own[...], wqkv[:, cols])
        keys = mm(a_ext[...], wqkv[:, span(D + 256 * t, 256)])
        v_ref[:, cols] = mm(a_ext[...], wqkv[:, span(2 * D + 256 * t, 256)]).astype(BF16)
        for s in range(2):
            tile, lanes = span(256 * t + 128 * s, 128), slice(128 * s, 128 * s + 128)
            for m in range(MICRO):
                part = queries[m * ROWS : (m + 1) * ROWS, lanes]
                turned = rotate(part, cos_ref[own_span, :], sin_ref[own_span, :]).astype(BF16)
                q_ref[pl.ds(m * ROWS, ROWS), tile] = turned * jnp.asarray(0.125, BF16)
                part = keys[m * EXT : (m + 1) * EXT, lanes]
                k_ref[pl.ds(m * EXT, EXT), tile] = rotate(part, cos_ref[...], sin_ref[...]).astype(BF16)

    repeat(3, project)

    def unit(t):
        cols = pl.ds(pl.multiple_of(t * 128, 128), 128)
        for m in range(MICRO):
            q2 = stack_heads(q_ref[pl.ds(m * ROWS, ROWS), cols])
            scores = mm_nt(k_ref[pl.ds(m * EXT, EXT), cols], q2) + bias_ref[m]
            terms = jnp.exp(scores - jnp.max(scores, axis=0, keepdims=True))
            probs = (terms * (1.0 / jnp.sum(terms, axis=0, keepdims=True))).astype(BF16)
            p_ref[m, t] = probs
            attended = mm_tn(probs, v_ref[pl.ds(m * EXT, EXT), cols])
            o_ref[pl.ds(m * ROWS, ROWS), cols] = join_heads(attended).astype(BF16)

    by_tiles(unit)


def forward_mlp(own, o_ref, wproj, mlp_gain, wlift, wdown, h2_ref, b_ref, m_ref, left_ref, right_ref, h3_ref, waits):
    finish(waits, "proj")

    def mix(t):
        cols = span(256 * t, 256)
        added = mm(o_ref[...], wproj[:, cols])
        for m in range(MICRO):
            rows = pl.ds(m * ROWS, ROWS)
            h2_ref[rows, cols] = own[m, :, cols].astype(F32) + added[m * ROWS : (m + 1) * ROWS]

    repeat(3, mix)
    norm_rows(h2_ref, mlp_gain, b_ref)
    finish(waits, "lift")

    def lift(t):
        cols = span(384 * t, 384)
        gate = mm(b_ref[...], wlift[:, cols])
        up = mm(b_ref[...], wlift[:, span(FF + 384 * t, 384)])
        cdf = 0.5 * (1.0 + lax.erf(gate * root_half))
        gelu = gate * cdf
        m_ref[:, cols] = (gelu * up).astype(BF16)
        if left_ref is not None:
            pdf = jnp.exp(-0.5 * gate * gate) * inv_root_tau
            left_ref[:, cols] = up * (cdf + gate * pdf)
            right_ref[:, cols] = gelu

    repeat(3, lift)
    finish(waits, "down")

    def down(t):
        cols = span(256 * t, 256)
        h3 = (h2_ref[:, cols] + mm(m_ref[...], wdown[:, cols])).astype(BF16)
        for m in range(MICRO):
            h3_ref[m, :, cols] = h3[m * ROWS : (m + 1) * ROWS]

    repeat(3, down)


def backward_mlp(grad_ref, h2_ref, mlp_gain, wproj, wlift, wdown, left_ref, right_ref, du_ref, gb_ref, do_ref,
                 dh2_ref, b_ref, mlp_ref):
    def lift(t):
        cols = span(384 * t, 384)
        dm = mm_nt(grad_ref[...], wdown[cols, :])
        du_ref[:, cols] = (dm * left_ref[:, cols]).astype(BF16)
        du_ref[:, span(FF + 384 * t, 384)] = (dm * right_ref[:, cols]).astype(BF16)

    repeat(3, lift)

    def source(t):
        rows = span(256 * t, 256)
        dh2_ref[:, rows] = mm_nt(du_ref[...], wlift[rows, :])

    repeat(3, source)
    if mlp_ref is not None:
        mlp_ref[...] = jnp.zeros_like(mlp_ref)

    def norm(i):
        rows = span(i * 128, 128)
        db = dh2_ref[rows, :]
        normed, inv_scale = norm_parts(h2_ref[rows, :])
        dh2 = grad_ref[rows, :].astype(F32) + norm_back(db, mlp_gain, normed, inv_scale)
        dh2_ref[rows, :] = dh2
        gb_ref[rows, :] = dh2.astype(BF16)
        if mlp_ref is not None:
            mlp_ref[...] += jnp.sum(db * normed, axis=0, keepdims=True)
            b_ref[rows, :] = (normed * mlp_gain).astype(BF16)

    repeat(2, norm)

    def attended(t):
        rows = span(256 * t, 256)
        do_ref[:, rows] = mm_nt(gb_ref[...], wproj[rows, :]).astype(BF16)

    repeat(3, attended)


def backward_attention(q_ref, k_ref, v_ref, p_ref, do_ref, cos_ref, sin_ref, dq_ref, dkv_ref, low_ref, high_ref):
    cosine, sine = cos_ref[...], sin_ref[...]
    cos_own, sin_own = cosine[HALF : HALF + ROWS], sine[HALF : HALF + ROWS]

    def unit(t):
        cols = pl.ds(pl.multiple_of(t * 128, 128), 128)
        value_cols = pl.ds(pl.multiple_of(D + t * 128, 128), 128)
        for m in range(MICRO):
            rows = pl.ds(m * ROWS, ROWS)
            q2 = stack_heads(q_ref[rows, cols])
            do2 = stack_heads(do_ref[rows, cols])
            probs = p_ref[m, t]
            dprobs = mm_nt(v_ref[pl.ds(m * EXT, EXT), cols], do2)
            wide = probs.astype(F32)
            inner = jnp.sum(wide * dprobs, axis=0, keepdims=True)
            ds = (wide * (dprobs - inner)).astype(BF16)
            dq = join_heads(mm_tn(ds, k_ref[pl.ds(m * EXT, EXT), cols])) * 0.125
            dq_ref[rows, cols] = rotate_back(dq, cos_own, sin_own).astype(BF16)
            dk = rotate_back(mm(ds, q2), cosine, sine)
            dv = mm(probs, do2)
            for grad, where in ((dk, cols), (dv, value_cols)):
                low_ref[m, :, where] = grad[:HALF].astype(BF16)
                dkv_ref[rows, where] = grad[HALF : HALF + ROWS]
                high_ref[m, :, where] = grad[HALF + ROWS :].astype(BF16)

    by_tiles(unit)


def place_shards(index, own, first, first_other, second, second_other, put):
    f, core = index[1], index[2]
    put(own, f, None)
    put(first, lax.rem(f + 3 + 2 * core, 4), None)
    put(first_other, lax.rem(f + 1 + 2 * core, 4), None)
    put(second, lax.rem(f + 2, 4), core)
    put(second_other, lax.rem(f + 2, 4), 1 - core)


def pack_qkv_kernel(index, qkv, gains, own, whole, half, first_rows, last_rows, sems):
    rows = pl.ds(pl.multiple_of(index[2] * 96, 16), 96)
    copies = [
        pltpu.make_async_copy(src, dst, sems.at[n])
        for n, (src, dst) in enumerate((
            (qkv, whole.at[:, pl.ds(0, WIDE)]),
            (gains, whole.at[pl.ds(0, 16), pl.ds(WIDE, 128)]),
            (qkv.at[rows], half.at[:, pl.ds(0, WIDE)]),
            (gains, half.at[pl.ds(0, 16), pl.ds(WIDE, 128)]),
            (own.at[:, pl.ds(0, HALF)], first_rows),
            (own.at[:, pl.ds(ROWS - HALF, HALF)], last_rows),
        ))
    ]
    for copy in copies:
        copy.start()
    for copy in copies:
        copy.wait()


def pack_kernel(index, lift, proj, down, rest, rest_half, sems):
    core = index[2]
    copies = []

    def go(src, dst):
        copy = pltpu.make_async_copy(src, dst, sems.at[len(copies)])
        copy.start()
        copies.append(copy)

    half = lambda size: pl.ds(pl.multiple_of(core * size, 16), size)
    go(lift, rest.at[pl.ds(0, 192)])
    go(lift.at[half(96)], rest_half.at[pl.ds(0, 96)])
    for block in range(3):
        cols = pl.ds(block * D, D)
        go(proj.at[pl.ds(64 * block, 64)], rest.at[pl.ds(192, 64), cols])
        go(down.at[pl.ds(96 * block, 96)], rest.at[pl.ds(256, 96), cols])
        go(
            proj.at[pl.ds(pl.multiple_of(64 * block + core * 32, 16), 32)],
            rest_half.at[pl.ds(96, 32), cols],
        )
        go(
            down.at[pl.ds(pl.multiple_of(96 * block + core * 48, 16), 48)],
            rest_half.at[pl.ds(128, 48), cols],
        )
    for copy in copies:
        copy.wait()


def gather_gain(tiles, row):
    parts = []
    for tile in tiles:
        parts += [tile[row : row + 1, :], tile[row + 1 : row + 2, :64]]
    return jnp.concatenate(parts, axis=1)


def forward_attention_kernel(index, own, low, high, gain_tile, cos_ref, sin_ref, bias_ref,
                             shard, first, first_other, second, second_other,
                             o, gains, whole, wqkv, tiles, ext, a_ext, q, k, v, p, sems, out_sem):
    copies = []

    def go(src, dst):
        copy = pltpu.make_async_copy(src, dst, sems.at[len(copies)])
        copy.start()
        copies.append(copy)

    def put(piece, f, half):
        at, size = (f * 192, 192) if half is None else (f * 192 + half * 96, 96)
        rows = pl.ds(pl.multiple_of(at, 16), size)
        go(piece if piece is shard else piece.at[:, pl.ds(0, WIDE)], wqkv.at[rows])
        if piece is not shard and piece is not second_other:
            go(piece.at[pl.ds(0, 16), pl.ds(WIDE, 128)], tiles.at[f])

    place_shards(index, shard, first, first_other, second, second_other, put)
    go(gain_tile, tiles.at[index[1]])
    load_stream(None, own, low, high, (None, None, None), ext)
    for copy in copies:
        copy.wait()
    out = pltpu.make_async_copy(wqkv, whole, out_sem)
    out.start()
    shards = [tiles[f].astype(F32) for f in range(SHARDS)]
    gains[0:1, :] = gather_gain(shards, 0)
    gains[1:2, :] = gather_gain(shards, 2)
    forward_attention(ext, gains[0:1], wqkv, cos_ref, sin_ref, bias_ref, a_ext, q, k, v, p, o)
    out.wait()


def forward_mlp_kernel(index, own, o, gains, lift, proj, down, first, first_other, second, second_other,
                       h3_ref, whole_proj, whole_lift, whole_down, wproj, wlift, wdown, h2, b, m_out, sems):
    waits = {"proj": [], "lift": [], "down": []}
    count = [0]

    def go(name, src, dst):
        copy = pltpu.make_async_copy(src, dst, sems.at[count[0]])
        copy.start()
        count[0] += 1
        waits[name].append(copy)

    f = index[1]

    def put(piece, s, half):
        rows = lambda at, size: pl.ds(pl.multiple_of(at, 16), size)
        if piece is None:
            go("proj", proj, wproj.at[rows(f * 192, 192)])
            go("lift", lift, wlift.at[rows(f * 192, 192)])
            go("down", down, wdown.at[rows(f * 288, 288)])
            return
        n = 2 if half is None else 1
        h = 0 if half is None else half
        go("lift", piece.at[pl.ds(0, 96 * n)], wlift.at[rows(s * 192 + h * 96, 96 * n)])
        for b in range(3):
            cols = pl.ds(b * D, D)
            go("proj", piece.at[pl.ds(96 * n, 32 * n), cols], wproj.at[rows(s * 192 + b * 64 + h * 32, 32 * n)])
            go("down", piece.at[pl.ds(128 * n, 48 * n), cols], wdown.at[rows(s * 288 + b * 96 + h * 48, 48 * n)])

    place_shards(index, None, first, first_other, second, second_other, put)
    outs = []
    for name, buffer, whole in (("proj", wproj, whole_proj), ("lift", wlift, whole_lift), ("down", wdown, whole_down)):
        finish(waits, name)
        copy = pltpu.make_async_copy(buffer, whole, sems.at[count[0]])
        copy.start()
        count[0] += 1
        outs.append(copy)
        waits[name] = []
    forward_mlp(own, o, wproj, gains[1:2], wlift, wdown, h2, b, m_out, None, None, h3_ref, waits)
    for copy in outs:
        copy.wait()


def start_all(pairs, sems, first):
    copies = [pltpu.make_async_copy(src, dst, sems.at[first + n]) for n, (src, dst) in enumerate(pairs)]
    for copy in copies:
        copy.start()
    return copies


def turning_kernel(flag_ref, own, low, high, other_own, other_low, other_high, cotangent, gains,
                   cos_ref, sin_ref, bias_ref, qkv_hbm, proj_hbm, lift_hbm, down_hbm, *refs):
    kept, (dh2_ref, dq, dkv, to_low, to_high) = refs[:11], refs[11:16]
    wqkv, wproj, wlift, wdown, ext, a_ext, mine, du, do, h3_ref, q, k, v, p, o, h2, m_out, left, right, src, sems = refs[16:]
    waits = start_weights(
        {"qkv": qkv_hbm, "proj": proj_hbm, "lift": lift_hbm, "down": down_hbm},
        {"qkv": wqkv, "proj": wproj, "lift": wlift, "down": wdown}, sems,
    )
    flag = flag_ref[0] == 1
    load_stream(flag, own, low, high, (other_own, other_low, other_high), ext)
    for m in range(MICRO):
        mine[m] = ext[pl.ds(m * EXT + HALF, ROWS), :]
        src[pl.ds(m * ROWS, ROWS), :] = mine[m]
    finish(waits, "qkv")
    forward_attention(ext, gains[0:1], wqkv, cos_ref, sin_ref, bias_ref, a_ext, q, k, v, p, o)
    outs = start_all(zip((q, k, v, p, o, src), kept[1:6] + kept[10:]), sems, 4)
    spare = a_ext.at[pl.ds(0, OWN)]
    forward_mlp(mine, o, wproj, gains[1:2], wlift, wdown, h2, spare, m_out, left, right, h3_ref, waits)
    outs += start_all(zip((h3_ref, h2, m_out, left, right), kept[:1] + kept[6:10]), sems, 10)
    grad = a_ext.at[pl.ds(OWN, OWN)]
    for m in range(MICRO):
        grad[pl.ds(m * ROWS, ROWS), :] = cotangent[m]
    backward_mlp(grad, h2, gains[1:2], wproj, wlift, wdown, left, right, du, spare, do, dh2_ref, None, None)
    backward_attention(q, k, v, p, do, cos_ref, sin_ref, dq, dkv, to_low, to_high)
    for copy in outs:
        copy.wait()


def back_kernel(flag_ref, incoming, cotangent, gains, cos_ref, sin_ref, proj_hbm, lift_hbm, down_hbm,
                q_hbm, k_hbm, v_hbm, p_hbm, h2_hbm, left_hbm, right_hbm, *refs):
    kept, (mlp_ref, dh2_ref, dq, dkv, to_low, to_high) = refs[:4], refs[4:10]
    wproj, wlift, wdown, do, q, k, v, p, h2, left, right, grad_ref, du, gb_ref, b_ref, sems = refs[10:]
    early = start_all(
        ((down_hbm, wdown), (left_hbm, left), (right_hbm, right), (lift_hbm, wlift), (h2_hbm, h2), (proj_hbm, wproj)),
        sems, 0,
    )
    late = start_all(((q_hbm, q), (v_hbm, v), (p_hbm, p), (k_hbm, k)), sems, 6)
    flag = flag_ref[0] == 1
    for m in range(MICRO):
        grad_ref[pl.ds(m * ROWS, ROWS), :] = jnp.where(flag, incoming[m], cotangent[m])
    for copy in early:
        copy.wait()
    backward_mlp(
        grad_ref, h2, gains[1:2], wproj, wlift, wdown, left, right, du, gb_ref, do, dh2_ref, b_ref, mlp_ref
    )
    outs = start_all(zip((grad_ref, du, gb_ref, b_ref), kept), sems, 10)
    for copy in late:
        copy.wait()
    backward_attention(q, k, v, p, do, cos_ref, sin_ref, dq, dkv, to_low, to_high)
    for copy in outs:
        copy.wait()


def joined_grads(dq, dkv, from_low, from_high, dqkv):
    dqkv[:, :D] = dq[...]
    for m in range(MICRO):
        first, last = pl.ds(m * ROWS, HALF), pl.ds(m * ROWS + HALF, HALF)
        dqkv[first, D:] = (dkv[first, :] + from_low[m].astype(F32)).astype(BF16)
        dqkv[last, D:] = (dkv[last, :] + from_high[m].astype(F32)).astype(BF16)


def source_kernel(src, gains, dh2, dq, dkv, from_low, from_high, qkv_hbm, out_ref, wqkv, dqkv, sems):
    waits = start_weights({"qkv": qkv_hbm}, {"qkv": wqkv}, sems)
    joined_grads(dq, dkv, from_low, from_high, dqkv)
    normed, inv_scale = norm_parts(src[...].astype(F32))
    finish(waits, "qkv")
    da = mm_nt(dqkv[...], wqkv[...])
    dh = dh2[...] + norm_back(da, gains[0:1], normed, inv_scale)
    for m in range(MICRO):
        out_ref[m] = dh[m * ROWS : (m + 1) * ROWS].astype(BF16)


def gain_block(attn, mlp, f):
    rows = []
    for gain in (attn, mlp):
        rows.append(gain[:, 192 * f : 192 * f + 128])
        rows.append(jnp.concatenate([gain[:, 192 * f + 128 : 192 * f + 192], jnp.zeros((1, 64), F32)], axis=1))
    return jnp.concatenate(rows + [jnp.zeros((92, 128), F32)], axis=0).astype(BF16)


def source_grad_kernel(index, src, gains, dh2, dq, dkv, from_low, from_high, mlp_grad, qkv_hbm,
                       out_ref, keep, send, wqkv, dqkv, qkv_ref, gain_ref, sems):
    waits = start_weights({"qkv": qkv_hbm}, {"qkv": wqkv}, sems)
    joined_grads(dq, dkv, from_low, from_high, dqkv)
    normed, inv_scale = norm_parts(src[...].astype(F32))
    finish(waits, "qkv")
    da = mm_nt(dqkv[...], wqkv[...])
    attn_grad = jnp.sum(da * normed, axis=0, keepdims=True)
    mlp = mlp_grad[...]
    for f in range(SHARDS):
        gain_ref[f] = gain_block(attn_grad, mlp, f)
    a = (normed * gains[0:1]).astype(BF16)
    for t in range(9):
        cols = pl.ds(256 * t, 256)
        qkv_ref[:, cols] = mm_tn(a, dqkv[:, cols]).astype(BF16)
    copies = []
    for target, half in ((send, 1 - index[2]), (keep, index[2])):
        for f in range(SHARDS):
            rows = pl.ds(pl.multiple_of(f * 192 + half * 96, 16), 96)
            for src_ref, dst_ref in (
                (qkv_ref.at[rows], target.at[f, :, pl.ds(0, WIDE)]),
                (gain_ref.at[f], target.at[f, :, pl.ds(WIDE, 128)]),
            ):
                copy = pltpu.make_async_copy(src_ref, dst_ref, sems.at[1 + len(copies)])
                copy.start()
                copies.append(copy)
    dh = dh2[...] + norm_back(da, gains[0:1], normed, inv_scale)
    for m in range(MICRO):
        out_ref[m] = dh[m * ROWS : (m + 1) * ROWS].astype(BF16)
    for copy in copies:
        copy.wait()


def weight_grad_kernel(index, m_ref, grad_ref, b_ref, du, o_ref, gb_ref, keep, send,
                       down_ref, lift_ref, proj_ref, pad_ref, sems):
    core = index[2]
    copies = []

    def go(src, dst):
        copy = pltpu.make_async_copy(src, dst, sems.at[len(copies)])
        copy.start()
        copies.append(copy)

    sides = ((send, 1 - core), (keep, core))
    rows = lambda at, size: pl.ds(pl.multiple_of(at, 16), size)
    pad_ref[...] = jnp.zeros_like(pad_ref)
    for target, _ in sides:
        for f in range(SHARDS):
            go(pad_ref, target.at[f, pl.ds(176, 16)])
    for t in range(9):
        cols = pl.ds(256 * t, 256)
        lift_ref[:, cols] = mm_tn(b_ref[...], du[:, cols]).astype(BF16)
    for target, half in sides:
        for f in range(SHARDS):
            go(lift_ref.at[rows(f * 192 + half * 96, 96)], target.at[f, pl.ds(0, 96)])
    for t in range(3):
        cols = pl.ds(256 * t, 256)
        down_ref[:, cols] = mm_tn(m_ref[...], grad_ref[:, cols]).astype(BF16)
        proj_ref[:, cols] = mm_tn(o_ref[...], gb_ref[:, cols]).astype(BF16)
    for target, half in sides:
        for f in range(SHARDS):
            for b in range(3):
                cols = pl.ds(b * D, D)
                go(proj_ref.at[rows(f * 192 + b * 64 + half * 32, 32)], target.at[f, pl.ds(96, 32), cols])
                go(down_ref.at[rows(f * 288 + b * 96 + half * 48, 48)], target.at[f, pl.ds(128, 48), cols])
    for copy in copies:
        copy.wait()


def add_up(parts):
    total = parts[0].astype(F32)
    for part in parts[1:]:
        total = total + part.astype(F32)
    return total.astype(BF16)


def rest_core_kernel(index, keep, other, *outs):
    for d, out in enumerate(outs):
        rows = pl.ds(pl.multiple_of(lax.rem(index[0] + d, 4) * 48, 16), 48)
        for f in range(SHARDS):
            out[f] = add_up([keep[f, rows, :], other[f, rows, :]])


def rest_z_kernel(index, own, a, b, c, *outs):
    for d, out in enumerate(outs):
        f = lax.rem(index[1] + d, 4)
        out[...] = add_up([own[f], a[f], b[f], c[f]])


def qkv_core_kernel(index, keep, other, *outs):
    for d, out in enumerate(outs):
        f = lax.rem(index[1] + d, 4)
        out[...] = add_up([keep[f], other[f]])


def qkv_y_kernel(index, own, a, b, c, out_0, out_1, out_2, out_3, total):
    total[...] = add_up([own[...], a[...], b[...], c[...]])
    for d, out in enumerate((out_0, out_1, out_2, out_3)):
        z = lax.rem(index[0] + d, 4)
        rows = pl.ds(pl.multiple_of(lax.div(z, 2) * 48, 16), 48)
        cols = pl.ds(pl.multiple_of(lax.rem(z, 2) * 1152, 128), 1152)
        out[:, pl.ds(0, 1152)] = total[rows, cols]
        out[:, pl.ds(1152, 128)] = total[pl.ds(0, 48), pl.ds(WIDE, 128)]


def joint_kernel(r0, r1, r2, r3, q0, q1, q2, q3, out):
    out[:, pl.ds(0, WIDE)] = add_up([r0[...], r1[...], r2[...], r3[...]])
    out[:, pl.ds(WIDE, 1280)] = add_up([q0[...], q1[...], q2[...], q3[...]])


def pair_kernel(a, b, out):
    out[...] = add_up([a[...], b[...]])


def final_kernel(index, *refs):
    pieces, (qkv_out, proj_out, lift_out, down_out, gain_out, rest) = refs[:8], refs[8:]
    core = index[2]
    for side in range(2):
        half = core if side == 0 else 1 - core
        for d in range(4):
            piece = pieces[4 * side + d]
            z = lax.rem(index[0] - d + 4, 4)
            rest[side, pl.ds(pl.multiple_of(z * 48, 16), 48), :] = piece[:, pl.ds(0, WIDE)]
            qkv_out[
                pl.ds(pl.multiple_of(half * 96 + lax.div(z, 2) * 48, 16), 48),
                pl.ds(pl.multiple_of(lax.rem(z, 2) * 1152, 128), 1152),
            ] = piece[:, pl.ds(WIDE, 1152)].astype(F32)
        rows = lambda at, size: pl.ds(pl.multiple_of(at, 16), size)
        lift_out[rows(half * 96, 96), :] = rest[side, pl.ds(0, 96), :].astype(F32)
        for b in range(3):
            cols = pl.ds(b * D, D)
            proj_out[rows(b * 64 + half * 32, 32), :] = rest[side, pl.ds(96, 32), cols].astype(F32)
            down_out[rows(b * 96 + half * 48, 48), :] = rest[side, pl.ds(128, 48), cols].astype(F32)
    gain_out[...] = pieces[0][pl.ds(0, 16), pl.ds(WIDE + 1152, 128)].astype(F32)


def call(kernel, name, ins, outs, scratch, flops, limit=24):
    places = {"v": pltpu.VMEM, "a": pl.ANY, "s": pltpu.SMEM}
    return pl.pallas_call(
        kernel,
        name=name,
        out_shape=[jax.ShapeDtypeStruct(out[0], out[1]) for out in outs],
        in_specs=[pl.BlockSpec(memory_space=places[place]) for _, place in ins],
        out_specs=[pl.BlockSpec(memory_space=places[out[2] if len(out) > 2 else "v"]) for out in outs],
        scratch_shapes=scratch,
        compiler_params=pltpu.CompilerParams(vmem_limit_bytes=limit * 2**20),
        cost_estimate=pl.CostEstimate(flops=flops, bytes_accessed=flops // 300, transcendentals=0),
    )(*[array for array, _ in ins])


def travel(block, target):
    pairs = []
    for ctx in range(16):
        for f in range(SHARDS):
            xlo, z, core, g = target(ctx // 8, ctx // 2 % 4, ctx % 2, f)
            pairs.append((ctx * SHARDS + f, (xlo * 8 + z % 4 * 2 + core) * SHARDS + g % 4))
    return lax.ppermute(block, ("ctx", "fsdp"), pairs)


def along_y(block, d):
    return travel(block, lambda x, z, c, f: (x, z, c, f + d))


def along_z(block, d):
    return travel(block, lambda x, z, c, f: (x, z + d, c, f))


def next_shard(block):
    return travel(block, lambda x, z, c, f: (x, z, c, f + 1 - 2 * c))


def swap_core(block):
    return travel(block, lambda x, z, c, f: (x, z, 1 - c, f))


def swap_x(block):
    return travel(block, lambda x, z, c, f: (1 - x, z, c, f))


def halo_rows(block, axis):
    count = lax.axis_size(axis)
    up = [(i, i + 1) for i in range(count - 1)]
    down = [(i + 1, i) for i in range(count - 1)]
    return (
        lax.ppermute(block[:, ROWS - HALF :], axis, up),
        lax.ppermute(block[:, :HALF], axis, down),
    )


def swap_halos(to_low, to_high):
    count = lax.axis_size("ctx")
    up = [(i, i + 1) for i in range(count - 1)]
    down = [(i + 1, i) for i in range(count - 1)]
    return lax.ppermute(to_high, "ctx", up), lax.ppermute(to_low, "ctx", down)


def tables(first_row, lengths):
    half = HD // 2
    frequencies = rope_base ** (-(jnp.arange(half, dtype=F32) * 2.0) / HD)
    positions = first_row - HALF + jnp.arange(EXT, dtype=jnp.int32)
    angles = positions.astype(F32)[:, None] * frequencies[None, :]
    cosine, sine = jnp.cos(angles), jnp.sin(angles)
    cosine = jnp.concatenate([cosine] * 4, axis=1)
    sine = jnp.concatenate([-sine, sine, -sine, sine], axis=1)
    ends = jnp.cumsum(lengths, axis=1)
    doc = jnp.sum((positions[None, :, None] >= ends[:, None, :]).astype(jnp.int32), axis=2)
    query = positions[HALF : HALF + ROWS]
    allowed = (
        (jnp.abs(query[None, :] - positions[:, None]) <= HALF)
        & (positions >= 0)[:, None]
        & (positions < SEQ_LEN)[:, None]
    )[None] & (doc[:, :, None] == doc[:, None, HALF : HALF + ROWS])
    bias = jnp.where(allowed, 0.0, masked_score).astype(F32)
    return cosine, sine, jnp.concatenate([bias, bias], axis=2)


WQKV, WPROJ, WLIFT, WDOWN = [
    pltpu.VMEM((D, WIDE), BF16),
    pltpu.VMEM((D, D), BF16),
    pltpu.VMEM((D, WIDE), BF16),
    pltpu.VMEM((FF, D), BF16),
]
SAVED = [
    ((OWN, D), BF16),
    ((MICRO * EXT, D), BF16),
    ((MICRO * EXT, D), BF16),
    ((MICRO, TILES, EXT, 2 * ROWS), BF16),
    ((OWN, D), BF16),
    ((OWN, D), F32),
    ((OWN, FF), BF16),
    ((OWN, FF), F32),
    ((OWN, FF), F32),
]
STREAM = [pltpu.VMEM((MICRO * EXT, D), BF16)] * 2
GRADS_OUT = [
    ((OWN, D), F32),
    ((OWN, D), BF16),
    ((OWN, 2 * D), F32),
    ((MICRO, HALF, 2 * D), BF16),
    ((MICRO, HALF, 2 * D), BF16),
]


TURN_OUT = [((MICRO, ROWS, D), BF16)] + SAVED + [((OWN, D), BF16)]
BACK_OUT = [((OWN, D), BF16), ((OWN, WIDE), BF16), ((OWN, D), BF16), ((OWN, D), BF16)]


def sems(count):
    return pltpu.SemaphoreType.DMA((count,))


def body(
    inputs, out_grad, doc_lengths, attn_gain, qkv_weight, proj_weight, mlp_gain, lift_weight, down_weight
):
    on_first = lax.axis_index("section") == 0
    flag = on_first.astype(jnp.int32).reshape(1)
    ctx, f = lax.axis_index("ctx"), lax.axis_index("fsdp")
    index = jnp.stack([ctx // 2 % 4, f, ctx % 2]).astype(jnp.int32)
    qkv_shard, lift_shard, proj_shard, down_shard = qkv_weight[0], lift_weight[0], proj_weight[0], down_weight[0]
    own, cotangent = inputs[:, 0], out_grad[:, 0]
    gain_tile = jnp.pad(
        jnp.pad(jnp.stack([attn_gain[0], mlp_gain[0]]), ((0, 0), (0, 64))).reshape(4, 128), ((0, 12), (0, 0))
    )
    edge = ((MICRO, HALF, D), BF16, "a")
    qkv_pack, qkv_half, first_rows, last_rows = call(
        pack_qkv_kernel, "pack_qkv",
        [(index, "s"), (qkv_shard, "a"), (gain_tile, "a"), (own, "a")],
        [((192, 2432), BF16, "a"), ((96, 2432), BF16, "a"), edge, edge],
        [sems(6)], 0, 8,
    )
    low, high = swap_halos(first_rows, last_rows)
    rest, rest_half = call(
        pack_kernel, "pack_rest",
        [(index, "s"), (lift_shard, "a"), (proj_shard, "a"), (down_shard, "a")],
        [((352, WIDE), BF16, "a"), ((176, WIDE), BF16, "a")],
        [sems(14)], 0, 8,
    )
    first = next_shard(qkv_pack)
    second = along_y(qkv_half, 2)
    cosine, sine, bias = tables(ctx * ROWS, doc_lengths[:, 0])
    first, second, rest, rest_half, cosine, sine, bias, low, high = lax.optimization_barrier(
        (first, second, rest, rest_half, cosine, sine, bias, low, high)
    )
    qkv_pieces = first, swap_core(first), second, swap_core(second)
    stream = ((MICRO, ROWS, D), BF16)
    scratch = lambda items: [pltpu.VMEM(s, k) for s, k in items]

    o, gains, wqkv = call(
        forward_attention_kernel, "forward_attention",
        [(index, "s"), (own, "v"), (low, "v"), (high, "v"), (gain_tile, "a"), (cosine, "v"), (sine, "v"), (bias, "v"),
         (qkv_shard, "a"), *[(piece, "a") for piece in qkv_pieces]],
        [((OWN, D), BF16), ((2, D), F32), ((D, WIDE), BF16, "a")],
        [WQKV, pltpu.VMEM((SHARDS, 16, 128), BF16)] + STREAM + scratch(SAVED[:4]) + [sems(9), pltpu.SemaphoreType.DMA(())],
        1_400_000_000, 56,
    )
    rest_first, rest_second, o = lax.optimization_barrier((next_shard(rest), along_y(rest_half, 2), o))
    rest_pieces = rest_first, swap_core(rest_first), rest_second, swap_core(rest_second)
    relay, wproj, wlift, wdown = call(
        forward_mlp_kernel, "forward_mlp",
        [(index, "s"), (own, "v"), (o, "v"), (gains, "v"), (lift_shard, "a"), (proj_shard, "a"), (down_shard, "a"),
         *[(piece, "a") for piece in rest_pieces]],
        [stream, ((D, D), BF16, "a"), ((D, WIDE), BF16, "a"), ((FF, D), BF16, "a")],
        [WPROJ, WLIFT, WDOWN] + scratch([SAVED[5], SAVED[0], SAVED[6]]) + [sems(34)],
        1_800_000_000, 56,
    )
    relayed = lax.ppermute(relay, "section", [(0, 1)])
    other_low, other_high = halo_rows(relayed, "ctx")
    (h3, q, k, v, p, o, h2, m_act, left, right, src, dh2, dq, dkv, to_low, to_high) = call(
        turning_kernel, "layer_turn",
        [(flag, "s"), (own, "v"), (low, "v"), (high, "v"), (relayed, "v"), (other_low, "v"), (other_high, "v"),
         (cotangent, "v"), (gains, "v"), (cosine, "v"), (sine, "v"), (bias, "v"),
         (wqkv, "a"), (wproj, "a"), (wlift, "a"), (wdown, "a")],
        [(*item, "a") for item in TURN_OUT] + GRADS_OUT,
        [WQKV, WPROJ, WLIFT, WDOWN] + STREAM
        + [pltpu.VMEM((MICRO, ROWS, D), BF16), pltpu.VMEM((OWN, WIDE), BF16), pltpu.VMEM((OWN, D), BF16)] + scratch(TURN_OUT) + [sems(15)],
        6_000_000_000, 44,
    )
    from_low, from_high = swap_halos(to_low, to_high)
    (grad_relay,) = call(
        source_kernel, "layer_source",
        [(src, "v"), (gains, "v"), (dh2, "v"), (dq, "v"), (dkv, "v"), (from_low, "v"), (from_high, "v"), (wqkv, "a")],
        [stream],
        [WQKV, pltpu.VMEM((OWN, WIDE), BF16), sems(1)],
        900_000_000,
    )
    incoming = lax.ppermute(grad_relay, "section", [(1, 0)])
    (grad_low, du, gb, b, mlp_gain_grad, dh2, dq, dkv, to_low, to_high) = call(
        back_kernel, "layer_back",
        [(flag, "s"), (incoming, "v"), (cotangent, "v"), (gains, "v"), (cosine, "v"), (sine, "v"),
         (wproj, "a"), (wlift, "a"), (wdown, "a"),
         *[(array, "a") for array in (q, k, v, p, h2, left, right)]],
        [(*item, "a") for item in BACK_OUT] + [((1, D), F32)] + GRADS_OUT,
        [WPROJ, WLIFT, WDOWN, pltpu.VMEM((OWN, D), BF16)]
        + scratch(SAVED[:4] + SAVED[5:6] + SAVED[7:] + BACK_OUT) + [sems(14)],
        3_000_000_000, 40,
    )
    from_low, from_high = swap_halos(to_low, to_high)
    rest_keep, rest_send = call(
        weight_grad_kernel, "weight_grads",
        [(index, "s"), (m_act, "v"), (grad_low, "v"), (b, "v"), (du, "v"), (o, "v"), (gb, "v")],
        [((SHARDS, 192, WIDE), BF16, "a")] * 2,
        [WDOWN, WLIFT, WPROJ, pltpu.VMEM((16, WIDE), BF16), sems(64)],
        1_600_000_000,
    )
    from_low, from_high, rest_send = lax.optimization_barrier((from_low, from_high, rest_send))
    rest_other = swap_core(rest_send)
    in_grad, qkv_keep, qkv_send = call(
        source_grad_kernel, "layer_source_grads",
        [(index, "s"), (src, "v"), (gains, "v"), (dh2, "v"), (dq, "v"), (dkv, "v"), (from_low, "v"),
         (from_high, "v"), (mlp_gain_grad, "v"), (wqkv, "a")],
        [stream, ((SHARDS, 96, 2432), BF16, "a"), ((SHARDS, 96, 2432), BF16, "a")],
        [WQKV, pltpu.VMEM((OWN, WIDE), BF16), WQKV, pltpu.VMEM((SHARDS, 96, 128), BF16), sems(17)],
        1_800_000_000,
    )
    qkv_other = swap_core(qkv_send)

    rest_z = call(
        rest_core_kernel, "rest_core_sum", [(index, "s"), (rest_keep, "v"), (rest_other, "v")],
        [((SHARDS, 48, WIDE), BF16)] * 4, [], 0, 24,
    )
    rest_y = call(
        rest_z_kernel, "rest_z_sum",
        [(index, "s"), (rest_z[0], "v"), *[(along_z(rest_z[d], d), "v") for d in (1, 2, 3)]],
        [((48, WIDE), BF16)] * 4, [], 0, 24,
    )
    qkv_y = call(
        qkv_core_kernel, "qkv_core_sum", [(index, "s"), (qkv_keep, "v"), (qkv_other, "v")],
        [((96, 2432), BF16)] * 4, [], 0, 24,
    )
    qkv_mine, _ = lax.optimization_barrier((qkv_y[0], rest_y[0]))
    qkv_z = call(
        qkv_y_kernel, "qkv_y_sum",
        [(index, "s"), (qkv_mine, "v"), *[(along_y(qkv_y[d], d), "v") for d in (1, 2, 3)]],
        [((48, 1280), BF16)] * 4, [pltpu.VMEM((96, 2432), BF16)], 0, 24,
    )
    (joint,) = call(
        joint_kernel, "joint_sum",
        [(rest_y[0], "v"), *[(along_y(rest_y[d], d), "v") for d in (1, 2, 3)],
         (qkv_z[0], "v"), *[(along_z(qkv_z[d], d), "v") for d in (1, 2, 3)]],
        [((48, 3584), BF16)], [], 0, 24,
    )
    (joint,) = call(
        pair_kernel, "pair_sum", [(joint, "v"), (swap_x(joint), "v")], [((48, 3584), BF16)], [], 0, 24
    )
    mine = [joint] + [along_z(joint, d) for d in (1, 2, 3)]
    theirs = [swap_core(piece) for piece in mine]
    qkv_sum, proj_sum, lift_sum, down_sum, gain_sums = call(
        final_kernel, "final_shard", [(index, "s"), *[(piece, "v") for piece in mine + theirs]],
        [((192, WIDE), F32), ((192, D), F32), ((192, WIDE), F32), ((288, D), F32), ((16, 128), F32)],
        [pltpu.VMEM((2, 192, WIDE), BF16)], 0, 24,
    )
    return (
        h3[None, :, None],
        in_grad[None, :, None],
        gain_sums[0:2].reshape(1, 256)[:, :192],
        qkv_sum[None],
        proj_sum[None],
        gain_sums[2:4].reshape(1, 256)[:, :192],
        lift_sum[None],
        down_sum[None],
    )


def solution(mesh):
    placed = (
        P(None, "fsdp", "ctx", None),
        P(None, "fsdp", "ctx", None),
        P(None, "fsdp", None),
        P("section", "fsdp"),
        P("section", "fsdp", None),
        P("section", "fsdp", None),
        P("section", "fsdp"),
        P("section", "fsdp", None),
        P("section", "fsdp", None),
    )
    return jax.shard_map(
        body,
        mesh=mesh,
        in_specs=placed,
        out_specs=(
            P("section", None, "fsdp", "ctx", None),
            P("section", None, "fsdp", "ctx", None),
            P("section", "fsdp"),
            P("section", "fsdp", None),
            P("section", "fsdp", None),
            P("section", "fsdp"),
            P("section", "fsdp", None),
            P("section", "fsdp", None),
        ),
        check_vma=False,
    )
```

```python
import functools

import jax
import jax.numpy as jnp
from jax import lax
from jax.experimental import pallas as pl
from jax.experimental.pallas import tpu as pltpu
from jax.sharding import PartitionSpec as P

D = 768
HD = 64
HALF = 64
SEQ_LEN = 2048
FF = 1152
WIDE = 2304
ROWS = 128
EXT = ROWS + 2 * HALF
MICRO = 2
OWN = MICRO * ROWS
SHARDS = 4
TILES = D // 128
norm_eps = 1e-05
rope_base = 10000.0
masked_score = -1e30
root_half = 0.7071067811865476
inv_root_tau = 0.3989422804014327
F32 = jnp.float32
BF16 = jnp.bfloat16


def mm(left, right):
    return lax.dot_general(left, right, (((1,), (0,)), ((), ())), preferred_element_type=F32)


def mm_nt(left, right):
    return lax.dot_general(left, right, (((1,), (1,)), ((), ())), preferred_element_type=F32)


def mm_tn(left, right):
    return lax.dot_general(left, right, (((0,), (0,)), ((), ())), preferred_element_type=F32)


def norm_parts(hidden):
    centre = hidden - jnp.mean(hidden, axis=-1, keepdims=True)
    inv_scale = lax.rsqrt(jnp.mean(centre * centre, axis=-1, keepdims=True) + norm_eps)
    return centre * inv_scale, inv_scale


def norm_back(grad_out, gain, normed, inv_scale):
    grad_normed = grad_out * gain
    inner = (
        grad_normed
        - jnp.mean(grad_normed, axis=-1, keepdims=True)
        - normed * jnp.mean(grad_normed * normed, axis=-1, keepdims=True)
    )
    return inner * inv_scale


def lane_is_low(shape, period):
    return lax.broadcasted_iota(jnp.int32, shape, 1) % period < period // 2


def turn(x):
    return jnp.where(lane_is_low(x.shape, HD), pltpu.roll(x, 96, 1), pltpu.roll(x, 32, 1))


def rotate(x, cosine, sine):
    return x * cosine + turn(x) * sine


def rotate_back(x, cosine, sine):
    return x * cosine - turn(x) * sine


def stack_heads(x):
    low = lane_is_low(x.shape, 128)
    zero = jnp.zeros_like(x)
    return jnp.concatenate([jnp.where(low, x, zero), jnp.where(low, zero, x)], axis=0)


def join_heads(x):
    half = x.shape[0] // 2
    low = lane_is_low((half, 128), 128)
    return jnp.where(low, x[:half], x[half:])


def start_weights(sources, buffers, sems):
    waits = {}
    for index, (name, source) in enumerate(sources.items()):
        copy = pltpu.make_async_copy(source, buffers[name], sems.at[index])
        copy.start()
        waits[name] = [copy]
    return waits


def finish(waits, name):
    for copy in waits[name]:
        copy.wait()


def load_stream(flag, own, low, high, other, ext):
    for m in range(MICRO):
        for ref, alt, start, size in (
            (low, other[1], 0, HALF),
            (own, other[0], HALF, ROWS),
            (high, other[2], HALF + ROWS, HALF),
        ):
            value = ref[m]
            if alt is not None:
                value = jnp.where(flag, value, alt[m])
            ext[pl.ds(m * EXT + start, size), :] = value


def own_rows(x):
    return jnp.concatenate([x[HALF : HALF + ROWS], x[EXT + HALF : EXT + HALF + ROWS]], axis=0)


def repeat(count, step):
    lax.fori_loop(0, count, lambda i, carry: (step(i), carry)[1], 0)


def span(start, size, unit=128):
    return pl.ds(pl.multiple_of(start, unit), size)


def by_tiles(unit, group):
    def step(i):
        for j in range(group):
            unit(i * group + j)

    repeat(TILES // group, step)


def norm_rows(source, gain, target):
    def step(i):
        rows = span(i * 128, 128)
        normed, _ = norm_parts(source[rows, :].astype(F32))
        target[rows, :] = (normed * gain).astype(BF16)

    repeat(source.shape[0] // 128, step)


def forward_attention(ext, gain, wqkv, cos_ref, sin_ref, bias_ref, a_ext, q_ref, k_ref, v_ref, p_ref, o_ref):
    norm_rows(ext, gain, a_ext)
    a_own = o_ref
    a_own[...] = own_rows(a_ext[...])
    own_span = pl.ds(HALF, ROWS)

    def project(t):
        cols = span(256 * t, 256)
        queries = mm(a_own[...], wqkv[:, cols])
        keys = mm(a_ext[...], wqkv[:, span(D + 256 * t, 256)])
        v_ref[:, cols] = mm(a_ext[...], wqkv[:, span(2 * D + 256 * t, 256)]).astype(BF16)
        for s in range(2):
            tile, lanes = span(256 * t + 128 * s, 128), slice(128 * s, 128 * s + 128)
            for m in range(MICRO):
                part = queries[m * ROWS : (m + 1) * ROWS, lanes]
                turned = rotate(part, cos_ref[own_span, :], sin_ref[own_span, :]).astype(BF16)
                q_ref[pl.ds(m * ROWS, ROWS), tile] = turned * jnp.asarray(0.125, BF16)
                part = keys[m * EXT : (m + 1) * EXT, lanes]
                k_ref[pl.ds(m * EXT, EXT), tile] = rotate(part, cos_ref[...], sin_ref[...]).astype(BF16)

    repeat(3, project)

    def unit(t):
        cols = pl.ds(pl.multiple_of(t * 128, 128), 128)
        for m in range(MICRO):
            q2 = stack_heads(q_ref[pl.ds(m * ROWS, ROWS), cols])
            scores = mm_nt(k_ref[pl.ds(m * EXT, EXT), cols], q2) + bias_ref[m]
            terms = jnp.exp(scores - jnp.max(scores, axis=0, keepdims=True))
            probs = (terms * (1.0 / jnp.sum(terms, axis=0, keepdims=True))).astype(BF16)
            p_ref[m, t] = probs
            attended = mm_tn(probs, v_ref[pl.ds(m * EXT, EXT), cols])
            o_ref[pl.ds(m * ROWS, ROWS), cols] = join_heads(attended).astype(BF16)

    by_tiles(unit, 3)


def forward_mlp(own, o_ref, wproj, mlp_gain, wlift, wdown, h2_ref, b_ref, m_ref, left_ref, right_ref, h3_ref, waits):
    finish(waits, "proj")

    def mix(t):
        cols = span(256 * t, 256)
        added = mm(o_ref[...], wproj[:, cols])
        for m in range(MICRO):
            rows = pl.ds(m * ROWS, ROWS)
            h2_ref[rows, cols] = own[m, :, cols].astype(F32) + added[m * ROWS : (m + 1) * ROWS]

    repeat(3, mix)
    norm_rows(h2_ref, mlp_gain, b_ref)
    finish(waits, "lift")

    def lift(t):
        cols = span(384 * t, 384)
        gate = mm(b_ref[...], wlift[:, cols])
        up = mm(b_ref[...], wlift[:, span(FF + 384 * t, 384)])
        cdf = 0.5 * (1.0 + lax.erf(gate * root_half))
        gelu = gate * cdf
        m_ref[:, cols] = (gelu * up).astype(BF16)
        if left_ref is not None:
            pdf = jnp.exp(-0.5 * gate * gate) * inv_root_tau
            left_ref[:, cols] = up * (cdf + gate * pdf)
            right_ref[:, cols] = gelu

    repeat(3, lift)
    finish(waits, "down")

    def down(t):
        cols = span(256 * t, 256)
        h3 = (h2_ref[:, cols] + mm(m_ref[...], wdown[:, cols])).astype(BF16)
        for m in range(MICRO):
            h3_ref[m, :, cols] = h3[m * ROWS : (m + 1) * ROWS]

    repeat(3, down)


def backward_mlp(grad_ref, h2_ref, mlp_gain, wproj, wlift, wdown, left_ref, right_ref, du_ref, gb_ref, do_ref,
                 dh2_ref, b_ref, mlp_ref):
    def lift(t):
        cols = span(384 * t, 384)
        dm = mm_nt(grad_ref[...], wdown[cols, :])
        du_ref[:, cols] = (dm * left_ref[:, cols]).astype(BF16)
        du_ref[:, span(FF + 384 * t, 384)] = (dm * right_ref[:, cols]).astype(BF16)

    repeat(3, lift)

    def source(t):
        rows = span(256 * t, 256)
        dh2_ref[:, rows] = mm_nt(du_ref[...], wlift[rows, :])

    repeat(3, source)
    if mlp_ref is not None:
        mlp_ref[...] = jnp.zeros_like(mlp_ref)

    def norm(i):
        rows = span(i * 128, 128)
        db = dh2_ref[rows, :]
        normed, inv_scale = norm_parts(h2_ref[rows, :])
        dh2 = grad_ref[rows, :].astype(F32) + norm_back(db, mlp_gain, normed, inv_scale)
        dh2_ref[rows, :] = dh2
        gb_ref[rows, :] = dh2.astype(BF16)
        if mlp_ref is not None:
            mlp_ref[...] += jnp.sum(db * normed, axis=0, keepdims=True)
            b_ref[rows, :] = (normed * mlp_gain).astype(BF16)

    repeat(2, norm)

    def attended(t):
        rows = span(256 * t, 256)
        do_ref[:, rows] = mm_nt(gb_ref[...], wproj[rows, :]).astype(BF16)

    repeat(3, attended)


def backward_attention(q_ref, k_ref, v_ref, p_ref, do_ref, cos_ref, sin_ref, dq_ref, dkv_ref, low_ref, high_ref, group):
    cosine, sine = cos_ref[...], sin_ref[...]
    cos_own, sin_own = cosine[HALF : HALF + ROWS], sine[HALF : HALF + ROWS]

    def unit(t):
        cols = pl.ds(pl.multiple_of(t * 128, 128), 128)
        value_cols = pl.ds(pl.multiple_of(D + t * 128, 128), 128)
        for m in range(MICRO):
            rows = pl.ds(m * ROWS, ROWS)
            q2 = stack_heads(q_ref[rows, cols])
            do2 = stack_heads(do_ref[rows, cols])
            probs = p_ref[m, t]
            dprobs = mm_nt(v_ref[pl.ds(m * EXT, EXT), cols], do2)
            wide = probs.astype(F32)
            inner = jnp.sum(wide * dprobs, axis=0, keepdims=True)
            ds = (wide * (dprobs - inner)).astype(BF16)
            dq = join_heads(mm_tn(ds, k_ref[pl.ds(m * EXT, EXT), cols])) * 0.125
            dq_ref[rows, cols] = rotate_back(dq, cos_own, sin_own).astype(BF16)
            dk = rotate_back(mm(ds, q2), cosine, sine)
            dv = mm(probs, do2)
            for grad, where in ((dk, cols), (dv, value_cols)):
                low_ref[m, :, where] = grad[:HALF].astype(BF16)
                dkv_ref[rows, where] = grad[HALF : HALF + ROWS]
                high_ref[m, :, where] = grad[HALF + ROWS :].astype(BF16)

    by_tiles(unit, group)


def place_shards(index, own, first, first_other, second, second_other, put):
    f, core = index[1], index[2]
    put(own, f, None)
    put(first, lax.rem(f + 3 + 2 * core, 4), None)
    put(first_other, lax.rem(f + 1 + 2 * core, 4), None)
    put(second, lax.rem(f + 2, 4), core)
    put(second_other, lax.rem(f + 2, 4), 1 - core)


def pack_qkv_kernel(index, qkv, gains, own, whole, half, first_rows, last_rows, sems):
    rows = pl.ds(pl.multiple_of(index[2] * 96, 16), 96)
    copies = [
        pltpu.make_async_copy(src, dst, sems.at[n])
        for n, (src, dst) in enumerate((
            (qkv, whole.at[:, pl.ds(0, WIDE)]),
            (gains, whole.at[pl.ds(0, 16), pl.ds(WIDE, 128)]),
            (qkv.at[rows], half.at[:, pl.ds(0, WIDE)]),
            (gains, half.at[pl.ds(0, 16), pl.ds(WIDE, 128)]),
            (own.at[:, pl.ds(0, HALF)], first_rows),
            (own.at[:, pl.ds(ROWS - HALF, HALF)], last_rows),
        ))
    ]
    for copy in copies:
        copy.start()
    for copy in copies:
        copy.wait()


def pack_kernel(index, lift, proj, down, rest, rest_half, sems):
    core = index[2]
    copies = []

    def go(src, dst):
        copy = pltpu.make_async_copy(src, dst, sems.at[len(copies)])
        copy.start()
        copies.append(copy)

    half = lambda size: pl.ds(pl.multiple_of(core * size, 16), size)
    go(lift, rest.at[pl.ds(0, 192)])
    go(lift.at[half(96)], rest_half.at[pl.ds(0, 96)])
    for block in range(3):
        cols = pl.ds(block * D, D)
        go(proj.at[pl.ds(64 * block, 64)], rest.at[pl.ds(192, 64), cols])
        go(down.at[pl.ds(96 * block, 96)], rest.at[pl.ds(256, 96), cols])
        go(
            proj.at[pl.ds(pl.multiple_of(64 * block + core * 32, 16), 32)],
            rest_half.at[pl.ds(96, 32), cols],
        )
        go(
            down.at[pl.ds(pl.multiple_of(96 * block + core * 48, 16), 48)],
            rest_half.at[pl.ds(128, 48), cols],
        )
    for copy in copies:
        copy.wait()


def gather_gain(tiles, row):
    parts = []
    for tile in tiles:
        parts += [tile[row : row + 1, :], tile[row + 1 : row + 2, :64]]
    return jnp.concatenate(parts, axis=1)


def forward_attention_kernel(index, own, low, high, gain_tile, cos_ref, sin_ref, bias_ref,
                             shard, first, first_other, second, second_other,
                             o, gains, whole, wqkv, tiles, ext, a_ext, q, k, v, p, sems, out_sem):
    copies = []

    def go(src, dst):
        copy = pltpu.make_async_copy(src, dst, sems.at[len(copies)])
        copy.start()
        copies.append(copy)

    def put(piece, f, half):
        at, size = (f * 192, 192) if half is None else (f * 192 + half * 96, 96)
        rows = pl.ds(pl.multiple_of(at, 16), size)
        go(piece if piece is shard else piece.at[:, pl.ds(0, WIDE)], wqkv.at[rows])
        if piece is not shard and piece is not second_other:
            go(piece.at[pl.ds(0, 16), pl.ds(WIDE, 128)], tiles.at[f])

    place_shards(index, shard, first, first_other, second, second_other, put)
    go(gain_tile, tiles.at[index[1]])
    load_stream(None, own, low, high, (None, None, None), ext)
    for copy in copies:
        copy.wait()
    out = pltpu.make_async_copy(wqkv, whole, out_sem)
    out.start()
    shards = [tiles[f].astype(F32) for f in range(SHARDS)]
    gains[0:1, :] = gather_gain(shards, 0)
    gains[1:2, :] = gather_gain(shards, 2)
    forward_attention(ext, gains[0:1], wqkv, cos_ref, sin_ref, bias_ref, a_ext, q, k, v, p, o)
    out.wait()


def place_rest(index, lift, proj, down, pieces, wlift, wproj, wdown, go):
    f = index[1]
    rows = lambda at, size: pl.ds(pl.multiple_of(at, 16), size)

    def put(piece, s, half):
        if piece is None:
            go("proj", proj, wproj.at[rows(f * 192, 192)])
            go("lift", lift, wlift.at[rows(f * 192, 192)])
            go("down", down, wdown.at[rows(f * 288, 288)])
            return
        n = 2 if half is None else 1
        h = 0 if half is None else half
        go("lift", piece.at[pl.ds(0, 96 * n)], wlift.at[rows(s * 192 + h * 96, 96 * n)])
        for b in range(3):
            cols = pl.ds(b * D, D)
            go("proj", piece.at[pl.ds(96 * n, 32 * n), cols], wproj.at[rows(s * 192 + b * 64 + h * 32, 32 * n)])
            go("down", piece.at[pl.ds(128 * n, 48 * n), cols], wdown.at[rows(s * 288 + b * 96 + h * 48, 48 * n)])

    place_shards(index, None, *pieces, put)


def starter(sems, waits):
    count = [0]

    def go(name, src, dst):
        copy = pltpu.make_async_copy(src, dst, sems.at[count[0]])
        copy.start()
        count[0] += 1
        waits.setdefault(name, []).append(copy)

    return go


def forward_mlp_kernel(index, own, o, gains, lift, proj, down, first, first_other, second, second_other,
                       h3_ref, wproj, wlift, wdown, h2, b, m_out, sems):
    waits = {}
    pieces = (first, first_other, second, second_other)
    place_rest(index, lift, proj, down, pieces, wlift, wproj, wdown, starter(sems, waits))
    forward_mlp(own, o, wproj, gains[1:2], wlift, wdown, h2, b, m_out, None, None, h3_ref, waits)


def assemble_kernel(index, lift, proj, down, first, first_other, second, second_other, _,
                    whole_lift, whole_proj, whole_down, sems):
    waits = {}
    pieces = (first, first_other, second, second_other)
    place_rest(index, lift, proj, down, pieces, whole_lift, whole_proj, whole_down, starter(sems, waits))
    for name in waits:
        finish(waits, name)


def start_all(pairs, sems, first):
    copies = [pltpu.make_async_copy(src, dst, sems.at[first + n]) for n, (src, dst) in enumerate(pairs)]
    for copy in copies:
        copy.start()
    return copies


def turning_kernel(flag_ref, own, low, high, other_own, other_low, other_high, cotangent, gains,
                   cos_ref, sin_ref, bias_ref, qkv_hbm, proj_hbm, lift_hbm, down_hbm, *refs):
    kept, (dh2_ref, dq, dkv, to_low, to_high) = refs[:11], refs[11:16]
    wqkv, wproj, wlift, wdown, ext, a_ext, mine, du, do, h3_ref, q, k, v, p, o, h2, m_out, left, right, src, sems = refs[16:]
    waits = start_weights(
        {"qkv": qkv_hbm, "proj": proj_hbm, "lift": lift_hbm, "down": down_hbm},
        {"qkv": wqkv, "proj": wproj, "lift": wlift, "down": wdown}, sems,
    )
    flag = flag_ref[0] == 1
    load_stream(flag, own, low, high, (other_own, other_low, other_high), ext)
    for m in range(MICRO):
        mine[m] = ext[pl.ds(m * EXT + HALF, ROWS), :]
        src[pl.ds(m * ROWS, ROWS), :] = mine[m]
    finish(waits, "qkv")
    forward_attention(ext, gains[0:1], wqkv, cos_ref, sin_ref, bias_ref, a_ext, q, k, v, p, o)
    outs = start_all(zip((q, k, v, p, o, src), kept[1:6] + kept[10:]), sems, 4)
    spare = a_ext.at[pl.ds(0, OWN)]
    forward_mlp(mine, o, wproj, gains[1:2], wlift, wdown, h2, spare, m_out, left, right, h3_ref, waits)
    outs += start_all(zip((h3_ref, h2, m_out, left, right), kept[:1] + kept[6:10]), sems, 10)
    grad = a_ext.at[pl.ds(OWN, OWN)]
    for m in range(MICRO):
        grad[pl.ds(m * ROWS, ROWS), :] = cotangent[m]
    backward_mlp(grad, h2, gains[1:2], wproj, wlift, wdown, left, right, du, spare, do, dh2_ref, None, None)
    backward_attention(q, k, v, p, do, cos_ref, sin_ref, dq, dkv, to_low, to_high, 3)
    for copy in outs:
        copy.wait()


def back_kernel(flag_ref, incoming, cotangent, gains, cos_ref, sin_ref, proj_hbm, lift_hbm, down_hbm,
                q_hbm, k_hbm, v_hbm, p_hbm, h2_hbm, left_hbm, right_hbm, *refs):
    kept, (mlp_ref, dh2_ref, dq, dkv, to_low, to_high) = refs[:4], refs[4:10]
    wproj, wlift, wdown, do, q, k, v, p, h2, left, right, grad_ref, du, gb_ref, b_ref, sems = refs[10:]
    early = start_all(
        ((down_hbm, wdown), (left_hbm, left), (right_hbm, right), (lift_hbm, wlift), (h2_hbm, h2), (proj_hbm, wproj)),
        sems, 0,
    )
    late = start_all(((q_hbm, q), (v_hbm, v), (p_hbm, p), (k_hbm, k)), sems, 6)
    flag = flag_ref[0] == 1
    for m in range(MICRO):
        grad_ref[pl.ds(m * ROWS, ROWS), :] = jnp.where(flag, incoming[m], cotangent[m])
    for copy in early:
        copy.wait()
    backward_mlp(
        grad_ref, h2, gains[1:2], wproj, wlift, wdown, left, right, du, gb_ref, do, dh2_ref, b_ref, mlp_ref
    )
    outs = start_all(zip((grad_ref, du, gb_ref, b_ref), kept), sems, 10)
    for copy in late:
        copy.wait()
    backward_attention(q, k, v, p, do, cos_ref, sin_ref, dq, dkv, to_low, to_high, 6)
    for copy in outs:
        copy.wait()


def joined_grads(dq, dkv, from_low, from_high, dqkv):
    dqkv[:, :D] = dq[...]
    for m in range(MICRO):
        first, last = pl.ds(m * ROWS, HALF), pl.ds(m * ROWS + HALF, HALF)
        dqkv[first, D:] = (dkv[first, :] + from_low[m].astype(F32)).astype(BF16)
        dqkv[last, D:] = (dkv[last, :] + from_high[m].astype(F32)).astype(BF16)


def source_kernel(src, gains, dh2, dq, dkv, from_low, from_high, qkv_hbm, out_ref, wqkv, dqkv, sems):
    waits = start_weights({"qkv": qkv_hbm}, {"qkv": wqkv}, sems)
    joined_grads(dq, dkv, from_low, from_high, dqkv)
    normed, inv_scale = norm_parts(src[...].astype(F32))
    finish(waits, "qkv")
    da = mm_nt(dqkv[...], wqkv[...])
    dh = dh2[...] + norm_back(da, gains[0:1], normed, inv_scale)
    for m in range(MICRO):
        out_ref[m] = dh[m * ROWS : (m + 1) * ROWS].astype(BF16)


def gain_block(attn, mlp, f):
    rows = []
    for gain in (attn, mlp):
        rows.append(gain[:, 192 * f : 192 * f + 128])
        rows.append(jnp.concatenate([gain[:, 192 * f + 128 : 192 * f + 192], jnp.zeros((1, 64), F32)], axis=1))
    return jnp.concatenate(rows + [jnp.zeros((92, 128), F32)], axis=0).astype(BF16)


def source_grad_kernel(index, src, gains, dh2, dq, dkv, from_low, from_high, mlp_grad, qkv_hbm,
                       out_ref, keep, send, wqkv, dqkv, qkv_ref, gain_ref, sems):
    waits = start_weights({"qkv": qkv_hbm}, {"qkv": wqkv}, sems)
    joined_grads(dq, dkv, from_low, from_high, dqkv)
    normed, inv_scale = norm_parts(src[...].astype(F32))
    finish(waits, "qkv")
    da = mm_nt(dqkv[...], wqkv[...])
    attn_grad = jnp.sum(da * normed, axis=0, keepdims=True)
    mlp = mlp_grad[...]
    for f in range(SHARDS):
        gain_ref[f] = gain_block(attn_grad, mlp, f)
    a = (normed * gains[0:1]).astype(BF16)
    for t in range(9):
        cols = pl.ds(256 * t, 256)
        qkv_ref[:, cols] = mm_tn(a, dqkv[:, cols]).astype(BF16)
    copies = []
    for target, half in ((send, 1 - index[2]), (keep, index[2])):
        for f in range(SHARDS):
            rows = pl.ds(pl.multiple_of(f * 192 + half * 96, 16), 96)
            for src_ref, dst_ref in (
                (qkv_ref.at[rows], target.at[f, :, pl.ds(0, WIDE)]),
                (gain_ref.at[f], target.at[f, :, pl.ds(WIDE, 128)]),
            ):
                copy = pltpu.make_async_copy(src_ref, dst_ref, sems.at[1 + len(copies)])
                copy.start()
                copies.append(copy)
    dh = dh2[...] + norm_back(da, gains[0:1], normed, inv_scale)
    for m in range(MICRO):
        out_ref[m] = dh[m * ROWS : (m + 1) * ROWS].astype(BF16)
    for copy in copies:
        copy.wait()


def weight_grad_kernel(index, m_ref, grad_ref, b_ref, du, o_ref, gb_ref, keep, send,
                       down_ref, lift_ref, proj_ref, pad_ref, sems):
    core = index[2]
    copies = []

    def go(src, dst):
        copy = pltpu.make_async_copy(src, dst, sems.at[len(copies)])
        copy.start()
        copies.append(copy)

    sides = ((send, 1 - core), (keep, core))
    rows = lambda at, size: pl.ds(pl.multiple_of(at, 16), size)
    pad_ref[...] = jnp.zeros_like(pad_ref)
    for target, _ in sides:
        for f in range(SHARDS):
            go(pad_ref, target.at[f, pl.ds(176, 16)])
    for t in range(9):
        cols = pl.ds(256 * t, 256)
        lift_ref[:, cols] = mm_tn(b_ref[...], du[:, cols]).astype(BF16)
    for target, half in sides:
        for f in range(SHARDS):
            go(lift_ref.at[rows(f * 192 + half * 96, 96)], target.at[f, pl.ds(0, 96)])
    for t in range(3):
        cols = pl.ds(256 * t, 256)
        down_ref[:, cols] = mm_tn(m_ref[...], grad_ref[:, cols]).astype(BF16)
        proj_ref[:, cols] = mm_tn(o_ref[...], gb_ref[:, cols]).astype(BF16)
    for target, half in sides:
        for f in range(SHARDS):
            for b in range(3):
                cols = pl.ds(b * D, D)
                go(proj_ref.at[rows(f * 192 + b * 64 + half * 32, 32)], target.at[f, pl.ds(96, 32), cols])
                go(down_ref.at[rows(f * 288 + b * 96 + half * 48, 48)], target.at[f, pl.ds(128, 48), cols])
    for copy in copies:
        copy.wait()


def add_up(parts):
    total = parts[0].astype(F32)
    for part in parts[1:]:
        total = total + part.astype(F32)
    return total.astype(BF16)


def rest_core_kernel(index, keep, other, *outs):
    for d, out in enumerate(outs):
        rows = pl.ds(pl.multiple_of(lax.rem(index[0] + d, 4) * 48, 16), 48)
        for f in range(SHARDS):
            out[f] = add_up([keep[f, rows, :], other[f, rows, :]])


def rest_z_kernel(index, own, a, b, c, *outs):
    for d, out in enumerate(outs):
        f = lax.rem(index[1] + d, 4)
        out[...] = add_up([own[f], a[f], b[f], c[f]])


def qkv_core_kernel(index, keep, other, *outs):
    for d, out in enumerate(outs):
        f = lax.rem(index[1] + d, 4)
        out[...] = add_up([keep[f], other[f]])


def partial_kernel(a, b, out):
    out[...] = a[...].astype(F32) + b[...].astype(F32)


def qkv_y_kernel(index, some, b, c, out_0, out_1, out_2, out_3, total):
    total[...] = add_up([some[...], b[...], c[...]])
    for d, out in enumerate((out_0, out_1, out_2, out_3)):
        z = lax.rem(index[0] + d, 4)
        rows = pl.ds(pl.multiple_of(lax.div(z, 2) * 48, 16), 48)
        cols = pl.ds(pl.multiple_of(lax.rem(z, 2) * 1152, 128), 1152)
        out[:, pl.ds(0, 1152)] = total[rows, cols]
        out[:, pl.ds(1152, 128)] = total[pl.ds(0, 48), pl.ds(WIDE, 128)]


def joint_kernel(r0, r1, r2, r3, q0, q1, q2, q3, out):
    out[:, pl.ds(0, WIDE)] = add_up([r0[...], r1[...], r2[...], r3[...]])
    out[:, pl.ds(WIDE, 1280)] = add_up([q0[...], q1[...], q2[...], q3[...]])


def pair_kernel(a, b, out):
    out[...] = add_up([a[...], b[...]])


def final_kernel(index, *refs):
    pieces, (qkv_out, proj_out, lift_out, down_out, gain_out, rest) = refs[:8], refs[8:]
    core = index[2]
    for side in range(2):
        half = core if side == 0 else 1 - core
        for d in range(4):
            piece = pieces[4 * side + d]
            z = lax.rem(index[0] - d + 4, 4)
            rest[side, pl.ds(pl.multiple_of(z * 48, 16), 48), :] = piece[:, pl.ds(0, WIDE)]
            qkv_out[
                pl.ds(pl.multiple_of(half * 96 + lax.div(z, 2) * 48, 16), 48),
                pl.ds(pl.multiple_of(lax.rem(z, 2) * 1152, 128), 1152),
            ] = piece[:, pl.ds(WIDE, 1152)].astype(F32)
        rows = lambda at, size: pl.ds(pl.multiple_of(at, 16), size)
        lift_out[rows(half * 96, 96), :] = rest[side, pl.ds(0, 96), :].astype(F32)
        for b in range(3):
            cols = pl.ds(b * D, D)
            proj_out[rows(b * 64 + half * 32, 32), :] = rest[side, pl.ds(96, 32), cols].astype(F32)
            down_out[rows(b * 96 + half * 48, 48), :] = rest[side, pl.ds(128, 48), cols].astype(F32)
    gain_out[...] = pieces[0][pl.ds(0, 16), pl.ds(WIDE + 1152, 128)].astype(F32)


def call(kernel, name, ins, outs, scratch, flops, limit=24):
    places = {"v": pltpu.VMEM, "a": pl.ANY, "s": pltpu.SMEM}
    return pl.pallas_call(
        kernel,
        name=name,
        out_shape=[jax.ShapeDtypeStruct(out[0], out[1]) for out in outs],
        in_specs=[pl.BlockSpec(memory_space=places[place]) for _, place in ins],
        out_specs=[pl.BlockSpec(memory_space=places[out[2] if len(out) > 2 else "v"]) for out in outs],
        scratch_shapes=scratch,
        compiler_params=pltpu.CompilerParams(vmem_limit_bytes=limit * 2**20),
        cost_estimate=pl.CostEstimate(flops=flops, bytes_accessed=flops // 300, transcendentals=0),
    )(*[array for array, _ in ins])


def travel(block, target):
    pairs = []
    for ctx in range(16):
        for f in range(SHARDS):
            xlo, z, core, g = target(ctx // 8, ctx // 2 % 4, ctx % 2, f)
            pairs.append((ctx * SHARDS + f, (xlo * 8 + z % 4 * 2 + core) * SHARDS + g % 4))
    return lax.ppermute(block, ("ctx", "fsdp"), pairs)


def along_y(block, d):
    return travel(block, lambda x, z, c, f: (x, z, c, f + d))


def along_z(block, d):
    return travel(block, lambda x, z, c, f: (x, z + d, c, f))


def next_shard(block):
    return travel(block, lambda x, z, c, f: (x, z, c, f + 1 - 2 * c))


def swap_core(block):
    return travel(block, lambda x, z, c, f: (x, z, 1 - c, f))


def swap_x(block):
    return travel(block, lambda x, z, c, f: (1 - x, z, c, f))


def halo_rows(block, axis):
    count = lax.axis_size(axis)
    up = [(i, i + 1) for i in range(count - 1)]
    down = [(i + 1, i) for i in range(count - 1)]
    return (
        lax.ppermute(block[:, ROWS - HALF :], axis, up),
        lax.ppermute(block[:, :HALF], axis, down),
    )


def swap_halos(to_low, to_high):
    count = lax.axis_size("ctx")
    up = [(i, i + 1) for i in range(count - 1)]
    down = [(i + 1, i) for i in range(count - 1)]
    return lax.ppermute(to_high, "ctx", up), lax.ppermute(to_low, "ctx", down)


def tables(first_row, lengths):
    half = HD // 2
    frequencies = rope_base ** (-(jnp.arange(half, dtype=F32) * 2.0) / HD)
    positions = first_row - HALF + jnp.arange(EXT, dtype=jnp.int32)
    angles = positions.astype(F32)[:, None] * frequencies[None, :]
    cosine, sine = jnp.cos(angles), jnp.sin(angles)
    cosine = jnp.concatenate([cosine] * 4, axis=1)
    sine = jnp.concatenate([-sine, sine, -sine, sine], axis=1)
    ends = jnp.cumsum(lengths, axis=1)
    doc = jnp.sum((positions[None, :, None] >= ends[:, None, :]).astype(jnp.int32), axis=2)
    query = positions[HALF : HALF + ROWS]
    allowed = (
        (jnp.abs(query[None, :] - positions[:, None]) <= HALF)
        & (positions >= 0)[:, None]
        & (positions < SEQ_LEN)[:, None]
    )[None] & (doc[:, :, None] == doc[:, None, HALF : HALF + ROWS])
    bias = jnp.where(allowed, 0.0, masked_score).astype(F32)
    return cosine, sine, jnp.concatenate([bias, bias], axis=2)


WQKV, WPROJ, WLIFT, WDOWN = [
    pltpu.VMEM((D, WIDE), BF16),
    pltpu.VMEM((D, D), BF16),
    pltpu.VMEM((D, WIDE), BF16),
    pltpu.VMEM((FF, D), BF16),
]
SAVED = [
    ((OWN, D), BF16),
    ((MICRO * EXT, D), BF16),
    ((MICRO * EXT, D), BF16),
    ((MICRO, TILES, EXT, 2 * ROWS), BF16),
    ((OWN, D), BF16),
    ((OWN, D), F32),
    ((OWN, FF), BF16),
    ((OWN, FF), F32),
    ((OWN, FF), F32),
]
STREAM = [pltpu.VMEM((MICRO * EXT, D), BF16)] * 2
GRADS_OUT = [
    ((OWN, D), F32),
    ((OWN, D), BF16),
    ((OWN, 2 * D), F32),
    ((MICRO, HALF, 2 * D), BF16),
    ((MICRO, HALF, 2 * D), BF16),
]


TURN_OUT = [((MICRO, ROWS, D), BF16)] + SAVED + [((OWN, D), BF16)]
BACK_OUT = [((OWN, D), BF16), ((OWN, WIDE), BF16), ((OWN, D), BF16), ((OWN, D), BF16)]


def sems(count):
    return pltpu.SemaphoreType.DMA((count,))


def body(
    inputs, out_grad, doc_lengths, attn_gain, qkv_weight, proj_weight, mlp_gain, lift_weight, down_weight
):
    on_first = lax.axis_index("section") == 0
    flag = on_first.astype(jnp.int32).reshape(1)
    ctx, f = lax.axis_index("ctx"), lax.axis_index("fsdp")
    index = jnp.stack([ctx // 2 % 4, f, ctx % 2]).astype(jnp.int32)
    qkv_shard, lift_shard, proj_shard, down_shard = qkv_weight[0], lift_weight[0], proj_weight[0], down_weight[0]
    own, cotangent = inputs[:, 0], out_grad[:, 0]
    gain_tile = jnp.pad(
        jnp.pad(jnp.stack([attn_gain[0], mlp_gain[0]]), ((0, 0), (0, 64))).reshape(4, 128), ((0, 12), (0, 0))
    )
    edge = ((MICRO, HALF, D), BF16, "a")
    qkv_pack, qkv_half, first_rows, last_rows = call(
        pack_qkv_kernel, "pack_qkv",
        [(index, "s"), (qkv_shard, "a"), (gain_tile, "a"), (own, "a")],
        [((192, 2432), BF16, "a"), ((96, 2432), BF16, "a"), edge, edge],
        [sems(6)], 0, 56,
    )
    rest, rest_half = call(
        pack_kernel, "pack_rest",
        [(index, "s"), (lift_shard, "a"), (proj_shard, "a"), (down_shard, "a")],
        [((352, WIDE), BF16, "a"), ((176, WIDE), BF16, "a")],
        [sems(14)], 0, 56,
    )
    first = next_shard(qkv_pack)
    second = along_y(qkv_half, 2)
    cosine, sine, bias = tables(ctx * ROWS, doc_lengths[:, 0])
    first_rows, last_rows, cosine = lax.optimization_barrier((first_rows, last_rows, cosine))
    low, high = swap_halos(first_rows, last_rows)
    first, second, rest, rest_half, cosine, sine, bias, low, high = lax.optimization_barrier(
        (first, second, rest, rest_half, cosine, sine, bias, low, high)
    )
    qkv_pieces = first, swap_core(first), second, swap_core(second)
    stream = ((MICRO, ROWS, D), BF16)
    scratch = lambda items: [pltpu.VMEM(s, k) for s, k in items]

    o, gains, wqkv = call(
        forward_attention_kernel, "forward_attention",
        [(index, "s"), (own, "v"), (low, "v"), (high, "v"), (gain_tile, "a"), (cosine, "v"), (sine, "v"), (bias, "v"),
         (qkv_shard, "a"), *[(piece, "a") for piece in qkv_pieces]],
        [((OWN, D), BF16), ((2, D), F32), ((D, WIDE), BF16, "a")],
        [WQKV, pltpu.VMEM((SHARDS, 16, 128), BF16)] + STREAM + scratch(SAVED[:4]) + [sems(9), pltpu.SemaphoreType.DMA(())],
        1_400_000_000,
    )
    rest_first, rest_second, o = lax.optimization_barrier((next_shard(rest), along_y(rest_half, 2), o))
    rest_pieces = rest_first, swap_core(rest_first), rest_second, swap_core(rest_second)
    rest_parts = [(part, "a") for part in (lift_shard, proj_shard, down_shard, *rest_pieces)]
    (relay,) = call(
        forward_mlp_kernel, "forward_mlp",
        [(index, "s"), (own, "v"), (o, "v"), (gains, "v"), *rest_parts],
        [stream],
        [WPROJ, WLIFT, WDOWN] + scratch([SAVED[5], SAVED[0], SAVED[6]]) + [sems(31)],
        1_800_000_000,
    )
    wlift, wproj, wdown = call(
        assemble_kernel, "assemble_weights",
        [(index, "s"), *rest_parts, (relay, "a")],
        [((D, WIDE), BF16, "a"), ((D, D), BF16, "a"), ((FF, D), BF16, "a")],
        [sems(31)], 1_800_000_000, 56,
    )
    relayed = lax.ppermute(relay, "section", [(0, 1)])
    other_low, other_high = halo_rows(relayed, "ctx")
    (h3, q, k, v, p, o, h2, m_act, left, right, src, dh2, dq, dkv, to_low, to_high) = call(
        turning_kernel, "layer_turn",
        [(flag, "s"), (own, "v"), (low, "v"), (high, "v"), (relayed, "v"), (other_low, "v"), (other_high, "v"),
         (cotangent, "v"), (gains, "v"), (cosine, "v"), (sine, "v"), (bias, "v"),
         (wqkv, "a"), (wproj, "a"), (wlift, "a"), (wdown, "a")],
        [(*item, "a") for item in TURN_OUT] + GRADS_OUT,
        [WQKV, WPROJ, WLIFT, WDOWN] + STREAM
        + [pltpu.VMEM((MICRO, ROWS, D), BF16), pltpu.VMEM((OWN, WIDE), BF16), pltpu.VMEM((OWN, D), BF16)] + scratch(TURN_OUT) + [sems(15)],
        6_000_000_000, 44,
    )
    from_low, from_high = swap_halos(to_low, to_high)
    (grad_relay,) = call(
        source_kernel, "layer_source",
        [(src, "v"), (gains, "v"), (dh2, "v"), (dq, "v"), (dkv, "v"), (from_low, "v"), (from_high, "v"), (wqkv, "a")],
        [stream],
        [WQKV, pltpu.VMEM((OWN, WIDE), BF16), sems(1)],
        900_000_000,
    )
    incoming = lax.ppermute(grad_relay, "section", [(1, 0)])
    (grad_low, du, gb, b, mlp_gain_grad, dh2, dq, dkv, to_low, to_high) = call(
        back_kernel, "layer_back",
        [(flag, "s"), (incoming, "v"), (cotangent, "v"), (gains, "v"), (cosine, "v"), (sine, "v"),
         (wproj, "a"), (wlift, "a"), (wdown, "a"),
         *[(array, "a") for array in (q, k, v, p, h2, left, right)]],
        [(*item, "a") for item in BACK_OUT] + [((1, D), F32)] + GRADS_OUT,
        [WPROJ, WLIFT, WDOWN, pltpu.VMEM((OWN, D), BF16)]
        + scratch(SAVED[:4] + SAVED[5:6] + SAVED[7:] + BACK_OUT) + [sems(14)],
        3_000_000_000, 40,
    )
    from_low, from_high = swap_halos(to_low, to_high)
    rest_keep, rest_send = call(
        weight_grad_kernel, "weight_grads",
        [(index, "s"), (m_act, "v"), (grad_low, "v"), (b, "v"), (du, "v"), (o, "v"), (gb, "v")],
        [((SHARDS, 192, WIDE), BF16, "a")] * 2,
        [WDOWN, WLIFT, WPROJ, pltpu.VMEM((16, WIDE), BF16), sems(64)],
        1_600_000_000,
    )
    from_low, from_high, rest_send = lax.optimization_barrier((from_low, from_high, rest_send))
    rest_other = swap_core(rest_send)
    in_grad, qkv_keep, qkv_send = call(
        source_grad_kernel, "layer_source_grads",
        [(index, "s"), (src, "v"), (gains, "v"), (dh2, "v"), (dq, "v"), (dkv, "v"), (from_low, "v"),
         (from_high, "v"), (mlp_gain_grad, "v"), (wqkv, "a")],
        [stream, ((SHARDS, 96, 2432), BF16, "a"), ((SHARDS, 96, 2432), BF16, "a")],
        [WQKV, pltpu.VMEM((OWN, WIDE), BF16), WQKV, pltpu.VMEM((SHARDS, 96, 128), BF16), sems(17)],
        1_800_000_000,
    )
    qkv_other = swap_core(qkv_send)

    rest_z = call(
        rest_core_kernel, "rest_core_sum", [(index, "s"), (rest_keep, "v"), (rest_other, "v")],
        [((SHARDS, 48, WIDE), BF16)] * 4, [], 0, 24,
    )
    qkv_keep, _ = lax.optimization_barrier((qkv_keep, rest_z[0]))
    qkv_y = call(
        qkv_core_kernel, "qkv_core_sum", [(index, "s"), (qkv_keep, "v"), (qkv_other, "v")],
        [((96, 2432), BF16)] * 4, [], 0, 24,
    )
    (some,) = call(
        partial_kernel, "qkv_y_first", [(qkv_y[0], "v"), (along_y(qkv_y[1], 1), "v")],
        [((96, 2432), F32)], [], 0, 24,
    )
    rest_mine, some = lax.optimization_barrier((rest_z[0], some))
    rest_y = call(
        rest_z_kernel, "rest_z_sum",
        [(index, "s"), (rest_mine, "v"), *[(along_z(rest_z[d], d), "v") for d in (1, 2, 3)]],
        [((48, WIDE), BF16)] * 4, [], 0, 24,
    )
    some, _ = lax.optimization_barrier((some, rest_y[0]))
    qkv_z = call(
        qkv_y_kernel, "qkv_y_sum",
        [(index, "s"), (some, "v"), *[(along_y(qkv_y[d], d), "v") for d in (2, 3)]],
        [((48, 1280), BF16)] * 4, [pltpu.VMEM((96, 2432), BF16)], 0, 24,
    )
    (joint,) = call(
        joint_kernel, "joint_sum",
        [(rest_y[0], "v"), *[(along_y(rest_y[d], d), "v") for d in (1, 2, 3)],
         (qkv_z[0], "v"), *[(along_z(qkv_z[d], d), "v") for d in (1, 2, 3)]],
        [((48, 3584), BF16)], [], 0, 24,
    )
    (joint,) = call(
        pair_kernel, "pair_sum", [(joint, "v"), (swap_x(joint), "v")], [((48, 3584), BF16)], [], 0, 24
    )
    mine = [joint] + [along_z(joint, d) for d in (1, 2, 3)]
    theirs = [swap_core(piece) for piece in mine]
    qkv_sum, proj_sum, lift_sum, down_sum, gain_sums = call(
        final_kernel, "final_shard", [(index, "s"), *[(piece, "v") for piece in mine + theirs]],
        [((192, WIDE), F32), ((192, D), F32), ((192, WIDE), F32), ((288, D), F32), ((16, 128), F32)],
        [pltpu.VMEM((2, 192, WIDE), BF16)], 0, 24,
    )
    return (
        h3[None, :, None],
        in_grad[None, :, None],
        gain_sums[0:2].reshape(1, 256)[:, :192],
        qkv_sum[None],
        proj_sum[None],
        gain_sums[2:4].reshape(1, 256)[:, :192],
        lift_sum[None],
        down_sum[None],
    )


def solution(mesh):
    placed = (
        P(None, "fsdp", "ctx", None),
        P(None, "fsdp", "ctx", None),
        P(None, "fsdp", None),
        P("section", "fsdp"),
        P("section", "fsdp", None),
        P("section", "fsdp", None),
        P("section", "fsdp"),
        P("section", "fsdp", None),
        P("section", "fsdp", None),
    )
    return jax.shard_map(
        body,
        mesh=mesh,
        in_specs=placed,
        out_specs=(
            P("section", None, "fsdp", "ctx", None),
            P("section", None, "fsdp", "ctx", None),
            P("section", "fsdp"),
            P("section", "fsdp", None),
            P("section", "fsdp", None),
            P("section", "fsdp"),
            P("section", "fsdp", None),
            P("section", "fsdp", None),
        ),
        check_vma=False,
    )
```

```python
import functools

import jax
import jax.numpy as jnp
from jax import lax
from jax.experimental import pallas as pl
from jax.experimental.pallas import tpu as pltpu
from jax.sharding import PartitionSpec as P

D = 768
HD = 64
HALF = 64
SEQ_LEN = 2048
FF = 1152
WIDE = 2304
ROWS = 128
EXT = ROWS + 2 * HALF
MICRO = 2
OWN = MICRO * ROWS
SHARDS = 4
TILES = D // 128
norm_eps = 1e-05
rope_base = 10000.0
masked_score = -1e30
root_half = 0.7071067811865476
inv_root_tau = 0.3989422804014327
F32 = jnp.float32
BF16 = jnp.bfloat16


def mm(left, right):
    return lax.dot_general(left, right, (((1,), (0,)), ((), ())), preferred_element_type=F32)


def mm_nt(left, right):
    return lax.dot_general(left, right, (((1,), (1,)), ((), ())), preferred_element_type=F32)


def mm_tn(left, right):
    return lax.dot_general(left, right, (((0,), (0,)), ((), ())), preferred_element_type=F32)


def norm_parts(hidden):
    centre = hidden - jnp.mean(hidden, axis=-1, keepdims=True)
    inv_scale = lax.rsqrt(jnp.mean(centre * centre, axis=-1, keepdims=True) + norm_eps)
    return centre * inv_scale, inv_scale


def norm_back(grad_out, gain, normed, inv_scale):
    grad_normed = grad_out * gain
    inner = (
        grad_normed
        - jnp.mean(grad_normed, axis=-1, keepdims=True)
        - normed * jnp.mean(grad_normed * normed, axis=-1, keepdims=True)
    )
    return inner * inv_scale


def lane_is_low(shape, period):
    return lax.broadcasted_iota(jnp.int32, shape, 1) % period < period // 2


def turn(x):
    return jnp.where(lane_is_low(x.shape, HD), pltpu.roll(x, 96, 1), pltpu.roll(x, 32, 1))


def rotate(x, cosine, sine):
    return x * cosine + turn(x) * sine


def rotate_back(x, cosine, sine):
    return x * cosine - turn(x) * sine


def stack_heads(x):
    low = lane_is_low(x.shape, 128)
    zero = jnp.zeros_like(x)
    return jnp.concatenate([jnp.where(low, x, zero), jnp.where(low, zero, x)], axis=0)


def join_heads(x):
    half = x.shape[0] // 2
    low = lane_is_low((half, 128), 128)
    return jnp.where(low, x[:half], x[half:])


def start_weights(sources, buffers, sems):
    waits = {}
    for index, (name, source) in enumerate(sources.items()):
        copy = pltpu.make_async_copy(source, buffers[name], sems.at[index])
        copy.start()
        waits[name] = [copy]
    return waits


def finish(waits, name):
    for copy in waits[name]:
        copy.wait()


def load_stream(flag, own, low, high, other, ext):
    for m in range(MICRO):
        for ref, alt, start, size in (
            (low, other[1], 0, HALF),
            (own, other[0], HALF, ROWS),
            (high, other[2], HALF + ROWS, HALF),
        ):
            value = ref[m]
            if alt is not None:
                value = jnp.where(flag, value, alt[m])
            ext[pl.ds(m * EXT + start, size), :] = value


def own_rows(x):
    return jnp.concatenate([x[HALF : HALF + ROWS], x[EXT + HALF : EXT + HALF + ROWS]], axis=0)


def repeat(count, step):
    lax.fori_loop(0, count, lambda i, carry: (step(i), carry)[1], 0)


def span(start, size, unit=128):
    return pl.ds(pl.multiple_of(start, unit), size)


def by_tiles(unit, group):
    def step(i):
        for j in range(group):
            unit(i * group + j)

    repeat(TILES // group, step)


def norm_rows(source, gain, target):
    def step(i):
        rows = span(i * 128, 128)
        normed, _ = norm_parts(source[rows, :].astype(F32))
        target[rows, :] = (normed * gain).astype(BF16)

    repeat(source.shape[0] // 128, step)


def forward_attention(ext, gain, wqkv, cos_ref, sin_ref, bias_ref, a_ext, q_ref, k_ref, v_ref, p_ref, o_ref):
    norm_rows(ext, gain, a_ext)
    a_own = o_ref
    a_own[...] = own_rows(a_ext[...])
    own_span = pl.ds(HALF, ROWS)

    def project(t):
        cols = span(256 * t, 256)
        queries = mm(a_own[...], wqkv[:, cols])
        keys = mm(a_ext[...], wqkv[:, span(D + 256 * t, 256)])
        v_ref[:, cols] = mm(a_ext[...], wqkv[:, span(2 * D + 256 * t, 256)]).astype(BF16)
        for s in range(2):
            tile, lanes = span(256 * t + 128 * s, 128), slice(128 * s, 128 * s + 128)
            for m in range(MICRO):
                part = queries[m * ROWS : (m + 1) * ROWS, lanes]
                turned = rotate(part, cos_ref[own_span, :], sin_ref[own_span, :]).astype(BF16)
                q_ref[pl.ds(m * ROWS, ROWS), tile] = turned * jnp.asarray(0.125, BF16)
                part = keys[m * EXT : (m + 1) * EXT, lanes]
                k_ref[pl.ds(m * EXT, EXT), tile] = rotate(part, cos_ref[...], sin_ref[...]).astype(BF16)

    repeat(3, project)

    def unit(t):
        cols = pl.ds(pl.multiple_of(t * 128, 128), 128)
        for m in range(MICRO):
            q2 = stack_heads(q_ref[pl.ds(m * ROWS, ROWS), cols])
            scores = mm_nt(k_ref[pl.ds(m * EXT, EXT), cols], q2) + bias_ref[m]
            terms = jnp.exp(scores - jnp.max(scores, axis=0, keepdims=True))
            probs = (terms * (1.0 / jnp.sum(terms, axis=0, keepdims=True))).astype(BF16)
            p_ref[m, t] = probs
            attended = mm_tn(probs, v_ref[pl.ds(m * EXT, EXT), cols])
            o_ref[pl.ds(m * ROWS, ROWS), cols] = join_heads(attended).astype(BF16)

    by_tiles(unit, 3)


def forward_mlp(own, o_ref, wproj, mlp_gain, wlift, wdown, h2_ref, b_ref, m_ref, left_ref, right_ref, h3_ref, waits):
    finish(waits, "proj")

    def mix(t):
        cols = span(256 * t, 256)
        added = mm(o_ref[...], wproj[:, cols])
        for m in range(MICRO):
            rows = pl.ds(m * ROWS, ROWS)
            h2_ref[rows, cols] = own[m, :, cols].astype(F32) + added[m * ROWS : (m + 1) * ROWS]

    repeat(3, mix)
    norm_rows(h2_ref, mlp_gain, b_ref)
    finish(waits, "lift")

    def lift(t):
        cols = span(384 * t, 384)
        gate = mm(b_ref[...], wlift[:, cols])
        up = mm(b_ref[...], wlift[:, span(FF + 384 * t, 384)])
        cdf = 0.5 * (1.0 + lax.erf(gate * root_half))
        gelu = gate * cdf
        m_ref[:, cols] = (gelu * up).astype(BF16)
        if left_ref is not None:
            pdf = jnp.exp(-0.5 * gate * gate) * inv_root_tau
            left_ref[:, cols] = up * (cdf + gate * pdf)
            right_ref[:, cols] = gelu

    repeat(3, lift)
    finish(waits, "down")

    def down(t):
        cols = span(256 * t, 256)
        h3 = (h2_ref[:, cols] + mm(m_ref[...], wdown[:, cols])).astype(BF16)
        for m in range(MICRO):
            h3_ref[m, :, cols] = h3[m * ROWS : (m + 1) * ROWS]

    repeat(3, down)


def backward_mlp(grad_ref, h2_ref, mlp_gain, wproj, wlift, wdown, left_ref, right_ref, du_ref, gb_ref, do_ref,
                 dh2_ref, b_ref, mlp_ref):
    def lift(t):
        cols = span(384 * t, 384)
        dm = mm_nt(grad_ref[...], wdown[cols, :])
        du_ref[:, cols] = (dm * left_ref[:, cols]).astype(BF16)
        du_ref[:, span(FF + 384 * t, 384)] = (dm * right_ref[:, cols]).astype(BF16)

    repeat(3, lift)

    def source(t):
        rows = span(256 * t, 256)
        dh2_ref[:, rows] = mm_nt(du_ref[...], wlift[rows, :])

    repeat(3, source)
    if mlp_ref is not None:
        mlp_ref[...] = jnp.zeros_like(mlp_ref)

    def norm(i):
        rows = span(i * 128, 128)
        db = dh2_ref[rows, :]
        normed, inv_scale = norm_parts(h2_ref[rows, :])
        dh2 = grad_ref[rows, :].astype(F32) + norm_back(db, mlp_gain, normed, inv_scale)
        dh2_ref[rows, :] = dh2
        gb_ref[rows, :] = dh2.astype(BF16)
        if mlp_ref is not None:
            mlp_ref[...] += jnp.sum(db * normed, axis=0, keepdims=True)
            b_ref[rows, :] = (normed * mlp_gain).astype(BF16)

    repeat(2, norm)

    def attended(t):
        rows = span(256 * t, 256)
        do_ref[:, rows] = mm_nt(gb_ref[...], wproj[rows, :]).astype(BF16)

    repeat(3, attended)


def backward_attention(q_ref, k_ref, v_ref, p_ref, do_ref, cos_ref, sin_ref, dq_ref, dkv_ref, low_ref, high_ref, group):
    cosine, sine = cos_ref[...], sin_ref[...]
    cos_own, sin_own = cosine[HALF : HALF + ROWS], sine[HALF : HALF + ROWS]

    def unit(t):
        cols = pl.ds(pl.multiple_of(t * 128, 128), 128)
        value_cols = pl.ds(pl.multiple_of(D + t * 128, 128), 128)
        for m in range(MICRO):
            rows = pl.ds(m * ROWS, ROWS)
            q2 = stack_heads(q_ref[rows, cols])
            do2 = stack_heads(do_ref[rows, cols])
            probs = p_ref[m, t]
            dprobs = mm_nt(v_ref[pl.ds(m * EXT, EXT), cols], do2)
            wide = probs.astype(F32)
            inner = jnp.sum(wide * dprobs, axis=0, keepdims=True)
            ds = (wide * (dprobs - inner)).astype(BF16)
            dq = join_heads(mm_tn(ds, k_ref[pl.ds(m * EXT, EXT), cols])) * 0.125
            dq_ref[rows, cols] = rotate_back(dq, cos_own, sin_own).astype(BF16)
            dk = rotate_back(mm(ds, q2), cosine, sine)
            dv = mm(probs, do2)
            for grad, where in ((dk, cols), (dv, value_cols)):
                low_ref[m, :, where] = grad[:HALF].astype(BF16)
                dkv_ref[rows, where] = grad[HALF : HALF + ROWS]
                high_ref[m, :, where] = grad[HALF + ROWS :].astype(BF16)

    by_tiles(unit, group)


def place_shards(index, own, first, first_other, second, second_other, put):
    f, core = index[1], index[2]
    put(own, f, None)
    put(first, lax.rem(f + 3 + 2 * core, 4), None)
    put(first_other, lax.rem(f + 1 + 2 * core, 4), None)
    put(second, lax.rem(f + 2, 4), core)
    put(second_other, lax.rem(f + 2, 4), 1 - core)


def pack_qkv_kernel(index, qkv, gains, own, whole, half, first_rows, last_rows):
    rows = pl.ds(pl.multiple_of(index[2] * 96, 16), 96)
    whole[:, pl.ds(0, WIDE)] = qkv[...]
    half[:, pl.ds(0, WIDE)] = qkv[rows, :]
    whole[:, pl.ds(WIDE, 128)] = jnp.zeros((192, 128), BF16)
    half[:, pl.ds(WIDE, 128)] = jnp.zeros((96, 128), BF16)
    whole[pl.ds(0, 16), pl.ds(WIDE, 128)] = gains[...]
    half[pl.ds(0, 16), pl.ds(WIDE, 128)] = gains[...]
    first_rows[...] = own[:, :HALF]
    last_rows[...] = own[:, ROWS - HALF :]


def pack_kernel(index, lift, proj, down, rest, rest_half):
    core = index[2]
    rows = lambda at, size: pl.ds(pl.multiple_of(at, 16), size)
    rest[pl.ds(0, 192), :] = lift[...]
    rest_half[pl.ds(0, 96), :] = lift[rows(core * 96, 96), :]
    for b in range(3):
        cols = pl.ds(b * D, D)
        rest[pl.ds(192, 64), cols] = proj[pl.ds(64 * b, 64), :]
        rest[pl.ds(256, 96), cols] = down[pl.ds(96 * b, 96), :]
        rest_half[pl.ds(96, 32), cols] = proj[rows(64 * b + core * 32, 32), :]
        rest_half[pl.ds(128, 48), cols] = down[rows(96 * b + core * 48, 48), :]


def gather_gain(tiles, row):
    parts = []
    for tile in tiles:
        parts += [tile[row : row + 1, :], tile[row + 1 : row + 2, :64]]
    return jnp.concatenate(parts, axis=1)


def forward_attention_kernel(index, own, low, high, gain_tile, cos_ref, sin_ref, bias_ref,
                             shard, first, first_other, second, second_other,
                             o, gains, whole, wqkv, tiles, ext, a_ext, q, k, v, p, sems, out_sem):
    copies = []

    def go(src, dst):
        copy = pltpu.make_async_copy(src, dst, sems.at[len(copies)])
        copy.start()
        copies.append(copy)

    def put(piece, f, half):
        at, size = (f * 192, 192) if half is None else (f * 192 + half * 96, 96)
        rows = pl.ds(pl.multiple_of(at, 16), size)
        go(piece if piece is shard else piece.at[:, pl.ds(0, WIDE)], wqkv.at[rows])
        if piece is not shard and piece is not second_other:
            go(piece.at[pl.ds(0, 16), pl.ds(WIDE, 128)], tiles.at[f])

    place_shards(index, shard, first, first_other, second, second_other, put)
    go(gain_tile, tiles.at[index[1]])
    load_stream(None, own, low, high, (None, None, None), ext)
    for copy in copies:
        copy.wait()
    out = pltpu.make_async_copy(wqkv, whole, out_sem)
    out.start()
    shards = [tiles[f].astype(F32) for f in range(SHARDS)]
    gains[0:1, :] = gather_gain(shards, 0)
    gains[1:2, :] = gather_gain(shards, 2)
    forward_attention(ext, gains[0:1], wqkv, cos_ref, sin_ref, bias_ref, a_ext, q, k, v, p, o)
    out.wait()


def place_rest(index, lift, proj, down, pieces, wlift, wproj, wdown, go):
    f = index[1]
    rows = lambda at, size: pl.ds(pl.multiple_of(at, 16), size)

    def put(piece, s, half):
        if piece is None:
            go("proj", proj, wproj.at[rows(f * 192, 192)])
            go("lift", lift, wlift.at[rows(f * 192, 192)])
            go("down", down, wdown.at[rows(f * 288, 288)])
            return
        n = 2 if half is None else 1
        h = 0 if half is None else half
        go("lift", piece.at[pl.ds(0, 96 * n)], wlift.at[rows(s * 192 + h * 96, 96 * n)])
        for b in range(3):
            cols = pl.ds(b * D, D)
            go("proj", piece.at[pl.ds(96 * n, 32 * n), cols], wproj.at[rows(s * 192 + b * 64 + h * 32, 32 * n)])
            go("down", piece.at[pl.ds(128 * n, 48 * n), cols], wdown.at[rows(s * 288 + b * 96 + h * 48, 48 * n)])

    place_shards(index, None, *pieces, put)


def starter(sems, waits):
    count = [0]

    def go(name, src, dst):
        copy = pltpu.make_async_copy(src, dst, sems.at[count[0]])
        copy.start()
        count[0] += 1
        waits.setdefault(name, []).append(copy)

    return go


def forward_mlp_kernel(index, own, o, gains, lift, proj, down, first, first_other, second, second_other,
                       h3_ref, wproj, wlift, wdown, h2, b, m_out, sems):
    waits = {}
    pieces = (first, first_other, second, second_other)
    place_rest(index, lift, proj, down, pieces, wlift, wproj, wdown, starter(sems, waits))
    forward_mlp(own, o, wproj, gains[1:2], wlift, wdown, h2, b, m_out, None, None, h3_ref, waits)


def assemble_kernel(index, lift, proj, down, first, first_other, second, second_other, _,
                    whole_lift, whole_proj, whole_down, wlift, wproj, wdown, sems):
    waits = {}
    go = starter(sems, waits)
    place_rest(index, lift, proj, down, (first, first_other, second, second_other), wlift, wproj, wdown, go)
    for name, buffer, whole in (("lift", wlift, whole_lift), ("proj", wproj, whole_proj), ("down", wdown, whole_down)):
        finish(waits, name)
        go("out", buffer, whole)
    finish(waits, "out")


def start_all(pairs, sems, first):
    copies = [pltpu.make_async_copy(src, dst, sems.at[first + n]) for n, (src, dst) in enumerate(pairs)]
    for copy in copies:
        copy.start()
    return copies


def turning_kernel(flag_ref, own, low, high, other_own, other_low, other_high, cotangent, gains,
                   cos_ref, sin_ref, bias_ref, qkv_hbm, proj_hbm, lift_hbm, down_hbm, *refs):
    kept, (dh2_ref, dq, dkv, to_low, to_high) = refs[:11], refs[11:16]
    wqkv, wproj, wlift, wdown, ext, a_ext, mine, du, do, h3_ref, q, k, v, p, o, h2, m_out, left, right, src, sems = refs[16:]
    waits = start_weights(
        {"qkv": qkv_hbm, "proj": proj_hbm, "lift": lift_hbm, "down": down_hbm},
        {"qkv": wqkv, "proj": wproj, "lift": wlift, "down": wdown}, sems,
    )
    flag = flag_ref[0] == 1
    load_stream(flag, own, low, high, (other_own, other_low, other_high), ext)
    for m in range(MICRO):
        mine[m] = ext[pl.ds(m * EXT + HALF, ROWS), :]
        src[pl.ds(m * ROWS, ROWS), :] = mine[m]
    finish(waits, "qkv")
    forward_attention(ext, gains[0:1], wqkv, cos_ref, sin_ref, bias_ref, a_ext, q, k, v, p, o)
    outs = start_all(zip((q, k, v, p, o, src), kept[1:6] + kept[10:]), sems, 4)
    spare = a_ext.at[pl.ds(0, OWN)]
    forward_mlp(mine, o, wproj, gains[1:2], wlift, wdown, h2, spare, m_out, left, right, h3_ref, waits)
    outs += start_all(zip((h3_ref, h2, m_out, left, right), kept[:1] + kept[6:10]), sems, 10)
    grad = a_ext.at[pl.ds(OWN, OWN)]
    for m in range(MICRO):
        grad[pl.ds(m * ROWS, ROWS), :] = cotangent[m]
    backward_mlp(grad, h2, gains[1:2], wproj, wlift, wdown, left, right, du, spare, do, dh2_ref, None, None)
    backward_attention(q, k, v, p, do, cos_ref, sin_ref, dq, dkv, to_low, to_high, 3)
    for copy in outs:
        copy.wait()


def back_kernel(flag_ref, incoming, cotangent, gains, cos_ref, sin_ref, proj_hbm, lift_hbm, down_hbm,
                q_hbm, k_hbm, v_hbm, p_hbm, h2_hbm, left_hbm, right_hbm, *refs):
    kept, (mlp_ref, dh2_ref, dq, dkv, to_low, to_high) = refs[:4], refs[4:10]
    wproj, wlift, wdown, do, q, k, v, p, h2, left, right, grad_ref, du, gb_ref, b_ref, sems = refs[10:]
    early = start_all(
        ((down_hbm, wdown), (left_hbm, left), (right_hbm, right), (lift_hbm, wlift), (h2_hbm, h2), (proj_hbm, wproj)),
        sems, 0,
    )
    late = start_all(((q_hbm, q), (v_hbm, v), (p_hbm, p), (k_hbm, k)), sems, 6)
    flag = flag_ref[0] == 1
    for m in range(MICRO):
        grad_ref[pl.ds(m * ROWS, ROWS), :] = jnp.where(flag, incoming[m], cotangent[m])
    for copy in early:
        copy.wait()
    backward_mlp(
        grad_ref, h2, gains[1:2], wproj, wlift, wdown, left, right, du, gb_ref, do, dh2_ref, b_ref, mlp_ref
    )
    outs = start_all(zip((grad_ref, du, gb_ref, b_ref), kept), sems, 10)
    for copy in late:
        copy.wait()
    backward_attention(q, k, v, p, do, cos_ref, sin_ref, dq, dkv, to_low, to_high, 6)
    for copy in outs:
        copy.wait()


def joined_grads(dq, dkv, from_low, from_high, dqkv):
    dqkv[:, :D] = dq[...]
    for m in range(MICRO):
        first, last = pl.ds(m * ROWS, HALF), pl.ds(m * ROWS + HALF, HALF)
        dqkv[first, D:] = (dkv[first, :] + from_low[m].astype(F32)).astype(BF16)
        dqkv[last, D:] = (dkv[last, :] + from_high[m].astype(F32)).astype(BF16)


def source_kernel(src, gains, dh2, dq, dkv, from_low, from_high, qkv_hbm, out_ref, wqkv, dqkv, sems):
    waits = start_weights({"qkv": qkv_hbm}, {"qkv": wqkv}, sems)
    joined_grads(dq, dkv, from_low, from_high, dqkv)
    normed, inv_scale = norm_parts(src[...].astype(F32))
    finish(waits, "qkv")
    da = mm_nt(dqkv[...], wqkv[...])
    dh = dh2[...] + norm_back(da, gains[0:1], normed, inv_scale)
    for m in range(MICRO):
        out_ref[m] = dh[m * ROWS : (m + 1) * ROWS].astype(BF16)


def gain_block(attn, mlp, f):
    rows = []
    for gain in (attn, mlp):
        rows.append(gain[:, 192 * f : 192 * f + 128])
        rows.append(jnp.concatenate([gain[:, 192 * f + 128 : 192 * f + 192], jnp.zeros((1, 64), F32)], axis=1))
    return jnp.concatenate(rows + [jnp.zeros((92, 128), F32)], axis=0).astype(BF16)


def source_grad_kernel(index, src, gains, dh2, dq, dkv, from_low, from_high, mlp_grad, qkv_hbm,
                       out_ref, keep, send, wqkv, dqkv, qkv_ref, gain_ref, sems):
    waits = start_weights({"qkv": qkv_hbm}, {"qkv": wqkv}, sems)
    joined_grads(dq, dkv, from_low, from_high, dqkv)
    normed, inv_scale = norm_parts(src[...].astype(F32))
    finish(waits, "qkv")
    da = mm_nt(dqkv[...], wqkv[...])
    attn_grad = jnp.sum(da * normed, axis=0, keepdims=True)
    mlp = mlp_grad[...]
    for f in range(SHARDS):
        gain_ref[f] = gain_block(attn_grad, mlp, f)
    a = (normed * gains[0:1]).astype(BF16)
    for t in range(9):
        cols = pl.ds(256 * t, 256)
        qkv_ref[:, cols] = mm_tn(a, dqkv[:, cols]).astype(BF16)
    copies = []
    for target, half in ((send, 1 - index[2]), (keep, index[2])):
        for f in range(SHARDS):
            rows = pl.ds(pl.multiple_of(f * 192 + half * 96, 16), 96)
            for src_ref, dst_ref in (
                (qkv_ref.at[rows], target.at[f, :, pl.ds(0, WIDE)]),
                (gain_ref.at[f], target.at[f, :, pl.ds(WIDE, 128)]),
            ):
                copy = pltpu.make_async_copy(src_ref, dst_ref, sems.at[1 + len(copies)])
                copy.start()
                copies.append(copy)
    dh = dh2[...] + norm_back(da, gains[0:1], normed, inv_scale)
    for m in range(MICRO):
        out_ref[m] = dh[m * ROWS : (m + 1) * ROWS].astype(BF16)
    for copy in copies:
        copy.wait()


def weight_grad_kernel(index, m_ref, grad_ref, b_ref, du, o_ref, gb_ref, keep, send,
                       down_ref, lift_ref, proj_ref, pad_ref, sems):
    core = index[2]
    copies = []

    def go(src, dst):
        copy = pltpu.make_async_copy(src, dst, sems.at[len(copies)])
        copy.start()
        copies.append(copy)

    sides = ((send, 1 - core), (keep, core))
    rows = lambda at, size: pl.ds(pl.multiple_of(at, 16), size)
    pad_ref[...] = jnp.zeros_like(pad_ref)
    for target, _ in sides:
        for f in range(SHARDS):
            go(pad_ref, target.at[f, pl.ds(176, 16)])
    for t in range(9):
        cols = pl.ds(256 * t, 256)
        lift_ref[:, cols] = mm_tn(b_ref[...], du[:, cols]).astype(BF16)
    for target, half in sides:
        for f in range(SHARDS):
            go(lift_ref.at[rows(f * 192 + half * 96, 96)], target.at[f, pl.ds(0, 96)])
    for t in range(3):
        cols = pl.ds(256 * t, 256)
        down_ref[:, cols] = mm_tn(m_ref[...], grad_ref[:, cols]).astype(BF16)
        proj_ref[:, cols] = mm_tn(o_ref[...], gb_ref[:, cols]).astype(BF16)
    for target, half in sides:
        for f in range(SHARDS):
            for b in range(3):
                cols = pl.ds(b * D, D)
                go(proj_ref.at[rows(f * 192 + b * 64 + half * 32, 32)], target.at[f, pl.ds(96, 32), cols])
                go(down_ref.at[rows(f * 288 + b * 96 + half * 48, 48)], target.at[f, pl.ds(128, 48), cols])
    for copy in copies:
        copy.wait()


def add_up(parts):
    total = parts[0].astype(F32)
    for part in parts[1:]:
        total = total + part.astype(F32)
    return total.astype(BF16)


def rest_core_kernel(index, keep, other, *outs):
    for d, out in enumerate(outs):
        rows = pl.ds(pl.multiple_of(lax.rem(index[0] + d, 4) * 48, 16), 48)
        for f in range(SHARDS):
            out[f] = add_up([keep[f, rows, :], other[f, rows, :]])


def rest_z_kernel(index, own, a, b, c, *outs):
    for d, out in enumerate(outs):
        f = lax.rem(index[1] + d, 4)
        out[...] = add_up([own[f], a[f], b[f], c[f]])


def qkv_core_kernel(index, keep, other, *outs):
    for d, out in enumerate(outs):
        f = lax.rem(index[1] + d, 4)
        out[...] = add_up([keep[f], other[f]])


def partial_kernel(a, b, out):
    out[...] = a[...].astype(F32) + b[...].astype(F32)


def qkv_y_kernel(index, some, b, c, out_0, out_1, out_2, out_3, total):
    total[...] = add_up([some[...], b[...], c[...]])
    for d, out in enumerate((out_0, out_1, out_2, out_3)):
        z = lax.rem(index[0] + d, 4)
        rows = pl.ds(pl.multiple_of(lax.div(z, 2) * 48, 16), 48)
        cols = pl.ds(pl.multiple_of(lax.rem(z, 2) * 1152, 128), 1152)
        out[:, pl.ds(0, 1152)] = total[rows, cols]
        out[:, pl.ds(1152, 128)] = total[pl.ds(0, 48), pl.ds(WIDE, 128)]


def joint_kernel(r0, r1, r2, r3, q0, q1, q2, q3, out):
    out[:, pl.ds(0, WIDE)] = add_up([r0[...], r1[...], r2[...], r3[...]])
    out[:, pl.ds(WIDE, 1280)] = add_up([q0[...], q1[...], q2[...], q3[...]])


def pair_kernel(a, b, out):
    out[...] = add_up([a[...], b[...]])


def final_kernel(index, *refs):
    pieces, (qkv_out, proj_out, lift_out, down_out, gain_out, rest) = refs[:8], refs[8:]
    core = index[2]
    for side in range(2):
        half = core if side == 0 else 1 - core
        for d in range(4):
            piece = pieces[4 * side + d]
            z = lax.rem(index[0] - d + 4, 4)
            rest[side, pl.ds(pl.multiple_of(z * 48, 16), 48), :] = piece[:, pl.ds(0, WIDE)]
            qkv_out[
                pl.ds(pl.multiple_of(half * 96 + lax.div(z, 2) * 48, 16), 48),
                pl.ds(pl.multiple_of(lax.rem(z, 2) * 1152, 128), 1152),
            ] = piece[:, pl.ds(WIDE, 1152)].astype(F32)
        rows = lambda at, size: pl.ds(pl.multiple_of(at, 16), size)
        lift_out[rows(half * 96, 96), :] = rest[side, pl.ds(0, 96), :].astype(F32)
        for b in range(3):
            cols = pl.ds(b * D, D)
            proj_out[rows(b * 64 + half * 32, 32), :] = rest[side, pl.ds(96, 32), cols].astype(F32)
            down_out[rows(b * 96 + half * 48, 48), :] = rest[side, pl.ds(128, 48), cols].astype(F32)
    gain_out[...] = pieces[0][pl.ds(0, 16), pl.ds(WIDE + 1152, 128)].astype(F32)


def call(kernel, name, ins, outs, scratch, flops, limit=24):
    places = {"v": pltpu.VMEM, "a": pl.ANY, "s": pltpu.SMEM}
    return pl.pallas_call(
        kernel,
        name=name,
        out_shape=[jax.ShapeDtypeStruct(out[0], out[1]) for out in outs],
        in_specs=[pl.BlockSpec(memory_space=places[place]) for _, place in ins],
        out_specs=[pl.BlockSpec(memory_space=places[out[2] if len(out) > 2 else "v"]) for out in outs],
        scratch_shapes=scratch,
        compiler_params=pltpu.CompilerParams(vmem_limit_bytes=limit * 2**20),
        cost_estimate=pl.CostEstimate(flops=flops, bytes_accessed=flops // 300, transcendentals=0),
    )(*[array for array, _ in ins])


def travel(block, target):
    pairs = []
    for ctx in range(16):
        for f in range(SHARDS):
            xlo, z, core, g = target(ctx // 8, ctx // 2 % 4, ctx % 2, f)
            pairs.append((ctx * SHARDS + f, (xlo * 8 + z % 4 * 2 + core) * SHARDS + g % 4))
    return lax.ppermute(block, ("ctx", "fsdp"), pairs)


def along_y(block, d):
    return travel(block, lambda x, z, c, f: (x, z, c, f + d))


def along_z(block, d):
    return travel(block, lambda x, z, c, f: (x, z + d, c, f))


def next_shard(block):
    return travel(block, lambda x, z, c, f: (x, z, c, f + 1 - 2 * c))


def swap_core(block):
    return travel(block, lambda x, z, c, f: (x, z, 1 - c, f))


def swap_x(block):
    return travel(block, lambda x, z, c, f: (1 - x, z, c, f))


def halo_rows(block, axis):
    count = lax.axis_size(axis)
    up = [(i, i + 1) for i in range(count - 1)]
    down = [(i + 1, i) for i in range(count - 1)]
    return (
        lax.ppermute(block[:, ROWS - HALF :], axis, up),
        lax.ppermute(block[:, :HALF], axis, down),
    )


def swap_halos(to_low, to_high):
    count = lax.axis_size("ctx")
    up = [(i, i + 1) for i in range(count - 1)]
    down = [(i + 1, i) for i in range(count - 1)]
    return lax.ppermute(to_high, "ctx", up), lax.ppermute(to_low, "ctx", down)


def tables(first_row, lengths):
    half = HD // 2
    frequencies = rope_base ** (-(jnp.arange(half, dtype=F32) * 2.0) / HD)
    positions = first_row - HALF + jnp.arange(EXT, dtype=jnp.int32)
    angles = positions.astype(F32)[:, None] * frequencies[None, :]
    cosine, sine = jnp.cos(angles), jnp.sin(angles)
    cosine = jnp.concatenate([cosine] * 4, axis=1)
    sine = jnp.concatenate([-sine, sine, -sine, sine], axis=1)
    ends = jnp.cumsum(lengths, axis=1)
    doc = jnp.sum((positions[None, :, None] >= ends[:, None, :]).astype(jnp.int32), axis=2)
    query = positions[HALF : HALF + ROWS]
    allowed = (
        (jnp.abs(query[None, :] - positions[:, None]) <= HALF)
        & (positions >= 0)[:, None]
        & (positions < SEQ_LEN)[:, None]
    )[None] & (doc[:, :, None] == doc[:, None, HALF : HALF + ROWS])
    bias = jnp.where(allowed, 0.0, masked_score).astype(F32)
    return cosine, sine, jnp.concatenate([bias, bias], axis=2)


WQKV, WPROJ, WLIFT, WDOWN = [
    pltpu.VMEM((D, WIDE), BF16),
    pltpu.VMEM((D, D), BF16),
    pltpu.VMEM((D, WIDE), BF16),
    pltpu.VMEM((FF, D), BF16),
]
SAVED = [
    ((OWN, D), BF16),
    ((MICRO * EXT, D), BF16),
    ((MICRO * EXT, D), BF16),
    ((MICRO, TILES, EXT, 2 * ROWS), BF16),
    ((OWN, D), BF16),
    ((OWN, D), F32),
    ((OWN, FF), BF16),
    ((OWN, FF), F32),
    ((OWN, FF), F32),
]
STREAM = [pltpu.VMEM((MICRO * EXT, D), BF16)] * 2
GRADS_OUT = [
    ((OWN, D), F32),
    ((OWN, D), BF16),
    ((OWN, 2 * D), F32),
    ((MICRO, HALF, 2 * D), BF16),
    ((MICRO, HALF, 2 * D), BF16),
]


TURN_OUT = [((MICRO, ROWS, D), BF16)] + SAVED + [((OWN, D), BF16)]
BACK_OUT = [((OWN, D), BF16), ((OWN, WIDE), BF16), ((OWN, D), BF16), ((OWN, D), BF16)]


def sems(count):
    return pltpu.SemaphoreType.DMA((count,))


def body(
    inputs, out_grad, doc_lengths, attn_gain, qkv_weight, proj_weight, mlp_gain, lift_weight, down_weight
):
    on_first = lax.axis_index("section") == 0
    flag = on_first.astype(jnp.int32).reshape(1)
    ctx, f = lax.axis_index("ctx"), lax.axis_index("fsdp")
    index = jnp.stack([ctx // 2 % 4, f, ctx % 2]).astype(jnp.int32)
    qkv_shard, lift_shard, proj_shard, down_shard = qkv_weight[0], lift_weight[0], proj_weight[0], down_weight[0]
    own, cotangent = inputs[:, 0], out_grad[:, 0]
    gain_tile = jnp.pad(
        jnp.pad(jnp.stack([attn_gain[0], mlp_gain[0]]), ((0, 0), (0, 64))).reshape(4, 128), ((0, 12), (0, 0))
    )
    edge = ((MICRO, HALF, D), BF16)
    qkv_pack, qkv_half, first_rows, last_rows = call(
        pack_qkv_kernel, "pack_qkv",
        [(index, "s"), (qkv_shard, "v"), (gain_tile, "v"), (own, "v")],
        [((192, 2432), BF16), ((96, 2432), BF16), edge, edge],
        [], 0, 12,
    )
    rest, rest_half = call(
        pack_kernel, "pack_rest",
        [(index, "s"), (lift_shard, "v"), (proj_shard, "v"), (down_shard, "v")],
        [((352, WIDE), BF16), ((176, WIDE), BF16)],
        [], 0, 12,
    )
    first = next_shard(qkv_pack)
    second = along_y(qkv_half, 2)
    cosine, sine, bias = tables(ctx * ROWS, doc_lengths[:, 0])
    first_rows, last_rows, cosine = lax.optimization_barrier((first_rows, last_rows, cosine))
    low, high = swap_halos(first_rows, last_rows)
    first, second, rest, rest_half, cosine, sine, bias, low, high = lax.optimization_barrier(
        (first, second, rest, rest_half, cosine, sine, bias, low, high)
    )
    qkv_pieces = first, swap_core(first), second, swap_core(second)
    stream = ((MICRO, ROWS, D), BF16)
    scratch = lambda items: [pltpu.VMEM(s, k) for s, k in items]

    o, gains, wqkv = call(
        forward_attention_kernel, "forward_attention",
        [(index, "s"), (own, "v"), (low, "v"), (high, "v"), (gain_tile, "a"), (cosine, "v"), (sine, "v"), (bias, "v"),
         (qkv_shard, "a"), *[(piece, "a") for piece in qkv_pieces]],
        [((OWN, D), BF16), ((2, D), F32), ((D, WIDE), BF16, "a")],
        [WQKV, pltpu.VMEM((SHARDS, 16, 128), BF16)] + STREAM + scratch(SAVED[:4]) + [sems(9), pltpu.SemaphoreType.DMA(())],
        1_400_000_000,
    )
    rest_first, rest_second, o = lax.optimization_barrier((next_shard(rest), along_y(rest_half, 2), o))
    rest_pieces = rest_first, swap_core(rest_first), rest_second, swap_core(rest_second)
    rest_parts = [(part, "a") for part in (lift_shard, proj_shard, down_shard, *rest_pieces)]
    (relay,) = call(
        forward_mlp_kernel, "forward_mlp",
        [(index, "s"), (own, "v"), (o, "v"), (gains, "v"), *rest_parts],
        [stream],
        [WPROJ, WLIFT, WDOWN] + scratch([SAVED[5], SAVED[0], SAVED[6]]) + [sems(31)],
        1_800_000_000,
    )
    wlift, wproj, wdown = call(
        assemble_kernel, "assemble_weights",
        [(index, "s"), *rest_parts, (relay, "a")],
        [((D, WIDE), BF16, "a"), ((D, D), BF16, "a"), ((FF, D), BF16, "a")],
        [WLIFT, WPROJ, WDOWN, sems(34)], 1_800_000_000, 56,
    )
    relayed = lax.ppermute(relay, "section", [(0, 1)])
    other_low, other_high = halo_rows(relayed, "ctx")
    (h3, q, k, v, p, o, h2, m_act, left, right, src, dh2, dq, dkv, to_low, to_high) = call(
        turning_kernel, "layer_turn",
        [(flag, "s"), (own, "v"), (low, "v"), (high, "v"), (relayed, "v"), (other_low, "v"), (other_high, "v"),
         (cotangent, "v"), (gains, "v"), (cosine, "v"), (sine, "v"), (bias, "v"),
         (wqkv, "a"), (wproj, "a"), (wlift, "a"), (wdown, "a")],
        [(*item, "a") for item in TURN_OUT] + GRADS_OUT,
        [WQKV, WPROJ, WLIFT, WDOWN] + STREAM
        + [pltpu.VMEM((MICRO, ROWS, D), BF16), pltpu.VMEM((OWN, WIDE), BF16), pltpu.VMEM((OWN, D), BF16)] + scratch(TURN_OUT) + [sems(15)],
        6_000_000_000, 44,
    )
    from_low, from_high = swap_halos(to_low, to_high)
    (grad_relay,) = call(
        source_kernel, "layer_source",
        [(src, "v"), (gains, "v"), (dh2, "v"), (dq, "v"), (dkv, "v"), (from_low, "v"), (from_high, "v"), (wqkv, "a")],
        [stream],
        [WQKV, pltpu.VMEM((OWN, WIDE), BF16), sems(1)],
        900_000_000,
    )
    incoming = lax.ppermute(grad_relay, "section", [(1, 0)])
    (grad_low, du, gb, b, mlp_gain_grad, dh2, dq, dkv, to_low, to_high) = call(
        back_kernel, "layer_back",
        [(flag, "s"), (incoming, "v"), (cotangent, "v"), (gains, "v"), (cosine, "v"), (sine, "v"),
         (wproj, "a"), (wlift, "a"), (wdown, "a"),
         *[(array, "a") for array in (q, k, v, p, h2, left, right)]],
        [(*item, "a") for item in BACK_OUT] + [((1, D), F32)] + GRADS_OUT,
        [WPROJ, WLIFT, WDOWN, pltpu.VMEM((OWN, D), BF16)]
        + scratch(SAVED[:4] + SAVED[5:6] + SAVED[7:] + BACK_OUT) + [sems(14)],
        3_000_000_000, 40,
    )
    from_low, from_high = swap_halos(to_low, to_high)
    rest_keep, rest_send = call(
        weight_grad_kernel, "weight_grads",
        [(index, "s"), (m_act, "v"), (grad_low, "v"), (b, "v"), (du, "v"), (o, "v"), (gb, "v")],
        [((SHARDS, 192, WIDE), BF16, "a")] * 2,
        [WDOWN, WLIFT, WPROJ, pltpu.VMEM((16, WIDE), BF16), sems(64)],
        1_600_000_000,
    )
    from_low, from_high, rest_send = lax.optimization_barrier((from_low, from_high, rest_send))
    rest_other = swap_core(rest_send)
    in_grad, qkv_keep, qkv_send = call(
        source_grad_kernel, "layer_source_grads",
        [(index, "s"), (src, "v"), (gains, "v"), (dh2, "v"), (dq, "v"), (dkv, "v"), (from_low, "v"),
         (from_high, "v"), (mlp_gain_grad, "v"), (wqkv, "a")],
        [stream, ((SHARDS, 96, 2432), BF16, "a"), ((SHARDS, 96, 2432), BF16, "a")],
        [WQKV, pltpu.VMEM((OWN, WIDE), BF16), WQKV, pltpu.VMEM((SHARDS, 96, 128), BF16), sems(17)],
        1_800_000_000,
    )
    qkv_other = swap_core(qkv_send)

    rest_z = call(
        rest_core_kernel, "rest_core_sum", [(index, "s"), (rest_keep, "v"), (rest_other, "v")],
        [((SHARDS, 48, WIDE), BF16)] * 4, [], 0, 24,
    )
    qkv_keep, _ = lax.optimization_barrier((qkv_keep, rest_z[0]))
    qkv_y = call(
        qkv_core_kernel, "qkv_core_sum", [(index, "s"), (qkv_keep, "v"), (qkv_other, "v")],
        [((96, 2432), BF16)] * 4, [], 0, 24,
    )
    (some,) = call(
        partial_kernel, "qkv_y_first", [(qkv_y[0], "v"), (along_y(qkv_y[1], 1), "v")],
        [((96, 2432), F32)], [], 0, 24,
    )
    rest_mine, some = lax.optimization_barrier((rest_z[0], some))
    rest_y = call(
        rest_z_kernel, "rest_z_sum",
        [(index, "s"), (rest_mine, "v"), *[(along_z(rest_z[d], d), "v") for d in (1, 2, 3)]],
        [((48, WIDE), BF16)] * 4, [], 0, 24,
    )
    some, _ = lax.optimization_barrier((some, rest_y[0]))
    qkv_z = call(
        qkv_y_kernel, "qkv_y_sum",
        [(index, "s"), (some, "v"), *[(along_y(qkv_y[d], d), "v") for d in (2, 3)]],
        [((48, 1280), BF16)] * 4, [pltpu.VMEM((96, 2432), BF16)], 0, 24,
    )
    (joint,) = call(
        joint_kernel, "joint_sum",
        [(rest_y[0], "v"), *[(along_y(rest_y[d], d), "v") for d in (1, 2, 3)],
         (qkv_z[0], "v"), *[(along_z(qkv_z[d], d), "v") for d in (1, 2, 3)]],
        [((48, 3584), BF16)], [], 0, 24,
    )
    (joint,) = call(
        pair_kernel, "pair_sum", [(joint, "v"), (swap_x(joint), "v")], [((48, 3584), BF16)], [], 0, 24
    )
    mine = [joint] + [along_z(joint, d) for d in (1, 2, 3)]
    theirs = [swap_core(piece) for piece in mine]
    qkv_sum, proj_sum, lift_sum, down_sum, gain_sums = call(
        final_kernel, "final_shard", [(index, "s"), *[(piece, "v") for piece in mine + theirs]],
        [((192, WIDE), F32), ((192, D), F32), ((192, WIDE), F32), ((288, D), F32), ((16, 128), F32)],
        [pltpu.VMEM((2, 192, WIDE), BF16)], 0, 24,
    )
    return (
        h3[None, :, None],
        in_grad[None, :, None],
        gain_sums[0:2].reshape(1, 256)[:, :192],
        qkv_sum[None],
        proj_sum[None],
        gain_sums[2:4].reshape(1, 256)[:, :192],
        lift_sum[None],
        down_sum[None],
    )


def solution(mesh):
    placed = (
        P(None, "fsdp", "ctx", None),
        P(None, "fsdp", "ctx", None),
        P(None, "fsdp", None),
        P("section", "fsdp"),
        P("section", "fsdp", None),
        P("section", "fsdp", None),
        P("section", "fsdp"),
        P("section", "fsdp", None),
        P("section", "fsdp", None),
    )
    return jax.shard_map(
        body,
        mesh=mesh,
        in_specs=placed,
        out_specs=(
            P("section", None, "fsdp", "ctx", None),
            P("section", None, "fsdp", "ctx", None),
            P("section", "fsdp"),
            P("section", "fsdp", None),
            P("section", "fsdp", None),
            P("section", "fsdp"),
            P("section", "fsdp", None),
            P("section", "fsdp", None),
        ),
        check_vma=False,
    )
```

```python
import functools

import jax
import jax.numpy as jnp
from jax import lax
from jax.experimental import pallas as pl
from jax.experimental.pallas import tpu as pltpu
from jax.sharding import PartitionSpec as P

D = 768
HD = 64
HALF = 64
SEQ_LEN = 2048
FF = 1152
WIDE = 2304
ROWS = 128
EXT = ROWS + 2 * HALF
MICRO = 2
OWN = MICRO * ROWS
SHARDS = 4
TILES = D // 128
norm_eps = 1e-05
rope_base = 10000.0
masked_score = -1e30
root_half = 0.7071067811865476
inv_root_tau = 0.3989422804014327
F32 = jnp.float32
BF16 = jnp.bfloat16


def mm(left, right):
    return lax.dot_general(left, right, (((1,), (0,)), ((), ())), preferred_element_type=F32)


def mm_nt(left, right):
    return lax.dot_general(left, right, (((1,), (1,)), ((), ())), preferred_element_type=F32)


def mm_tn(left, right):
    return lax.dot_general(left, right, (((0,), (0,)), ((), ())), preferred_element_type=F32)


def norm_parts(hidden):
    centre = hidden - jnp.mean(hidden, axis=-1, keepdims=True)
    inv_scale = lax.rsqrt(jnp.mean(centre * centre, axis=-1, keepdims=True) + norm_eps)
    return centre * inv_scale, inv_scale


def norm_back(grad_out, gain, normed, inv_scale):
    grad_normed = grad_out * gain
    inner = (
        grad_normed
        - jnp.mean(grad_normed, axis=-1, keepdims=True)
        - normed * jnp.mean(grad_normed * normed, axis=-1, keepdims=True)
    )
    return inner * inv_scale


def lane_is_low(shape, period):
    return lax.broadcasted_iota(jnp.int32, shape, 1) % period < period // 2


def turn(x):
    return jnp.where(lane_is_low(x.shape, HD), pltpu.roll(x, 96, 1), pltpu.roll(x, 32, 1))


def rotate(x, cosine, sine):
    return x * cosine + turn(x) * sine


def rotate_back(x, cosine, sine):
    return x * cosine - turn(x) * sine


def stack_heads(x):
    low = lane_is_low(x.shape, 128)
    zero = jnp.zeros_like(x)
    return jnp.concatenate([jnp.where(low, x, zero), jnp.where(low, zero, x)], axis=0)


def join_heads(x):
    half = x.shape[0] // 2
    low = lane_is_low((half, 128), 128)
    return jnp.where(low, x[:half], x[half:])


def start_weights(sources, buffers, sems):
    waits = {}
    for index, (name, source) in enumerate(sources.items()):
        copy = pltpu.make_async_copy(source, buffers[name], sems.at[index])
        copy.start()
        waits[name] = [copy]
    return waits


def finish(waits, name):
    for copy in waits[name]:
        copy.wait()


def load_stream(flag, own, low, high, other, ext):
    for m in range(MICRO):
        for ref, alt, start, size in (
            (low, other[1], 0, HALF),
            (own, other[0], HALF, ROWS),
            (high, other[2], HALF + ROWS, HALF),
        ):
            value = ref[m]
            if alt is not None:
                value = jnp.where(flag, value, alt[m])
            ext[pl.ds(m * EXT + start, size), :] = value


def own_rows(x):
    return jnp.concatenate([x[HALF : HALF + ROWS], x[EXT + HALF : EXT + HALF + ROWS]], axis=0)


def repeat(count, step):
    lax.fori_loop(0, count, lambda i, carry: (step(i), carry)[1], 0)


def each(count, step):
    for i in range(count):
        step(i)


def span(start, size, unit=128):
    return pl.ds(start if isinstance(start, int) else pl.multiple_of(start, unit), size)


def by_tiles(unit, group):
    def step(i):
        for j in range(group):
            unit(i * group + j)

    repeat(TILES // group, step)


def norm_rows(source, gain, target):
    def step(i):
        rows = span(i * 128, 128)
        normed, _ = norm_parts(source[rows, :].astype(F32))
        target[rows, :] = (normed * gain).astype(BF16)

    repeat(source.shape[0] // 128, step)


def forward_attention(ext, gain, wqkv, cos_ref, sin_ref, bias_ref, a_ext, q_ref, k_ref, v_ref, p_ref, o_ref):
    norm_rows(ext, gain, a_ext)
    a_own = o_ref
    a_own[...] = own_rows(a_ext[...])
    own_span = pl.ds(HALF, ROWS)

    def project(t):
        cols = span(256 * t, 256)
        queries = mm(a_own[...], wqkv[:, cols])
        keys = mm(a_ext[...], wqkv[:, span(D + 256 * t, 256)])
        v_ref[:, cols] = mm(a_ext[...], wqkv[:, span(2 * D + 256 * t, 256)]).astype(BF16)
        for s in range(2):
            tile, lanes = span(256 * t + 128 * s, 128), slice(128 * s, 128 * s + 128)
            for m in range(MICRO):
                part = queries[m * ROWS : (m + 1) * ROWS, lanes]
                turned = rotate(part, cos_ref[own_span, :], sin_ref[own_span, :]).astype(BF16)
                q_ref[pl.ds(m * ROWS, ROWS), tile] = turned * jnp.asarray(0.125, BF16)
                part = keys[m * EXT : (m + 1) * EXT, lanes]
                k_ref[pl.ds(m * EXT, EXT), tile] = rotate(part, cos_ref[...], sin_ref[...]).astype(BF16)

    repeat(3, project)

    def unit(t):
        cols = pl.ds(pl.multiple_of(t * 128, 128), 128)
        for m in range(MICRO):
            q2 = stack_heads(q_ref[pl.ds(m * ROWS, ROWS), cols])
            scores = mm_nt(k_ref[pl.ds(m * EXT, EXT), cols], q2) + bias_ref[m]
            terms = jnp.exp(scores - jnp.max(scores, axis=0, keepdims=True))
            probs = (terms * (1.0 / jnp.sum(terms, axis=0, keepdims=True))).astype(BF16)
            p_ref[m, t] = probs
            attended = mm_tn(probs, v_ref[pl.ds(m * EXT, EXT), cols])
            o_ref[pl.ds(m * ROWS, ROWS), cols] = join_heads(attended).astype(BF16)

    by_tiles(unit, 3)


def forward_mlp(own, o_ref, wproj, mlp_gain, wlift, wdown, h2_ref, b_ref, m_ref, left_ref, right_ref, h3_ref, waits):
    finish(waits, "proj")

    def mix(t):
        cols = span(256 * t, 256)
        added = mm(o_ref[...], wproj[:, cols])
        for m in range(MICRO):
            rows = pl.ds(m * ROWS, ROWS)
            h2_ref[rows, cols] = own[m, :, cols].astype(F32) + added[m * ROWS : (m + 1) * ROWS]

    each(3, mix)
    norm_rows(h2_ref, mlp_gain, b_ref)
    finish(waits, "lift")

    def lift(t):
        cols = span(384 * t, 384)
        gate = mm(b_ref[...], wlift[:, cols])
        up = mm(b_ref[...], wlift[:, span(FF + 384 * t, 384)])
        cdf = 0.5 * (1.0 + lax.erf(gate * root_half))
        gelu = gate * cdf
        m_ref[:, cols] = (gelu * up).astype(BF16)
        if left_ref is not None:
            pdf = jnp.exp(-0.5 * gate * gate) * inv_root_tau
            left_ref[:, cols] = up * (cdf + gate * pdf)
            right_ref[:, cols] = gelu

    repeat(3, lift)
    finish(waits, "down")

    def down(t):
        cols = span(256 * t, 256)
        h3 = (h2_ref[:, cols] + mm(m_ref[...], wdown[:, cols])).astype(BF16)
        for m in range(MICRO):
            h3_ref[m, :, cols] = h3[m * ROWS : (m + 1) * ROWS]

    each(3, down)


def backward_mlp(grad_ref, h2_ref, mlp_gain, wproj, wlift, wdown, left_ref, right_ref, du_ref, gb_ref, do_ref,
                 dh2_ref, b_ref, mlp_ref):
    def lift(t):
        cols = span(384 * t, 384)
        dm = mm_nt(grad_ref[...], wdown[cols, :])
        du_ref[:, cols] = (dm * left_ref[:, cols]).astype(BF16)
        du_ref[:, span(FF + 384 * t, 384)] = (dm * right_ref[:, cols]).astype(BF16)

    each(3, lift)

    def source(t):
        rows = span(256 * t, 256)
        dh2_ref[:, rows] = mm_nt(du_ref[...], wlift[rows, :])

    each(3, source)
    if mlp_ref is not None:
        mlp_ref[...] = jnp.zeros_like(mlp_ref)

    def norm(i):
        rows = span(i * 128, 128)
        db = dh2_ref[rows, :]
        normed, inv_scale = norm_parts(h2_ref[rows, :])
        dh2 = grad_ref[rows, :].astype(F32) + norm_back(db, mlp_gain, normed, inv_scale)
        dh2_ref[rows, :] = dh2
        gb_ref[rows, :] = dh2.astype(BF16)
        if mlp_ref is not None:
            mlp_ref[...] += jnp.sum(db * normed, axis=0, keepdims=True)
            b_ref[rows, :] = (normed * mlp_gain).astype(BF16)

    repeat(2, norm)

    def attended(t):
        rows = span(256 * t, 256)
        do_ref[:, rows] = mm_nt(gb_ref[...], wproj[rows, :]).astype(BF16)

    each(3, attended)


def backward_attention(q_ref, k_ref, v_ref, p_ref, do_ref, cos_ref, sin_ref, dq_ref, dkv_ref, low_ref, high_ref, group):
    cosine, sine = cos_ref[...], sin_ref[...]
    cos_own, sin_own = cosine[HALF : HALF + ROWS], sine[HALF : HALF + ROWS]

    def unit(t):
        cols = pl.ds(pl.multiple_of(t * 128, 128), 128)
        value_cols = pl.ds(pl.multiple_of(D + t * 128, 128), 128)
        for m in range(MICRO):
            rows = pl.ds(m * ROWS, ROWS)
            q2 = stack_heads(q_ref[rows, cols])
            do2 = stack_heads(do_ref[rows, cols])
            probs = p_ref[m, t]
            dprobs = mm_nt(v_ref[pl.ds(m * EXT, EXT), cols], do2)
            wide = probs.astype(F32)
            inner = jnp.sum(wide * dprobs, axis=0, keepdims=True)
            ds = (wide * (dprobs - inner)).astype(BF16)
            dq = join_heads(mm_tn(ds, k_ref[pl.ds(m * EXT, EXT), cols])) * 0.125
            dq_ref[rows, cols] = rotate_back(dq, cos_own, sin_own).astype(BF16)
            dk = rotate_back(mm(ds, q2), cosine, sine)
            dv = mm(probs, do2)
            for grad, where in ((dk, cols), (dv, value_cols)):
                low_ref[m, :, where] = grad[:HALF].astype(BF16)
                dkv_ref[rows, where] = grad[HALF : HALF + ROWS]
                high_ref[m, :, where] = grad[HALF + ROWS :].astype(BF16)

    by_tiles(unit, group)


def place_shards(index, own, pieces, put):
    f, core, xlo = index[1], index[2], index[3]
    first, first_other, second, second_x, second_core, second_both = pieces
    put(own, f, None, None)
    put(first, lax.rem(f + 3 + 2 * core, 4), None, None)
    put(first_other, lax.rem(f + 1 + 2 * core, 4), None, None)
    across = lax.rem(f + 2, 4)
    put(second, across, core, xlo)
    put(second_x, across, core, 1 - xlo)
    put(second_core, across, 1 - core, xlo)
    put(second_both, across, 1 - core, 1 - xlo)


def pack_qkv_kernel(index, qkv, gains, own, whole, quarter, first_rows, last_rows):
    rows = pl.ds(pl.multiple_of(index[2] * 96, 16), 96)
    whole[:, pl.ds(0, WIDE)] = qkv[...]
    quarter[:, pl.ds(0, 1152)] = qkv[rows, pl.ds(pl.multiple_of(index[3] * 1152, 128), 1152)]
    whole[:, pl.ds(WIDE, 128)] = jnp.zeros((192, 128), BF16)
    quarter[:, pl.ds(1152, 128)] = jnp.zeros((96, 128), BF16)
    whole[pl.ds(0, 16), pl.ds(WIDE, 128)] = gains[...]
    quarter[pl.ds(0, 16), pl.ds(1152, 128)] = gains[...]
    first_rows[...] = own[:, :HALF]
    last_rows[...] = own[:, ROWS - HALF :]


def pack_kernel(index, lift, proj, down, rest, quarter, half):
    core = index[2]
    rows = lambda at, size: pl.ds(pl.multiple_of(at, 16), size)
    rest[pl.ds(0, 192), :] = lift[...]
    half[pl.ds(0, 96), :] = lift[rows(core * 96, 96), :]
    for b in range(3):
        cols = pl.ds(b * D, D)
        rest[pl.ds(192, 64), cols] = proj[pl.ds(64 * b, 64), :]
        rest[pl.ds(256, 96), cols] = down[pl.ds(96 * b, 96), :]
        half[pl.ds(96, 32), cols] = proj[rows(64 * b + core * 32, 32), :]
        half[pl.ds(128, 48), cols] = down[rows(96 * b + core * 48, 48), :]
    quarter[...] = half[:, pl.ds(pl.multiple_of(index[3] * 1152, 128), 1152)]


def gather_gain(tiles, row):
    parts = []
    for tile in tiles:
        parts += [tile[row : row + 1, :], tile[row + 1 : row + 2, :64]]
    return jnp.concatenate(parts, axis=1)


def forward_attention_kernel(index, own, low, high, gain_tile, cos_ref, sin_ref, bias_ref,
                             shard, first, first_other, second, second_x, second_core, second_both,
                             o, gains, whole, wqkv, tiles, ext, a_ext, q, k, v, p, sems, out_sem):
    copies = []

    def go(src, dst):
        copy = pltpu.make_async_copy(src, dst, sems.at[len(copies)])
        copy.start()
        copies.append(copy)

    def put(piece, f, half, side):
        if half is None:
            target = wqkv.at[pl.ds(pl.multiple_of(f * 192, 16), 192)]
            go(piece if piece is shard else piece.at[:, pl.ds(0, WIDE)], target)
        else:
            target = wqkv.at[
                pl.ds(pl.multiple_of(f * 192 + half * 96, 16), 96),
                pl.ds(pl.multiple_of(side * 1152, 128), 1152),
            ]
            go(piece.at[:, pl.ds(0, 1152)], target)
        if piece is first or piece is first_other:
            go(piece.at[pl.ds(0, 16), pl.ds(WIDE, 128)], tiles.at[f])
        if piece is second:
            go(piece.at[pl.ds(0, 16), pl.ds(1152, 128)], tiles.at[f])

    place_shards(index, shard, (first, first_other, second, second_x, second_core, second_both), put)
    go(gain_tile, tiles.at[index[1]])
    load_stream(None, own, low, high, (None, None, None), ext)
    for copy in copies:
        copy.wait()
    out = pltpu.make_async_copy(wqkv, whole, out_sem)
    out.start()
    shards = [tiles[f].astype(F32) for f in range(SHARDS)]
    gains[0:1, :] = gather_gain(shards, 0)
    gains[1:2, :] = gather_gain(shards, 2)
    forward_attention(ext, gains[0:1], wqkv, cos_ref, sin_ref, bias_ref, a_ext, q, k, v, p, o)
    out.wait()


def place_rest(index, lift, proj, down, pieces, wlift, wproj, wdown, go):
    f = index[1]
    rows = lambda at, size: pl.ds(pl.multiple_of(at, 16), size)
    lanes = lambda at, size: pl.ds(pl.multiple_of(at, 128), size)

    def put(piece, s, half, side):
        if piece is None:
            go("proj", proj, wproj.at[rows(f * 192, 192)])
            go("lift", lift, wlift.at[rows(f * 192, 192)])
            go("down", down, wdown.at[rows(f * 288, 288)])
        elif half is None:
            go("lift", piece.at[pl.ds(0, 192)], wlift.at[rows(s * 192, 192)])
            for b in range(3):
                cols = pl.ds(b * D, D)
                go("proj", piece.at[pl.ds(192, 64), cols], wproj.at[rows(s * 192 + b * 64, 64)])
                go("down", piece.at[pl.ds(256, 96), cols], wdown.at[rows(s * 288 + b * 96, 96)])
        else:
            go("lift", piece.at[pl.ds(0, 96)], wlift.at[rows(s * 192 + half * 96, 96), lanes(side * 1152, 1152)])
            for j in range(3):
                cols = pl.ds(j * 384, 384)
                b, right = lax.div(3 * side + j, 2), lanes(lax.rem(3 * side + j, 2) * 384, 384)
                go("proj", piece.at[pl.ds(96, 32), cols], wproj.at[rows(s * 192 + b * 64 + half * 32, 32), right])
                go("down", piece.at[pl.ds(128, 48), cols], wdown.at[rows(s * 288 + b * 96 + half * 48, 48), right])

    place_shards(index, None, pieces, put)


def starter(sems, waits):
    count = [0]

    def go(name, src, dst):
        copy = pltpu.make_async_copy(src, dst, sems.at[count[0]])
        copy.start()
        count[0] += 1
        waits.setdefault(name, []).append(copy)

    return go


def forward_mlp_kernel(index, own, o, gains, lift, proj, down, *refs):
    pieces, (h3_ref, wproj, wlift, wdown, h2, b, m_out, sems) = refs[:6], refs[6:]
    waits = {}
    place_rest(index, lift, proj, down, pieces, wlift, wproj, wdown, starter(sems, waits))
    forward_mlp(own, o, wproj, gains[1:2], wlift, wdown, h2, b, m_out, None, None, h3_ref, waits)


def assemble_kernel(index, lift, proj, down, *refs):
    pieces, (whole_lift, whole_proj, whole_down, wlift, wproj, wdown, sems) = refs[:6], refs[7:]
    waits = {}
    go = starter(sems, waits)
    place_rest(index, lift, proj, down, pieces, wlift, wproj, wdown, go)
    for name, buffer, whole in (("lift", wlift, whole_lift), ("proj", wproj, whole_proj), ("down", wdown, whole_down)):
        finish(waits, name)
        go("out", buffer, whole)
    finish(waits, "out")


def start_all(pairs, sems, first):
    copies = [pltpu.make_async_copy(src, dst, sems.at[first + n]) for n, (src, dst) in enumerate(pairs)]
    for copy in copies:
        copy.start()
    return copies


def turning_kernel(flag_ref, own, low, high, other_own, other_low, other_high, cotangent, gains,
                   cos_ref, sin_ref, bias_ref, qkv_hbm, proj_hbm, lift_hbm, down_hbm, *refs):
    kept, (dh2_ref, dq, dkv, to_low, to_high) = refs[:11], refs[11:16]
    wqkv, wproj, wlift, wdown, ext, a_ext, mine, du, do, h3_ref, q, k, v, p, o, h2, m_out, left, right, src, sems = refs[16:]
    waits = start_weights(
        {"qkv": qkv_hbm, "proj": proj_hbm, "lift": lift_hbm, "down": down_hbm},
        {"qkv": wqkv, "proj": wproj, "lift": wlift, "down": wdown}, sems,
    )
    flag = flag_ref[0] == 1
    load_stream(flag, own, low, high, (other_own, other_low, other_high), ext)
    for m in range(MICRO):
        mine[m] = ext[pl.ds(m * EXT + HALF, ROWS), :]
        src[pl.ds(m * ROWS, ROWS), :] = mine[m]
    finish(waits, "qkv")
    forward_attention(ext, gains[0:1], wqkv, cos_ref, sin_ref, bias_ref, a_ext, q, k, v, p, o)
    outs = start_all(zip((q, k, v, p, o, src), kept[1:6] + kept[10:]), sems, 4)
    spare = a_ext.at[pl.ds(0, OWN)]
    forward_mlp(mine, o, wproj, gains[1:2], wlift, wdown, h2, spare, m_out, left, right, h3_ref, waits)
    outs += start_all(zip((h3_ref, h2, m_out, left, right), kept[:1] + kept[6:10]), sems, 10)
    grad = a_ext.at[pl.ds(OWN, OWN)]
    for m in range(MICRO):
        grad[pl.ds(m * ROWS, ROWS), :] = cotangent[m]
    backward_mlp(grad, h2, gains[1:2], wproj, wlift, wdown, left, right, du, spare, do, dh2_ref, None, None)
    backward_attention(q, k, v, p, do, cos_ref, sin_ref, dq, dkv, to_low, to_high, 3)
    for copy in outs:
        copy.wait()


def back_kernel(flag_ref, incoming, cotangent, gains, cos_ref, sin_ref, proj_hbm, lift_hbm, down_hbm,
                q_hbm, k_hbm, v_hbm, p_hbm, h2_hbm, left_hbm, right_hbm, *refs):
    kept, (mlp_ref, dh2_ref, dq, dkv, to_low, to_high) = refs[:4], refs[4:10]
    wproj, wlift, wdown, do, q, k, v, p, h2, left, right, grad_ref, du, gb_ref, b_ref, sems = refs[10:]
    early = start_all(
        ((down_hbm, wdown), (left_hbm, left), (right_hbm, right), (lift_hbm, wlift), (h2_hbm, h2), (proj_hbm, wproj)),
        sems, 0,
    )
    late = start_all(((q_hbm, q), (v_hbm, v), (p_hbm, p), (k_hbm, k)), sems, 6)
    flag = flag_ref[0] == 1
    for m in range(MICRO):
        grad_ref[pl.ds(m * ROWS, ROWS), :] = jnp.where(flag, incoming[m], cotangent[m])
    for copy in early:
        copy.wait()
    backward_mlp(
        grad_ref, h2, gains[1:2], wproj, wlift, wdown, left, right, du, gb_ref, do, dh2_ref, b_ref, mlp_ref
    )
    outs = start_all(zip((grad_ref, du, gb_ref, b_ref), kept), sems, 10)
    for copy in late:
        copy.wait()
    backward_attention(q, k, v, p, do, cos_ref, sin_ref, dq, dkv, to_low, to_high, 6)
    for copy in outs:
        copy.wait()


def joined_grads(dq, dkv, from_low, from_high, dqkv):
    dqkv[:, :D] = dq[...]
    for m in range(MICRO):
        first, last = pl.ds(m * ROWS, HALF), pl.ds(m * ROWS + HALF, HALF)
        dqkv[first, D:] = (dkv[first, :] + from_low[m].astype(F32)).astype(BF16)
        dqkv[last, D:] = (dkv[last, :] + from_high[m].astype(F32)).astype(BF16)


def source_kernel(src, gains, dh2, dq, dkv, from_low, from_high, qkv_hbm, out_ref, wqkv, dqkv, sems):
    waits = start_weights({"qkv": qkv_hbm}, {"qkv": wqkv}, sems)
    joined_grads(dq, dkv, from_low, from_high, dqkv)
    normed, inv_scale = norm_parts(src[...].astype(F32))
    finish(waits, "qkv")
    da = mm_nt(dqkv[...], wqkv[...])
    dh = dh2[...] + norm_back(da, gains[0:1], normed, inv_scale)
    for m in range(MICRO):
        out_ref[m] = dh[m * ROWS : (m + 1) * ROWS].astype(BF16)


def gain_block(attn, mlp, f):
    rows = []
    for gain in (attn, mlp):
        rows.append(gain[:, 192 * f : 192 * f + 128])
        rows.append(jnp.concatenate([gain[:, 192 * f + 128 : 192 * f + 192], jnp.zeros((1, 64), F32)], axis=1))
    return jnp.concatenate(rows + [jnp.zeros((92, 128), F32)], axis=0).astype(BF16)


def source_grad_kernel(index, src, gains, dh2, dq, dkv, from_low, from_high, mlp_grad, qkv_hbm,
                       out_ref, keep, send, wqkv, dqkv, qkv_ref, gain_ref, sems):
    waits = start_weights({"qkv": qkv_hbm}, {"qkv": wqkv}, sems)
    joined_grads(dq, dkv, from_low, from_high, dqkv)
    normed, inv_scale = norm_parts(src[...].astype(F32))
    finish(waits, "qkv")
    da = mm_nt(dqkv[...], wqkv[...])
    attn_grad = jnp.sum(da * normed, axis=0, keepdims=True)
    mlp = mlp_grad[...]
    for f in range(SHARDS):
        gain_ref[f] = gain_block(attn_grad, mlp, f)
    a = (normed * gains[0:1]).astype(BF16)
    for t in range(9):
        cols = pl.ds(256 * t, 256)
        qkv_ref[:, cols] = mm_tn(a, dqkv[:, cols]).astype(BF16)
    copies = []
    for target, half in ((send, 1 - index[2]), (keep, index[2])):
        for f in range(SHARDS):
            rows = pl.ds(pl.multiple_of(f * 192 + half * 96, 16), 96)
            for src_ref, dst_ref in (
                (qkv_ref.at[rows], target.at[f, :, pl.ds(0, WIDE)]),
                (gain_ref.at[f], target.at[f, :, pl.ds(WIDE, 128)]),
            ):
                copy = pltpu.make_async_copy(src_ref, dst_ref, sems.at[1 + len(copies)])
                copy.start()
                copies.append(copy)
    dh = dh2[...] + norm_back(da, gains[0:1], normed, inv_scale)
    for m in range(MICRO):
        out_ref[m] = dh[m * ROWS : (m + 1) * ROWS].astype(BF16)
    for copy in copies:
        copy.wait()


def weight_grad_kernel(index, m_ref, grad_ref, b_ref, du, o_ref, gb_ref, keep, send,
                       down_ref, lift_ref, proj_ref, pad_ref, sems):
    core = index[2]
    copies = []

    def go(src, dst):
        copy = pltpu.make_async_copy(src, dst, sems.at[len(copies)])
        copy.start()
        copies.append(copy)

    sides = ((send, 1 - core), (keep, core))
    rows = lambda at, size: pl.ds(pl.multiple_of(at, 16), size)
    pad_ref[...] = jnp.zeros_like(pad_ref)
    for target, _ in sides:
        for f in range(SHARDS):
            go(pad_ref, target.at[f, pl.ds(176, 16)])
    for t in range(9):
        cols = pl.ds(256 * t, 256)
        lift_ref[:, cols] = mm_tn(b_ref[...], du[:, cols]).astype(BF16)
    for target, half in sides:
        for f in range(SHARDS):
            go(lift_ref.at[rows(f * 192 + half * 96, 96)], target.at[f, pl.ds(0, 96)])
    for t in range(3):
        cols = pl.ds(256 * t, 256)
        down_ref[:, cols] = mm_tn(m_ref[...], grad_ref[:, cols]).astype(BF16)
        proj_ref[:, cols] = mm_tn(o_ref[...], gb_ref[:, cols]).astype(BF16)
    for target, half in sides:
        for f in range(SHARDS):
            for b in range(3):
                cols = pl.ds(b * D, D)
                go(proj_ref.at[rows(f * 192 + b * 64 + half * 32, 32)], target.at[f, pl.ds(96, 32), cols])
                go(down_ref.at[rows(f * 288 + b * 96 + half * 48, 48)], target.at[f, pl.ds(128, 48), cols])
    for copy in copies:
        copy.wait()


def add_up(parts):
    total = parts[0].astype(F32)
    for part in parts[1:]:
        total = total + part.astype(F32)
    return total.astype(BF16)


def rest_core_kernel(index, keep, other, *outs):
    for d, out in enumerate(outs):
        rows = pl.ds(pl.multiple_of(lax.rem(index[0] + d, 4) * 48, 16), 48)
        for f in range(SHARDS):
            out[f] = add_up([keep[f, rows, :], other[f, rows, :]])


def rest_z_kernel(index, own, a, b, c, *outs):
    for d, out in enumerate(outs):
        f = lax.rem(index[1] + d, 4)
        out[...] = add_up([own[f], a[f], b[f], c[f]])


def qkv_core_kernel(index, keep, other, *outs):
    for d, out in enumerate(outs):
        f = lax.rem(index[1] + d, 4)
        out[...] = add_up([keep[f], other[f]])


def partial_kernel(a, b, out):
    out[...] = a[...].astype(F32) + b[...].astype(F32)


def qkv_y_kernel(index, some, b, c, out_0, out_1, out_2, out_3, total):
    total[...] = add_up([some[...], b[...], c[...]])
    for d, out in enumerate((out_0, out_1, out_2, out_3)):
        z = lax.rem(index[0] + d, 4)
        rows = pl.ds(pl.multiple_of(lax.div(z, 2) * 48, 16), 48)
        cols = pl.ds(pl.multiple_of(lax.rem(z, 2) * 1152, 128), 1152)
        out[:, pl.ds(0, 1152)] = total[rows, cols]
        out[:, pl.ds(1152, 128)] = total[pl.ds(0, 48), pl.ds(WIDE, 128)]


def joint_kernel(r0, r1, r2, r3, q0, q1, q2, q3, out):
    out[:, pl.ds(0, WIDE)] = add_up([r0[...], r1[...], r2[...], r3[...]])
    out[:, pl.ds(WIDE, 1280)] = add_up([q0[...], q1[...], q2[...], q3[...]])


def pair_kernel(a, b, out):
    out[...] = add_up([a[...], b[...]])


def final_kernel(index, *refs):
    pieces, (qkv_out, proj_out, lift_out, down_out, gain_out, rest) = refs[:8], refs[8:]
    core = index[2]
    for side in range(2):
        half = core if side == 0 else 1 - core
        for d in range(4):
            piece = pieces[4 * side + d]
            z = lax.rem(index[0] - d + 4, 4)
            rest[side, pl.ds(pl.multiple_of(z * 48, 16), 48), :] = piece[:, pl.ds(0, WIDE)]
            qkv_out[
                pl.ds(pl.multiple_of(half * 96 + lax.div(z, 2) * 48, 16), 48),
                pl.ds(pl.multiple_of(lax.rem(z, 2) * 1152, 128), 1152),
            ] = piece[:, pl.ds(WIDE, 1152)].astype(F32)
        rows = lambda at, size: pl.ds(pl.multiple_of(at, 16), size)
        lift_out[rows(half * 96, 96), :] = rest[side, pl.ds(0, 96), :].astype(F32)
        for b in range(3):
            cols = pl.ds(b * D, D)
            proj_out[rows(b * 64 + half * 32, 32), :] = rest[side, pl.ds(96, 32), cols].astype(F32)
            down_out[rows(b * 96 + half * 48, 48), :] = rest[side, pl.ds(128, 48), cols].astype(F32)
    gain_out[...] = pieces[0][pl.ds(0, 16), pl.ds(WIDE + 1152, 128)].astype(F32)


def call(kernel, name, ins, outs, scratch, flops, limit=24):
    places = {"v": pltpu.VMEM, "a": pl.ANY, "s": pltpu.SMEM}
    return pl.pallas_call(
        kernel,
        name=name,
        out_shape=[jax.ShapeDtypeStruct(out[0], out[1]) for out in outs],
        in_specs=[pl.BlockSpec(memory_space=places[place]) for _, place in ins],
        out_specs=[pl.BlockSpec(memory_space=places[out[2] if len(out) > 2 else "v"]) for out in outs],
        scratch_shapes=scratch,
        compiler_params=pltpu.CompilerParams(vmem_limit_bytes=limit * 2**20),
        cost_estimate=pl.CostEstimate(flops=flops, bytes_accessed=flops // 300, transcendentals=0),
    )(*[array for array, _ in ins])


def travel(block, target):
    pairs = []
    for ctx in range(16):
        for f in range(SHARDS):
            xlo, z, core, g = target(ctx // 8, ctx // 2 % 4, ctx % 2, f)
            pairs.append((ctx * SHARDS + f, (xlo * 8 + z % 4 * 2 + core) * SHARDS + g % 4))
    return lax.ppermute(block, ("ctx", "fsdp"), pairs)


def along_y(block, d):
    return travel(block, lambda x, z, c, f: (x, z, c, f + d))


def along_z(block, d):
    return travel(block, lambda x, z, c, f: (x, z + d, c, f))


def next_shard(block):
    return travel(block, lambda x, z, c, f: (x, z, c, f + 1 - 2 * c))


def swap_core(block):
    return travel(block, lambda x, z, c, f: (x, z, 1 - c, f))


def spread_quarter(block, across):
    return block, across, swap_core(block), swap_core(across)


def swap_x(block):
    return travel(block, lambda x, z, c, f: (1 - x, z, c, f))


def halo_rows(block, axis):
    count = lax.axis_size(axis)
    up = [(i, i + 1) for i in range(count - 1)]
    down = [(i + 1, i) for i in range(count - 1)]
    return (
        lax.ppermute(block[:, ROWS - HALF :], axis, up),
        lax.ppermute(block[:, :HALF], axis, down),
    )


def swap_halos(to_low, to_high):
    count = lax.axis_size("ctx")
    up = [(i, i + 1) for i in range(count - 1)]
    down = [(i + 1, i) for i in range(count - 1)]
    return lax.ppermute(to_high, "ctx", up), lax.ppermute(to_low, "ctx", down)


def tables(first_row, lengths):
    half = HD // 2
    frequencies = rope_base ** (-(jnp.arange(half, dtype=F32) * 2.0) / HD)
    positions = first_row - HALF + jnp.arange(EXT, dtype=jnp.int32)
    angles = positions.astype(F32)[:, None] * frequencies[None, :]
    cosine, sine = jnp.cos(angles), jnp.sin(angles)
    cosine = jnp.concatenate([cosine] * 4, axis=1)
    sine = jnp.concatenate([-sine, sine, -sine, sine], axis=1)
    ends = jnp.cumsum(lengths, axis=1)
    doc = jnp.sum((positions[None, :, None] >= ends[:, None, :]).astype(jnp.int32), axis=2)
    query = positions[HALF : HALF + ROWS]
    allowed = (
        (jnp.abs(query[None, :] - positions[:, None]) <= HALF)
        & (positions >= 0)[:, None]
        & (positions < SEQ_LEN)[:, None]
    )[None] & (doc[:, :, None] == doc[:, None, HALF : HALF + ROWS])
    bias = jnp.where(allowed, 0.0, masked_score).astype(F32)
    return cosine, sine, jnp.concatenate([bias, bias], axis=2)


WQKV, WPROJ, WLIFT, WDOWN = [
    pltpu.VMEM((D, WIDE), BF16),
    pltpu.VMEM((D, D), BF16),
    pltpu.VMEM((D, WIDE), BF16),
    pltpu.VMEM((FF, D), BF16),
]
SAVED = [
    ((OWN, D), BF16),
    ((MICRO * EXT, D), BF16),
    ((MICRO * EXT, D), BF16),
    ((MICRO, TILES, EXT, 2 * ROWS), BF16),
    ((OWN, D), BF16),
    ((OWN, D), F32),
    ((OWN, FF), BF16),
    ((OWN, FF), F32),
    ((OWN, FF), F32),
]
STREAM = [pltpu.VMEM((MICRO * EXT, D), BF16)] * 2
GRADS_OUT = [
    ((OWN, D), F32),
    ((OWN, D), BF16),
    ((OWN, 2 * D), F32),
    ((MICRO, HALF, 2 * D), BF16),
    ((MICRO, HALF, 2 * D), BF16),
]


TURN_OUT = [((MICRO, ROWS, D), BF16)] + SAVED + [((OWN, D), BF16)]
BACK_OUT = [((OWN, D), BF16), ((OWN, WIDE), BF16), ((OWN, D), BF16), ((OWN, D), BF16)]


def sems(count):
    return pltpu.SemaphoreType.DMA((count,))


def body(
    inputs, out_grad, doc_lengths, attn_gain, qkv_weight, proj_weight, mlp_gain, lift_weight, down_weight
):
    on_first = lax.axis_index("section") == 0
    flag = on_first.astype(jnp.int32).reshape(1)
    ctx, f = lax.axis_index("ctx"), lax.axis_index("fsdp")
    index = jnp.stack([ctx // 2 % 4, f, ctx % 2, ctx // 8]).astype(jnp.int32)
    qkv_shard, lift_shard, proj_shard, down_shard = qkv_weight[0], lift_weight[0], proj_weight[0], down_weight[0]
    own, cotangent = inputs[:, 0], out_grad[:, 0]
    gain_tile = jnp.pad(
        jnp.pad(jnp.stack([attn_gain[0], mlp_gain[0]]), ((0, 0), (0, 64))).reshape(4, 128), ((0, 12), (0, 0))
    )
    edge = ((MICRO, HALF, D), BF16)
    qkv_pack, qkv_quarter, first_rows, last_rows = call(
        pack_qkv_kernel, "pack_qkv",
        [(index, "s"), (qkv_shard, "v"), (gain_tile, "v"), (own, "v")],
        [((192, 2432), BF16), ((96, 1280), BF16), edge, edge],
        [], 0, 12,
    )
    rest, rest_quarter = call(
        pack_kernel, "pack_rest",
        [(index, "s"), (lift_shard, "v"), (proj_shard, "v"), (down_shard, "v")],
        [((352, WIDE), BF16), ((176, 1152), BF16)],
        [pltpu.VMEM((176, WIDE), BF16)], 0, 12,
    )
    first = next_shard(qkv_pack)
    second = along_y(qkv_quarter, 2)
    rest_second = along_y(rest_quarter, 2)
    cosine, sine, bias = tables(ctx * ROWS, doc_lengths[:, 0])
    first_rows, last_rows, cosine = lax.optimization_barrier((first_rows, last_rows, cosine))
    low, high = swap_halos(first_rows, last_rows)
    first, second, rest_second, rest, cosine, sine, bias, low, high = lax.optimization_barrier(
        (first, second, rest_second, rest, cosine, sine, bias, low, high)
    )
    rest_first = next_shard(rest)
    second_x, rest_x = lax.optimization_barrier((swap_x(second), swap_x(rest_second)))
    qkv_pieces = first, swap_core(first), *spread_quarter(second, second_x)
    stream = ((MICRO, ROWS, D), BF16)
    scratch = lambda items: [pltpu.VMEM(s, k) for s, k in items]

    o, gains, wqkv = call(
        forward_attention_kernel, "forward_attention",
        [(index, "s"), (own, "v"), (low, "v"), (high, "v"), (gain_tile, "a"), (cosine, "v"), (sine, "v"), (bias, "v"),
         (qkv_shard, "a"), *[(piece, "a") for piece in qkv_pieces]],
        [((OWN, D), BF16), ((2, D), F32), ((D, WIDE), BF16, "a")],
        [WQKV, pltpu.VMEM((SHARDS, 16, 128), BF16)] + STREAM + scratch(SAVED[:4]) + [sems(11), pltpu.SemaphoreType.DMA(())],
        1_400_000_000,
    )
    rest_first, rest_second, rest_x, o = lax.optimization_barrier((rest_first, rest_second, rest_x, o))
    rest_pieces = rest_first, swap_core(rest_first), *spread_quarter(rest_second, rest_x)
    rest_parts = [(part, "a") for part in (lift_shard, proj_shard, down_shard, *rest_pieces)]
    (relay,) = call(
        forward_mlp_kernel, "forward_mlp",
        [(index, "s"), (own, "v"), (o, "v"), (gains, "v"), *rest_parts],
        [stream],
        [WPROJ, WLIFT, WDOWN] + scratch([SAVED[5], SAVED[0], SAVED[6]]) + [sems(45)],
        1_800_000_000,
    )
    wlift, wproj, wdown = call(
        assemble_kernel, "assemble_weights",
        [(index, "s"), *rest_parts, (relay, "a")],
        [((D, WIDE), BF16, "a"), ((D, D), BF16, "a"), ((FF, D), BF16, "a")],
        [WLIFT, WPROJ, WDOWN, sems(48)], 1_800_000_000, 56,
    )
    relayed = lax.ppermute(relay, "section", [(0, 1)])
    relayed, wlift, wproj, wdown = lax.optimization_barrier((relayed, wlift, wproj, wdown))
    other_low, other_high = halo_rows(relayed, "ctx")
    (h3, q, k, v, p, o, h2, m_act, left, right, src, dh2, dq, dkv, to_low, to_high) = call(
        turning_kernel, "layer_turn",
        [(flag, "s"), (own, "v"), (low, "v"), (high, "v"), (relayed, "v"), (other_low, "v"), (other_high, "v"),
         (cotangent, "v"), (gains, "v"), (cosine, "v"), (sine, "v"), (bias, "v"),
         (wqkv, "a"), (wproj, "a"), (wlift, "a"), (wdown, "a")],
        [(*item, "a") for item in TURN_OUT] + GRADS_OUT,
        [WQKV, WPROJ, WLIFT, WDOWN] + STREAM
        + [pltpu.VMEM((MICRO, ROWS, D), BF16), pltpu.VMEM((OWN, WIDE), BF16), pltpu.VMEM((OWN, D), BF16)] + scratch(TURN_OUT) + [sems(15)],
        6_000_000_000, 36,
    )
    from_low, from_high = swap_halos(to_low, to_high)
    (grad_relay,) = call(
        source_kernel, "layer_source",
        [(src, "v"), (gains, "v"), (dh2, "v"), (dq, "v"), (dkv, "v"), (from_low, "v"), (from_high, "v"), (wqkv, "a")],
        [stream],
        [WQKV, pltpu.VMEM((OWN, WIDE), BF16), sems(1)],
        900_000_000,
    )
    incoming = lax.ppermute(grad_relay, "section", [(1, 0)])
    (grad_low, du, gb, b, mlp_gain_grad, dh2, dq, dkv, to_low, to_high) = call(
        back_kernel, "layer_back",
        [(flag, "s"), (incoming, "v"), (cotangent, "v"), (gains, "v"), (cosine, "v"), (sine, "v"),
         (wproj, "a"), (wlift, "a"), (wdown, "a"),
         *[(array, "a") for array in (q, k, v, p, h2, left, right)]],
        [(*item, "a") for item in BACK_OUT] + [((1, D), F32)] + GRADS_OUT,
        [WPROJ, WLIFT, WDOWN, pltpu.VMEM((OWN, D), BF16)]
        + scratch(SAVED[:4] + SAVED[5:6] + SAVED[7:] + BACK_OUT) + [sems(14)],
        3_000_000_000, 30,
    )
    from_low, from_high = swap_halos(to_low, to_high)
    rest_keep, rest_send = call(
        weight_grad_kernel, "weight_grads",
        [(index, "s"), (m_act, "v"), (grad_low, "v"), (b, "v"), (du, "v"), (o, "v"), (gb, "v")],
        [((SHARDS, 192, WIDE), BF16, "a")] * 2,
        [WDOWN, WLIFT, WPROJ, pltpu.VMEM((16, WIDE), BF16), sems(64)],
        1_600_000_000,
    )
    from_low, from_high, rest_send = lax.optimization_barrier((from_low, from_high, rest_send))
    rest_other = swap_core(rest_send)
    in_grad, qkv_keep, qkv_send = call(
        source_grad_kernel, "layer_source_grads",
        [(index, "s"), (src, "v"), (gains, "v"), (dh2, "v"), (dq, "v"), (dkv, "v"), (from_low, "v"),
         (from_high, "v"), (mlp_gain_grad, "v"), (wqkv, "a")],
        [stream, ((SHARDS, 96, 2432), BF16, "a"), ((SHARDS, 96, 2432), BF16, "a")],
        [WQKV, pltpu.VMEM((OWN, WIDE), BF16), WQKV, pltpu.VMEM((SHARDS, 96, 128), BF16), sems(17)],
        1_800_000_000,
    )
    qkv_other = swap_core(qkv_send)

    rest_z = call(
        rest_core_kernel, "rest_core_sum", [(index, "s"), (rest_keep, "v"), (rest_other, "v")],
        [((SHARDS, 48, WIDE), BF16)] * 4, [], 0, 24,
    )
    qkv_keep, _ = lax.optimization_barrier((qkv_keep, rest_z[0]))
    qkv_y = call(
        qkv_core_kernel, "qkv_core_sum", [(index, "s"), (qkv_keep, "v"), (qkv_other, "v")],
        [((96, 2432), BF16)] * 4, [], 0, 24,
    )
    (some,) = call(
        partial_kernel, "qkv_y_first", [(qkv_y[0], "v"), (along_y(qkv_y[1], 1), "v")],
        [((96, 2432), F32)], [], 0, 24,
    )
    rest_mine, some = lax.optimization_barrier((rest_z[0], some))
    rest_y = call(
        rest_z_kernel, "rest_z_sum",
        [(index, "s"), (rest_mine, "v"), *[(along_z(rest_z[d], d), "v") for d in (1, 2, 3)]],
        [((48, WIDE), BF16)] * 4, [], 0, 24,
    )
    some, _ = lax.optimization_barrier((some, rest_y[0]))
    qkv_z = call(
        qkv_y_kernel, "qkv_y_sum",
        [(index, "s"), (some, "v"), *[(along_y(qkv_y[d], d), "v") for d in (2, 3)]],
        [((48, 1280), BF16)] * 4, [pltpu.VMEM((96, 2432), BF16)], 0, 24,
    )
    (joint,) = call(
        joint_kernel, "joint_sum",
        [(rest_y[0], "v"), *[(along_y(rest_y[d], d), "v") for d in (1, 2, 3)],
         (qkv_z[0], "v"), *[(along_z(qkv_z[d], d), "v") for d in (1, 2, 3)]],
        [((48, 3584), BF16)], [], 0, 24,
    )
    (joint,) = call(
        pair_kernel, "pair_sum", [(joint, "v"), (swap_x(joint), "v")], [((48, 3584), BF16)], [], 0, 24
    )
    mine = [joint] + [along_z(joint, d) for d in (1, 2, 3)]
    theirs = [swap_core(piece) for piece in mine]
    qkv_sum, proj_sum, lift_sum, down_sum, gain_sums = call(
        final_kernel, "final_shard", [(index, "s"), *[(piece, "v") for piece in mine + theirs]],
        [((192, WIDE), F32), ((192, D), F32), ((192, WIDE), F32), ((288, D), F32), ((16, 128), F32)],
        [pltpu.VMEM((2, 192, WIDE), BF16)], 0, 24,
    )
    return (
        h3[None, :, None],
        in_grad[None, :, None],
        gain_sums[0:2].reshape(1, 256)[:, :192],
        qkv_sum[None],
        proj_sum[None],
        gain_sums[2:4].reshape(1, 256)[:, :192],
        lift_sum[None],
        down_sum[None],
    )


def solution(mesh):
    placed = (
        P(None, "fsdp", "ctx", None),
        P(None, "fsdp", "ctx", None),
        P(None, "fsdp", None),
        P("section", "fsdp"),
        P("section", "fsdp", None),
        P("section", "fsdp", None),
        P("section", "fsdp"),
        P("section", "fsdp", None),
        P("section", "fsdp", None),
    )
    return jax.shard_map(
        body,
        mesh=mesh,
        in_specs=placed,
        out_specs=(
            P("section", None, "fsdp", "ctx", None),
            P("section", None, "fsdp", "ctx", None),
            P("section", "fsdp"),
            P("section", "fsdp", None),
            P("section", "fsdp", None),
            P("section", "fsdp"),
            P("section", "fsdp", None),
            P("section", "fsdp", None),
        ),
        check_vma=False,
    )
```

```python
import functools

import jax
import jax.numpy as jnp
from jax import lax
from jax.experimental import pallas as pl
from jax.experimental.pallas import tpu as pltpu
from jax.sharding import PartitionSpec as P

D = 768
HD = 64
HALF = 64
SEQ_LEN = 2048
FF = 1152
WIDE = 2304
ROWS = 128
EXT = ROWS + 2 * HALF
MICRO = 2
OWN = MICRO * ROWS
SHARDS = 4
TILES = D // 128
norm_eps = 1e-05
rope_base = 10000.0
masked_score = -1e30
root_half = 0.7071067811865476
inv_root_tau = 0.3989422804014327
F32 = jnp.float32
BF16 = jnp.bfloat16


def mm(left, right):
    return lax.dot_general(left, right, (((1,), (0,)), ((), ())), preferred_element_type=F32)


def mm_nt(left, right):
    return lax.dot_general(left, right, (((1,), (1,)), ((), ())), preferred_element_type=F32)


def mm_tn(left, right):
    return lax.dot_general(left, right, (((0,), (0,)), ((), ())), preferred_element_type=F32)


def norm_parts(hidden):
    centre = hidden - jnp.mean(hidden, axis=-1, keepdims=True)
    inv_scale = lax.rsqrt(jnp.mean(centre * centre, axis=-1, keepdims=True) + norm_eps)
    return centre * inv_scale, inv_scale


def norm_back(grad_out, gain, normed, inv_scale):
    grad_normed = grad_out * gain
    inner = (
        grad_normed
        - jnp.mean(grad_normed, axis=-1, keepdims=True)
        - normed * jnp.mean(grad_normed * normed, axis=-1, keepdims=True)
    )
    return inner * inv_scale


def lane_is_low(shape, period):
    return lax.broadcasted_iota(jnp.int32, shape, 1) % period < period // 2


def turn(x):
    return jnp.where(lane_is_low(x.shape, HD), pltpu.roll(x, 96, 1), pltpu.roll(x, 32, 1))


def rotate(x, cosine, sine):
    return x * cosine + turn(x) * sine


def rotate_back(x, cosine, sine):
    return x * cosine - turn(x) * sine


def stack_heads(x):
    low = lane_is_low(x.shape, 128)
    zero = jnp.zeros_like(x)
    return jnp.concatenate([jnp.where(low, x, zero), jnp.where(low, zero, x)], axis=0)


def join_heads(x):
    half = x.shape[0] // 2
    low = lane_is_low((half, 128), 128)
    return jnp.where(low, x[:half], x[half:])


def start_weights(sources, buffers, sems):
    waits = {}
    for index, (name, source) in enumerate(sources.items()):
        copy = pltpu.make_async_copy(source, buffers[name], sems.at[index])
        copy.start()
        waits[name] = [copy]
    return waits


def finish(waits, name):
    for copy in waits[name]:
        copy.wait()


def load_stream(flag, own, low, high, other, ext):
    for m in range(MICRO):
        for ref, alt, start, size in (
            (low, other[1], 0, HALF),
            (own, other[0], HALF, ROWS),
            (high, other[2], HALF + ROWS, HALF),
        ):
            value = ref[m]
            if alt is not None:
                value = jnp.where(flag, value, alt[m])
            ext[pl.ds(m * EXT + start, size), :] = value


def own_rows(x):
    return jnp.concatenate([x[HALF : HALF + ROWS], x[EXT + HALF : EXT + HALF + ROWS]], axis=0)


def repeat(count, step):
    lax.fori_loop(0, count, lambda i, carry: (step(i), carry)[1], 0)


def each(count, step):
    for i in range(count):
        step(i)


def span(start, size, unit=128):
    return pl.ds(start if isinstance(start, int) else pl.multiple_of(start, unit), size)


def by_tiles(unit, group):
    def step(i):
        for j in range(group):
            unit(i * group + j)

    repeat(TILES // group, step)


def norm_rows(source, gain, target):
    def step(i):
        rows = span(i * 128, 128)
        normed, _ = norm_parts(source[rows, :].astype(F32))
        target[rows, :] = (normed * gain).astype(BF16)

    repeat(source.shape[0] // 128, step)


def forward_attention(ext, gain, wqkv, cos_ref, sin_ref, bias_ref, a_ext, q_ref, k_ref, v_ref, p_ref, o_ref):
    norm_rows(ext, gain, a_ext)
    a_own = o_ref
    a_own[...] = own_rows(a_ext[...])
    own_span = pl.ds(HALF, ROWS)

    def project(t):
        cols = span(256 * t, 256)
        queries = mm(a_own[...], wqkv[:, cols])
        keys = mm(a_ext[...], wqkv[:, span(D + 256 * t, 256)])
        v_ref[:, cols] = mm(a_ext[...], wqkv[:, span(2 * D + 256 * t, 256)]).astype(BF16)
        for s in range(2):
            tile, lanes = span(256 * t + 128 * s, 128), slice(128 * s, 128 * s + 128)
            for m in range(MICRO):
                part = queries[m * ROWS : (m + 1) * ROWS, lanes]
                turned = rotate(part, cos_ref[own_span, :], sin_ref[own_span, :]).astype(BF16)
                q_ref[pl.ds(m * ROWS, ROWS), tile] = turned * jnp.asarray(0.125, BF16)
                part = keys[m * EXT : (m + 1) * EXT, lanes]
                k_ref[pl.ds(m * EXT, EXT), tile] = rotate(part, cos_ref[...], sin_ref[...]).astype(BF16)

    repeat(3, project)

    def unit(t):
        cols = pl.ds(pl.multiple_of(t * 128, 128), 128)
        for m in range(MICRO):
            q2 = stack_heads(q_ref[pl.ds(m * ROWS, ROWS), cols])
            scores = mm_nt(k_ref[pl.ds(m * EXT, EXT), cols], q2) + bias_ref[m]
            terms = jnp.exp(scores - jnp.max(scores, axis=0, keepdims=True))
            probs = (terms * (1.0 / jnp.sum(terms, axis=0, keepdims=True))).astype(BF16)
            p_ref[m, t] = probs
            attended = mm_tn(probs, v_ref[pl.ds(m * EXT, EXT), cols])
            o_ref[pl.ds(m * ROWS, ROWS), cols] = join_heads(attended).astype(BF16)

    by_tiles(unit, 3)


def forward_mlp(own, o_ref, wproj, mlp_gain, wlift, wdown, h2_ref, b_ref, m_ref, left_ref, right_ref, h3_ref, waits):
    finish(waits, "proj")

    def mix(t):
        cols = span(256 * t, 256)
        added = mm(o_ref[...], wproj[:, cols])
        for m in range(MICRO):
            rows = pl.ds(m * ROWS, ROWS)
            h2_ref[rows, cols] = own[m, :, cols].astype(F32) + added[m * ROWS : (m + 1) * ROWS]

    each(3, mix)
    norm_rows(h2_ref, mlp_gain, b_ref)
    finish(waits, "lift")

    def lift(t):
        cols = span(384 * t, 384)
        gate = mm(b_ref[...], wlift[:, cols])
        up = mm(b_ref[...], wlift[:, span(FF + 384 * t, 384)])
        cdf = 0.5 * (1.0 + lax.erf(gate * root_half))
        gelu = gate * cdf
        m_ref[:, cols] = (gelu * up).astype(BF16)
        if left_ref is not None:
            pdf = jnp.exp(-0.5 * gate * gate) * inv_root_tau
            left_ref[:, cols] = up * (cdf + gate * pdf)
            right_ref[:, cols] = gelu

    repeat(3, lift)
    finish(waits, "down")

    def down(t):
        cols = span(256 * t, 256)
        h3 = (h2_ref[:, cols] + mm(m_ref[...], wdown[:, cols])).astype(BF16)
        for m in range(MICRO):
            h3_ref[m, :, cols] = h3[m * ROWS : (m + 1) * ROWS]

    each(3, down)


def backward_mlp(grad_ref, h2_ref, mlp_gain, wproj, wlift, wdown, left_ref, right_ref, du_ref, gb_ref, do_ref,
                 dh2_ref, b_ref, mlp_ref):
    def lift(t):
        cols = span(384 * t, 384)
        dm = mm_nt(grad_ref[...], wdown[cols, :])
        du_ref[:, cols] = (dm * left_ref[:, cols]).astype(BF16)
        du_ref[:, span(FF + 384 * t, 384)] = (dm * right_ref[:, cols]).astype(BF16)

    each(3, lift)

    def source(t):
        rows = span(256 * t, 256)
        dh2_ref[:, rows] = mm_nt(du_ref[...], wlift[rows, :])

    each(3, source)
    if mlp_ref is not None:
        mlp_ref[...] = jnp.zeros_like(mlp_ref)

    def norm(i):
        rows = span(i * 128, 128)
        db = dh2_ref[rows, :]
        normed, inv_scale = norm_parts(h2_ref[rows, :])
        dh2 = grad_ref[rows, :].astype(F32) + norm_back(db, mlp_gain, normed, inv_scale)
        dh2_ref[rows, :] = dh2
        gb_ref[rows, :] = dh2.astype(BF16)
        if mlp_ref is not None:
            mlp_ref[...] += jnp.sum(db * normed, axis=0, keepdims=True)
            b_ref[rows, :] = (normed * mlp_gain).astype(BF16)

    repeat(2, norm)

    def attended(t):
        rows = span(256 * t, 256)
        do_ref[:, rows] = mm_nt(gb_ref[...], wproj[rows, :]).astype(BF16)

    each(3, attended)


def backward_attention(q_ref, k_ref, v_ref, p_ref, do_ref, cos_ref, sin_ref, dq_ref, dkv_ref, low_ref, high_ref, group):
    cosine, sine = cos_ref[...], sin_ref[...]
    cos_own, sin_own = cosine[HALF : HALF + ROWS], sine[HALF : HALF + ROWS]

    def unit(t):
        cols = pl.ds(pl.multiple_of(t * 128, 128), 128)
        value_cols = pl.ds(pl.multiple_of(D + t * 128, 128), 128)
        for m in range(MICRO):
            rows = pl.ds(m * ROWS, ROWS)
            q2 = stack_heads(q_ref[rows, cols])
            do2 = stack_heads(do_ref[rows, cols])
            probs = p_ref[m, t]
            dprobs = mm_nt(v_ref[pl.ds(m * EXT, EXT), cols], do2)
            wide = probs.astype(F32)
            inner = jnp.sum(wide * dprobs, axis=0, keepdims=True)
            ds = (wide * (dprobs - inner)).astype(BF16)
            dq = join_heads(mm_tn(ds, k_ref[pl.ds(m * EXT, EXT), cols])) * 0.125
            dq_ref[rows, cols] = rotate_back(dq, cos_own, sin_own).astype(BF16)
            dk = rotate_back(mm(ds, q2), cosine, sine)
            dv = mm(probs, do2)
            for grad, where in ((dk, cols), (dv, value_cols)):
                low_ref[m, :, where] = grad[:HALF].astype(BF16)
                dkv_ref[rows, where] = grad[HALF : HALF + ROWS]
                high_ref[m, :, where] = grad[HALF + ROWS :].astype(BF16)

    by_tiles(unit, group)


def place_shards(index, own, pieces, put):
    f, core, xlo = index[1], index[2], index[3]
    first, first_other, second, second_x, second_core, second_both = pieces
    put(own, f, None, None)
    put(first, lax.rem(f + 3 + 2 * core, 4), None, None)
    put(first_other, lax.rem(f + 1 + 2 * core, 4), None, None)
    across = lax.rem(f + 2, 4)
    put(second, across, core, xlo)
    put(second_x, across, core, 1 - xlo)
    put(second_core, across, 1 - core, xlo)
    put(second_both, across, 1 - core, 1 - xlo)


def pack_qkv_kernel(index, qkv, gains, own, whole, half, first_rows, last_rows):
    rows = pl.ds(pl.multiple_of(index[2] * 96, 16), 96)
    whole[:, pl.ds(0, WIDE)] = qkv[...]
    half[:, pl.ds(0, WIDE)] = qkv[rows, :]
    whole[:, pl.ds(WIDE, 128)] = jnp.zeros((192, 128), BF16)
    half[:, pl.ds(WIDE, 128)] = jnp.zeros((96, 128), BF16)
    whole[pl.ds(0, 16), pl.ds(WIDE, 128)] = gains[...]
    half[pl.ds(0, 16), pl.ds(WIDE, 128)] = gains[...]
    first_rows[...] = own[:, :HALF]
    last_rows[...] = own[:, ROWS - HALF :]


def pack_kernel(index, lift, proj, down, rest, quarter, half):
    core = index[2]
    rows = lambda at, size: pl.ds(pl.multiple_of(at, 16), size)
    rest[pl.ds(0, 192), :] = lift[...]
    half[pl.ds(0, 96), :] = lift[rows(core * 96, 96), :]
    for b in range(3):
        cols = pl.ds(b * D, D)
        rest[pl.ds(192, 64), cols] = proj[pl.ds(64 * b, 64), :]
        rest[pl.ds(256, 96), cols] = down[pl.ds(96 * b, 96), :]
        half[pl.ds(96, 32), cols] = proj[rows(64 * b + core * 32, 32), :]
        half[pl.ds(128, 48), cols] = down[rows(96 * b + core * 48, 48), :]
    quarter[...] = half[:, pl.ds(pl.multiple_of(index[3] * 1152, 128), 1152)]


def gather_gain(tiles, row):
    parts = []
    for tile in tiles:
        parts += [tile[row : row + 1, :], tile[row + 1 : row + 2, :64]]
    return jnp.concatenate(parts, axis=1)


def forward_attention_kernel(index, own, low, high, gain_tile, cos_ref, sin_ref, bias_ref,
                             shard, first, first_other, second, second_core,
                             o, gains, whole, wqkv, tiles, ext, a_ext, q, k, v, p, sems, out_sem):
    copies = []

    def go(src, dst):
        copy = pltpu.make_async_copy(src, dst, sems.at[len(copies)])
        copy.start()
        copies.append(copy)

    def put(piece, f, half, side):
        if piece is None:
            return
        at, size = (f * 192, 192) if half is None else (f * 192 + half * 96, 96)
        rows = pl.ds(pl.multiple_of(at, 16), size)
        go(piece if piece is shard else piece.at[:, pl.ds(0, WIDE)], wqkv.at[rows])
        if piece is not shard and piece is not second_core:
            go(piece.at[pl.ds(0, 16), pl.ds(WIDE, 128)], tiles.at[f])

    place_shards(index, shard, (first, first_other, second, None, second_core, None), put)
    go(gain_tile, tiles.at[index[1]])
    load_stream(None, own, low, high, (None, None, None), ext)
    for copy in copies:
        copy.wait()
    out = pltpu.make_async_copy(wqkv, whole, out_sem)
    out.start()
    shards = [tiles[f].astype(F32) for f in range(SHARDS)]
    gains[0:1, :] = gather_gain(shards, 0)
    gains[1:2, :] = gather_gain(shards, 2)
    forward_attention(ext, gains[0:1], wqkv, cos_ref, sin_ref, bias_ref, a_ext, q, k, v, p, o)
    out.wait()


def place_rest(index, lift, proj, down, pieces, wlift, wproj, wdown, go):
    f = index[1]
    rows = lambda at, size: pl.ds(pl.multiple_of(at, 16), size)
    lanes = lambda at, size: pl.ds(pl.multiple_of(at, 128), size)

    def put(piece, s, half, side):
        if piece is None:
            go("proj", proj, wproj.at[rows(f * 192, 192)])
            go("lift", lift, wlift.at[rows(f * 192, 192)])
            go("down", down, wdown.at[rows(f * 288, 288)])
        elif half is None:
            go("lift", piece.at[pl.ds(0, 192)], wlift.at[rows(s * 192, 192)])
            for b in range(3):
                cols = pl.ds(b * D, D)
                go("proj", piece.at[pl.ds(192, 64), cols], wproj.at[rows(s * 192 + b * 64, 64)])
                go("down", piece.at[pl.ds(256, 96), cols], wdown.at[rows(s * 288 + b * 96, 96)])
        else:
            go("lift", piece.at[pl.ds(0, 96)], wlift.at[rows(s * 192 + half * 96, 96), lanes(side * 1152, 1152)])
            for j in range(3):
                cols = pl.ds(j * 384, 384)
                b, right = lax.div(3 * side + j, 2), lanes(lax.rem(3 * side + j, 2) * 384, 384)
                go("proj", piece.at[pl.ds(96, 32), cols], wproj.at[rows(s * 192 + b * 64 + half * 32, 32), right])
                go("down", piece.at[pl.ds(128, 48), cols], wdown.at[rows(s * 288 + b * 96 + half * 48, 48), right])

    place_shards(index, None, pieces, put)


def starter(sems, waits):
    count = [0]

    def go(name, src, dst):
        copy = pltpu.make_async_copy(src, dst, sems.at[count[0]])
        copy.start()
        count[0] += 1
        waits.setdefault(name, []).append(copy)

    return go


def forward_mlp_kernel(index, own, o, gains, lift, proj, down, *refs):
    pieces, (h3_ref, wproj, wlift, wdown, h2, b, m_out, sems) = refs[:6], refs[6:]
    waits = {}
    place_rest(index, lift, proj, down, pieces, wlift, wproj, wdown, starter(sems, waits))
    forward_mlp(own, o, wproj, gains[1:2], wlift, wdown, h2, b, m_out, None, None, h3_ref, waits)


def assemble_kernel(index, lift, proj, down, *refs):
    pieces, (whole_lift, whole_proj, whole_down, wlift, wproj, wdown, sems) = refs[:6], refs[7:]
    waits = {}
    go = starter(sems, waits)
    place_rest(index, lift, proj, down, pieces, wlift, wproj, wdown, go)
    for name, buffer, whole in (("lift", wlift, whole_lift), ("proj", wproj, whole_proj), ("down", wdown, whole_down)):
        finish(waits, name)
        go("out", buffer, whole)
    finish(waits, "out")


def start_all(pairs, sems, first):
    copies = [pltpu.make_async_copy(src, dst, sems.at[first + n]) for n, (src, dst) in enumerate(pairs)]
    for copy in copies:
        copy.start()
    return copies


def turning_kernel(flag_ref, own, low, high, other_own, other_low, other_high, cotangent, gains,
                   cos_ref, sin_ref, bias_ref, qkv_hbm, proj_hbm, lift_hbm, down_hbm, *refs):
    kept, (dh2_ref, dq, dkv, to_low, to_high) = refs[:11], refs[11:16]
    wqkv, wproj, wlift, wdown, ext, a_ext, mine, du, do, h3_ref, q, k, v, p, o, h2, m_out, left, right, src, sems = refs[16:]
    waits = start_weights(
        {"qkv": qkv_hbm, "proj": proj_hbm, "lift": lift_hbm, "down": down_hbm},
        {"qkv": wqkv, "proj": wproj, "lift": wlift, "down": wdown}, sems,
    )
    flag = flag_ref[0] == 1
    load_stream(flag, own, low, high, (other_own, other_low, other_high), ext)
    for m in range(MICRO):
        mine[m] = ext[pl.ds(m * EXT + HALF, ROWS), :]
        src[pl.ds(m * ROWS, ROWS), :] = mine[m]
    finish(waits, "qkv")
    forward_attention(ext, gains[0:1], wqkv, cos_ref, sin_ref, bias_ref, a_ext, q, k, v, p, o)
    outs = start_all(zip((q, k, v, p, o, src), kept[1:6] + kept[10:]), sems, 4)
    spare = a_ext.at[pl.ds(0, OWN)]
    forward_mlp(mine, o, wproj, gains[1:2], wlift, wdown, h2, spare, m_out, left, right, h3_ref, waits)
    outs += start_all(zip((h3_ref, h2, m_out, left, right), kept[:1] + kept[6:10]), sems, 10)
    grad = a_ext.at[pl.ds(OWN, OWN)]
    for m in range(MICRO):
        grad[pl.ds(m * ROWS, ROWS), :] = cotangent[m]
    backward_mlp(grad, h2, gains[1:2], wproj, wlift, wdown, left, right, du, spare, do, dh2_ref, None, None)
    backward_attention(q, k, v, p, do, cos_ref, sin_ref, dq, dkv, to_low, to_high, 3)
    for copy in outs:
        copy.wait()


def back_kernel(flag_ref, incoming, cotangent, gains, cos_ref, sin_ref, proj_hbm, lift_hbm, down_hbm,
                q_hbm, k_hbm, v_hbm, p_hbm, h2_hbm, left_hbm, right_hbm, *refs):
    kept, (mlp_ref, dh2_ref, dq, dkv, to_low, to_high) = refs[:4], refs[4:10]
    wproj, wlift, wdown, do, q, k, v, p, h2, left, right, grad_ref, du, gb_ref, b_ref, sems = refs[10:]
    early = start_all(
        ((down_hbm, wdown), (left_hbm, left), (right_hbm, right), (lift_hbm, wlift), (h2_hbm, h2), (proj_hbm, wproj)),
        sems, 0,
    )
    late = start_all(((q_hbm, q), (v_hbm, v), (p_hbm, p), (k_hbm, k)), sems, 6)
    flag = flag_ref[0] == 1
    for m in range(MICRO):
        grad_ref[pl.ds(m * ROWS, ROWS), :] = jnp.where(flag, incoming[m], cotangent[m])
    for copy in early:
        copy.wait()
    backward_mlp(
        grad_ref, h2, gains[1:2], wproj, wlift, wdown, left, right, du, gb_ref, do, dh2_ref, b_ref, mlp_ref
    )
    outs = start_all(zip((grad_ref, du, gb_ref, b_ref), kept), sems, 10)
    for copy in late:
        copy.wait()
    backward_attention(q, k, v, p, do, cos_ref, sin_ref, dq, dkv, to_low, to_high, 6)
    for copy in outs:
        copy.wait()


def joined_grads(dq, dkv, from_low, from_high, dqkv):
    dqkv[:, :D] = dq[...]
    for m in range(MICRO):
        first, last = pl.ds(m * ROWS, HALF), pl.ds(m * ROWS + HALF, HALF)
        dqkv[first, D:] = (dkv[first, :] + from_low[m].astype(F32)).astype(BF16)
        dqkv[last, D:] = (dkv[last, :] + from_high[m].astype(F32)).astype(BF16)


def source_kernel(src, gains, dh2, dq, dkv, from_low, from_high, qkv_hbm, out_ref, wqkv, dqkv, sems):
    waits = start_weights({"qkv": qkv_hbm}, {"qkv": wqkv}, sems)
    joined_grads(dq, dkv, from_low, from_high, dqkv)
    normed, inv_scale = norm_parts(src[...].astype(F32))
    finish(waits, "qkv")
    da = mm_nt(dqkv[...], wqkv[...])
    dh = dh2[...] + norm_back(da, gains[0:1], normed, inv_scale)
    for m in range(MICRO):
        out_ref[m] = dh[m * ROWS : (m + 1) * ROWS].astype(BF16)


def gain_block(attn, mlp, f):
    rows = []
    for gain in (attn, mlp):
        rows.append(gain[:, 192 * f : 192 * f + 128])
        rows.append(jnp.concatenate([gain[:, 192 * f + 128 : 192 * f + 192], jnp.zeros((1, 64), F32)], axis=1))
    return jnp.concatenate(rows + [jnp.zeros((92, 128), F32)], axis=0).astype(BF16)


def source_grad_kernel(index, src, gains, dh2, dq, dkv, from_low, from_high, mlp_grad, qkv_hbm,
                       out_ref, keep, send, wqkv, dqkv, qkv_ref, gain_ref, sems):
    waits = start_weights({"qkv": qkv_hbm}, {"qkv": wqkv}, sems)
    joined_grads(dq, dkv, from_low, from_high, dqkv)
    normed, inv_scale = norm_parts(src[...].astype(F32))
    finish(waits, "qkv")
    da = mm_nt(dqkv[...], wqkv[...])
    attn_grad = jnp.sum(da * normed, axis=0, keepdims=True)
    mlp = mlp_grad[...]
    for f in range(SHARDS):
        gain_ref[f] = gain_block(attn_grad, mlp, f)
    a = (normed * gains[0:1]).astype(BF16)
    for t in range(9):
        cols = pl.ds(256 * t, 256)
        qkv_ref[:, cols] = mm_tn(a, dqkv[:, cols]).astype(BF16)
    copies = []
    for target, half in ((send, 1 - index[2]), (keep, index[2])):
        for f in range(SHARDS):
            rows = pl.ds(pl.multiple_of(f * 192 + half * 96, 16), 96)
            for src_ref, dst_ref in (
                (qkv_ref.at[rows], target.at[f, :, pl.ds(0, WIDE)]),
                (gain_ref.at[f], target.at[f, :, pl.ds(WIDE, 128)]),
            ):
                copy = pltpu.make_async_copy(src_ref, dst_ref, sems.at[1 + len(copies)])
                copy.start()
                copies.append(copy)
    dh = dh2[...] + norm_back(da, gains[0:1], normed, inv_scale)
    for m in range(MICRO):
        out_ref[m] = dh[m * ROWS : (m + 1) * ROWS].astype(BF16)
    for copy in copies:
        copy.wait()


def weight_grad_kernel(index, m_ref, grad_ref, b_ref, du, o_ref, gb_ref, keep, send,
                       down_ref, lift_ref, proj_ref, pad_ref, sems):
    core = index[2]
    copies = []

    def go(src, dst):
        copy = pltpu.make_async_copy(src, dst, sems.at[len(copies)])
        copy.start()
        copies.append(copy)

    sides = ((send, 1 - core), (keep, core))
    rows = lambda at, size: pl.ds(pl.multiple_of(at, 16), size)
    pad_ref[...] = jnp.zeros_like(pad_ref)
    for target, _ in sides:
        for f in range(SHARDS):
            go(pad_ref, target.at[f, pl.ds(176, 16)])
    for t in range(9):
        cols = pl.ds(256 * t, 256)
        lift_ref[:, cols] = mm_tn(b_ref[...], du[:, cols]).astype(BF16)
    for target, half in sides:
        for f in range(SHARDS):
            go(lift_ref.at[rows(f * 192 + half * 96, 96)], target.at[f, pl.ds(0, 96)])
    for t in range(3):
        cols = pl.ds(256 * t, 256)
        down_ref[:, cols] = mm_tn(m_ref[...], grad_ref[:, cols]).astype(BF16)
        proj_ref[:, cols] = mm_tn(o_ref[...], gb_ref[:, cols]).astype(BF16)
    for target, half in sides:
        for f in range(SHARDS):
            for b in range(3):
                cols = pl.ds(b * D, D)
                go(proj_ref.at[rows(f * 192 + b * 64 + half * 32, 32)], target.at[f, pl.ds(96, 32), cols])
                go(down_ref.at[rows(f * 288 + b * 96 + half * 48, 48)], target.at[f, pl.ds(128, 48), cols])
    for copy in copies:
        copy.wait()


def add_up(parts):
    total = parts[0].astype(F32)
    for part in parts[1:]:
        total = total + part.astype(F32)
    return total.astype(BF16)


def rest_core_kernel(index, keep, other, *outs):
    for d, out in enumerate(outs):
        rows = pl.ds(pl.multiple_of(lax.rem(index[0] + d, 4) * 48, 16), 48)
        for f in range(SHARDS):
            out[f] = add_up([keep[f, rows, :], other[f, rows, :]])


def rest_z_kernel(index, own, a, b, c, *outs):
    for d, out in enumerate(outs):
        f = lax.rem(index[1] + d, 4)
        out[...] = add_up([own[f], a[f], b[f], c[f]])


def qkv_core_kernel(index, keep, other, *outs):
    for d, out in enumerate(outs):
        f = lax.rem(index[1] + d, 4)
        out[...] = add_up([keep[f], other[f]])


def partial_kernel(a, b, out):
    out[...] = a[...].astype(F32) + b[...].astype(F32)


def qkv_y_kernel(index, some, b, c, out_0, out_1, out_2, out_3, total):
    total[...] = add_up([some[...], b[...], c[...]])
    for d, out in enumerate((out_0, out_1, out_2, out_3)):
        z = lax.rem(index[0] + d, 4)
        rows = pl.ds(pl.multiple_of(lax.div(z, 2) * 48, 16), 48)
        cols = pl.ds(pl.multiple_of(lax.rem(z, 2) * 1152, 128), 1152)
        out[:, pl.ds(0, 1152)] = total[rows, cols]
        out[:, pl.ds(1152, 128)] = total[pl.ds(0, 48), pl.ds(WIDE, 128)]


def joint_kernel(r0, r1, r2, r3, q0, q1, q2, q3, out):
    out[:, pl.ds(0, WIDE)] = add_up([r0[...], r1[...], r2[...], r3[...]])
    out[:, pl.ds(WIDE, 1280)] = add_up([q0[...], q1[...], q2[...], q3[...]])


def pair_kernel(a, b, out):
    out[...] = add_up([a[...], b[...]])


def final_kernel(index, *refs):
    pieces, (qkv_out, proj_out, lift_out, down_out, gain_out, rest) = refs[:8], refs[8:]
    core = index[2]
    for side in range(2):
        half = core if side == 0 else 1 - core
        for d in range(4):
            piece = pieces[4 * side + d]
            z = lax.rem(index[0] - d + 4, 4)
            rest[side, pl.ds(pl.multiple_of(z * 48, 16), 48), :] = piece[:, pl.ds(0, WIDE)]
            qkv_out[
                pl.ds(pl.multiple_of(half * 96 + lax.div(z, 2) * 48, 16), 48),
                pl.ds(pl.multiple_of(lax.rem(z, 2) * 1152, 128), 1152),
            ] = piece[:, pl.ds(WIDE, 1152)].astype(F32)
        rows = lambda at, size: pl.ds(pl.multiple_of(at, 16), size)
        lift_out[rows(half * 96, 96), :] = rest[side, pl.ds(0, 96), :].astype(F32)
        for b in range(3):
            cols = pl.ds(b * D, D)
            proj_out[rows(b * 64 + half * 32, 32), :] = rest[side, pl.ds(96, 32), cols].astype(F32)
            down_out[rows(b * 96 + half * 48, 48), :] = rest[side, pl.ds(128, 48), cols].astype(F32)
    gain_out[...] = pieces[0][pl.ds(0, 16), pl.ds(WIDE + 1152, 128)].astype(F32)


def call(kernel, name, ins, outs, scratch, flops, limit=24):
    places = {"v": pltpu.VMEM, "a": pl.ANY, "s": pltpu.SMEM}
    return pl.pallas_call(
        kernel,
        name=name,
        out_shape=[jax.ShapeDtypeStruct(out[0], out[1]) for out in outs],
        in_specs=[pl.BlockSpec(memory_space=places[place]) for _, place in ins],
        out_specs=[pl.BlockSpec(memory_space=places[out[2] if len(out) > 2 else "v"]) for out in outs],
        scratch_shapes=scratch,
        compiler_params=pltpu.CompilerParams(vmem_limit_bytes=limit * 2**20),
        cost_estimate=pl.CostEstimate(flops=flops, bytes_accessed=flops // 300, transcendentals=0),
    )(*[array for array, _ in ins])


def travel(block, target):
    pairs = []
    for ctx in range(16):
        for f in range(SHARDS):
            xlo, z, core, g = target(ctx // 8, ctx // 2 % 4, ctx % 2, f)
            pairs.append((ctx * SHARDS + f, (xlo * 8 + z % 4 * 2 + core) * SHARDS + g % 4))
    return lax.ppermute(block, ("ctx", "fsdp"), pairs)


def along_y(block, d):
    return travel(block, lambda x, z, c, f: (x, z, c, f + d))


def along_z(block, d):
    return travel(block, lambda x, z, c, f: (x, z + d, c, f))


def next_shard(block):
    return travel(block, lambda x, z, c, f: (x, z, c, f + 1 - 2 * c))


def swap_core(block):
    return travel(block, lambda x, z, c, f: (x, z, 1 - c, f))


def spread_quarter(block, across):
    return block, across, swap_core(block), swap_core(across)


def swap_x(block):
    return travel(block, lambda x, z, c, f: (1 - x, z, c, f))


def halo_rows(block, axis):
    count = lax.axis_size(axis)
    up = [(i, i + 1) for i in range(count - 1)]
    down = [(i + 1, i) for i in range(count - 1)]
    return (
        lax.ppermute(block[:, ROWS - HALF :], axis, up),
        lax.ppermute(block[:, :HALF], axis, down),
    )


def swap_halos(to_low, to_high):
    count = lax.axis_size("ctx")
    up = [(i, i + 1) for i in range(count - 1)]
    down = [(i + 1, i) for i in range(count - 1)]
    return lax.ppermute(to_high, "ctx", up), lax.ppermute(to_low, "ctx", down)


def tables(first_row, lengths):
    half = HD // 2
    frequencies = rope_base ** (-(jnp.arange(half, dtype=F32) * 2.0) / HD)
    positions = first_row - HALF + jnp.arange(EXT, dtype=jnp.int32)
    angles = positions.astype(F32)[:, None] * frequencies[None, :]
    cosine, sine = jnp.cos(angles), jnp.sin(angles)
    cosine = jnp.concatenate([cosine] * 4, axis=1)
    sine = jnp.concatenate([-sine, sine, -sine, sine], axis=1)
    ends = jnp.cumsum(lengths, axis=1)
    doc = jnp.sum((positions[None, :, None] >= ends[:, None, :]).astype(jnp.int32), axis=2)
    query = positions[HALF : HALF + ROWS]
    allowed = (
        (jnp.abs(query[None, :] - positions[:, None]) <= HALF)
        & (positions >= 0)[:, None]
        & (positions < SEQ_LEN)[:, None]
    )[None] & (doc[:, :, None] == doc[:, None, HALF : HALF + ROWS])
    bias = jnp.where(allowed, 0.0, masked_score).astype(F32)
    return cosine, sine, jnp.concatenate([bias, bias], axis=2)


WQKV, WPROJ, WLIFT, WDOWN = [
    pltpu.VMEM((D, WIDE), BF16),
    pltpu.VMEM((D, D), BF16),
    pltpu.VMEM((D, WIDE), BF16),
    pltpu.VMEM((FF, D), BF16),
]
SAVED = [
    ((OWN, D), BF16),
    ((MICRO * EXT, D), BF16),
    ((MICRO * EXT, D), BF16),
    ((MICRO, TILES, EXT, 2 * ROWS), BF16),
    ((OWN, D), BF16),
    ((OWN, D), F32),
    ((OWN, FF), BF16),
    ((OWN, FF), F32),
    ((OWN, FF), F32),
]
STREAM = [pltpu.VMEM((MICRO * EXT, D), BF16)] * 2
GRADS_OUT = [
    ((OWN, D), F32),
    ((OWN, D), BF16),
    ((OWN, 2 * D), F32),
    ((MICRO, HALF, 2 * D), BF16),
    ((MICRO, HALF, 2 * D), BF16),
]


TURN_OUT = [((MICRO, ROWS, D), BF16)] + SAVED + [((OWN, D), BF16)]
BACK_OUT = [((OWN, D), BF16), ((OWN, WIDE), BF16), ((OWN, D), BF16), ((OWN, D), BF16)]


def sems(count):
    return pltpu.SemaphoreType.DMA((count,))


def body(
    inputs, out_grad, doc_lengths, attn_gain, qkv_weight, proj_weight, mlp_gain, lift_weight, down_weight
):
    on_first = lax.axis_index("section") == 0
    flag = on_first.astype(jnp.int32).reshape(1)
    ctx, f = lax.axis_index("ctx"), lax.axis_index("fsdp")
    index = jnp.stack([ctx // 2 % 4, f, ctx % 2, ctx // 8]).astype(jnp.int32)
    qkv_shard, lift_shard, proj_shard, down_shard = qkv_weight[0], lift_weight[0], proj_weight[0], down_weight[0]
    own, cotangent = inputs[:, 0], out_grad[:, 0]
    gain_tile = jnp.pad(
        jnp.pad(jnp.stack([attn_gain[0], mlp_gain[0]]), ((0, 0), (0, 64))).reshape(4, 128), ((0, 12), (0, 0))
    )
    edge = ((MICRO, HALF, D), BF16)
    qkv_pack, qkv_half, first_rows, last_rows = call(
        pack_qkv_kernel, "pack_qkv",
        [(index, "s"), (qkv_shard, "v"), (gain_tile, "v"), (own, "v")],
        [((192, 2432), BF16), ((96, 2432), BF16), edge, edge],
        [], 0, 12,
    )
    rest, rest_quarter = call(
        pack_kernel, "pack_rest",
        [(index, "s"), (lift_shard, "v"), (proj_shard, "v"), (down_shard, "v")],
        [((352, WIDE), BF16), ((176, 1152), BF16)],
        [pltpu.VMEM((176, WIDE), BF16)], 0, 12,
    )
    first = next_shard(qkv_pack)
    second = along_y(qkv_half, 2)
    rest_second = along_y(rest_quarter, 2)
    cosine, sine, bias = tables(ctx * ROWS, doc_lengths[:, 0])
    first_rows, last_rows, cosine = lax.optimization_barrier((first_rows, last_rows, cosine))
    low, high = swap_halos(first_rows, last_rows)
    first, second, rest_second, rest, cosine, sine, bias, low, high = lax.optimization_barrier(
        (first, second, rest_second, rest, cosine, sine, bias, low, high)
    )
    rest_first = next_shard(rest)
    first_other, rest_x = lax.optimization_barrier((swap_core(first), swap_x(rest_second)))
    qkv_pieces = first, first_other, second, swap_core(second)
    stream = ((MICRO, ROWS, D), BF16)
    scratch = lambda items: [pltpu.VMEM(s, k) for s, k in items]

    o, gains, wqkv = call(
        forward_attention_kernel, "forward_attention",
        [(index, "s"), (own, "v"), (low, "v"), (high, "v"), (gain_tile, "a"), (cosine, "v"), (sine, "v"), (bias, "v"),
         (qkv_shard, "a"), *[(piece, "a") for piece in qkv_pieces]],
        [((OWN, D), BF16), ((2, D), F32), ((D, WIDE), BF16, "a")],
        [WQKV, pltpu.VMEM((SHARDS, 16, 128), BF16)] + STREAM + scratch(SAVED[:4]) + [sems(9), pltpu.SemaphoreType.DMA(())],
        1_400_000_000,
    )
    rest_first, rest_second, rest_x, o = lax.optimization_barrier((rest_first, rest_second, rest_x, o))
    rest_pieces = rest_first, swap_core(rest_first), *spread_quarter(rest_second, rest_x)
    rest_parts = [(part, "a") for part in (lift_shard, proj_shard, down_shard, *rest_pieces)]
    (relay,) = call(
        forward_mlp_kernel, "forward_mlp",
        [(index, "s"), (own, "v"), (o, "v"), (gains, "v"), *rest_parts],
        [stream],
        [WPROJ, WLIFT, WDOWN] + scratch([SAVED[5], SAVED[0], SAVED[6]]) + [sems(45)],
        1_800_000_000,
    )
    wlift, wproj, wdown = call(
        assemble_kernel, "assemble_weights",
        [(index, "s"), *rest_parts, (relay, "a")],
        [((D, WIDE), BF16, "a"), ((D, D), BF16, "a"), ((FF, D), BF16, "a")],
        [WLIFT, WPROJ, WDOWN, sems(48)], 1_800_000_000, 56,
    )
    relayed = lax.ppermute(relay, "section", [(0, 1)])
    relayed, wlift, wproj, wdown = lax.optimization_barrier((relayed, wlift, wproj, wdown))
    other_low, other_high = halo_rows(relayed, "ctx")
    (h3, q, k, v, p, o, h2, m_act, left, right, src, dh2, dq, dkv, to_low, to_high) = call(
        turning_kernel, "layer_turn",
        [(flag, "s"), (own, "v"), (low, "v"), (high, "v"), (relayed, "v"), (other_low, "v"), (other_high, "v"),
         (cotangent, "v"), (gains, "v"), (cosine, "v"), (sine, "v"), (bias, "v"),
         (wqkv, "a"), (wproj, "a"), (wlift, "a"), (wdown, "a")],
        [(*item, "a") for item in TURN_OUT] + GRADS_OUT,
        [WQKV, WPROJ, WLIFT, WDOWN] + STREAM
        + [pltpu.VMEM((MICRO, ROWS, D), BF16), pltpu.VMEM((OWN, WIDE), BF16), pltpu.VMEM((OWN, D), BF16)] + scratch(TURN_OUT) + [sems(15)],
        6_000_000_000, 44,
    )
    from_low, from_high = swap_halos(to_low, to_high)
    (grad_relay,) = call(
        source_kernel, "layer_source",
        [(src, "v"), (gains, "v"), (dh2, "v"), (dq, "v"), (dkv, "v"), (from_low, "v"), (from_high, "v"), (wqkv, "a")],
        [stream],
        [WQKV, pltpu.VMEM((OWN, WIDE), BF16), sems(1)],
        900_000_000,
    )
    incoming = lax.ppermute(grad_relay, "section", [(1, 0)])
    (grad_low, du, gb, b, mlp_gain_grad, dh2, dq, dkv, to_low, to_high) = call(
        back_kernel, "layer_back",
        [(flag, "s"), (incoming, "v"), (cotangent, "v"), (gains, "v"), (cosine, "v"), (sine, "v"),
         (wproj, "a"), (wlift, "a"), (wdown, "a"),
         *[(array, "a") for array in (q, k, v, p, h2, left, right)]],
        [(*item, "a") for item in BACK_OUT] + [((1, D), F32)] + GRADS_OUT,
        [WPROJ, WLIFT, WDOWN, pltpu.VMEM((OWN, D), BF16)]
        + scratch(SAVED[:4] + SAVED[5:6] + SAVED[7:] + BACK_OUT) + [sems(14)],
        3_000_000_000, 40,
    )
    from_low, from_high = swap_halos(to_low, to_high)
    rest_keep, rest_send = call(
        weight_grad_kernel, "weight_grads",
        [(index, "s"), (m_act, "v"), (grad_low, "v"), (b, "v"), (du, "v"), (o, "v"), (gb, "v")],
        [((SHARDS, 192, WIDE), BF16, "a")] * 2,
        [WDOWN, WLIFT, WPROJ, pltpu.VMEM((16, WIDE), BF16), sems(64)],
        1_600_000_000,
    )
    from_low, from_high, rest_send = lax.optimization_barrier((from_low, from_high, rest_send))
    rest_other = swap_core(rest_send)
    in_grad, qkv_keep, qkv_send = call(
        source_grad_kernel, "layer_source_grads",
        [(index, "s"), (src, "v"), (gains, "v"), (dh2, "v"), (dq, "v"), (dkv, "v"), (from_low, "v"),
         (from_high, "v"), (mlp_gain_grad, "v"), (wqkv, "a")],
        [stream, ((SHARDS, 96, 2432), BF16, "a"), ((SHARDS, 96, 2432), BF16, "a")],
        [WQKV, pltpu.VMEM((OWN, WIDE), BF16), WQKV, pltpu.VMEM((SHARDS, 96, 128), BF16), sems(17)],
        1_800_000_000,
    )
    qkv_other = swap_core(qkv_send)

    rest_z = call(
        rest_core_kernel, "rest_core_sum", [(index, "s"), (rest_keep, "v"), (rest_other, "v")],
        [((SHARDS, 48, WIDE), BF16)] * 4, [], 0, 24,
    )
    qkv_keep, _ = lax.optimization_barrier((qkv_keep, rest_z[0]))
    qkv_y = call(
        qkv_core_kernel, "qkv_core_sum", [(index, "s"), (qkv_keep, "v"), (qkv_other, "v")],
        [((96, 2432), BF16)] * 4, [], 0, 24,
    )
    (some,) = call(
        partial_kernel, "qkv_y_first", [(qkv_y[0], "v"), (along_y(qkv_y[1], 1), "v")],
        [((96, 2432), F32)], [], 0, 24,
    )
    rest_mine, some = lax.optimization_barrier((rest_z[0], some))
    rest_y = call(
        rest_z_kernel, "rest_z_sum",
        [(index, "s"), (rest_mine, "v"), *[(along_z(rest_z[d], d), "v") for d in (1, 2, 3)]],
        [((48, WIDE), BF16)] * 4, [], 0, 24,
    )
    some, _ = lax.optimization_barrier((some, rest_y[0]))
    qkv_z = call(
        qkv_y_kernel, "qkv_y_sum",
        [(index, "s"), (some, "v"), *[(along_y(qkv_y[d], d), "v") for d in (2, 3)]],
        [((48, 1280), BF16)] * 4, [pltpu.VMEM((96, 2432), BF16)], 0, 24,
    )
    (joint,) = call(
        joint_kernel, "joint_sum",
        [(rest_y[0], "v"), *[(along_y(rest_y[d], d), "v") for d in (1, 2, 3)],
         (qkv_z[0], "v"), *[(along_z(qkv_z[d], d), "v") for d in (1, 2, 3)]],
        [((48, 3584), BF16)], [], 0, 24,
    )
    (joint,) = call(
        pair_kernel, "pair_sum", [(joint, "v"), (swap_x(joint), "v")], [((48, 3584), BF16)], [], 0, 24
    )
    mine = [joint] + [along_z(joint, d) for d in (1, 2, 3)]
    theirs = [swap_core(piece) for piece in mine]
    qkv_sum, proj_sum, lift_sum, down_sum, gain_sums = call(
        final_kernel, "final_shard", [(index, "s"), *[(piece, "v") for piece in mine + theirs]],
        [((192, WIDE), F32), ((192, D), F32), ((192, WIDE), F32), ((288, D), F32), ((16, 128), F32)],
        [pltpu.VMEM((2, 192, WIDE), BF16)], 0, 24,
    )
    return (
        h3[None, :, None],
        in_grad[None, :, None],
        gain_sums[0:2].reshape(1, 256)[:, :192],
        qkv_sum[None],
        proj_sum[None],
        gain_sums[2:4].reshape(1, 256)[:, :192],
        lift_sum[None],
        down_sum[None],
    )


def solution(mesh):
    placed = (
        P(None, "fsdp", "ctx", None),
        P(None, "fsdp", "ctx", None),
        P(None, "fsdp", None),
        P("section", "fsdp"),
        P("section", "fsdp", None),
        P("section", "fsdp", None),
        P("section", "fsdp"),
        P("section", "fsdp", None),
        P("section", "fsdp", None),
    )
    return jax.shard_map(
        body,
        mesh=mesh,
        in_specs=placed,
        out_specs=(
            P("section", None, "fsdp", "ctx", None),
            P("section", None, "fsdp", "ctx", None),
            P("section", "fsdp"),
            P("section", "fsdp", None),
            P("section", "fsdp", None),
            P("section", "fsdp"),
            P("section", "fsdp", None),
            P("section", "fsdp", None),
        ),
        check_vma=False,
    )
```

```python
import functools

import jax
import jax.numpy as jnp
from jax import lax
from jax.experimental import pallas as pl
from jax.experimental.pallas import tpu as pltpu
from jax.sharding import PartitionSpec as P

D = 768
HD = 64
HALF = 64
SEQ_LEN = 2048
FF = 1152
WIDE = 2304
ROWS = 128
EXT = ROWS + 2 * HALF
MICRO = 2
OWN = MICRO * ROWS
SHARDS = 4
TILES = D // 128
norm_eps = 1e-05
rope_base = 10000.0
masked_score = -1e30
root_half = 0.7071067811865476
inv_root_tau = 0.3989422804014327
F32 = jnp.float32
BF16 = jnp.bfloat16


def mm(left, right):
    return lax.dot_general(left, right, (((1,), (0,)), ((), ())), preferred_element_type=F32)


def mm_nt(left, right):
    return lax.dot_general(left, right, (((1,), (1,)), ((), ())), preferred_element_type=F32)


def mm_tn(left, right):
    return lax.dot_general(left, right, (((0,), (0,)), ((), ())), preferred_element_type=F32)


def norm_parts(hidden):
    centre = hidden - jnp.mean(hidden, axis=-1, keepdims=True)
    inv_scale = lax.rsqrt(jnp.mean(centre * centre, axis=-1, keepdims=True) + norm_eps)
    return centre * inv_scale, inv_scale


def norm_back(grad_out, gain, normed, inv_scale):
    grad_normed = grad_out * gain
    inner = (
        grad_normed
        - jnp.mean(grad_normed, axis=-1, keepdims=True)
        - normed * jnp.mean(grad_normed * normed, axis=-1, keepdims=True)
    )
    return inner * inv_scale


def lane_is_low(shape, period):
    return lax.broadcasted_iota(jnp.int32, shape, 1) % period < period // 2


def turn(x):
    return jnp.where(lane_is_low(x.shape, HD), pltpu.roll(x, 96, 1), pltpu.roll(x, 32, 1))


def rotate(x, cosine, sine):
    return x * cosine + turn(x) * sine


def rotate_back(x, cosine, sine):
    return x * cosine - turn(x) * sine


def stack_heads(x):
    low = lane_is_low(x.shape, 128)
    zero = jnp.zeros_like(x)
    return jnp.concatenate([jnp.where(low, x, zero), jnp.where(low, zero, x)], axis=0)


def join_heads(x):
    half = x.shape[0] // 2
    low = lane_is_low((half, 128), 128)
    return jnp.where(low, x[:half], x[half:])


def start_weights(sources, buffers, sems):
    waits = {}
    for index, (name, source) in enumerate(sources.items()):
        copy = pltpu.make_async_copy(source, buffers[name], sems.at[index])
        copy.start()
        waits[name] = [copy]
    return waits


def finish(waits, name):
    for copy in waits[name]:
        copy.wait()


def load_stream(flag, own, low, high, other, ext):
    for m in range(MICRO):
        for ref, alt, start, size in (
            (low, other[1], 0, HALF),
            (own, other[0], HALF, ROWS),
            (high, other[2], HALF + ROWS, HALF),
        ):
            value = ref[m]
            if alt is not None:
                value = jnp.where(flag, value, alt[m])
            ext[pl.ds(m * EXT + start, size), :] = value


def own_rows(x):
    return jnp.concatenate([x[HALF : HALF + ROWS], x[EXT + HALF : EXT + HALF + ROWS]], axis=0)


def repeat(count, step):
    lax.fori_loop(0, count, lambda i, carry: (step(i), carry)[1], 0)


def each(count, step):
    for i in range(count):
        step(i)


def span(start, size, unit=128):
    return pl.ds(start if isinstance(start, int) else pl.multiple_of(start, unit), size)


def by_tiles(unit, group):
    def step(i):
        for j in range(group):
            unit(i * group + j)

    repeat(TILES // group, step)


def norm_rows(source, gain, target):
    def step(i):
        rows = span(i * 128, 128)
        normed, _ = norm_parts(source[rows, :].astype(F32))
        target[rows, :] = (normed * gain).astype(BF16)

    repeat(source.shape[0] // 128, step)


def forward_attention(ext, gain, wqkv, cos_ref, sin_ref, bias_ref, a_ext, q_ref, k_ref, v_ref, p_ref, o_ref):
    norm_rows(ext, gain, a_ext)
    a_own = o_ref
    a_own[...] = own_rows(a_ext[...])
    own_span = pl.ds(HALF, ROWS)

    def project(t):
        cols = span(256 * t, 256)
        queries = mm(a_own[...], wqkv[:, cols])
        keys = mm(a_ext[...], wqkv[:, span(D + 256 * t, 256)])
        v_ref[:, cols] = mm(a_ext[...], wqkv[:, span(2 * D + 256 * t, 256)]).astype(BF16)
        for s in range(2):
            tile, lanes = span(256 * t + 128 * s, 128), slice(128 * s, 128 * s + 128)
            for m in range(MICRO):
                part = queries[m * ROWS : (m + 1) * ROWS, lanes]
                turned = rotate(part, cos_ref[own_span, :], sin_ref[own_span, :]).astype(BF16)
                q_ref[pl.ds(m * ROWS, ROWS), tile] = turned * jnp.asarray(0.125, BF16)
                part = keys[m * EXT : (m + 1) * EXT, lanes]
                k_ref[pl.ds(m * EXT, EXT), tile] = rotate(part, cos_ref[...], sin_ref[...]).astype(BF16)

    repeat(3, project)

    def unit(t):
        cols = pl.ds(pl.multiple_of(t * 128, 128), 128)
        for m in range(MICRO):
            q2 = stack_heads(q_ref[pl.ds(m * ROWS, ROWS), cols])
            scores = mm_nt(k_ref[pl.ds(m * EXT, EXT), cols], q2) + bias_ref[m]
            terms = jnp.exp(scores - jnp.max(scores, axis=0, keepdims=True))
            probs = (terms * (1.0 / jnp.sum(terms, axis=0, keepdims=True))).astype(BF16)
            p_ref[m, t] = probs
            attended = mm_tn(probs, v_ref[pl.ds(m * EXT, EXT), cols])
            o_ref[pl.ds(m * ROWS, ROWS), cols] = join_heads(attended).astype(BF16)

    by_tiles(unit, 3)


def forward_mlp(own, o_ref, wproj, mlp_gain, wlift, wdown, h2_ref, b_ref, m_ref, left_ref, right_ref, h3_ref, waits):
    finish(waits, "proj")

    def mix(t):
        cols = span(256 * t, 256)
        added = mm(o_ref[...], wproj[:, cols])
        for m in range(MICRO):
            rows = pl.ds(m * ROWS, ROWS)
            h2_ref[rows, cols] = own[m, :, cols].astype(F32) + added[m * ROWS : (m + 1) * ROWS]

    each(3, mix)
    norm_rows(h2_ref, mlp_gain, b_ref)
    finish(waits, "lift")

    def lift(t):
        cols = span(384 * t, 384)
        gate = mm(b_ref[...], wlift[:, cols])
        up = mm(b_ref[...], wlift[:, span(FF + 384 * t, 384)])
        cdf = 0.5 * (1.0 + lax.erf(gate * root_half))
        gelu = gate * cdf
        m_ref[:, cols] = (gelu * up).astype(BF16)
        if left_ref is not None:
            pdf = jnp.exp(-0.5 * gate * gate) * inv_root_tau
            left_ref[:, cols] = up * (cdf + gate * pdf)
            right_ref[:, cols] = gelu

    repeat(3, lift)
    finish(waits, "down")

    def down(t):
        cols = span(256 * t, 256)
        h3 = (h2_ref[:, cols] + mm(m_ref[...], wdown[:, cols])).astype(BF16)
        for m in range(MICRO):
            h3_ref[m, :, cols] = h3[m * ROWS : (m + 1) * ROWS]

    each(3, down)


def backward_mlp(grad_ref, h2_ref, mlp_gain, wproj, wlift, wdown, left_ref, right_ref, du_ref, gb_ref, do_ref,
                 dh2_ref, b_ref, mlp_ref):
    def lift(t):
        cols = span(384 * t, 384)
        dm = mm_nt(grad_ref[...], wdown[cols, :])
        du_ref[:, cols] = (dm * left_ref[:, cols]).astype(BF16)
        du_ref[:, span(FF + 384 * t, 384)] = (dm * right_ref[:, cols]).astype(BF16)

    each(3, lift)

    def source(t):
        rows = span(256 * t, 256)
        dh2_ref[:, rows] = mm_nt(du_ref[...], wlift[rows, :])

    each(3, source)
    if mlp_ref is not None:
        mlp_ref[...] = jnp.zeros_like(mlp_ref)

    def norm(i):
        rows = span(i * 128, 128)
        db = dh2_ref[rows, :]
        normed, inv_scale = norm_parts(h2_ref[rows, :])
        dh2 = grad_ref[rows, :].astype(F32) + norm_back(db, mlp_gain, normed, inv_scale)
        dh2_ref[rows, :] = dh2
        gb_ref[rows, :] = dh2.astype(BF16)
        if mlp_ref is not None:
            mlp_ref[...] += jnp.sum(db * normed, axis=0, keepdims=True)
            b_ref[rows, :] = (normed * mlp_gain).astype(BF16)

    repeat(2, norm)

    def attended(t):
        rows = span(256 * t, 256)
        do_ref[:, rows] = mm_nt(gb_ref[...], wproj[rows, :]).astype(BF16)

    each(3, attended)


def backward_attention(q_ref, k_ref, v_ref, p_ref, do_ref, cos_ref, sin_ref, dq_ref, dkv_ref, low_ref, high_ref, group):
    cosine, sine = cos_ref[...], sin_ref[...]
    cos_own, sin_own = cosine[HALF : HALF + ROWS], sine[HALF : HALF + ROWS]

    def unit(t):
        cols = pl.ds(pl.multiple_of(t * 128, 128), 128)
        value_cols = pl.ds(pl.multiple_of(D + t * 128, 128), 128)
        for m in range(MICRO):
            rows = pl.ds(m * ROWS, ROWS)
            q2 = stack_heads(q_ref[rows, cols])
            do2 = stack_heads(do_ref[rows, cols])
            probs = p_ref[m, t]
            dprobs = mm_nt(v_ref[pl.ds(m * EXT, EXT), cols], do2)
            wide = probs.astype(F32)
            inner = jnp.sum(wide * dprobs, axis=0, keepdims=True)
            ds = (wide * (dprobs - inner)).astype(BF16)
            dq = join_heads(mm_tn(ds, k_ref[pl.ds(m * EXT, EXT), cols])) * 0.125
            dq_ref[rows, cols] = rotate_back(dq, cos_own, sin_own).astype(BF16)
            dk = rotate_back(mm(ds, q2), cosine, sine)
            dv = mm(probs, do2)
            for grad, where in ((dk, cols), (dv, value_cols)):
                low_ref[m, :, where] = grad[:HALF].astype(BF16)
                dkv_ref[rows, where] = grad[HALF : HALF + ROWS]
                high_ref[m, :, where] = grad[HALF + ROWS :].astype(BF16)

    by_tiles(unit, group)


def place_shards(index, own, pieces, put):
    f, core, xlo = index[1], index[2], index[3]
    first, first_other, second, second_x, second_core, second_both = pieces
    put(own, f, None, None)
    put(first, lax.rem(f + 3 + 2 * core, 4), None, None)
    put(first_other, lax.rem(f + 1 + 2 * core, 4), None, None)
    across = lax.rem(f + 2, 4)
    put(second, across, core, xlo)
    put(second_x, across, core, 1 - xlo)
    put(second_core, across, 1 - core, xlo)
    put(second_both, across, 1 - core, 1 - xlo)


def pack_qkv_kernel(index, qkv, gains, own, whole, half, first_rows, last_rows):
    rows = pl.ds(pl.multiple_of(index[2] * 96, 16), 96)
    whole[:, pl.ds(0, WIDE)] = qkv[...]
    half[:, pl.ds(0, WIDE)] = qkv[rows, :]
    whole[:, pl.ds(WIDE, 128)] = jnp.zeros((192, 128), BF16)
    half[:, pl.ds(WIDE, 128)] = jnp.zeros((96, 128), BF16)
    whole[pl.ds(0, 16), pl.ds(WIDE, 128)] = gains[...]
    half[pl.ds(0, 16), pl.ds(WIDE, 128)] = gains[...]
    first_rows[...] = own[:, :HALF]
    last_rows[...] = own[:, ROWS - HALF :]


def pack_kernel(index, lift, proj, down, rest, quarter, half):
    core = index[2]
    rows = lambda at, size: pl.ds(pl.multiple_of(at, 16), size)
    rest[pl.ds(0, 192), :] = lift[...]
    half[pl.ds(0, 96), :] = lift[rows(core * 96, 96), :]
    for b in range(3):
        cols = pl.ds(b * D, D)
        rest[pl.ds(192, 64), cols] = proj[pl.ds(64 * b, 64), :]
        rest[pl.ds(256, 96), cols] = down[pl.ds(96 * b, 96), :]
        half[pl.ds(96, 32), cols] = proj[rows(64 * b + core * 32, 32), :]
        half[pl.ds(128, 48), cols] = down[rows(96 * b + core * 48, 48), :]
    quarter[...] = half[:, pl.ds(pl.multiple_of(index[3] * 1152, 128), 1152)]


def gather_gain(tiles, row):
    parts = []
    for tile in tiles:
        parts += [tile[row : row + 1, :], tile[row + 1 : row + 2, :64]]
    return jnp.concatenate(parts, axis=1)


def forward_attention_kernel(index, own, low, high, gain_tile, cos_ref, sin_ref, bias_ref,
                             shard, first, first_other, second, second_core,
                             o, gains, whole, wqkv, tiles, ext, a_ext, q, k, v, p, sems, out_sem):
    copies = []

    def go(src, dst):
        copy = pltpu.make_async_copy(src, dst, sems.at[len(copies)])
        copy.start()
        copies.append(copy)

    def put(piece, f, half, side):
        if piece is None:
            return
        at, size = (f * 192, 192) if half is None else (f * 192 + half * 96, 96)
        rows = pl.ds(pl.multiple_of(at, 16), size)
        go(piece if piece is shard else piece.at[:, pl.ds(0, WIDE)], wqkv.at[rows])
        if piece is not shard and piece is not second_core:
            go(piece.at[pl.ds(0, 16), pl.ds(WIDE, 128)], tiles.at[f])

    place_shards(index, shard, (first, first_other, second, None, second_core, None), put)
    go(gain_tile, tiles.at[index[1]])
    load_stream(None, own, low, high, (None, None, None), ext)
    for copy in copies:
        copy.wait()
    out = pltpu.make_async_copy(wqkv, whole, out_sem)
    out.start()
    shards = [tiles[f].astype(F32) for f in range(SHARDS)]
    gains[0:1, :] = gather_gain(shards, 0)
    gains[1:2, :] = gather_gain(shards, 2)
    forward_attention(ext, gains[0:1], wqkv, cos_ref, sin_ref, bias_ref, a_ext, q, k, v, p, o)
    out.wait()


def place_rest(index, lift, proj, down, pieces, wlift, wproj, wdown, go):
    f = index[1]
    rows = lambda at, size: pl.ds(pl.multiple_of(at, 16), size)
    lanes = lambda at, size: pl.ds(pl.multiple_of(at, 128), size)

    def put(piece, s, half, side):
        if piece is None:
            go("proj", proj, wproj.at[rows(f * 192, 192)])
            go("lift", lift, wlift.at[rows(f * 192, 192)])
            go("down", down, wdown.at[rows(f * 288, 288)])
        elif half is None:
            go("lift", piece.at[pl.ds(0, 192)], wlift.at[rows(s * 192, 192)])
            for b in range(3):
                cols = pl.ds(b * D, D)
                go("proj", piece.at[pl.ds(192, 64), cols], wproj.at[rows(s * 192 + b * 64, 64)])
                go("down", piece.at[pl.ds(256, 96), cols], wdown.at[rows(s * 288 + b * 96, 96)])
        else:
            go("lift", piece.at[pl.ds(0, 96)], wlift.at[rows(s * 192 + half * 96, 96), lanes(side * 1152, 1152)])
            for j in range(3):
                cols = pl.ds(j * 384, 384)
                b, right = lax.div(3 * side + j, 2), lanes(lax.rem(3 * side + j, 2) * 384, 384)
                go("proj", piece.at[pl.ds(96, 32), cols], wproj.at[rows(s * 192 + b * 64 + half * 32, 32), right])
                go("down", piece.at[pl.ds(128, 48), cols], wdown.at[rows(s * 288 + b * 96 + half * 48, 48), right])

    place_shards(index, None, pieces, put)


def starter(sems, waits):
    count = [0]

    def go(name, src, dst):
        copy = pltpu.make_async_copy(src, dst, sems.at[count[0]])
        copy.start()
        count[0] += 1
        waits.setdefault(name, []).append(copy)

    return go


def forward_mlp_kernel(index, own, o, gains, lift, proj, down, *refs):
    pieces, (h3_ref, wproj, wlift, wdown, h2, b, m_out, sems) = refs[:6], refs[6:]
    waits = {}
    place_rest(index, lift, proj, down, pieces, wlift, wproj, wdown, starter(sems, waits))
    forward_mlp(own, o, wproj, gains[1:2], wlift, wdown, h2, b, m_out, None, None, h3_ref, waits)


def assemble_kernel(index, lift, proj, down, *refs):
    pieces, (whole_lift, whole_proj, whole_down, wlift, wproj, wdown, sems) = refs[:6], refs[7:]
    waits = {}
    go = starter(sems, waits)
    place_rest(index, lift, proj, down, pieces, wlift, wproj, wdown, go)
    for name, buffer, whole in (("lift", wlift, whole_lift), ("proj", wproj, whole_proj), ("down", wdown, whole_down)):
        finish(waits, name)
        go("out", buffer, whole)
    finish(waits, "out")


def start_all(pairs, sems, first):
    copies = [pltpu.make_async_copy(src, dst, sems.at[first + n]) for n, (src, dst) in enumerate(pairs)]
    for copy in copies:
        copy.start()
    return copies


def turning_kernel(flag_ref, own, low, high, other_own, other_low, other_high, cotangent, gains,
                   cos_ref, sin_ref, bias_ref, qkv_hbm, proj_hbm, lift_hbm, down_hbm, *refs):
    kept, (dh2_ref, dq, dkv, to_low, to_high) = refs[:11], refs[11:16]
    wqkv, wproj, wlift, wdown, ext, a_ext, mine, du, do, h3_ref, q, k, v, p, o, h2, m_out, left, right, src, sems = refs[16:]
    waits = start_weights(
        {"qkv": qkv_hbm, "proj": proj_hbm, "lift": lift_hbm, "down": down_hbm},
        {"qkv": wqkv, "proj": wproj, "lift": wlift, "down": wdown}, sems,
    )
    flag = flag_ref[0] == 1
    load_stream(flag, own, low, high, (other_own, other_low, other_high), ext)
    for m in range(MICRO):
        mine[m] = ext[pl.ds(m * EXT + HALF, ROWS), :]
        src[pl.ds(m * ROWS, ROWS), :] = mine[m]
    finish(waits, "qkv")
    forward_attention(ext, gains[0:1], wqkv, cos_ref, sin_ref, bias_ref, a_ext, q, k, v, p, o)
    outs = start_all(zip((q, k, v, p, o, src), kept[1:6] + kept[10:]), sems, 4)
    spare = a_ext.at[pl.ds(0, OWN)]
    forward_mlp(mine, o, wproj, gains[1:2], wlift, wdown, h2, spare, m_out, left, right, h3_ref, waits)
    outs += start_all(zip((h3_ref, h2, m_out, left, right), kept[:1] + kept[6:10]), sems, 10)
    grad = a_ext.at[pl.ds(OWN, OWN)]
    for m in range(MICRO):
        grad[pl.ds(m * ROWS, ROWS), :] = cotangent[m]
    backward_mlp(grad, h2, gains[1:2], wproj, wlift, wdown, left, right, du, spare, do, dh2_ref, None, None)
    backward_attention(q, k, v, p, do, cos_ref, sin_ref, dq, dkv, to_low, to_high, 3)
    for copy in outs:
        copy.wait()


def back_kernel(flag_ref, incoming, cotangent, gains, cos_ref, sin_ref, proj_hbm, lift_hbm, down_hbm,
                q_hbm, k_hbm, v_hbm, p_hbm, h2_hbm, left_hbm, right_hbm, *refs):
    kept, (mlp_ref, dh2_ref, dq, dkv, to_low, to_high) = refs[:4], refs[4:10]
    wproj, wlift, wdown, do, q, k, v, p, h2, left, right, grad_ref, du, gb_ref, b_ref, sems = refs[10:]
    early = start_all(
        ((down_hbm, wdown), (left_hbm, left), (right_hbm, right), (lift_hbm, wlift), (h2_hbm, h2), (proj_hbm, wproj)),
        sems, 0,
    )
    late = start_all(((q_hbm, q), (v_hbm, v), (p_hbm, p), (k_hbm, k)), sems, 6)
    flag = flag_ref[0] == 1
    for m in range(MICRO):
        grad_ref[pl.ds(m * ROWS, ROWS), :] = jnp.where(flag, incoming[m], cotangent[m])
    for copy in early:
        copy.wait()
    backward_mlp(
        grad_ref, h2, gains[1:2], wproj, wlift, wdown, left, right, du, gb_ref, do, dh2_ref, b_ref, mlp_ref
    )
    outs = start_all(zip((grad_ref, du, gb_ref, b_ref), kept), sems, 10)
    for copy in late:
        copy.wait()
    backward_attention(q, k, v, p, do, cos_ref, sin_ref, dq, dkv, to_low, to_high, 6)
    for copy in outs:
        copy.wait()


def joined_grads(dq, dkv, from_low, from_high, dqkv):
    dqkv[:, :D] = dq[...]
    for m in range(MICRO):
        first, last = pl.ds(m * ROWS, HALF), pl.ds(m * ROWS + HALF, HALF)
        dqkv[first, D:] = (dkv[first, :] + from_low[m].astype(F32)).astype(BF16)
        dqkv[last, D:] = (dkv[last, :] + from_high[m].astype(F32)).astype(BF16)


def source_kernel(src, gains, dh2, dq, dkv, from_low, from_high, qkv_hbm, out_ref, wqkv, dqkv, sems):
    waits = start_weights({"qkv": qkv_hbm}, {"qkv": wqkv}, sems)
    joined_grads(dq, dkv, from_low, from_high, dqkv)
    normed, inv_scale = norm_parts(src[...].astype(F32))
    finish(waits, "qkv")
    da = mm_nt(dqkv[...], wqkv[...])
    dh = dh2[...] + norm_back(da, gains[0:1], normed, inv_scale)
    for m in range(MICRO):
        out_ref[m] = dh[m * ROWS : (m + 1) * ROWS].astype(BF16)


def gain_block(attn, mlp, f):
    rows = []
    for gain in (attn, mlp):
        rows.append(gain[:, 192 * f : 192 * f + 128])
        rows.append(jnp.concatenate([gain[:, 192 * f + 128 : 192 * f + 192], jnp.zeros((1, 64), F32)], axis=1))
    return jnp.concatenate(rows + [jnp.zeros((124, 128), F32)], axis=0).astype(BF16)


def source_grad_kernel(index, src, gains, dh2, dq, dkv, from_low, from_high, mlp_grad, proj_keep, proj_send,
                       qkv_hbm, out_ref, keep, send, wqkv, dqkv, qkv_ref, gain_ref, sems):
    waits = start_weights({"qkv": qkv_hbm}, {"qkv": wqkv}, sems)
    joined_grads(dq, dkv, from_low, from_high, dqkv)
    normed, inv_scale = norm_parts(src[...].astype(F32))
    finish(waits, "qkv")
    da = mm_nt(dqkv[...], wqkv[...])
    attn_grad = jnp.sum(da * normed, axis=0, keepdims=True)
    mlp = mlp_grad[...]
    for f in range(SHARDS):
        gain_ref[f] = gain_block(attn_grad, mlp, f)
    a = (normed * gains[0:1]).astype(BF16)
    for t in range(9):
        cols = pl.ds(256 * t, 256)
        qkv_ref[:, cols] = mm_tn(a, dqkv[:, cols]).astype(BF16)
    copies = []
    for target, proj, half in ((send, proj_send, 1 - index[2]), (keep, proj_keep, index[2])):
        for f in range(SHARDS):
            rows = pl.ds(pl.multiple_of(f * 192 + half * 96, 16), 96)
            for src_ref, dst_ref in (
                (qkv_ref.at[rows], target.at[f, pl.ds(0, 96), pl.ds(0, WIDE)]),
                (proj.at[f], target.at[f, pl.ds(96, 32), pl.ds(0, WIDE)]),
                (gain_ref.at[f], target.at[f, :, pl.ds(WIDE, 128)]),
            ):
                copy = pltpu.make_async_copy(src_ref, dst_ref, sems.at[1 + len(copies)])
                copy.start()
                copies.append(copy)
    dh = dh2[...] + norm_back(da, gains[0:1], normed, inv_scale)
    for m in range(MICRO):
        out_ref[m] = dh[m * ROWS : (m + 1) * ROWS].astype(BF16)
    for copy in copies:
        copy.wait()


def weight_grad_kernel(index, m_ref, grad_ref, b_ref, du, o_ref, gb_ref, keep, send, proj_keep, proj_send,
                       down_ref, lift_ref, proj_ref, pad_ref, sems):
    core = index[2]
    copies = []

    def go(src, dst):
        copy = pltpu.make_async_copy(src, dst, sems.at[len(copies)])
        copy.start()
        copies.append(copy)

    sides = ((send, proj_send, 1 - core), (keep, proj_keep, core))
    rows = lambda at, size: pl.ds(pl.multiple_of(at, 16), size)
    pad_ref[...] = jnp.zeros_like(pad_ref)
    for target, _, _ in sides:
        for f in range(SHARDS):
            go(pad_ref, target.at[f, pl.ds(144, 16)])
    for t in range(9):
        cols = pl.ds(256 * t, 256)
        lift_ref[:, cols] = mm_tn(b_ref[...], du[:, cols]).astype(BF16)
    for target, _, half in sides:
        for f in range(SHARDS):
            go(lift_ref.at[rows(f * 192 + half * 96, 96)], target.at[f, pl.ds(0, 96)])
    for t in range(3):
        cols = pl.ds(256 * t, 256)
        down_ref[:, cols] = mm_tn(m_ref[...], grad_ref[:, cols]).astype(BF16)
        proj_ref[:, cols] = mm_tn(o_ref[...], gb_ref[:, cols]).astype(BF16)
    for target, proj_target, half in sides:
        for f in range(SHARDS):
            for b in range(3):
                cols = pl.ds(b * D, D)
                go(proj_ref.at[rows(f * 192 + b * 64 + half * 32, 32)], proj_target.at[f, :, cols])
                go(down_ref.at[rows(f * 288 + b * 96 + half * 48, 48)], target.at[f, pl.ds(96, 48), cols])
    for copy in copies:
        copy.wait()


def add_up(parts):
    total = parts[0].astype(F32)
    for part in parts[1:]:
        total = total + part.astype(F32)
    return total.astype(BF16)


def rest_core_kernel(index, keep, other, *outs):
    for d, out in enumerate(outs):
        z = lax.rem(index[0] + d, 4)
        rows = pl.ds(pl.multiple_of(lax.div(z, 2) * 80, 16), 80)
        cols = pl.ds(pl.multiple_of(lax.rem(z, 2) * 1152, 128), 1152)
        for f in range(SHARDS):
            out[f] = add_up([keep[f, rows, cols], other[f, rows, cols]])


def rest_z_kernel(index, own, a, b, c, *outs):
    for d, out in enumerate(outs):
        f = lax.rem(index[1] + d, 4)
        out[...] = add_up([own[f], a[f], b[f], c[f]])


def qkv_core_kernel(index, keep, other, *outs):
    for d, out in enumerate(outs):
        f = lax.rem(index[1] + d, 4)
        out[...] = add_up([keep[f], other[f]])


def partial_kernel(a, b, out):
    out[...] = a[...].astype(F32) + b[...].astype(F32)


def qkv_y_kernel(index, some, b, c, out_0, out_1, out_2, out_3, total):
    total[...] = add_up([some[...], b[...], c[...]])
    for d, out in enumerate((out_0, out_1, out_2, out_3)):
        z = lax.rem(index[0] + d, 4)
        rows = pl.ds(pl.multiple_of(lax.div(z, 2) * 64, 16), 64)
        cols = pl.ds(pl.multiple_of(lax.rem(z, 2) * 1152, 128), 1152)
        out[:, pl.ds(0, 1152)] = total[rows, cols]
        out[:, pl.ds(1152, 128)] = total[pl.ds(0, 64), pl.ds(WIDE, 128)]


def joint_kernel(r0, r1, r2, r3, q0, q1, q2, q3, out):
    out[pl.ds(0, 80), :] = add_up([r0[...], r1[...], r2[...], r3[...]])
    cols, gains = pl.ds(0, 1152), (pl.ds(0, 16), pl.ds(1152, 128))
    out[pl.ds(80, 64), :] = add_up([q0[:, cols], q1[:, cols], q2[:, cols], q3[:, cols]])
    out[pl.ds(144, 16), :] = jnp.zeros((16, 1152), BF16)
    out[pl.ds(144, 16), pl.ds(0, 128)] = add_up([q0[gains], q1[gains], q2[gains], q3[gains]])


def pair_kernel(a, b, out):
    out[...] = add_up([a[...], b[...]])


def final_kernel(index, *refs):
    pieces, (qkv_out, proj_out, lift_out, down_out, gain_out, one, two) = refs[:8], refs[8:]
    core = index[2]
    rows = lambda at, size: pl.ds(pl.multiple_of(at, 16), size)
    for side in range(2):
        half = core if side == 0 else 1 - core
        for d in range(4):
            piece = pieces[4 * side + d]
            z = lax.rem(index[0] - d + 4, 4)
            cols = pl.ds(pl.multiple_of(lax.rem(z, 2) * 1152, 128), 1152)
            one[side, rows(lax.div(z, 2) * 80, 80), cols] = piece[pl.ds(0, 80), :]
            two[side, rows(lax.div(z, 2) * 64, 64), cols] = piece[pl.ds(80, 64), :]
        lift_out[rows(half * 96, 96), :] = one[side, pl.ds(0, 96), :].astype(F32)
        qkv_out[rows(half * 96, 96), :] = two[side, pl.ds(0, 96), :].astype(F32)
        for b in range(3):
            cols = pl.ds(b * D, D)
            proj_out[rows(b * 64 + half * 32, 32), :] = two[side, pl.ds(96, 32), cols].astype(F32)
            down_out[rows(b * 96 + half * 48, 48), :] = one[side, pl.ds(96, 48), cols].astype(F32)
    gain_out[...] = pieces[0][pl.ds(144, 16), pl.ds(0, 128)].astype(F32)


def call(kernel, name, ins, outs, scratch, flops, limit=24):
    places = {"v": pltpu.VMEM, "a": pl.ANY, "s": pltpu.SMEM}
    return pl.pallas_call(
        kernel,
        name=name,
        out_shape=[jax.ShapeDtypeStruct(out[0], out[1]) for out in outs],
        in_specs=[pl.BlockSpec(memory_space=places[place]) for _, place in ins],
        out_specs=[pl.BlockSpec(memory_space=places[out[2] if len(out) > 2 else "v"]) for out in outs],
        scratch_shapes=scratch,
        compiler_params=pltpu.CompilerParams(vmem_limit_bytes=limit * 2**20),
        cost_estimate=pl.CostEstimate(flops=flops, bytes_accessed=flops // 300, transcendentals=0),
    )(*[array for array, _ in ins])


def travel(block, target):
    pairs = []
    for ctx in range(16):
        for f in range(SHARDS):
            xlo, z, core, g = target(ctx // 8, ctx // 2 % 4, ctx % 2, f)
            pairs.append((ctx * SHARDS + f, (xlo * 8 + z % 4 * 2 + core) * SHARDS + g % 4))
    return lax.ppermute(block, ("ctx", "fsdp"), pairs)


def along_y(block, d):
    return travel(block, lambda x, z, c, f: (x, z, c, f + d))


def along_z(block, d):
    return travel(block, lambda x, z, c, f: (x, z + d, c, f))


def next_shard(block):
    return travel(block, lambda x, z, c, f: (x, z, c, f + 1 - 2 * c))


def swap_core(block):
    return travel(block, lambda x, z, c, f: (x, z, 1 - c, f))


def spread_quarter(block, across):
    return block, across, swap_core(block), swap_core(across)


def swap_x(block):
    return travel(block, lambda x, z, c, f: (1 - x, z, c, f))


def halo_rows(block, axis):
    count = lax.axis_size(axis)
    up = [(i, i + 1) for i in range(count - 1)]
    down = [(i + 1, i) for i in range(count - 1)]
    return (
        lax.ppermute(block[:, ROWS - HALF :], axis, up),
        lax.ppermute(block[:, :HALF], axis, down),
    )


def swap_halos(to_low, to_high):
    count = lax.axis_size("ctx")
    up = [(i, i + 1) for i in range(count - 1)]
    down = [(i + 1, i) for i in range(count - 1)]
    return lax.ppermute(to_high, "ctx", up), lax.ppermute(to_low, "ctx", down)


def tables(first_row, lengths):
    half = HD // 2
    frequencies = rope_base ** (-(jnp.arange(half, dtype=F32) * 2.0) / HD)
    positions = first_row - HALF + jnp.arange(EXT, dtype=jnp.int32)
    angles = positions.astype(F32)[:, None] * frequencies[None, :]
    cosine, sine = jnp.cos(angles), jnp.sin(angles)
    cosine = jnp.concatenate([cosine] * 4, axis=1)
    sine = jnp.concatenate([-sine, sine, -sine, sine], axis=1)
    ends = jnp.cumsum(lengths, axis=1)
    doc = jnp.sum((positions[None, :, None] >= ends[:, None, :]).astype(jnp.int32), axis=2)
    query = positions[HALF : HALF + ROWS]
    allowed = (
        (jnp.abs(query[None, :] - positions[:, None]) <= HALF)
        & (positions >= 0)[:, None]
        & (positions < SEQ_LEN)[:, None]
    )[None] & (doc[:, :, None] == doc[:, None, HALF : HALF + ROWS])
    bias = jnp.where(allowed, 0.0, masked_score).astype(F32)
    return cosine, sine, jnp.concatenate([bias, bias], axis=2)


WQKV, WPROJ, WLIFT, WDOWN = [
    pltpu.VMEM((D, WIDE), BF16),
    pltpu.VMEM((D, D), BF16),
    pltpu.VMEM((D, WIDE), BF16),
    pltpu.VMEM((FF, D), BF16),
]
SAVED = [
    ((OWN, D), BF16),
    ((MICRO * EXT, D), BF16),
    ((MICRO * EXT, D), BF16),
    ((MICRO, TILES, EXT, 2 * ROWS), BF16),
    ((OWN, D), BF16),
    ((OWN, D), F32),
    ((OWN, FF), BF16),
    ((OWN, FF), F32),
    ((OWN, FF), F32),
]
STREAM = [pltpu.VMEM((MICRO * EXT, D), BF16)] * 2
GRADS_OUT = [
    ((OWN, D), F32),
    ((OWN, D), BF16),
    ((OWN, 2 * D), F32),
    ((MICRO, HALF, 2 * D), BF16),
    ((MICRO, HALF, 2 * D), BF16),
]


TURN_OUT = [((MICRO, ROWS, D), BF16)] + SAVED + [((OWN, D), BF16)]
BACK_OUT = [((OWN, D), BF16), ((OWN, WIDE), BF16), ((OWN, D), BF16), ((OWN, D), BF16)]


def sems(count):
    return pltpu.SemaphoreType.DMA((count,))


def body(
    inputs, out_grad, doc_lengths, attn_gain, qkv_weight, proj_weight, mlp_gain, lift_weight, down_weight
):
    on_first = lax.axis_index("section") == 0
    flag = on_first.astype(jnp.int32).reshape(1)
    ctx, f = lax.axis_index("ctx"), lax.axis_index("fsdp")
    index = jnp.stack([ctx // 2 % 4, f, ctx % 2, ctx // 8]).astype(jnp.int32)
    qkv_shard, lift_shard, proj_shard, down_shard = qkv_weight[0], lift_weight[0], proj_weight[0], down_weight[0]
    own, cotangent = inputs[:, 0], out_grad[:, 0]
    gain_tile = jnp.pad(
        jnp.pad(jnp.stack([attn_gain[0], mlp_gain[0]]), ((0, 0), (0, 64))).reshape(4, 128), ((0, 12), (0, 0))
    )
    edge = ((MICRO, HALF, D), BF16)
    qkv_pack, qkv_half, first_rows, last_rows = call(
        pack_qkv_kernel, "pack_qkv",
        [(index, "s"), (qkv_shard, "v"), (gain_tile, "v"), (own, "v")],
        [((192, 2432), BF16), ((96, 2432), BF16), edge, edge],
        [], 0, 12,
    )
    rest, rest_quarter = call(
        pack_kernel, "pack_rest",
        [(index, "s"), (lift_shard, "v"), (proj_shard, "v"), (down_shard, "v")],
        [((352, WIDE), BF16), ((176, 1152), BF16)],
        [pltpu.VMEM((176, WIDE), BF16)], 0, 12,
    )
    first = next_shard(qkv_pack)
    second = along_y(qkv_half, 2)
    rest_second = along_y(rest_quarter, 2)
    cosine, sine, bias = tables(ctx * ROWS, doc_lengths[:, 0])
    first_rows, last_rows, cosine = lax.optimization_barrier((first_rows, last_rows, cosine))
    low, high = swap_halos(first_rows, last_rows)
    first, second, rest_second, rest, cosine, sine, bias, low, high = lax.optimization_barrier(
        (first, second, rest_second, rest, cosine, sine, bias, low, high)
    )
    rest_first = next_shard(rest)
    rest_x = swap_x(rest_second)
    qkv_pieces = first, swap_core(first), second, swap_core(second)
    stream = ((MICRO, ROWS, D), BF16)
    scratch = lambda items: [pltpu.VMEM(s, k) for s, k in items]

    o, gains, wqkv = call(
        forward_attention_kernel, "forward_attention",
        [(index, "s"), (own, "v"), (low, "v"), (high, "v"), (gain_tile, "a"), (cosine, "v"), (sine, "v"), (bias, "v"),
         (qkv_shard, "a"), *[(piece, "a") for piece in qkv_pieces]],
        [((OWN, D), BF16), ((2, D), F32), ((D, WIDE), BF16, "a")],
        [WQKV, pltpu.VMEM((SHARDS, 16, 128), BF16)] + STREAM + scratch(SAVED[:4]) + [sems(9), pltpu.SemaphoreType.DMA(())],
        1_400_000_000,
    )
    rest_first, rest_second, rest_x, o = lax.optimization_barrier((rest_first, rest_second, rest_x, o))
    rest_pieces = rest_first, swap_core(rest_first), *spread_quarter(rest_second, rest_x)
    rest_parts = [(part, "a") for part in (lift_shard, proj_shard, down_shard, *rest_pieces)]
    (relay,) = call(
        forward_mlp_kernel, "forward_mlp",
        [(index, "s"), (own, "v"), (o, "v"), (gains, "v"), *rest_parts],
        [stream],
        [WPROJ, WLIFT, WDOWN] + scratch([SAVED[5], SAVED[0], SAVED[6]]) + [sems(45)],
        1_800_000_000,
    )
    wlift, wproj, wdown = call(
        assemble_kernel, "assemble_weights",
        [(index, "s"), *rest_parts, (relay, "a")],
        [((D, WIDE), BF16, "a"), ((D, D), BF16, "a"), ((FF, D), BF16, "a")],
        [WLIFT, WPROJ, WDOWN, sems(48)], 1_800_000_000, 56,
    )
    relayed = lax.ppermute(relay, "section", [(0, 1)])
    relayed, wlift, wproj, wdown = lax.optimization_barrier((relayed, wlift, wproj, wdown))
    other_low, other_high = halo_rows(relayed, "ctx")
    (h3, q, k, v, p, o, h2, m_act, left, right, src, dh2, dq, dkv, to_low, to_high) = call(
        turning_kernel, "layer_turn",
        [(flag, "s"), (own, "v"), (low, "v"), (high, "v"), (relayed, "v"), (other_low, "v"), (other_high, "v"),
         (cotangent, "v"), (gains, "v"), (cosine, "v"), (sine, "v"), (bias, "v"),
         (wqkv, "a"), (wproj, "a"), (wlift, "a"), (wdown, "a")],
        [(*item, "a") for item in TURN_OUT] + GRADS_OUT,
        [WQKV, WPROJ, WLIFT, WDOWN] + STREAM
        + [pltpu.VMEM((MICRO, ROWS, D), BF16), pltpu.VMEM((OWN, WIDE), BF16), pltpu.VMEM((OWN, D), BF16)] + scratch(TURN_OUT) + [sems(15)],
        6_000_000_000, 44,
    )
    from_low, from_high = swap_halos(to_low, to_high)
    (grad_relay,) = call(
        source_kernel, "layer_source",
        [(src, "v"), (gains, "v"), (dh2, "v"), (dq, "v"), (dkv, "v"), (from_low, "v"), (from_high, "v"), (wqkv, "a")],
        [stream],
        [WQKV, pltpu.VMEM((OWN, WIDE), BF16), sems(1)],
        900_000_000,
    )
    incoming = lax.ppermute(grad_relay, "section", [(1, 0)])
    (grad_low, du, gb, b, mlp_gain_grad, dh2, dq, dkv, to_low, to_high) = call(
        back_kernel, "layer_back",
        [(flag, "s"), (incoming, "v"), (cotangent, "v"), (gains, "v"), (cosine, "v"), (sine, "v"),
         (wproj, "a"), (wlift, "a"), (wdown, "a"),
         *[(array, "a") for array in (q, k, v, p, h2, left, right)]],
        [(*item, "a") for item in BACK_OUT] + [((1, D), F32)] + GRADS_OUT,
        [WPROJ, WLIFT, WDOWN, pltpu.VMEM((OWN, D), BF16)]
        + scratch(SAVED[:4] + SAVED[5:6] + SAVED[7:] + BACK_OUT) + [sems(14)],
        3_000_000_000, 40,
    )
    from_low, from_high = swap_halos(to_low, to_high)
    rest_keep, rest_send, proj_keep, proj_send = call(
        weight_grad_kernel, "weight_grads",
        [(index, "s"), (m_act, "v"), (grad_low, "v"), (b, "v"), (du, "v"), (o, "v"), (gb, "v")],
        [((SHARDS, 160, WIDE), BF16, "a")] * 2 + [((SHARDS, 32, WIDE), BF16, "a")] * 2,
        [WDOWN, WLIFT, WPROJ, pltpu.VMEM((16, WIDE), BF16), sems(64)],
        1_600_000_000,
    )
    from_low, from_high, rest_send = lax.optimization_barrier((from_low, from_high, rest_send))
    rest_other = swap_core(rest_send)
    in_grad, qkv_keep, qkv_send = call(
        source_grad_kernel, "layer_source_grads",
        [(index, "s"), (src, "v"), (gains, "v"), (dh2, "v"), (dq, "v"), (dkv, "v"), (from_low, "v"),
         (from_high, "v"), (mlp_gain_grad, "v"), (proj_keep, "v"), (proj_send, "v"), (wqkv, "a")],
        [stream, ((SHARDS, 128, 2432), BF16, "a"), ((SHARDS, 128, 2432), BF16, "a")],
        [WQKV, pltpu.VMEM((OWN, WIDE), BF16), WQKV, pltpu.VMEM((SHARDS, 128, 128), BF16), sems(25)],
        1_800_000_000,
    )
    qkv_other = swap_core(qkv_send)

    rest_z = call(
        rest_core_kernel, "rest_core_sum", [(index, "s"), (rest_keep, "v"), (rest_other, "v")],
        [((SHARDS, 80, 1152), BF16)] * 4, [], 0, 24,
    )
    qkv_keep, _ = lax.optimization_barrier((qkv_keep, rest_z[0]))
    qkv_y = call(
        qkv_core_kernel, "qkv_core_sum", [(index, "s"), (qkv_keep, "v"), (qkv_other, "v")],
        [((128, 2432), BF16)] * 4, [], 0, 24,
    )
    (some,) = call(
        partial_kernel, "qkv_y_first", [(qkv_y[0], "v"), (along_y(qkv_y[1], 1), "v")],
        [((128, 2432), F32)], [], 0, 24,
    )
    rest_mine, some = lax.optimization_barrier((rest_z[0], some))
    rest_y = call(
        rest_z_kernel, "rest_z_sum",
        [(index, "s"), (rest_mine, "v"), *[(along_z(rest_z[d], d), "v") for d in (1, 2, 3)]],
        [((80, 1152), BF16)] * 4, [], 0, 24,
    )
    some, _ = lax.optimization_barrier((some, rest_y[0]))
    qkv_z = call(
        qkv_y_kernel, "qkv_y_sum",
        [(index, "s"), (some, "v"), *[(along_y(qkv_y[d], d), "v") for d in (2, 3)]],
        [((64, 1280), BF16)] * 4, [pltpu.VMEM((128, 2432), BF16)], 0, 24,
    )
    (joint,) = call(
        joint_kernel, "joint_sum",
        [(rest_y[0], "v"), *[(along_y(rest_y[d], d), "v") for d in (1, 2, 3)],
         (qkv_z[0], "v"), *[(along_z(qkv_z[d], d), "v") for d in (1, 2, 3)]],
        [((160, 1152), BF16)], [], 0, 24,
    )
    (joint,) = call(
        pair_kernel, "pair_sum", [(joint, "v"), (swap_x(joint), "v")], [((160, 1152), BF16)], [], 0, 24
    )
    mine = [joint] + [along_z(joint, d) for d in (1, 2, 3)]
    theirs = [swap_core(piece) for piece in mine]
    qkv_sum, proj_sum, lift_sum, down_sum, gain_sums = call(
        final_kernel, "final_shard", [(index, "s"), *[(piece, "v") for piece in mine + theirs]],
        [((192, WIDE), F32), ((192, D), F32), ((192, WIDE), F32), ((288, D), F32), ((16, 128), F32)],
        [pltpu.VMEM((2, 160, WIDE), BF16), pltpu.VMEM((2, 128, WIDE), BF16)], 0, 24,
    )
    return (
        h3[None, :, None],
        in_grad[None, :, None],
        gain_sums[0:2].reshape(1, 256)[:, :192],
        qkv_sum[None],
        proj_sum[None],
        gain_sums[2:4].reshape(1, 256)[:, :192],
        lift_sum[None],
        down_sum[None],
    )


def solution(mesh):
    placed = (
        P(None, "fsdp", "ctx", None),
        P(None, "fsdp", "ctx", None),
        P(None, "fsdp", None),
        P("section", "fsdp"),
        P("section", "fsdp", None),
        P("section", "fsdp", None),
        P("section", "fsdp"),
        P("section", "fsdp", None),
        P("section", "fsdp", None),
    )
    return jax.shard_map(
        body,
        mesh=mesh,
        in_specs=placed,
        out_specs=(
            P("section", None, "fsdp", "ctx", None),
            P("section", None, "fsdp", "ctx", None),
            P("section", "fsdp"),
            P("section", "fsdp", None),
            P("section", "fsdp", None),
            P("section", "fsdp"),
            P("section", "fsdp", None),
            P("section", "fsdp", None),
        ),
        check_vma=False,
    )
```

```python
import functools

import jax
import jax.numpy as jnp
from jax import lax
from jax.experimental import pallas as pl
from jax.experimental.pallas import tpu as pltpu
from jax.sharding import PartitionSpec as P

D = 768
HD = 64
HALF = 64
SEQ_LEN = 2048
FF = 1152
WIDE = 2304
ROWS = 128
EXT = ROWS + 2 * HALF
MICRO = 2
OWN = MICRO * ROWS
SHARDS = 4
TILES = D // 128
norm_eps = 1e-05
rope_base = 10000.0
masked_score = -1e30
root_half = 0.7071067811865476
inv_root_tau = 0.3989422804014327
F32 = jnp.float32
BF16 = jnp.bfloat16


def mm(left, right):
    return lax.dot_general(left, right, (((1,), (0,)), ((), ())), preferred_element_type=F32)


def mm_nt(left, right):
    return lax.dot_general(left, right, (((1,), (1,)), ((), ())), preferred_element_type=F32)


def mm_tn(left, right):
    return lax.dot_general(left, right, (((0,), (0,)), ((), ())), preferred_element_type=F32)


def norm_parts(hidden):
    centre = hidden - jnp.mean(hidden, axis=-1, keepdims=True)
    inv_scale = lax.rsqrt(jnp.mean(centre * centre, axis=-1, keepdims=True) + norm_eps)
    return centre * inv_scale, inv_scale


def norm_back(grad_out, gain, normed, inv_scale):
    grad_normed = grad_out * gain
    inner = (
        grad_normed
        - jnp.mean(grad_normed, axis=-1, keepdims=True)
        - normed * jnp.mean(grad_normed * normed, axis=-1, keepdims=True)
    )
    return inner * inv_scale


def lane_is_low(shape, period):
    return lax.broadcasted_iota(jnp.int32, shape, 1) % period < period // 2


def turn(x):
    return jnp.where(lane_is_low(x.shape, HD), pltpu.roll(x, 96, 1), pltpu.roll(x, 32, 1))


def rotate(x, cosine, sine):
    return x * cosine + turn(x) * sine


def rotate_back(x, cosine, sine):
    return x * cosine - turn(x) * sine


def stack_heads(x):
    low = lane_is_low(x.shape, 128)
    zero = jnp.zeros_like(x)
    return jnp.concatenate([jnp.where(low, x, zero), jnp.where(low, zero, x)], axis=0)


def join_heads(x):
    half = x.shape[0] // 2
    low = lane_is_low((half, 128), 128)
    return jnp.where(low, x[:half], x[half:])


def start_weights(sources, buffers, sems):
    waits = {}
    for index, (name, source) in enumerate(sources.items()):
        copy = pltpu.make_async_copy(source, buffers[name], sems.at[index])
        copy.start()
        waits[name] = [copy]
    return waits


def finish(waits, name):
    for copy in waits[name]:
        copy.wait()


def load_stream(flag, own, low, high, other, ext):
    for m in range(MICRO):
        for ref, alt, start, size in (
            (low, other[1], 0, HALF),
            (own, other[0], HALF, ROWS),
            (high, other[2], HALF + ROWS, HALF),
        ):
            value = ref[m]
            if alt is not None:
                value = jnp.where(flag, value, alt[m])
            ext[pl.ds(m * EXT + start, size), :] = value


def own_rows(x):
    return jnp.concatenate([x[HALF : HALF + ROWS], x[EXT + HALF : EXT + HALF + ROWS]], axis=0)


def repeat(count, step):
    lax.fori_loop(0, count, lambda i, carry: (step(i), carry)[1], 0)


def each(count, step):
    for i in range(count):
        step(i)


def span(start, size, unit=128):
    return pl.ds(start if isinstance(start, int) else pl.multiple_of(start, unit), size)


def by_tiles(unit, group):
    def step(i):
        for j in range(group):
            unit(i * group + j)

    repeat(TILES // group, step)


def norm_rows(source, gain, target):
    def step(i):
        rows = span(i * 128, 128)
        normed, _ = norm_parts(source[rows, :].astype(F32))
        target[rows, :] = (normed * gain).astype(BF16)

    repeat(source.shape[0] // 128, step)


def forward_attention(ext, gain, wqkv, cos_ref, sin_ref, bias_ref, a_ext, q_ref, k_ref, v_ref, p_ref, o_ref):
    norm_rows(ext, gain, a_ext)
    a_own = o_ref
    a_own[...] = own_rows(a_ext[...])
    own_span = pl.ds(HALF, ROWS)

    def project(t):
        cols = span(256 * t, 256)
        queries = mm(a_own[...], wqkv[:, cols])
        keys = mm(a_ext[...], wqkv[:, span(D + 256 * t, 256)])
        v_ref[:, cols] = mm(a_ext[...], wqkv[:, span(2 * D + 256 * t, 256)]).astype(BF16)
        for s in range(2):
            tile, lanes = span(256 * t + 128 * s, 128), slice(128 * s, 128 * s + 128)
            for m in range(MICRO):
                part = queries[m * ROWS : (m + 1) * ROWS, lanes]
                turned = rotate(part, cos_ref[own_span, :], sin_ref[own_span, :]).astype(BF16)
                q_ref[pl.ds(m * ROWS, ROWS), tile] = turned * jnp.asarray(0.125, BF16)
                part = keys[m * EXT : (m + 1) * EXT, lanes]
                k_ref[pl.ds(m * EXT, EXT), tile] = rotate(part, cos_ref[...], sin_ref[...]).astype(BF16)

    repeat(3, project)

    def unit(t):
        cols = pl.ds(pl.multiple_of(t * 128, 128), 128)
        for m in range(MICRO):
            q2 = stack_heads(q_ref[pl.ds(m * ROWS, ROWS), cols])
            scores = mm_nt(k_ref[pl.ds(m * EXT, EXT), cols], q2) + bias_ref[m]
            terms = jnp.exp(scores - jnp.max(scores, axis=0, keepdims=True))
            probs = (terms * (1.0 / jnp.sum(terms, axis=0, keepdims=True))).astype(BF16)
            p_ref[m, t] = probs
            attended = mm_tn(probs, v_ref[pl.ds(m * EXT, EXT), cols])
            o_ref[pl.ds(m * ROWS, ROWS), cols] = join_heads(attended).astype(BF16)

    by_tiles(unit, 3)


def forward_mlp(own, o_ref, wproj, mlp_gain, wlift, wdown, h2_ref, b_ref, m_ref, left_ref, right_ref, h3_ref, waits):
    finish(waits, "proj")

    def mix(t):
        cols = span(256 * t, 256)
        added = mm(o_ref[...], wproj[:, cols])
        for m in range(MICRO):
            rows = pl.ds(m * ROWS, ROWS)
            h2_ref[rows, cols] = own[m, :, cols].astype(F32) + added[m * ROWS : (m + 1) * ROWS]

    each(3, mix)
    norm_rows(h2_ref, mlp_gain, b_ref)
    finish(waits, "lift")

    def lift(t):
        cols = span(384 * t, 384)
        gate = mm(b_ref[...], wlift[:, cols])
        up = mm(b_ref[...], wlift[:, span(FF + 384 * t, 384)])
        cdf = 0.5 * (1.0 + lax.erf(gate * root_half))
        gelu = gate * cdf
        m_ref[:, cols] = (gelu * up).astype(BF16)
        if left_ref is not None:
            pdf = jnp.exp(-0.5 * gate * gate) * inv_root_tau
            left_ref[:, cols] = up * (cdf + gate * pdf)
            right_ref[:, cols] = gelu

    repeat(3, lift)
    finish(waits, "down")

    def down(t):
        cols = span(256 * t, 256)
        h3 = (h2_ref[:, cols] + mm(m_ref[...], wdown[:, cols])).astype(BF16)
        for m in range(MICRO):
            h3_ref[m, :, cols] = h3[m * ROWS : (m + 1) * ROWS]

    each(3, down)


def backward_mlp(grad_ref, h2_ref, mlp_gain, wproj, wlift, wdown, left_ref, right_ref, du_ref, gb_ref, do_ref,
                 dh2_ref, b_ref, mlp_ref):
    def lift(t):
        cols = span(384 * t, 384)
        dm = mm_nt(grad_ref[...], wdown[cols, :])
        du_ref[:, cols] = (dm * left_ref[:, cols]).astype(BF16)
        du_ref[:, span(FF + 384 * t, 384)] = (dm * right_ref[:, cols]).astype(BF16)

    each(3, lift)

    def source(t):
        rows = span(256 * t, 256)
        dh2_ref[:, rows] = mm_nt(du_ref[...], wlift[rows, :])

    each(3, source)
    if mlp_ref is not None:
        mlp_ref[...] = jnp.zeros_like(mlp_ref)

    def norm(i):
        rows = span(i * 128, 128)
        db = dh2_ref[rows, :]
        normed, inv_scale = norm_parts(h2_ref[rows, :])
        dh2 = grad_ref[rows, :].astype(F32) + norm_back(db, mlp_gain, normed, inv_scale)
        dh2_ref[rows, :] = dh2
        gb_ref[rows, :] = dh2.astype(BF16)
        if mlp_ref is not None:
            mlp_ref[...] += jnp.sum(db * normed, axis=0, keepdims=True)
            b_ref[rows, :] = (normed * mlp_gain).astype(BF16)

    repeat(2, norm)

    def attended(t):
        rows = span(256 * t, 256)
        do_ref[:, rows] = mm_nt(gb_ref[...], wproj[rows, :]).astype(BF16)

    each(3, attended)


def backward_attention(q_ref, k_ref, v_ref, p_ref, do_ref, cos_ref, sin_ref, dq_ref, dkv_ref, low_ref, high_ref, group):
    cosine, sine = cos_ref[...], sin_ref[...]
    cos_own, sin_own = cosine[HALF : HALF + ROWS], sine[HALF : HALF + ROWS]

    def unit(t):
        cols = pl.ds(pl.multiple_of(t * 128, 128), 128)
        value_cols = pl.ds(pl.multiple_of(D + t * 128, 128), 128)
        for m in range(MICRO):
            rows = pl.ds(m * ROWS, ROWS)
            q2 = stack_heads(q_ref[rows, cols])
            do2 = stack_heads(do_ref[rows, cols])
            probs = p_ref[m, t]
            dprobs = mm_nt(v_ref[pl.ds(m * EXT, EXT), cols], do2)
            wide = probs.astype(F32)
            inner = jnp.sum(wide * dprobs, axis=0, keepdims=True)
            ds = (wide * (dprobs - inner)).astype(BF16)
            dq = join_heads(mm_tn(ds, k_ref[pl.ds(m * EXT, EXT), cols])) * 0.125
            dq_ref[rows, cols] = rotate_back(dq, cos_own, sin_own).astype(BF16)
            dk = rotate_back(mm(ds, q2), cosine, sine)
            dv = mm(probs, do2)
            for grad, where in ((dk, cols), (dv, value_cols)):
                low_ref[m, :, where] = grad[:HALF].astype(BF16)
                dkv_ref[rows, where] = grad[HALF : HALF + ROWS]
                high_ref[m, :, where] = grad[HALF + ROWS :].astype(BF16)

    by_tiles(unit, group)


def place_shards(index, own, pieces, put):
    f, core, xlo = index[1], index[2], index[3]
    first, first_other, second, second_x, second_core, second_both = pieces
    put(own, f, None, None)
    put(first, lax.rem(f + 3 + 2 * core, 4), None, None)
    put(first_other, lax.rem(f + 1 + 2 * core, 4), None, None)
    across = lax.rem(f + 2, 4)
    put(second, across, core, xlo)
    put(second_x, across, core, 1 - xlo)
    put(second_core, across, 1 - core, xlo)
    put(second_both, across, 1 - core, 1 - xlo)


def pack_qkv_kernel(index, qkv, gains, own, whole, half, first_rows, last_rows):
    rows = pl.ds(pl.multiple_of(index[2] * 96, 16), 96)
    whole[:, pl.ds(0, WIDE)] = qkv[...]
    half[:, pl.ds(0, WIDE)] = qkv[rows, :]
    whole[:, pl.ds(WIDE, 128)] = jnp.zeros((192, 128), BF16)
    half[:, pl.ds(WIDE, 128)] = jnp.zeros((96, 128), BF16)
    whole[pl.ds(0, 16), pl.ds(WIDE, 128)] = gains[...]
    half[pl.ds(0, 16), pl.ds(WIDE, 128)] = gains[...]
    first_rows[...] = own[:, :HALF]
    last_rows[...] = own[:, ROWS - HALF :]


def pack_kernel(index, lift, proj, down, rest, quarter, half):
    core = index[2]
    rows = lambda at, size: pl.ds(pl.multiple_of(at, 16), size)
    rest[pl.ds(0, 192), :] = lift[...]
    half[pl.ds(0, 96), :] = lift[rows(core * 96, 96), :]
    for b in range(3):
        cols = pl.ds(b * D, D)
        rest[pl.ds(192, 64), cols] = proj[pl.ds(64 * b, 64), :]
        rest[pl.ds(256, 96), cols] = down[pl.ds(96 * b, 96), :]
        half[pl.ds(96, 32), cols] = proj[rows(64 * b + core * 32, 32), :]
        half[pl.ds(128, 48), cols] = down[rows(96 * b + core * 48, 48), :]
    quarter[...] = half[:, pl.ds(pl.multiple_of(index[3] * 1152, 128), 1152)]


def gather_gain(tiles, row):
    parts = []
    for tile in tiles:
        parts += [tile[row : row + 1, :], tile[row + 1 : row + 2, :64]]
    return jnp.concatenate(parts, axis=1)


def forward_attention_kernel(index, own, low, high, gain_tile, cos_ref, sin_ref, bias_ref,
                             shard, first, first_other, second, second_core,
                             o, gains, whole, wqkv, tiles, ext, a_ext, q, k, v, p, sems, out_sem):
    copies = []

    def go(src, dst):
        copy = pltpu.make_async_copy(src, dst, sems.at[len(copies)])
        copy.start()
        copies.append(copy)

    def put(piece, f, half, side):
        if piece is None:
            return
        at, size = (f * 192, 192) if half is None else (f * 192 + half * 96, 96)
        rows = pl.ds(pl.multiple_of(at, 16), size)
        go(piece if piece is shard else piece.at[:, pl.ds(0, WIDE)], wqkv.at[rows])
        if piece is not shard and piece is not second_core:
            go(piece.at[pl.ds(0, 16), pl.ds(WIDE, 128)], tiles.at[f])

    place_shards(index, shard, (first, first_other, second, None, second_core, None), put)
    go(gain_tile, tiles.at[index[1]])
    load_stream(None, own, low, high, (None, None, None), ext)
    for copy in copies:
        copy.wait()
    out = pltpu.make_async_copy(wqkv, whole, out_sem)
    out.start()
    shards = [tiles[f].astype(F32) for f in range(SHARDS)]
    gains[0:1, :] = gather_gain(shards, 0)
    gains[1:2, :] = gather_gain(shards, 2)
    forward_attention(ext, gains[0:1], wqkv, cos_ref, sin_ref, bias_ref, a_ext, q, k, v, p, o)
    out.wait()


def place_rest(index, lift, proj, down, pieces, wlift, wproj, wdown, go):
    f = index[1]
    rows = lambda at, size: pl.ds(pl.multiple_of(at, 16), size)
    lanes = lambda at, size: pl.ds(pl.multiple_of(at, 128), size)

    def put(piece, s, half, side):
        if piece is None:
            go("proj", proj, wproj.at[rows(f * 192, 192)])
            go("lift", lift, wlift.at[rows(f * 192, 192)])
            go("down", down, wdown.at[rows(f * 288, 288)])
        elif half is None:
            go("lift", piece.at[pl.ds(0, 192)], wlift.at[rows(s * 192, 192)])
            for b in range(3):
                cols = pl.ds(b * D, D)
                go("proj", piece.at[pl.ds(192, 64), cols], wproj.at[rows(s * 192 + b * 64, 64)])
                go("down", piece.at[pl.ds(256, 96), cols], wdown.at[rows(s * 288 + b * 96, 96)])
        else:
            go("lift", piece.at[pl.ds(0, 96)], wlift.at[rows(s * 192 + half * 96, 96), lanes(side * 1152, 1152)])
            for j in range(3):
                cols = pl.ds(j * 384, 384)
                b, right = lax.div(3 * side + j, 2), lanes(lax.rem(3 * side + j, 2) * 384, 384)
                go("proj", piece.at[pl.ds(96, 32), cols], wproj.at[rows(s * 192 + b * 64 + half * 32, 32), right])
                go("down", piece.at[pl.ds(128, 48), cols], wdown.at[rows(s * 288 + b * 96 + half * 48, 48), right])

    place_shards(index, None, pieces, put)


def starter(sems, waits):
    count = [0]

    def go(name, src, dst):
        copy = pltpu.make_async_copy(src, dst, sems.at[count[0]])
        copy.start()
        count[0] += 1
        waits.setdefault(name, []).append(copy)

    return go


def forward_mlp_kernel(index, own, o, gains, lift, proj, down, *refs):
    pieces, (h3_ref, wproj, wlift, wdown, h2, b, m_out, sems) = refs[:6], refs[6:]
    waits = {}
    place_rest(index, lift, proj, down, pieces, wlift, wproj, wdown, starter(sems, waits))
    forward_mlp(own, o, wproj, gains[1:2], wlift, wdown, h2, b, m_out, None, None, h3_ref, waits)


def assemble_kernel(index, lift, proj, down, *refs):
    pieces, (whole_lift, whole_proj, whole_down, wlift, wproj, wdown, sems) = refs[:6], refs[7:]
    waits = {}
    go = starter(sems, waits)
    place_rest(index, lift, proj, down, pieces, wlift, wproj, wdown, go)
    for name, buffer, whole in (("lift", wlift, whole_lift), ("proj", wproj, whole_proj), ("down", wdown, whole_down)):
        finish(waits, name)
        go("out", buffer, whole)
    finish(waits, "out")


def start_all(pairs, sems, first):
    copies = [pltpu.make_async_copy(src, dst, sems.at[first + n]) for n, (src, dst) in enumerate(pairs)]
    for copy in copies:
        copy.start()
    return copies


def turning_kernel(flag_ref, own, low, high, other_own, other_low, other_high, cotangent, gains,
                   cos_ref, sin_ref, bias_ref, qkv_hbm, proj_hbm, lift_hbm, down_hbm, *refs):
    kept, (dh2_ref, dq, dkv, to_low, to_high) = refs[:11], refs[11:16]
    wqkv, wproj, wlift, wdown, ext, a_ext, mine, du, do, h3_ref, q, k, v, p, o, h2, m_out, left, right, src, sems = refs[16:]
    waits = start_weights(
        {"qkv": qkv_hbm, "proj": proj_hbm, "lift": lift_hbm, "down": down_hbm},
        {"qkv": wqkv, "proj": wproj, "lift": wlift, "down": wdown}, sems,
    )
    flag = flag_ref[0] == 1
    load_stream(flag, own, low, high, (other_own, other_low, other_high), ext)
    for m in range(MICRO):
        mine[m] = ext[pl.ds(m * EXT + HALF, ROWS), :]
        src[pl.ds(m * ROWS, ROWS), :] = mine[m]
    finish(waits, "qkv")
    forward_attention(ext, gains[0:1], wqkv, cos_ref, sin_ref, bias_ref, a_ext, q, k, v, p, o)
    outs = start_all(zip((q, k, v, p, o, src), kept[1:6] + kept[10:]), sems, 4)
    spare = a_ext.at[pl.ds(0, OWN)]
    forward_mlp(mine, o, wproj, gains[1:2], wlift, wdown, h2, spare, m_out, left, right, h3_ref, waits)
    outs += start_all(zip((h3_ref, h2, m_out, left, right), kept[:1] + kept[6:10]), sems, 10)
    grad = a_ext.at[pl.ds(OWN, OWN)]
    for m in range(MICRO):
        grad[pl.ds(m * ROWS, ROWS), :] = cotangent[m]
    backward_mlp(grad, h2, gains[1:2], wproj, wlift, wdown, left, right, du, spare, do, dh2_ref, None, None)
    backward_attention(q, k, v, p, do, cos_ref, sin_ref, dq, dkv, to_low, to_high, 3)
    for copy in outs:
        copy.wait()


def back_kernel(flag_ref, incoming, cotangent, gains, cos_ref, sin_ref, proj_hbm, lift_hbm, down_hbm,
                q_hbm, k_hbm, v_hbm, p_hbm, h2_hbm, left_hbm, right_hbm, *refs):
    kept, (mlp_ref, dh2_ref, dq, dkv, to_low, to_high) = refs[:4], refs[4:10]
    wproj, wlift, wdown, do, q, k, v, p, h2, left, right, grad_ref, du, gb_ref, b_ref, sems = refs[10:]
    early = start_all(
        ((down_hbm, wdown), (left_hbm, left), (right_hbm, right), (lift_hbm, wlift), (h2_hbm, h2), (proj_hbm, wproj)),
        sems, 0,
    )
    late = start_all(((q_hbm, q), (v_hbm, v), (p_hbm, p), (k_hbm, k)), sems, 6)
    flag = flag_ref[0] == 1
    for m in range(MICRO):
        grad_ref[pl.ds(m * ROWS, ROWS), :] = jnp.where(flag, incoming[m], cotangent[m])
    for copy in early:
        copy.wait()
    backward_mlp(
        grad_ref, h2, gains[1:2], wproj, wlift, wdown, left, right, du, gb_ref, do, dh2_ref, b_ref, mlp_ref
    )
    outs = start_all(zip((grad_ref, du, gb_ref, b_ref), kept), sems, 10)
    for copy in late:
        copy.wait()
    backward_attention(q, k, v, p, do, cos_ref, sin_ref, dq, dkv, to_low, to_high, 6)
    for copy in outs:
        copy.wait()


def joined_grads(dq, dkv, from_low, from_high, dqkv):
    dqkv[:, :D] = dq[...]
    for m in range(MICRO):
        first, last = pl.ds(m * ROWS, HALF), pl.ds(m * ROWS + HALF, HALF)
        dqkv[first, D:] = (dkv[first, :] + from_low[m].astype(F32)).astype(BF16)
        dqkv[last, D:] = (dkv[last, :] + from_high[m].astype(F32)).astype(BF16)


def source_kernel(src, gains, dh2, dq, dkv, from_low, from_high, qkv_hbm, out_ref, wqkv, dqkv, sems):
    waits = start_weights({"qkv": qkv_hbm}, {"qkv": wqkv}, sems)
    joined_grads(dq, dkv, from_low, from_high, dqkv)
    normed, inv_scale = norm_parts(src[...].astype(F32))
    finish(waits, "qkv")
    da = mm_nt(dqkv[...], wqkv[...])
    dh = dh2[...] + norm_back(da, gains[0:1], normed, inv_scale)
    for m in range(MICRO):
        out_ref[m] = dh[m * ROWS : (m + 1) * ROWS].astype(BF16)


def gain_block(attn, mlp, f):
    rows = []
    for gain in (attn, mlp):
        rows.append(gain[:, 192 * f : 192 * f + 128])
        rows.append(jnp.concatenate([gain[:, 192 * f + 128 : 192 * f + 192], jnp.zeros((1, 64), F32)], axis=1))
    return jnp.concatenate(rows + [jnp.zeros((92, 128), F32)], axis=0).astype(BF16)


def source_grad_kernel(index, src, gains, dh2, dq, dkv, from_low, from_high, mlp_grad, qkv_hbm,
                       out_ref, keep, send, wqkv, dqkv, qkv_ref, gain_ref, sems):
    waits = start_weights({"qkv": qkv_hbm}, {"qkv": wqkv}, sems)
    joined_grads(dq, dkv, from_low, from_high, dqkv)
    normed, inv_scale = norm_parts(src[...].astype(F32))
    finish(waits, "qkv")
    da = mm_nt(dqkv[...], wqkv[...])
    attn_grad = jnp.sum(da * normed, axis=0, keepdims=True)
    mlp = mlp_grad[...]
    for f in range(SHARDS):
        gain_ref[f] = gain_block(attn_grad, mlp, f)
    a = (normed * gains[0:1]).astype(BF16)
    for t in range(9):
        cols = pl.ds(256 * t, 256)
        qkv_ref[:, cols] = mm_tn(a, dqkv[:, cols]).astype(BF16)
    copies = []
    for target, half in ((send, 1 - index[2]), (keep, index[2])):
        for f in range(SHARDS):
            rows = pl.ds(pl.multiple_of(f * 192 + half * 96, 16), 96)
            for src_ref, dst_ref in (
                (qkv_ref.at[rows], target.at[f, :, pl.ds(0, WIDE)]),
                (gain_ref.at[f], target.at[f, :, pl.ds(WIDE, 128)]),
            ):
                copy = pltpu.make_async_copy(src_ref, dst_ref, sems.at[1 + len(copies)])
                copy.start()
                copies.append(copy)
    dh = dh2[...] + norm_back(da, gains[0:1], normed, inv_scale)
    for m in range(MICRO):
        out_ref[m] = dh[m * ROWS : (m + 1) * ROWS].astype(BF16)
    for copy in copies:
        copy.wait()


def weight_grad_kernel(index, m_ref, grad_ref, b_ref, du, o_ref, gb_ref, keep, send,
                       down_ref, lift_ref, proj_ref, pad_ref, sems):
    core = index[2]
    copies = []

    def go(src, dst):
        copy = pltpu.make_async_copy(src, dst, sems.at[len(copies)])
        copy.start()
        copies.append(copy)

    sides = ((send, 1 - core), (keep, core))
    rows = lambda at, size: pl.ds(pl.multiple_of(at, 16), size)
    pad_ref[...] = jnp.zeros_like(pad_ref)
    for target, _ in sides:
        for f in range(SHARDS):
            go(pad_ref, target.at[f, pl.ds(176, 16)])
    for t in range(9):
        cols = pl.ds(256 * t, 256)
        lift_ref[:, cols] = mm_tn(b_ref[...], du[:, cols]).astype(BF16)
    for target, half in sides:
        for f in range(SHARDS):
            go(lift_ref.at[rows(f * 192 + half * 96, 96)], target.at[f, pl.ds(0, 96)])
    for t in range(3):
        cols = pl.ds(256 * t, 256)
        down_ref[:, cols] = mm_tn(m_ref[...], grad_ref[:, cols]).astype(BF16)
        proj_ref[:, cols] = mm_tn(o_ref[...], gb_ref[:, cols]).astype(BF16)
    for target, half in sides:
        for f in range(SHARDS):
            for b in range(3):
                cols = pl.ds(b * D, D)
                go(proj_ref.at[rows(f * 192 + b * 64 + half * 32, 32)], target.at[f, pl.ds(96, 32), cols])
                go(down_ref.at[rows(f * 288 + b * 96 + half * 48, 48)], target.at[f, pl.ds(128, 48), cols])
    for copy in copies:
        copy.wait()


def add_up(parts):
    total = parts[0].astype(F32)
    for part in parts[1:]:
        total = total + part.astype(F32)
    return total.astype(BF16)


def rest_core_kernel(index, keep, other, *outs):
    for d, out in enumerate(outs):
        rows = pl.ds(pl.multiple_of(lax.rem(index[0] + d, 4) * 48, 16), 48)
        for f in range(SHARDS):
            out[f] = add_up([keep[f, rows, :], other[f, rows, :]])


def rest_z_kernel(index, own, a, b, c, *outs):
    for d, out in enumerate(outs):
        f = lax.rem(index[1] + d, 4)
        out[...] = add_up([own[f], a[f], b[f], c[f]])


def qkv_core_kernel(index, keep, other, *outs):
    for d, out in enumerate(outs):
        f = lax.rem(index[1] + d, 4)
        out[...] = add_up([keep[f], other[f]])


def partial_kernel(a, b, out):
    out[...] = a[...].astype(F32) + b[...].astype(F32)


def qkv_y_kernel(index, some, b, c, out_0, out_1, out_2, out_3, total):
    total[...] = add_up([some[...], b[...], c[...]])
    for d, out in enumerate((out_0, out_1, out_2, out_3)):
        z = lax.rem(index[0] + d, 4)
        rows = pl.ds(pl.multiple_of(lax.div(z, 2) * 48, 16), 48)
        cols = pl.ds(pl.multiple_of(lax.rem(z, 2) * 1152, 128), 1152)
        out[:, pl.ds(0, 1152)] = total[rows, cols]
        out[:, pl.ds(1152, 128)] = total[pl.ds(0, 48), pl.ds(WIDE, 128)]


def joint_kernel(r0, r1, r2, r3, q0, q1, q2, q3, out):
    out[:, pl.ds(0, WIDE)] = add_up([r0[...], r1[...], r2[...], r3[...]])
    out[:, pl.ds(WIDE, 1280)] = add_up([q0[...], q1[...], q2[...], q3[...]])


def pair_kernel(a, b, out):
    out[...] = add_up([a[...], b[...]])


def final_kernel(index, *refs):
    pieces, (qkv_out, proj_out, lift_out, down_out, gain_out, rest) = refs[:8], refs[8:]
    core = index[2]
    for side in range(2):
        half = core if side == 0 else 1 - core
        for d in range(4):
            piece = pieces[4 * side + d]
            z = lax.rem(index[0] - d + 4, 4)
            rest[side, pl.ds(pl.multiple_of(z * 48, 16), 48), :] = piece[:, pl.ds(0, WIDE)]
            qkv_out[
                pl.ds(pl.multiple_of(half * 96 + lax.div(z, 2) * 48, 16), 48),
                pl.ds(pl.multiple_of(lax.rem(z, 2) * 1152, 128), 1152),
            ] = piece[:, pl.ds(WIDE, 1152)].astype(F32)
        rows = lambda at, size: pl.ds(pl.multiple_of(at, 16), size)
        lift_out[rows(half * 96, 96), :] = rest[side, pl.ds(0, 96), :].astype(F32)
        for b in range(3):
            cols = pl.ds(b * D, D)
            proj_out[rows(b * 64 + half * 32, 32), :] = rest[side, pl.ds(96, 32), cols].astype(F32)
            down_out[rows(b * 96 + half * 48, 48), :] = rest[side, pl.ds(128, 48), cols].astype(F32)
    gain_out[...] = pieces[0][pl.ds(0, 16), pl.ds(WIDE + 1152, 128)].astype(F32)


def call(kernel, name, ins, outs, scratch, flops, limit=24):
    places = {"v": pltpu.VMEM, "a": pl.ANY, "s": pltpu.SMEM}
    return pl.pallas_call(
        kernel,
        name=name,
        out_shape=[jax.ShapeDtypeStruct(out[0], out[1]) for out in outs],
        in_specs=[pl.BlockSpec(memory_space=places[place]) for _, place in ins],
        out_specs=[pl.BlockSpec(memory_space=places[out[2] if len(out) > 2 else "v"]) for out in outs],
        scratch_shapes=scratch,
        compiler_params=pltpu.CompilerParams(vmem_limit_bytes=limit * 2**20),
        cost_estimate=pl.CostEstimate(flops=flops, bytes_accessed=flops // 300, transcendentals=0),
    )(*[array for array, _ in ins])


def travel(block, target):
    pairs = []
    for ctx in range(16):
        for f in range(SHARDS):
            xlo, z, core, g = target(ctx // 8, ctx // 2 % 4, ctx % 2, f)
            pairs.append((ctx * SHARDS + f, (xlo * 8 + z % 4 * 2 + core) * SHARDS + g % 4))
    return lax.ppermute(block, ("ctx", "fsdp"), pairs)


def along_y(block, d):
    return travel(block, lambda x, z, c, f: (x, z, c, f + d))


def along_z(block, d):
    return travel(block, lambda x, z, c, f: (x, z + d, c, f))


def next_shard(block):
    return travel(block, lambda x, z, c, f: (x, z, c, f + 1 - 2 * c))


def swap_core(block):
    return travel(block, lambda x, z, c, f: (x, z, 1 - c, f))


def spread_quarter(block, across):
    return block, across, swap_core(block), swap_core(across)


def swap_x(block):
    return travel(block, lambda x, z, c, f: (1 - x, z, c, f))


def halo_rows(block, axis):
    count = lax.axis_size(axis)
    up = [(i, i + 1) for i in range(count - 1)]
    down = [(i + 1, i) for i in range(count - 1)]
    return (
        lax.ppermute(block[:, ROWS - HALF :], axis, up),
        lax.ppermute(block[:, :HALF], axis, down),
    )


def swap_halos(to_low, to_high):
    count = lax.axis_size("ctx")
    up = [(i, i + 1) for i in range(count - 1)]
    down = [(i + 1, i) for i in range(count - 1)]
    return lax.ppermute(to_high, "ctx", up), lax.ppermute(to_low, "ctx", down)


def tables(first_row, lengths):
    half = HD // 2
    frequencies = rope_base ** (-(jnp.arange(half, dtype=F32) * 2.0) / HD)
    positions = first_row - HALF + jnp.arange(EXT, dtype=jnp.int32)
    angles = positions.astype(F32)[:, None] * frequencies[None, :]
    cosine, sine = jnp.cos(angles), jnp.sin(angles)
    cosine = jnp.concatenate([cosine] * 4, axis=1)
    sine = jnp.concatenate([-sine, sine, -sine, sine], axis=1)
    ends = jnp.cumsum(lengths, axis=1)
    doc = jnp.sum((positions[None, :, None] >= ends[:, None, :]).astype(jnp.int32), axis=2)
    query = positions[HALF : HALF + ROWS]
    allowed = (
        (jnp.abs(query[None, :] - positions[:, None]) <= HALF)
        & (positions >= 0)[:, None]
        & (positions < SEQ_LEN)[:, None]
    )[None] & (doc[:, :, None] == doc[:, None, HALF : HALF + ROWS])
    bias = jnp.where(allowed, 0.0, masked_score).astype(F32)
    return cosine, sine, jnp.concatenate([bias, bias], axis=2)


WQKV, WPROJ, WLIFT, WDOWN = [
    pltpu.VMEM((D, WIDE), BF16),
    pltpu.VMEM((D, D), BF16),
    pltpu.VMEM((D, WIDE), BF16),
    pltpu.VMEM((FF, D), BF16),
]
SAVED = [
    ((OWN, D), BF16),
    ((MICRO * EXT, D), BF16),
    ((MICRO * EXT, D), BF16),
    ((MICRO, TILES, EXT, 2 * ROWS), BF16),
    ((OWN, D), BF16),
    ((OWN, D), F32),
    ((OWN, FF), BF16),
    ((OWN, FF), F32),
    ((OWN, FF), F32),
]
STREAM = [pltpu.VMEM((MICRO * EXT, D), BF16)] * 2
GRADS_OUT = [
    ((OWN, D), F32),
    ((OWN, D), BF16),
    ((OWN, 2 * D), F32),
    ((MICRO, HALF, 2 * D), BF16),
    ((MICRO, HALF, 2 * D), BF16),
]


TURN_OUT = [((MICRO, ROWS, D), BF16)] + SAVED + [((OWN, D), BF16)]
BACK_OUT = [((OWN, D), BF16), ((OWN, WIDE), BF16), ((OWN, D), BF16), ((OWN, D), BF16)]


def sems(count):
    return pltpu.SemaphoreType.DMA((count,))


def body(
    inputs, out_grad, doc_lengths, attn_gain, qkv_weight, proj_weight, mlp_gain, lift_weight, down_weight
):
    on_first = lax.axis_index("section") == 0
    flag = on_first.astype(jnp.int32).reshape(1)
    ctx, f = lax.axis_index("ctx"), lax.axis_index("fsdp")
    index = jnp.stack([ctx // 2 % 4, f, ctx % 2, ctx // 8]).astype(jnp.int32)
    qkv_shard, lift_shard, proj_shard, down_shard = qkv_weight[0], lift_weight[0], proj_weight[0], down_weight[0]
    own, cotangent = inputs[:, 0], out_grad[:, 0]
    gain_tile = jnp.pad(
        jnp.pad(jnp.stack([attn_gain[0], mlp_gain[0]]), ((0, 0), (0, 64))).reshape(4, 128), ((0, 12), (0, 0))
    )
    edge = ((MICRO, HALF, D), BF16)
    qkv_pack, qkv_half, first_rows, last_rows = call(
        pack_qkv_kernel, "pack_qkv",
        [(index, "s"), (qkv_shard, "v"), (gain_tile, "v"), (own, "v")],
        [((192, 2432), BF16), ((96, 2432), BF16), edge, edge],
        [], 0, 12,
    )
    rest, rest_quarter = call(
        pack_kernel, "pack_rest",
        [(index, "s"), (lift_shard, "v"), (proj_shard, "v"), (down_shard, "v")],
        [((352, WIDE), BF16), ((176, 1152), BF16)],
        [pltpu.VMEM((176, WIDE), BF16)], 0, 12,
    )
    first = next_shard(qkv_pack)
    second = along_y(qkv_half, 2)
    rest_second = along_y(rest_quarter, 2)
    cosine, sine, bias = tables(ctx * ROWS, doc_lengths[:, 0])
    first_rows, last_rows, cosine = lax.optimization_barrier((first_rows, last_rows, cosine))
    low, high = swap_halos(first_rows, last_rows)
    first, second, rest_second, rest, cosine, sine, bias, low, high = lax.optimization_barrier(
        (first, second, rest_second, rest, cosine, sine, bias, low, high)
    )
    rest_first = next_shard(rest)
    rest_x = swap_x(rest_second)
    qkv_pieces = first, swap_core(first), second, swap_core(second)
    stream = ((MICRO, ROWS, D), BF16)
    scratch = lambda items: [pltpu.VMEM(s, k) for s, k in items]

    o, gains, wqkv = call(
        forward_attention_kernel, "forward_attention",
        [(index, "s"), (own, "v"), (low, "v"), (high, "v"), (gain_tile, "a"), (cosine, "v"), (sine, "v"), (bias, "v"),
         (qkv_shard, "a"), *[(piece, "a") for piece in qkv_pieces]],
        [((OWN, D), BF16), ((2, D), F32), ((D, WIDE), BF16, "a")],
        [WQKV, pltpu.VMEM((SHARDS, 16, 128), BF16)] + STREAM + scratch(SAVED[:4]) + [sems(9), pltpu.SemaphoreType.DMA(())],
        1_400_000_000,
    )
    rest_first, rest_second, rest_x, o = lax.optimization_barrier((rest_first, rest_second, rest_x, o))
    rest_pieces = rest_first, swap_core(rest_first), *spread_quarter(rest_second, rest_x)
    rest_parts = [(part, "a") for part in (lift_shard, proj_shard, down_shard, *rest_pieces)]
    (relay,) = call(
        forward_mlp_kernel, "forward_mlp",
        [(index, "s"), (own, "v"), (o, "v"), (gains, "v"), *rest_parts],
        [stream],
        [WPROJ, WLIFT, WDOWN] + scratch([SAVED[5], SAVED[0], SAVED[6]]) + [sems(45)],
        1_800_000_000,
    )
    wlift, wproj, wdown = call(
        assemble_kernel, "assemble_weights",
        [(index, "s"), *rest_parts, (relay, "a")],
        [((D, WIDE), BF16, "a"), ((D, D), BF16, "a"), ((FF, D), BF16, "a")],
        [WLIFT, WPROJ, WDOWN, sems(48)], 1_800_000_000, 56,
    )
    relayed = lax.ppermute(relay, "section", [(0, 1)])
    relayed, wlift, wproj, wdown = lax.optimization_barrier((relayed, wlift, wproj, wdown))
    other_low, other_high = halo_rows(relayed, "ctx")
    (h3, q, k, v, p, o, h2, m_act, left, right, src, dh2, dq, dkv, to_low, to_high) = call(
        turning_kernel, "layer_turn",
        [(flag, "s"), (own, "v"), (low, "v"), (high, "v"), (relayed, "v"), (other_low, "v"), (other_high, "v"),
         (cotangent, "v"), (gains, "v"), (cosine, "v"), (sine, "v"), (bias, "v"),
         (wqkv, "a"), (wproj, "a"), (wlift, "a"), (wdown, "a")],
        [(*item, "a") for item in TURN_OUT] + GRADS_OUT,
        [WQKV, WPROJ, WLIFT, WDOWN] + STREAM
        + [pltpu.VMEM((MICRO, ROWS, D), BF16), pltpu.VMEM((OWN, WIDE), BF16), pltpu.VMEM((OWN, D), BF16)] + scratch(TURN_OUT) + [sems(15)],
        6_000_000_000, 44,
    )
    from_low, from_high = swap_halos(to_low, to_high)
    (grad_relay,) = call(
        source_kernel, "layer_source",
        [(src, "v"), (gains, "v"), (dh2, "v"), (dq, "v"), (dkv, "v"), (from_low, "v"), (from_high, "v"), (wqkv, "a")],
        [stream],
        [WQKV, pltpu.VMEM((OWN, WIDE), BF16), sems(1)],
        900_000_000,
    )
    incoming = lax.ppermute(grad_relay, "section", [(1, 0)])
    (grad_low, du, gb, b, mlp_gain_grad, dh2, dq, dkv, to_low, to_high) = call(
        back_kernel, "layer_back",
        [(flag, "s"), (incoming, "v"), (cotangent, "v"), (gains, "v"), (cosine, "v"), (sine, "v"),
         (wproj, "a"), (wlift, "a"), (wdown, "a"),
         *[(array, "a") for array in (q, k, v, p, h2, left, right)]],
        [(*item, "a") for item in BACK_OUT] + [((1, D), F32)] + GRADS_OUT,
        [WPROJ, WLIFT, WDOWN, pltpu.VMEM((OWN, D), BF16)]
        + scratch(SAVED[:4] + SAVED[5:6] + SAVED[7:] + BACK_OUT) + [sems(14)],
        3_000_000_000, 40,
    )
    from_low, from_high = swap_halos(to_low, to_high)
    rest_keep, rest_send = call(
        weight_grad_kernel, "weight_grads",
        [(index, "s"), (m_act, "v"), (grad_low, "v"), (b, "v"), (du, "v"), (o, "v"), (gb, "v")],
        [((SHARDS, 192, WIDE), BF16, "a")] * 2,
        [WDOWN, WLIFT, WPROJ, pltpu.VMEM((16, WIDE), BF16), sems(64)],
        1_600_000_000,
    )
    from_low, from_high, rest_send = lax.optimization_barrier((from_low, from_high, rest_send))
    rest_other = swap_core(rest_send)
    in_grad, qkv_keep, qkv_send = call(
        source_grad_kernel, "layer_source_grads",
        [(index, "s"), (src, "v"), (gains, "v"), (dh2, "v"), (dq, "v"), (dkv, "v"), (from_low, "v"),
         (from_high, "v"), (mlp_gain_grad, "v"), (wqkv, "a")],
        [stream, ((SHARDS, 96, 2432), BF16, "a"), ((SHARDS, 96, 2432), BF16, "a")],
        [WQKV, pltpu.VMEM((OWN, WIDE), BF16), WQKV, pltpu.VMEM((SHARDS, 96, 128), BF16), sems(17)],
        1_800_000_000,
    )
    qkv_other = swap_core(qkv_send)

    rest_z = call(
        rest_core_kernel, "rest_core_sum", [(index, "s"), (rest_keep, "v"), (rest_other, "v")],
        [((SHARDS, 48, WIDE), BF16)] * 4, [], 0, 24,
    )
    qkv_keep, _ = lax.optimization_barrier((qkv_keep, rest_z[0]))
    qkv_y = call(
        qkv_core_kernel, "qkv_core_sum", [(index, "s"), (qkv_keep, "v"), (qkv_other, "v")],
        [((96, 2432), BF16)] * 4, [], 0, 24,
    )
    (some,) = call(
        partial_kernel, "qkv_y_first", [(qkv_y[0], "v"), (along_y(qkv_y[1], 1), "v")],
        [((96, 2432), F32)], [], 0, 24,
    )
    rest_mine, some = lax.optimization_barrier((rest_z[0], some))
    rest_y = call(
        rest_z_kernel, "rest_z_sum",
        [(index, "s"), (rest_mine, "v"), *[(along_z(rest_z[d], d), "v") for d in (1, 2, 3)]],
        [((48, WIDE), BF16)] * 4, [], 0, 24,
    )
    qkv_z = call(
        qkv_y_kernel, "qkv_y_sum",
        [(index, "s"), (some, "v"), *[(along_y(qkv_y[d], d), "v") for d in (2, 3)]],
        [((48, 1280), BF16)] * 4, [pltpu.VMEM((96, 2432), BF16)], 0, 24,
    )
    (joint,) = call(
        joint_kernel, "joint_sum",
        [(rest_y[0], "v"), *[(along_y(rest_y[d], d), "v") for d in (1, 2, 3)],
         (qkv_z[0], "v"), *[(along_z(qkv_z[d], d), "v") for d in (1, 2, 3)]],
        [((48, 3584), BF16)], [], 0, 24,
    )
    (joint,) = call(
        pair_kernel, "pair_sum", [(joint, "v"), (swap_x(joint), "v")], [((48, 3584), BF16)], [], 0, 24
    )
    mine = [joint] + [along_z(joint, d) for d in (1, 2, 3)]
    theirs = [swap_core(piece) for piece in mine]
    qkv_sum, proj_sum, lift_sum, down_sum, gain_sums = call(
        final_kernel, "final_shard", [(index, "s"), *[(piece, "v") for piece in mine + theirs]],
        [((192, WIDE), F32), ((192, D), F32), ((192, WIDE), F32), ((288, D), F32), ((16, 128), F32)],
        [pltpu.VMEM((2, 192, WIDE), BF16)], 0, 24,
    )
    return (
        h3[None, :, None],
        in_grad[None, :, None],
        gain_sums[0:2].reshape(1, 256)[:, :192],
        qkv_sum[None],
        proj_sum[None],
        gain_sums[2:4].reshape(1, 256)[:, :192],
        lift_sum[None],
        down_sum[None],
    )


def solution(mesh):
    placed = (
        P(None, "fsdp", "ctx", None),
        P(None, "fsdp", "ctx", None),
        P(None, "fsdp", None),
        P("section", "fsdp"),
        P("section", "fsdp", None),
        P("section", "fsdp", None),
        P("section", "fsdp"),
        P("section", "fsdp", None),
        P("section", "fsdp", None),
    )
    return jax.shard_map(
        body,
        mesh=mesh,
        in_specs=placed,
        out_specs=(
            P("section", None, "fsdp", "ctx", None),
            P("section", None, "fsdp", "ctx", None),
            P("section", "fsdp"),
            P("section", "fsdp", None),
            P("section", "fsdp", None),
            P("section", "fsdp"),
            P("section", "fsdp", None),
            P("section", "fsdp", None),
        ),
        check_vma=False,
    )
```

```python
import functools

import jax
import jax.numpy as jnp
from jax import lax
from jax.experimental import pallas as pl
from jax.experimental.pallas import tpu as pltpu
from jax.sharding import PartitionSpec as P

D = 768
HD = 64
HALF = 64
SEQ_LEN = 2048
FF = 1152
WIDE = 2304
ROWS = 128
EXT = ROWS + 2 * HALF
MICRO = 2
OWN = MICRO * ROWS
SHARDS = 4
TILES = D // 128
norm_eps = 1e-05
rope_base = 10000.0
masked_score = -1e30
root_half = 0.7071067811865476
inv_root_tau = 0.3989422804014327
F32 = jnp.float32
BF16 = jnp.bfloat16


def mm(left, right):
    return lax.dot_general(left, right, (((1,), (0,)), ((), ())), preferred_element_type=F32)


def mm_nt(left, right):
    return lax.dot_general(left, right, (((1,), (1,)), ((), ())), preferred_element_type=F32)


def mm_tn(left, right):
    return lax.dot_general(left, right, (((0,), (0,)), ((), ())), preferred_element_type=F32)


def norm_parts(hidden):
    centre = hidden - jnp.mean(hidden, axis=-1, keepdims=True)
    inv_scale = lax.rsqrt(jnp.mean(centre * centre, axis=-1, keepdims=True) + norm_eps)
    return centre * inv_scale, inv_scale


def norm_back(grad_out, gain, normed, inv_scale):
    grad_normed = grad_out * gain
    inner = (
        grad_normed
        - jnp.mean(grad_normed, axis=-1, keepdims=True)
        - normed * jnp.mean(grad_normed * normed, axis=-1, keepdims=True)
    )
    return inner * inv_scale


def lane_is_low(shape, period):
    return lax.broadcasted_iota(jnp.int32, shape, 1) % period < period // 2


def turn(x):
    return jnp.where(lane_is_low(x.shape, HD), pltpu.roll(x, 96, 1), pltpu.roll(x, 32, 1))


def rotate(x, cosine, sine):
    return x * cosine + turn(x) * sine


def rotate_back(x, cosine, sine):
    return x * cosine - turn(x) * sine


def stack_heads(x):
    low = lane_is_low(x.shape, 128)
    zero = jnp.zeros_like(x)
    return jnp.concatenate([jnp.where(low, x, zero), jnp.where(low, zero, x)], axis=0)


def join_heads(x):
    half = x.shape[0] // 2
    low = lane_is_low((half, 128), 128)
    return jnp.where(low, x[:half], x[half:])


def start_weights(sources, buffers, sems):
    waits = {}
    for index, (name, source) in enumerate(sources.items()):
        copy = pltpu.make_async_copy(source, buffers[name], sems.at[index])
        copy.start()
        waits[name] = [copy]
    return waits


def finish(waits, name):
    for copy in waits[name]:
        copy.wait()


def load_stream(flag, own, low, high, other, ext):
    for m in range(MICRO):
        for ref, alt, start, size in (
            (low, other[1], 0, HALF),
            (own, other[0], HALF, ROWS),
            (high, other[2], HALF + ROWS, HALF),
        ):
            value = ref[m]
            if alt is not None:
                value = jnp.where(flag, value, alt[m])
            ext[pl.ds(m * EXT + start, size), :] = value


def own_rows(x):
    return jnp.concatenate([x[HALF : HALF + ROWS], x[EXT + HALF : EXT + HALF + ROWS]], axis=0)


def repeat(count, step):
    lax.fori_loop(0, count, lambda i, carry: (step(i), carry)[1], 0)


def each(count, step):
    for i in range(count):
        step(i)


def span(start, size, unit=128):
    return pl.ds(start if isinstance(start, int) else pl.multiple_of(start, unit), size)


def by_tiles(unit, group):
    def step(i):
        for j in range(group):
            unit(i * group + j)

    repeat(TILES // group, step)


def norm_rows(source, gain, target):
    def step(i):
        rows = span(i * 128, 128)
        normed, _ = norm_parts(source[rows, :].astype(F32))
        target[rows, :] = (normed * gain).astype(BF16)

    repeat(source.shape[0] // 128, step)


def forward_attention(ext, gain, wqkv, cos_ref, sin_ref, bias_ref, a_ext, q_ref, k_ref, v_ref, p_ref, o_ref):
    norm_rows(ext, gain, a_ext)
    a_own = o_ref
    a_own[...] = own_rows(a_ext[...])
    own_span = pl.ds(HALF, ROWS)

    def project(t):
        cols = span(256 * t, 256)
        queries = mm(a_own[...], wqkv[:, cols])
        keys = mm(a_ext[...], wqkv[:, span(D + 256 * t, 256)])
        v_ref[:, cols] = mm(a_ext[...], wqkv[:, span(2 * D + 256 * t, 256)]).astype(BF16)
        for s in range(2):
            tile, lanes = span(256 * t + 128 * s, 128), slice(128 * s, 128 * s + 128)
            for m in range(MICRO):
                part = queries[m * ROWS : (m + 1) * ROWS, lanes]
                turned = rotate(part, cos_ref[own_span, :], sin_ref[own_span, :]).astype(BF16)
                q_ref[pl.ds(m * ROWS, ROWS), tile] = turned * jnp.asarray(0.125, BF16)
                part = keys[m * EXT : (m + 1) * EXT, lanes]
                k_ref[pl.ds(m * EXT, EXT), tile] = rotate(part, cos_ref[...], sin_ref[...]).astype(BF16)

    repeat(3, project)

    def unit(t):
        cols = pl.ds(pl.multiple_of(t * 128, 128), 128)
        for m in range(MICRO):
            q2 = stack_heads(q_ref[pl.ds(m * ROWS, ROWS), cols])
            scores = mm_nt(k_ref[pl.ds(m * EXT, EXT), cols], q2) + bias_ref[m]
            terms = jnp.exp(scores - jnp.max(scores, axis=0, keepdims=True))
            probs = (terms * (1.0 / jnp.sum(terms, axis=0, keepdims=True))).astype(BF16)
            p_ref[m, t] = probs
            attended = mm_tn(probs, v_ref[pl.ds(m * EXT, EXT), cols])
            o_ref[pl.ds(m * ROWS, ROWS), cols] = join_heads(attended).astype(BF16)

    by_tiles(unit, 3)


def forward_mlp(own, o_ref, wproj, mlp_gain, wlift, wdown, h2_ref, b_ref, m_ref, left_ref, right_ref, h3_ref, waits):
    finish(waits, "proj")

    def mix(t):
        cols = span(256 * t, 256)
        added = mm(o_ref[...], wproj[:, cols])
        for m in range(MICRO):
            rows = pl.ds(m * ROWS, ROWS)
            h2_ref[rows, cols] = own[m, :, cols].astype(F32) + added[m * ROWS : (m + 1) * ROWS]

    each(3, mix)
    norm_rows(h2_ref, mlp_gain, b_ref)
    finish(waits, "lift")

    def lift(t):
        cols = span(384 * t, 384)
        gate = mm(b_ref[...], wlift[:, cols])
        up = mm(b_ref[...], wlift[:, span(FF + 384 * t, 384)])
        cdf = 0.5 * (1.0 + lax.erf(gate * root_half))
        gelu = gate * cdf
        m_ref[:, cols] = (gelu * up).astype(BF16)
        if left_ref is not None:
            pdf = jnp.exp(-0.5 * gate * gate) * inv_root_tau
            left_ref[:, cols] = up * (cdf + gate * pdf)
            right_ref[:, cols] = gelu

    repeat(3, lift)
    finish(waits, "down")

    def down(t):
        cols = span(256 * t, 256)
        h3 = (h2_ref[:, cols] + mm(m_ref[...], wdown[:, cols])).astype(BF16)
        for m in range(MICRO):
            h3_ref[m, :, cols] = h3[m * ROWS : (m + 1) * ROWS]

    each(3, down)


def backward_mlp(grad_ref, h2_ref, mlp_gain, wproj, wlift, wdown, left_ref, right_ref, du_ref, gb_ref, do_ref,
                 dh2_ref, b_ref, mlp_ref, ready):
    ready("left", "right", "down")

    def lift(t):
        cols = span(384 * t, 384)
        dm = mm_nt(grad_ref[...], wdown[cols, :])
        du_ref[:, cols] = (dm * left_ref[:, cols]).astype(BF16)
        du_ref[:, span(FF + 384 * t, 384)] = (dm * right_ref[:, cols]).astype(BF16)

    each(3, lift)

    ready("lift")

    def source(t):
        rows = span(256 * t, 256)
        dh2_ref[:, rows] = mm_nt(du_ref[...], wlift[rows, :])

    each(3, source)
    ready("h2")
    if mlp_ref is not None:
        mlp_ref[...] = jnp.zeros_like(mlp_ref)

    def norm(i):
        rows = span(i * 128, 128)
        db = dh2_ref[rows, :]
        normed, inv_scale = norm_parts(h2_ref[rows, :])
        dh2 = grad_ref[rows, :].astype(F32) + norm_back(db, mlp_gain, normed, inv_scale)
        dh2_ref[rows, :] = dh2
        gb_ref[rows, :] = dh2.astype(BF16)
        if mlp_ref is not None:
            mlp_ref[...] += jnp.sum(db * normed, axis=0, keepdims=True)
            b_ref[rows, :] = (normed * mlp_gain).astype(BF16)

    repeat(2, norm)

    ready("proj")

    def attended(t):
        rows = span(256 * t, 256)
        do_ref[:, rows] = mm_nt(gb_ref[...], wproj[rows, :]).astype(BF16)

    each(3, attended)


def backward_attention(q_ref, k_ref, v_ref, p_ref, do_ref, cos_ref, sin_ref, dq_ref, dkv_ref, low_ref, high_ref, group):
    cosine, sine = cos_ref[...], sin_ref[...]
    cos_own, sin_own = cosine[HALF : HALF + ROWS], sine[HALF : HALF + ROWS]

    def unit(t):
        cols = pl.ds(pl.multiple_of(t * 128, 128), 128)
        value_cols = pl.ds(pl.multiple_of(D + t * 128, 128), 128)
        for m in range(MICRO):
            rows = pl.ds(m * ROWS, ROWS)
            q2 = stack_heads(q_ref[rows, cols])
            do2 = stack_heads(do_ref[rows, cols])
            probs = p_ref[m, t]
            dprobs = mm_nt(v_ref[pl.ds(m * EXT, EXT), cols], do2)
            wide = probs.astype(F32)
            inner = jnp.sum(wide * dprobs, axis=0, keepdims=True)
            ds = (wide * (dprobs - inner)).astype(BF16)
            dq = join_heads(mm_tn(ds, k_ref[pl.ds(m * EXT, EXT), cols])) * 0.125
            dq_ref[rows, cols] = rotate_back(dq, cos_own, sin_own).astype(BF16)
            dk = rotate_back(mm(ds, q2), cosine, sine)
            dv = mm(probs, do2)
            for grad, where in ((dk, cols), (dv, value_cols)):
                low_ref[m, :, where] = grad[:HALF].astype(BF16)
                dkv_ref[rows, where] = grad[HALF : HALF + ROWS].astype(BF16)
                high_ref[m, :, where] = grad[HALF + ROWS :].astype(BF16)

    by_tiles(unit, group)


def place_shards(index, own, pieces, put):
    f, core, xlo = index[1], index[2], index[3]
    first, first_other, second, second_x, second_core, second_both = pieces
    put(own, f, None, None)
    put(first, lax.rem(f + 3 + 2 * core, 4), None, None)
    put(first_other, lax.rem(f + 1 + 2 * core, 4), None, None)
    across = lax.rem(f + 2, 4)
    put(second, across, core, xlo)
    put(second_x, across, core, 1 - xlo)
    put(second_core, across, 1 - core, xlo)
    put(second_both, across, 1 - core, 1 - xlo)


def pack_qkv_kernel(index, qkv, gains, own, whole, half, first_rows, last_rows):
    rows = pl.ds(pl.multiple_of(index[2] * 96, 16), 96)
    whole[:, pl.ds(0, WIDE)] = qkv[...]
    half[:, pl.ds(0, WIDE)] = qkv[rows, :]
    whole[:, pl.ds(WIDE, 128)] = jnp.zeros((192, 128), BF16)
    half[:, pl.ds(WIDE, 128)] = jnp.zeros((96, 128), BF16)
    whole[pl.ds(0, 16), pl.ds(WIDE, 128)] = gains[...]
    half[pl.ds(0, 16), pl.ds(WIDE, 128)] = gains[...]
    first_rows[...] = own[:, :HALF]
    last_rows[...] = own[:, ROWS - HALF :]


def pack_kernel(index, lift, proj, down, rest, quarter, half):
    core = index[2]
    rows = lambda at, size: pl.ds(pl.multiple_of(at, 16), size)
    rest[pl.ds(0, 192), :] = lift[...]
    half[pl.ds(0, 96), :] = lift[rows(core * 96, 96), :]
    for b in range(3):
        cols = pl.ds(b * D, D)
        rest[pl.ds(192, 64), cols] = proj[pl.ds(64 * b, 64), :]
        rest[pl.ds(256, 96), cols] = down[pl.ds(96 * b, 96), :]
        half[pl.ds(96, 32), cols] = proj[rows(64 * b + core * 32, 32), :]
        half[pl.ds(128, 48), cols] = down[rows(96 * b + core * 48, 48), :]
    quarter[...] = half[:, pl.ds(pl.multiple_of(index[3] * 1152, 128), 1152)]


def gather_gain(tiles, row):
    parts = []
    for tile in tiles:
        parts += [tile[row : row + 1, :], tile[row + 1 : row + 2, :64]]
    return jnp.concatenate(parts, axis=1)


def forward_attention_kernel(index, own, low, high, gain_tile, cos_ref, sin_ref, bias_ref,
                             shard, first, first_other, second, second_core,
                             o, gains, whole, wqkv, tiles, ext, a_ext, q, k, v, p, sems, out_sem):
    copies = []

    def go(src, dst):
        copy = pltpu.make_async_copy(src, dst, sems.at[len(copies)])
        copy.start()
        copies.append(copy)

    def put(piece, f, half, side):
        if piece is None:
            return
        at, size = (f * 192, 192) if half is None else (f * 192 + half * 96, 96)
        rows = pl.ds(pl.multiple_of(at, 16), size)
        go(piece if piece is shard else piece.at[:, pl.ds(0, WIDE)], wqkv.at[rows])
        if piece is not shard and piece is not second_core:
            go(piece.at[pl.ds(0, 16), pl.ds(WIDE, 128)], tiles.at[f])

    place_shards(index, shard, (first, first_other, second, None, second_core, None), put)
    go(gain_tile, tiles.at[index[1]])
    load_stream(None, own, low, high, (None, None, None), ext)
    for copy in copies:
        copy.wait()
    out = pltpu.make_async_copy(wqkv, whole, out_sem)
    out.start()
    shards = [tiles[f].astype(F32) for f in range(SHARDS)]
    gains[0:1, :] = gather_gain(shards, 0)
    gains[1:2, :] = gather_gain(shards, 2)
    forward_attention(ext, gains[0:1], wqkv, cos_ref, sin_ref, bias_ref, a_ext, q, k, v, p, o)
    out.wait()


def place_rest(index, lift, proj, down, pieces, wlift, wproj, wdown, go):
    f = index[1]
    rows = lambda at, size: pl.ds(pl.multiple_of(at, 16), size)
    lanes = lambda at, size: pl.ds(pl.multiple_of(at, 128), size)

    def put(piece, s, half, side):
        if piece is None:
            go("proj", proj, wproj.at[rows(f * 192, 192)])
            go("lift", lift, wlift.at[rows(f * 192, 192)])
            go("down", down, wdown.at[rows(f * 288, 288)])
        elif half is None:
            go("lift", piece.at[pl.ds(0, 192)], wlift.at[rows(s * 192, 192)])
            for b in range(3):
                cols = pl.ds(b * D, D)
                go("proj", piece.at[pl.ds(192, 64), cols], wproj.at[rows(s * 192 + b * 64, 64)])
                go("down", piece.at[pl.ds(256, 96), cols], wdown.at[rows(s * 288 + b * 96, 96)])
        else:
            go("lift", piece.at[pl.ds(0, 96)], wlift.at[rows(s * 192 + half * 96, 96), lanes(side * 1152, 1152)])
            for j in range(3):
                cols = pl.ds(j * 384, 384)
                b, right = lax.div(3 * side + j, 2), lanes(lax.rem(3 * side + j, 2) * 384, 384)
                go("proj", piece.at[pl.ds(96, 32), cols], wproj.at[rows(s * 192 + b * 64 + half * 32, 32), right])
                go("down", piece.at[pl.ds(128, 48), cols], wdown.at[rows(s * 288 + b * 96 + half * 48, 48), right])

    place_shards(index, None, pieces, put)


def starter(sems, waits):
    count = [0]

    def go(name, src, dst):
        copy = pltpu.make_async_copy(src, dst, sems.at[count[0]])
        copy.start()
        count[0] += 1
        waits.setdefault(name, []).append(copy)

    return go


def forward_mlp_kernel(index, own, o, gains, lift, proj, down, *refs):
    pieces, (h3_ref, wproj, wlift, wdown, h2, b, m_out, sems) = refs[:6], refs[6:]
    waits = {}
    place_rest(index, lift, proj, down, pieces, wlift, wproj, wdown, starter(sems, waits))
    forward_mlp(own, o, wproj, gains[1:2], wlift, wdown, h2, b, m_out, None, None, h3_ref, waits)


def assemble_kernel(index, lift, proj, down, *refs):
    pieces, (whole_lift, whole_proj, whole_down, wlift, wproj, wdown, sems) = refs[:6], refs[7:]
    waits = {}
    go = starter(sems, waits)
    place_rest(index, lift, proj, down, pieces, wlift, wproj, wdown, go)
    for name, buffer, whole in (("lift", wlift, whole_lift), ("proj", wproj, whole_proj), ("down", wdown, whole_down)):
        finish(waits, name)
        go("out", buffer, whole)
    finish(waits, "out")


def start_all(pairs, sems, first):
    copies = [pltpu.make_async_copy(src, dst, sems.at[first + n]) for n, (src, dst) in enumerate(pairs)]
    for copy in copies:
        copy.start()
    return copies


def turning_kernel(flag_ref, own, low, high, other_own, other_low, other_high, cotangent, gains,
                   cos_ref, sin_ref, bias_ref, qkv_hbm, proj_hbm, lift_hbm, down_hbm, *refs):
    kept, (dh2_ref, dq, dkv, to_low, to_high) = refs[:11], refs[11:16]
    wqkv, wproj, wlift, wdown, ext, a_ext, mine, du, do, h3_ref, q, k, v, p, o, h2, m_out, left, right, src, sems = refs[16:]
    waits = start_weights(
        {"qkv": qkv_hbm, "proj": proj_hbm, "lift": lift_hbm, "down": down_hbm},
        {"qkv": wqkv, "proj": wproj, "lift": wlift, "down": wdown}, sems,
    )
    flag = flag_ref[0] == 1
    load_stream(flag, own, low, high, (other_own, other_low, other_high), ext)
    for m in range(MICRO):
        mine[m] = ext[pl.ds(m * EXT + HALF, ROWS), :]
        src[pl.ds(m * ROWS, ROWS), :] = mine[m]
    finish(waits, "qkv")
    forward_attention(ext, gains[0:1], wqkv, cos_ref, sin_ref, bias_ref, a_ext, q, k, v, p, o)
    outs = start_all(zip((q, k, v, p, o, src), kept[1:6] + kept[10:]), sems, 4)
    spare = a_ext.at[pl.ds(0, OWN)]
    forward_mlp(mine, o, wproj, gains[1:2], wlift, wdown, h2, spare, m_out, left, right, h3_ref, waits)
    outs += start_all(zip((h3_ref, h2, m_out, left, right), kept[:1] + kept[6:10]), sems, 10)
    grad = a_ext.at[pl.ds(OWN, OWN)]
    for m in range(MICRO):
        grad[pl.ds(m * ROWS, ROWS), :] = cotangent[m]
    backward_mlp(grad, h2, gains[1:2], wproj, wlift, wdown, left, right, du, spare, do, dh2_ref, None, None,
                 lambda *names: None)
    backward_attention(q, k, v, p, do, cos_ref, sin_ref, dq, dkv, to_low, to_high, 3)
    for copy in outs:
        copy.wait()


def back_kernel(flag_ref, incoming, cotangent, gains, cos_ref, sin_ref, proj_hbm, lift_hbm, down_hbm,
                q_hbm, k_hbm, v_hbm, p_hbm, h2_hbm, left_hbm, right_hbm, *refs):
    kept, (mlp_ref, dh2_ref, dq, dkv, to_low, to_high) = refs[:4], refs[4:10]
    wproj, wlift, wdown, do, q, k, v, p, h2, left, right, grad_ref, du, gb_ref, b_ref, sems = refs[10:]
    early = start_all(
        ((down_hbm, wdown), (left_hbm, left), (right_hbm, right), (lift_hbm, wlift), (h2_hbm, h2), (proj_hbm, wproj)),
        sems, 0,
    )
    late = start_all(((q_hbm, q), (v_hbm, v), (p_hbm, p), (k_hbm, k)), sems, 6)
    flag = flag_ref[0] == 1
    for m in range(MICRO):
        grad_ref[pl.ds(m * ROWS, ROWS), :] = jnp.where(flag, incoming[m], cotangent[m])
    early = dict(zip(("down", "left", "right", "lift", "h2", "proj"), early))

    def ready(*names):
        for name in names:
            early[name].wait()

    backward_mlp(
        grad_ref, h2, gains[1:2], wproj, wlift, wdown, left, right, du, gb_ref, do, dh2_ref, b_ref, mlp_ref, ready
    )
    outs = start_all(zip((grad_ref, du, gb_ref, b_ref), kept), sems, 10)
    for copy in late:
        copy.wait()
    backward_attention(q, k, v, p, do, cos_ref, sin_ref, dq, dkv, to_low, to_high, 6)
    for copy in outs:
        copy.wait()


def joined_grads(dq, dkv, from_low, from_high, dqkv):
    dqkv[:, :D] = dq[...]
    for m in range(MICRO):
        first, last = pl.ds(m * ROWS, HALF), pl.ds(m * ROWS + HALF, HALF)
        dqkv[first, D:] = (dkv[first, :].astype(F32) + from_low[m].astype(F32)).astype(BF16)
        dqkv[last, D:] = (dkv[last, :].astype(F32) + from_high[m].astype(F32)).astype(BF16)


def source_kernel(src, gains, dh2, dq, dkv, from_low, from_high, qkv_hbm, out_ref, wqkv, dqkv, sems):
    waits = start_weights({"qkv": qkv_hbm}, {"qkv": wqkv}, sems)
    joined_grads(dq, dkv, from_low, from_high, dqkv)
    normed, inv_scale = norm_parts(src[...].astype(F32))
    finish(waits, "qkv")
    da = mm_nt(dqkv[...], wqkv[...])
    dh = dh2[...] + norm_back(da, gains[0:1], normed, inv_scale)
    for m in range(MICRO):
        out_ref[m] = dh[m * ROWS : (m + 1) * ROWS].astype(BF16)


def gain_block(attn, mlp, f):
    rows = []
    for gain in (attn, mlp):
        rows.append(gain[:, 192 * f : 192 * f + 128])
        rows.append(jnp.concatenate([gain[:, 192 * f + 128 : 192 * f + 192], jnp.zeros((1, 64), F32)], axis=1))
    return jnp.concatenate(rows + [jnp.zeros((92, 128), F32)], axis=0).astype(BF16)


def source_grad_kernel(index, src, gains, dh2, dq, dkv, from_low, from_high, mlp_grad, qkv_hbm,
                       out_ref, keep, send, wqkv, dqkv, qkv_ref, gain_ref, sems):
    waits = start_weights({"qkv": qkv_hbm}, {"qkv": wqkv}, sems)
    joined_grads(dq, dkv, from_low, from_high, dqkv)
    normed, inv_scale = norm_parts(src[...].astype(F32))
    finish(waits, "qkv")
    da = mm_nt(dqkv[...], wqkv[...])
    attn_grad = jnp.sum(da * normed, axis=0, keepdims=True)
    mlp = mlp_grad[...]
    for f in range(SHARDS):
        gain_ref[f] = gain_block(attn_grad, mlp, f)
    a = (normed * gains[0:1]).astype(BF16)
    for t in range(9):
        cols = pl.ds(256 * t, 256)
        qkv_ref[:, cols] = mm_tn(a, dqkv[:, cols]).astype(BF16)
    copies = []
    for target, half in ((send, 1 - index[2]), (keep, index[2])):
        for f in range(SHARDS):
            rows = pl.ds(pl.multiple_of(f * 192 + half * 96, 16), 96)
            for src_ref, dst_ref in (
                (qkv_ref.at[rows], target.at[f, :, pl.ds(0, WIDE)]),
                (gain_ref.at[f], target.at[f, :, pl.ds(WIDE, 128)]),
            ):
                copy = pltpu.make_async_copy(src_ref, dst_ref, sems.at[1 + len(copies)])
                copy.start()
                copies.append(copy)
    dh = dh2[...] + norm_back(da, gains[0:1], normed, inv_scale)
    for m in range(MICRO):
        out_ref[m] = dh[m * ROWS : (m + 1) * ROWS].astype(BF16)
    for copy in copies:
        copy.wait()


def weight_grad_kernel(index, m_ref, grad_ref, b_ref, du, o_ref, gb_ref, keep, send,
                       down_ref, lift_ref, proj_ref, pad_ref, sems):
    core = index[2]
    copies = []

    def go(src, dst):
        copy = pltpu.make_async_copy(src, dst, sems.at[len(copies)])
        copy.start()
        copies.append(copy)

    sides = ((send, 1 - core), (keep, core))
    rows = lambda at, size: pl.ds(pl.multiple_of(at, 16), size)
    pad_ref[...] = jnp.zeros_like(pad_ref)
    for target, _ in sides:
        for f in range(SHARDS):
            go(pad_ref, target.at[f, pl.ds(176, 16)])
    for t in range(9):
        cols = pl.ds(256 * t, 256)
        lift_ref[:, cols] = mm_tn(b_ref[...], du[:, cols]).astype(BF16)
    for target, half in sides:
        for f in range(SHARDS):
            go(lift_ref.at[rows(f * 192 + half * 96, 96)], target.at[f, pl.ds(0, 96)])
    for t in range(3):
        cols = pl.ds(256 * t, 256)
        down_ref[:, cols] = mm_tn(m_ref[...], grad_ref[:, cols]).astype(BF16)
        proj_ref[:, cols] = mm_tn(o_ref[...], gb_ref[:, cols]).astype(BF16)
    for target, half in sides:
        for f in range(SHARDS):
            for b in range(3):
                cols = pl.ds(b * D, D)
                go(proj_ref.at[rows(f * 192 + b * 64 + half * 32, 32)], target.at[f, pl.ds(96, 32), cols])
                go(down_ref.at[rows(f * 288 + b * 96 + half * 48, 48)], target.at[f, pl.ds(128, 48), cols])
    for copy in copies:
        copy.wait()


def add_up(parts):
    total = parts[0].astype(F32)
    for part in parts[1:]:
        total = total + part.astype(F32)
    return total.astype(BF16)


def rest_core_kernel(index, keep, other, *outs):
    for d, out in enumerate(outs):
        rows = pl.ds(pl.multiple_of(lax.rem(index[0] + d, 4) * 48, 16), 48)
        for f in range(SHARDS):
            out[f] = add_up([keep[f, rows, :], other[f, rows, :]])


def rest_z_kernel(index, own, a, b, c, *outs):
    for d, out in enumerate(outs):
        f = lax.rem(index[1] + d, 4)
        out[...] = add_up([own[f], a[f], b[f], c[f]])


def qkv_core_kernel(index, keep, other, *outs):
    for d, out in enumerate(outs):
        f = lax.rem(index[1] + d, 4)
        out[...] = add_up([keep[f], other[f]])


def partial_kernel(a, b, out):
    out[...] = a[...].astype(F32) + b[...].astype(F32)


def qkv_y_kernel(index, some, b, c, out_0, out_1, out_2, out_3, total):
    total[...] = add_up([some[...], b[...], c[...]])
    for d, out in enumerate((out_0, out_1, out_2, out_3)):
        z = lax.rem(index[0] + d, 4)
        rows = pl.ds(pl.multiple_of(lax.div(z, 2) * 48, 16), 48)
        cols = pl.ds(pl.multiple_of(lax.rem(z, 2) * 1152, 128), 1152)
        out[:, pl.ds(0, 1152)] = total[rows, cols]
        out[:, pl.ds(1152, 128)] = total[pl.ds(0, 48), pl.ds(WIDE, 128)]


def joint_kernel(r0, r1, r2, r3, q0, q1, q2, q3, out):
    out[:, pl.ds(0, WIDE)] = add_up([r0[...], r1[...], r2[...], r3[...]])
    out[:, pl.ds(WIDE, 1280)] = add_up([q0[...], q1[...], q2[...], q3[...]])


def pair_kernel(a, b, out):
    out[...] = add_up([a[...], b[...]])


def final_kernel(index, *refs):
    pieces, (qkv_out, proj_out, lift_out, down_out, gain_out, rest) = refs[:8], refs[8:]
    core = index[2]
    for side in range(2):
        half = core if side == 0 else 1 - core
        for d in range(4):
            piece = pieces[4 * side + d]
            z = lax.rem(index[0] - d + 4, 4)
            rest[side, pl.ds(pl.multiple_of(z * 48, 16), 48), :] = piece[:, pl.ds(0, WIDE)]
            qkv_out[
                pl.ds(pl.multiple_of(half * 96 + lax.div(z, 2) * 48, 16), 48),
                pl.ds(pl.multiple_of(lax.rem(z, 2) * 1152, 128), 1152),
            ] = piece[:, pl.ds(WIDE, 1152)].astype(F32)
        rows = lambda at, size: pl.ds(pl.multiple_of(at, 16), size)
        lift_out[rows(half * 96, 96), :] = rest[side, pl.ds(0, 96), :].astype(F32)
        for b in range(3):
            cols = pl.ds(b * D, D)
            proj_out[rows(b * 64 + half * 32, 32), :] = rest[side, pl.ds(96, 32), cols].astype(F32)
            down_out[rows(b * 96 + half * 48, 48), :] = rest[side, pl.ds(128, 48), cols].astype(F32)
    gain_out[...] = pieces[0][pl.ds(0, 16), pl.ds(WIDE + 1152, 128)].astype(F32)


def call(kernel, name, ins, outs, scratch, flops, limit=24):
    places = {"v": pltpu.VMEM, "a": pl.ANY, "s": pltpu.SMEM}
    return pl.pallas_call(
        kernel,
        name=name,
        out_shape=[jax.ShapeDtypeStruct(out[0], out[1]) for out in outs],
        in_specs=[pl.BlockSpec(memory_space=places[place]) for _, place in ins],
        out_specs=[pl.BlockSpec(memory_space=places[out[2] if len(out) > 2 else "v"]) for out in outs],
        scratch_shapes=scratch,
        compiler_params=pltpu.CompilerParams(vmem_limit_bytes=limit * 2**20),
        cost_estimate=pl.CostEstimate(flops=flops, bytes_accessed=flops // 300, transcendentals=0),
    )(*[array for array, _ in ins])


def travel(block, target):
    pairs = []
    for ctx in range(16):
        for f in range(SHARDS):
            xlo, z, core, g = target(ctx // 8, ctx // 2 % 4, ctx % 2, f)
            pairs.append((ctx * SHARDS + f, (xlo * 8 + z % 4 * 2 + core) * SHARDS + g % 4))
    return lax.ppermute(block, ("ctx", "fsdp"), pairs)


def along_y(block, d):
    return travel(block, lambda x, z, c, f: (x, z, c, f + d))


def along_z(block, d):
    return travel(block, lambda x, z, c, f: (x, z + d, c, f))


def next_shard(block):
    return travel(block, lambda x, z, c, f: (x, z, c, f + 1 - 2 * c))


def swap_core(block):
    return travel(block, lambda x, z, c, f: (x, z, 1 - c, f))


def spread_quarter(block, across):
    return block, across, swap_core(block), swap_core(across)


def swap_x(block):
    return travel(block, lambda x, z, c, f: (1 - x, z, c, f))


def halo_rows(block, axis):
    count = lax.axis_size(axis)
    up = [(i, i + 1) for i in range(count - 1)]
    down = [(i + 1, i) for i in range(count - 1)]
    return (
        lax.ppermute(block[:, ROWS - HALF :], axis, up),
        lax.ppermute(block[:, :HALF], axis, down),
    )


def swap_halos(to_low, to_high):
    count = lax.axis_size("ctx")
    up = [(i, i + 1) for i in range(count - 1)]
    down = [(i + 1, i) for i in range(count - 1)]
    return lax.ppermute(to_high, "ctx", up), lax.ppermute(to_low, "ctx", down)


def tables(first_row, lengths):
    half = HD // 2
    frequencies = rope_base ** (-(jnp.arange(half, dtype=F32) * 2.0) / HD)
    positions = first_row - HALF + jnp.arange(EXT, dtype=jnp.int32)
    angles = positions.astype(F32)[:, None] * frequencies[None, :]
    cosine, sine = jnp.cos(angles), jnp.sin(angles)
    cosine = jnp.concatenate([cosine] * 4, axis=1)
    sine = jnp.concatenate([-sine, sine, -sine, sine], axis=1)
    ends = jnp.cumsum(lengths, axis=1)
    doc = jnp.sum((positions[None, :, None] >= ends[:, None, :]).astype(jnp.int32), axis=2)
    query = positions[HALF : HALF + ROWS]
    allowed = (
        (jnp.abs(query[None, :] - positions[:, None]) <= HALF)
        & (positions >= 0)[:, None]
        & (positions < SEQ_LEN)[:, None]
    )[None] & (doc[:, :, None] == doc[:, None, HALF : HALF + ROWS])
    bias = jnp.where(allowed, 0.0, masked_score).astype(F32)
    return cosine, sine, jnp.concatenate([bias, bias], axis=2)


WQKV, WPROJ, WLIFT, WDOWN = [
    pltpu.VMEM((D, WIDE), BF16),
    pltpu.VMEM((D, D), BF16),
    pltpu.VMEM((D, WIDE), BF16),
    pltpu.VMEM((FF, D), BF16),
]
SAVED = [
    ((OWN, D), BF16),
    ((MICRO * EXT, D), BF16),
    ((MICRO * EXT, D), BF16),
    ((MICRO, TILES, EXT, 2 * ROWS), BF16),
    ((OWN, D), BF16),
    ((OWN, D), F32),
    ((OWN, FF), BF16),
    ((OWN, FF), F32),
    ((OWN, FF), F32),
]
STREAM = [pltpu.VMEM((MICRO * EXT, D), BF16)] * 2
GRADS_OUT = [
    ((OWN, D), F32),
    ((OWN, D), BF16),
    ((OWN, 2 * D), BF16),
    ((MICRO, HALF, 2 * D), BF16),
    ((MICRO, HALF, 2 * D), BF16),
]


TURN_OUT = [((MICRO, ROWS, D), BF16)] + SAVED + [((OWN, D), BF16)]
BACK_OUT = [((OWN, D), BF16), ((OWN, WIDE), BF16), ((OWN, D), BF16), ((OWN, D), BF16)]


def sems(count):
    return pltpu.SemaphoreType.DMA((count,))


def body(
    inputs, out_grad, doc_lengths, attn_gain, qkv_weight, proj_weight, mlp_gain, lift_weight, down_weight
):
    on_first = lax.axis_index("section") == 0
    flag = on_first.astype(jnp.int32).reshape(1)
    ctx, f = lax.axis_index("ctx"), lax.axis_index("fsdp")
    index = jnp.stack([ctx // 2 % 4, f, ctx % 2, ctx // 8]).astype(jnp.int32)
    qkv_shard, lift_shard, proj_shard, down_shard = qkv_weight[0], lift_weight[0], proj_weight[0], down_weight[0]
    own, cotangent = inputs[:, 0], out_grad[:, 0]
    gain_tile = jnp.pad(
        jnp.pad(jnp.stack([attn_gain[0], mlp_gain[0]]), ((0, 0), (0, 64))).reshape(4, 128), ((0, 12), (0, 0))
    )
    edge = ((MICRO, HALF, D), BF16)
    qkv_pack, qkv_half, first_rows, last_rows = call(
        pack_qkv_kernel, "pack_qkv",
        [(index, "s"), (qkv_shard, "v"), (gain_tile, "v"), (own, "v")],
        [((192, 2432), BF16), ((96, 2432), BF16), edge, edge],
        [], 0, 12,
    )
    rest, rest_quarter = call(
        pack_kernel, "pack_rest",
        [(index, "s"), (lift_shard, "v"), (proj_shard, "v"), (down_shard, "v")],
        [((352, WIDE), BF16), ((176, 1152), BF16)],
        [pltpu.VMEM((176, WIDE), BF16)], 0, 12,
    )
    first = next_shard(qkv_pack)
    second = along_y(qkv_half, 2)
    rest_second = along_y(rest_quarter, 2)
    cosine, sine, bias = tables(ctx * ROWS, doc_lengths[:, 0])
    first_rows, last_rows, cosine = lax.optimization_barrier((first_rows, last_rows, cosine))
    low, high = swap_halos(first_rows, last_rows)
    first, second, rest_second, rest, cosine, sine, bias, low, high = lax.optimization_barrier(
        (first, second, rest_second, rest, cosine, sine, bias, low, high)
    )
    rest_first = next_shard(rest)
    rest_x = swap_x(rest_second)
    qkv_pieces = first, swap_core(first), second, swap_core(second)
    stream = ((MICRO, ROWS, D), BF16)
    scratch = lambda items: [pltpu.VMEM(s, k) for s, k in items]

    o, gains, wqkv = call(
        forward_attention_kernel, "forward_attention",
        [(index, "s"), (own, "v"), (low, "v"), (high, "v"), (gain_tile, "a"), (cosine, "v"), (sine, "v"), (bias, "v"),
         (qkv_shard, "a"), *[(piece, "a") for piece in qkv_pieces]],
        [((OWN, D), BF16), ((2, D), F32), ((D, WIDE), BF16, "a")],
        [WQKV, pltpu.VMEM((SHARDS, 16, 128), BF16)] + STREAM + scratch(SAVED[:4]) + [sems(9), pltpu.SemaphoreType.DMA(())],
        1_400_000_000,
    )
    rest_first, rest_second, rest_x, o = lax.optimization_barrier((rest_first, rest_second, rest_x, o))
    rest_pieces = rest_first, swap_core(rest_first), *spread_quarter(rest_second, rest_x)
    rest_parts = [(part, "a") for part in (lift_shard, proj_shard, down_shard, *rest_pieces)]
    (relay,) = call(
        forward_mlp_kernel, "forward_mlp",
        [(index, "s"), (own, "v"), (o, "v"), (gains, "v"), *rest_parts],
        [stream],
        [WPROJ, WLIFT, WDOWN] + scratch([SAVED[5], SAVED[0], SAVED[6]]) + [sems(45)],
        1_800_000_000,
    )
    wlift, wproj, wdown = call(
        assemble_kernel, "assemble_weights",
        [(index, "s"), *rest_parts, (relay, "a")],
        [((D, WIDE), BF16, "a"), ((D, D), BF16, "a"), ((FF, D), BF16, "a")],
        [WLIFT, WPROJ, WDOWN, sems(48)], 1_800_000_000, 56,
    )
    relayed = lax.ppermute(relay, "section", [(0, 1)])
    relayed, wlift, wproj, wdown = lax.optimization_barrier((relayed, wlift, wproj, wdown))
    other_low, other_high = halo_rows(relayed, "ctx")
    (h3, q, k, v, p, o, h2, m_act, left, right, src, dh2, dq, dkv, to_low, to_high) = call(
        turning_kernel, "layer_turn",
        [(flag, "s"), (own, "v"), (low, "v"), (high, "v"), (relayed, "v"), (other_low, "v"), (other_high, "v"),
         (cotangent, "v"), (gains, "v"), (cosine, "v"), (sine, "v"), (bias, "v"),
         (wqkv, "a"), (wproj, "a"), (wlift, "a"), (wdown, "a")],
        [(*item, "a") for item in TURN_OUT] + GRADS_OUT,
        [WQKV, WPROJ, WLIFT, WDOWN] + STREAM
        + [pltpu.VMEM((MICRO, ROWS, D), BF16), pltpu.VMEM((OWN, WIDE), BF16), pltpu.VMEM((OWN, D), BF16)] + scratch(TURN_OUT) + [sems(15)],
        6_000_000_000, 44,
    )
    from_low, from_high = swap_halos(to_low, to_high)
    (grad_relay,) = call(
        source_kernel, "layer_source",
        [(src, "v"), (gains, "v"), (dh2, "v"), (dq, "v"), (dkv, "v"), (from_low, "v"), (from_high, "v"), (wqkv, "a")],
        [stream],
        [WQKV, pltpu.VMEM((OWN, WIDE), BF16), sems(1)],
        900_000_000,
    )
    incoming = lax.ppermute(grad_relay, "section", [(1, 0)])
    (grad_low, du, gb, b, mlp_gain_grad, dh2, dq, dkv, to_low, to_high) = call(
        back_kernel, "layer_back",
        [(flag, "s"), (incoming, "v"), (cotangent, "v"), (gains, "v"), (cosine, "v"), (sine, "v"),
         (wproj, "a"), (wlift, "a"), (wdown, "a"),
         *[(array, "a") for array in (q, k, v, p, h2, left, right)]],
        [(*item, "a") for item in BACK_OUT] + [((1, D), F32)] + GRADS_OUT,
        [WPROJ, WLIFT, WDOWN, pltpu.VMEM((OWN, D), BF16)]
        + scratch(SAVED[:4] + SAVED[5:6] + SAVED[7:] + BACK_OUT) + [sems(14)],
        3_000_000_000, 40,
    )
    from_low, from_high = swap_halos(to_low, to_high)
    rest_keep, rest_send = call(
        weight_grad_kernel, "weight_grads",
        [(index, "s"), (m_act, "v"), (grad_low, "v"), (b, "v"), (du, "v"), (o, "v"), (gb, "v")],
        [((SHARDS, 192, WIDE), BF16, "a")] * 2,
        [WDOWN, WLIFT, WPROJ, pltpu.VMEM((16, WIDE), BF16), sems(64)],
        1_600_000_000,
    )
    from_low, from_high, rest_send = lax.optimization_barrier((from_low, from_high, rest_send))
    rest_other = swap_core(rest_send)
    in_grad, qkv_keep, qkv_send = call(
        source_grad_kernel, "layer_source_grads",
        [(index, "s"), (src, "v"), (gains, "v"), (dh2, "v"), (dq, "v"), (dkv, "v"), (from_low, "v"),
         (from_high, "v"), (mlp_gain_grad, "v"), (wqkv, "a")],
        [stream, ((SHARDS, 96, 2432), BF16, "a"), ((SHARDS, 96, 2432), BF16, "a")],
        [WQKV, pltpu.VMEM((OWN, WIDE), BF16), WQKV, pltpu.VMEM((SHARDS, 96, 128), BF16), sems(17)],
        1_800_000_000,
    )
    qkv_other = swap_core(qkv_send)

    rest_z = call(
        rest_core_kernel, "rest_core_sum", [(index, "s"), (rest_keep, "v"), (rest_other, "v")],
        [((SHARDS, 48, WIDE), BF16)] * 4, [], 0, 24,
    )
    qkv_keep, _ = lax.optimization_barrier((qkv_keep, rest_z[0]))
    qkv_y = call(
        qkv_core_kernel, "qkv_core_sum", [(index, "s"), (qkv_keep, "v"), (qkv_other, "v")],
        [((96, 2432), BF16)] * 4, [], 0, 24,
    )
    (some,) = call(
        partial_kernel, "qkv_y_first", [(qkv_y[0], "v"), (along_y(qkv_y[1], 1), "v")],
        [((96, 2432), F32)], [], 0, 24,
    )
    rest_mine, some = lax.optimization_barrier((rest_z[0], some))
    rest_y = call(
        rest_z_kernel, "rest_z_sum",
        [(index, "s"), (rest_mine, "v"), *[(along_z(rest_z[d], d), "v") for d in (1, 2, 3)]],
        [((48, WIDE), BF16)] * 4, [], 0, 24,
    )
    qkv_z = call(
        qkv_y_kernel, "qkv_y_sum",
        [(index, "s"), (some, "v"), *[(along_y(qkv_y[d], d), "v") for d in (2, 3)]],
        [((48, 1280), BF16)] * 4, [pltpu.VMEM((96, 2432), BF16)], 0, 24,
    )
    (joint,) = call(
        joint_kernel, "joint_sum",
        [(rest_y[0], "v"), *[(along_y(rest_y[d], d), "v") for d in (1, 2, 3)],
         (qkv_z[0], "v"), *[(along_z(qkv_z[d], d), "v") for d in (1, 2, 3)]],
        [((48, 3584), BF16)], [], 0, 24,
    )
    (joint,) = call(
        pair_kernel, "pair_sum", [(joint, "v"), (swap_x(joint), "v")], [((48, 3584), BF16)], [], 0, 24
    )
    mine = [joint] + [along_z(joint, d) for d in (1, 2, 3)]
    theirs = [swap_core(piece) for piece in mine]
    qkv_sum, proj_sum, lift_sum, down_sum, gain_sums = call(
        final_kernel, "final_shard", [(index, "s"), *[(piece, "v") for piece in mine + theirs]],
        [((192, WIDE), F32), ((192, D), F32), ((192, WIDE), F32), ((288, D), F32), ((16, 128), F32)],
        [pltpu.VMEM((2, 192, WIDE), BF16)], 0, 24,
    )
    return (
        h3[None, :, None],
        in_grad[None, :, None],
        gain_sums[0:2].reshape(1, 256)[:, :192],
        qkv_sum[None],
        proj_sum[None],
        gain_sums[2:4].reshape(1, 256)[:, :192],
        lift_sum[None],
        down_sum[None],
    )


def solution(mesh):
    placed = (
        P(None, "fsdp", "ctx", None),
        P(None, "fsdp", "ctx", None),
        P(None, "fsdp", None),
        P("section", "fsdp"),
        P("section", "fsdp", None),
        P("section", "fsdp", None),
        P("section", "fsdp"),
        P("section", "fsdp", None),
        P("section", "fsdp", None),
    )
    return jax.shard_map(
        body,
        mesh=mesh,
        in_specs=placed,
        out_specs=(
            P("section", None, "fsdp", "ctx", None),
            P("section", None, "fsdp", "ctx", None),
            P("section", "fsdp"),
            P("section", "fsdp", None),
            P("section", "fsdp", None),
            P("section", "fsdp"),
            P("section", "fsdp", None),
            P("section", "fsdp", None),
        ),
        check_vma=False,
    )
```
